128 devices in a mesh: dp: 8 (over x, z_lo), strip: 16 (over z_hi, y, core).
Axes of the slice: x: 4, y: 4, z: 4 (z_hi: 2, z_lo: 2; z = z_hi * 2 + z_lo), core: 2. Of those that a mesh axis runs over, the one named last changes fastest.
Arguments:
- block_in: bfloat16 [32, 16, 128, 640], P('dp', 'strip'), may hold values from -30 to 30
- upstream: bfloat16 [32, 16, 128, 640], P('dp', 'strip'), may hold values from -6 to 6
- gn_gain: float32 [640], replicated, may hold values from 0.25 to 1.75
- gn_bias: float32 [640], replicated, may hold values from -3 to 3
- conv_weight: bfloat16 [3, 3, 640, 640], replicated, may hold values from -0.078125 to 0.078125
- conv_bias: float32 [640], replicated, may hold values from -3 to 3
- ln_gain: float32 [640], replicated, may hold values from 0.25 to 1.75
- ln_bias: float32 [640], replicated, may hold values from -2 to 2
- w_query: bfloat16 [640, 640], replicated, may hold values from -0.3125 to 0.3125
- w_key: bfloat16 [640, 640], replicated, may hold values from -0.3125 to 0.3125
- w_value: bfloat16 [640, 640], replicated, may hold values from -0.25 to 0.25
- w_out: bfloat16 [640, 640], replicated, may hold values from -0.625 to 0.625
- out_bias: float32 [640], replicated, may hold values from -3 to 3
Outputs:
- block_out: bfloat16 [32, 16, 128, 640], P('dp', 'strip')
- grad_input: bfloat16 [32, 16, 128, 640], P('dp', 'strip')
- grad_conv_weight: float32 [3, 3, 640, 640], P(None, None, None, ('dp', 'strip'))
- grad_query: float32 [640, 640], P(None, ('dp', 'strip'))
- grad_key: float32 [640, 640], P(None, ('dp', 'strip'))
- grad_value: float32 [640, 640], P(None, ('dp', 'strip'))
- grad_out_proj: float32 [640, 640], P(None, ('dp', 'strip'))
- grad_gn_gain: float32 [640], P(('dp', 'strip'))
- grad_gn_bias: float32 [640], P(('dp', 'strip'))
- grad_conv_bias: float32 [640], P(('dp', 'strip'))
- grad_ln_gain: float32 [640], P(('dp', 'strip'))
- grad_ln_bias: float32 [640], P(('dp', 'strip'))
- grad_out_bias: float32 [640], P(('dp', 'strip'))
The draws below stay inside these ranges and needn't reach their ends.
All inputs are finite; a program needn't handle non-finite values.
Results may differ from the reference program's by a relative error of at most 0.022.
Values may be sent and summed in bfloat16 or wider, within the bound.
No kernel may reach another device: no remote copies, remote signals or barrier semaphores. Data moves between devices by JAX's collectives and lax.ppermute only.
A program may use at most 192 MiB of HBM per device.

```python
import math
import jax
import jax.numpy as jnp
from jax import lax

C = 640
HEADS = 8
GROUPS = 32
W = 128
ROWS = 16
CELLS = 2048
BATCH = 32


def draw_block_in(key, part):
    key = jax.random.fold_in(key, 7)
    noise_key = jax.random.fold_in(key, 0)
    channel_key = jax.random.fold_in(key, 1)
    row_key = jax.random.fold_in(key, 3)
    offset_key = jax.random.fold_in(key, 4)
    shape = (BATCH, ROWS, W, C)
    position = jnp.arange(ROWS, dtype=jnp.float32) / max(ROWS - 1, 1)
    jitter = jax.random.uniform(row_key, (BATCH, ROWS), jnp.float32, -0.35, 0.35)
    noise = jnp.clip(jax.random.normal(noise_key, shape, jnp.float32), -4.0, 4.0) * 0.7
    offset = jnp.clip(jax.random.normal(offset_key, (BATCH, ROWS, 1, GROUPS, 1), jnp.float32), -4.0, 4.0) * 0.7
    trend = 10.0 ** (0.6 * (position - 0.5))
    channel_factor = 10.0 ** jax.random.uniform(channel_key, (C,), jnp.float32, -0.35, 0.35)
    base = (noise.reshape(BATCH, ROWS, W, GROUPS, C // GROUPS) + offset).reshape(shape)
    row_factor = trend[None, :] * 10.0 ** jitter
    values = base * row_factor[:, :, None, None] * channel_factor
    return jnp.clip(values, -30.0, 30.0).astype(jnp.bfloat16)


def draw_upstream(key, part):
    key = jax.random.fold_in(key, 11)
    noise_key, offset_key = jax.random.split(key, 2)
    shape = (BATCH, ROWS, W, C)
    noise = jnp.clip(jax.random.normal(noise_key, shape, jnp.float32), -4.0, 4.0) * 0.8
    offset = jnp.clip(jax.random.normal(offset_key, (BATCH, 1, 1, C), jnp.float32), -3.0, 3.0) * 0.7
    return jnp.clip(noise + offset, -6.0, 6.0).astype(jnp.bfloat16)


def gaussian(rng, extent, scale, bound, kind=jnp.bfloat16):
    return jnp.clip(scale * jax.random.normal(rng, extent, jnp.float32), -bound, bound).astype(kind)


def setup_inputs(seed: int = 0) -> dict:
    seeds = jax.random.split(jax.random.key(seed), 14)
    block_in = draw_block_in(jax.random.fold_in(seeds[13], 71), 0)
    upstream = draw_upstream(jax.random.fold_in(seeds[13], 71), 0)
    gn_gain = jnp.clip(1.0 + 0.15 * jax.random.normal(seeds[2], (C,), jnp.float32), 0.25, 1.75)
    gn_bias = gaussian(seeds[3], (C,), 0.5, 3.0, jnp.float32)
    conv_weight = gaussian(seeds[4], (3, 3, C, C), (9 * C) ** -0.5, 0.078125)
    conv_bias = gaussian(seeds[5], (C,), 0.5, 3.0, jnp.float32)
    ln_gain = jnp.clip(1.0 + 0.15 * jax.random.normal(seeds[6], (C,), jnp.float32), 0.25, 1.75)
    ln_bias = gaussian(seeds[7], (C,), 0.3, 2.0, jnp.float32)
    w_query = gaussian(seeds[8], (C, C), (C // 2) ** -0.5, 0.3125)
    w_key = gaussian(seeds[9], (C, C), (C // 2) ** -0.5, 0.3125)
    w_value = gaussian(seeds[10], (C, C), C ** -0.5, 0.25)
    w_out = gaussian(seeds[11], (C, C), (C // 8) ** -0.5, 0.625)
    out_bias = gaussian(seeds[12], (C,), 0.5, 3.0, jnp.float32)
    return dict(block_in=block_in, upstream=upstream, gn_gain=gn_gain, gn_bias=gn_bias, conv_weight=conv_weight, conv_bias=conv_bias, ln_gain=ln_gain, ln_bias=ln_bias, w_query=w_query, w_key=w_key, w_value=w_value, w_out=w_out, out_bias=out_bias)


EPSILON = 1e-05

def silu_slope(value):
    sigma = jax.nn.sigmoid(value)
    return sigma * (1.0 + value * (1.0 - sigma))

def forward_item(tensors):
    query_t, key_t, value_t = tensors
    head_dim = query_t.shape[0]
    length = query_t.shape[1]
    block_rows = math.gcd(length, 512)
    factor = 1.0 / math.sqrt(head_dim)

    def one_block(offset):
        query_block = lax.dynamic_slice_in_dim(query_t, offset, block_rows, 1)
        scores = jnp.dot(query_block.T, key_t, preferred_element_type=jnp.float32) * factor
        raised = jnp.exp(scores)
        probs = (raised / lax.optimization_barrier(jnp.sum(raised, axis=1, keepdims=True))).astype(jnp.bfloat16)
        return jnp.dot(value_t, probs.T, preferred_element_type=jnp.float32).astype(jnp.bfloat16)
    offsets = jnp.arange(length // block_rows, dtype=jnp.int32) * block_rows
    pieces = lax.map(one_block, offsets)
    return jnp.transpose(pieces, (1, 0, 2)).reshape(head_dim, length)

def backward_item(tensors):
    query_t, key_t, value_t, out_t, grad_t = tensors
    head_dim = query_t.shape[0]
    length = query_t.shape[1]
    block_rows = math.gcd(length, 512)
    factor = 1.0 / math.sqrt(head_dim)
    delta_all = lax.optimization_barrier(jnp.sum(grad_t.astype(jnp.float32) * out_t.astype(jnp.float32), axis=0))

    def step(carry, offset):
        key_acc, value_acc = carry
        query_block = lax.dynamic_slice_in_dim(query_t, offset, block_rows, 1)
        grad_block = lax.dynamic_slice_in_dim(grad_t, offset, block_rows, 1)
        delta = lax.dynamic_slice_in_dim(delta_all, offset, block_rows, 0)
        scores = jnp.dot(query_block.T, key_t, preferred_element_type=jnp.float32) * factor
        raised = jnp.exp(scores)
        weights = raised / lax.optimization_barrier(jnp.sum(raised, axis=1, keepdims=True))
        probs = weights.astype(jnp.bfloat16)
        value_acc = value_acc + jnp.dot(grad_block, probs, preferred_element_type=jnp.float32)
        prob_grad = jnp.dot(grad_block.T, value_t, preferred_element_type=jnp.float32)
        score_grad = (weights * (prob_grad - delta[:, None]) * factor).astype(jnp.bfloat16)
        query_part = jnp.dot(key_t, score_grad.T, preferred_element_type=jnp.float32).astype(jnp.bfloat16)
        key_acc = key_acc + jnp.dot(query_block, score_grad, preferred_element_type=jnp.float32)
        return ((key_acc, value_acc), query_part)
    offsets = jnp.arange(length // block_rows, dtype=jnp.int32) * block_rows
    empty = jnp.zeros((head_dim, length), jnp.float32)
    (key_acc, value_acc), query_parts = lax.scan(step, (empty, empty), offsets)
    query_grad = jnp.transpose(query_parts, (1, 0, 2)).reshape(head_dim, length)
    return (query_grad, key_acc.astype(jnp.bfloat16), value_acc.astype(jnp.bfloat16))

def reference(block_in, upstream, gn_gain, gn_bias, conv_weight, conv_bias, ln_gain, ln_bias, w_query, w_key, w_value, w_out, out_bias):
    per_group = C // GROUPS
    head_dim = C // HEADS
    x_float = block_in.astype(jnp.float32)
    grouped = x_float.reshape(BATCH, ROWS, W, GROUPS, per_group)
    group_mean = lax.optimization_barrier(jnp.mean(grouped, axis=(1, 2, 4), keepdims=True))
    centered = grouped - group_mean
    group_var = lax.optimization_barrier(jnp.mean(centered * centered, axis=(1, 2, 4), keepdims=True))
    group_scale = lax.rsqrt(group_var + EPSILON)
    x_standard = (centered * group_scale).reshape(BATCH, ROWS, W, C)
    activation_in = x_standard * gn_gain + gn_bias
    hidden = jax.nn.silu(activation_in).astype(jnp.bfloat16)
    padded = jnp.pad(hidden, ((0, 0), (1, 1), (1, 1), (0, 0)))
    conv_out = lax.conv_general_dilated(padded, conv_weight, (1, 1), 'VALID', dimension_numbers=('NHWC', 'HWIO', 'NHWC'), preferred_element_type=jnp.float32)
    residual = (x_float + conv_out + conv_bias).astype(jnp.bfloat16)
    tokens = residual.astype(jnp.float32).reshape(BATCH, CELLS, C)
    deviation = tokens - lax.optimization_barrier(jnp.mean(tokens, axis=2, keepdims=True))
    token_scale = lax.rsqrt(lax.optimization_barrier(jnp.mean(deviation * deviation, axis=2, keepdims=True)) + EPSILON)
    token_standard = deviation * token_scale
    normed = (token_standard * ln_gain + ln_bias).astype(jnp.bfloat16)
    normed_float = normed.astype(jnp.float32)
    projections = jnp.stack([w_query, w_key, w_value]).astype(jnp.float32)
    projected = jnp.einsum('btc,sck->sbkt', normed_float, projections).astype(jnp.bfloat16)
    items = projected.reshape(3, BATCH * HEADS, head_dim, CELLS)
    attended = lax.map(forward_item, (items[0], items[1], items[2]))
    attended_tokens = attended.reshape(BATCH, C, CELLS)
    attended_float = attended_tokens.astype(jnp.float32)
    mixed = jnp.einsum('bct,cd->btd', attended_float, w_out.astype(jnp.float32))
    block_out = (tokens + mixed + out_bias).astype(jnp.bfloat16).reshape(BATCH, ROWS, W, C)
    gscale = 1.0 / math.sqrt(BATCH * CELLS)
    upstream_float = upstream.reshape(BATCH, CELLS, C).astype(jnp.float32)
    grad_out_proj = gscale * jnp.einsum('bct,btd->cd', attended_float, upstream_float)
    grad_out_bias = gscale * lax.optimization_barrier(jnp.sum(upstream_float, axis=(0, 1)))
    attended_grad = jnp.einsum('btd,cd->bct', upstream_float, w_out.astype(jnp.float32)).astype(jnp.bfloat16)
    grad_items = attended_grad.reshape(BATCH * HEADS, head_dim, CELLS)
    query_grad, key_grad, value_grad = lax.map(backward_item, (items[0], items[1], items[2], attended, grad_items))
    proj_grads = jnp.stack([query_grad, key_grad, value_grad]).reshape(3, BATCH, C, CELLS).astype(jnp.float32)
    grad_proj = gscale * jnp.einsum('btc,sbkt->sck', normed_float, proj_grads)
    normed_grad = jnp.einsum('sbkt,sck->btc', proj_grads, projections)
    grad_ln_gain = gscale * lax.optimization_barrier(jnp.sum(normed_grad * token_standard, axis=(0, 1)))
    grad_ln_bias = gscale * lax.optimization_barrier(jnp.sum(normed_grad, axis=(0, 1)))
    scaled = normed_grad * ln_gain
    tokens_grad = token_scale * (scaled - lax.optimization_barrier(jnp.mean(scaled, axis=2, keepdims=True)) - token_standard * lax.optimization_barrier(jnp.mean(scaled * token_standard, axis=2, keepdims=True)))
    residual_grad = (upstream_float + tokens_grad).astype(jnp.bfloat16).reshape(BATCH, ROWS, W, C)
    residual_float = residual_grad.astype(jnp.float32)
    grad_conv_bias = gscale * lax.optimization_barrier(jnp.sum(residual_float, axis=(0, 1, 2)))
    taps = []
    for tap_row in range(3):
        for tap_col in range(3):
            window = padded[:, tap_row:tap_row + ROWS, tap_col:tap_col + W, :].astype(jnp.float32)
            taps.append(jnp.einsum('nijc,nijd->cd', window, residual_float))
    grad_conv_weight = gscale * jnp.stack(taps).reshape(3, 3, C, C)
    grad_padded = jnp.pad(residual_grad, ((0, 0), (1, 1), (1, 1), (0, 0)))
    hidden_grad = lax.conv_general_dilated(grad_padded, jnp.flip(conv_weight, (0, 1)), (1, 1), 'VALID', dimension_numbers=('NHWC', 'HWOI', 'NHWC'), preferred_element_type=jnp.float32)
    activation_grad = hidden_grad * silu_slope(activation_in)
    grad_gn_gain = gscale * lax.optimization_barrier(jnp.sum(activation_grad * x_standard, axis=(0, 1, 2)))
    grad_gn_bias = gscale * lax.optimization_barrier(jnp.sum(activation_grad, axis=(0, 1, 2)))
    spread = (activation_grad * gn_gain).reshape(BATCH, ROWS, W, GROUPS, per_group)
    standard_grouped = x_standard.reshape(BATCH, ROWS, W, GROUPS, per_group)
    input_part = group_scale * (spread - lax.optimization_barrier(jnp.mean(spread, axis=(1, 2, 4), keepdims=True)) - standard_grouped * lax.optimization_barrier(jnp.mean(spread * standard_grouped, axis=(1, 2, 4), keepdims=True)))
    grad_input = (residual_float + input_part.reshape(BATCH, ROWS, W, C)).astype(jnp.bfloat16)
    return (block_out, grad_input, grad_conv_weight, grad_proj[0], grad_proj[1], grad_proj[2], grad_out_proj, grad_gn_gain, grad_gn_bias, grad_conv_bias, grad_ln_gain, grad_ln_bias, grad_out_bias)
```

```python
import functools
import math

import jax
import jax.numpy as jnp
import numpy as np
from jax import lax
from jax.experimental import pallas as pl
from jax.experimental.pallas import tpu as pltpu
from jax.sharding import PartitionSpec as P

HEADS = 8
GROUPS = 32
EPSILON = 1e-05
F32 = jnp.float32
BF16 = jnp.bfloat16
NT = (((1,), (1,)), ((), ()))
HIGH = lax.Precision.HIGHEST
VMEM_LIMIT = 56 * 1024 * 1024
LOG2E = math.log2(math.e)
QUERY_BLOCK = 256
KEY_CHUNK = 512
ORDERS = (("y", "x", "z"), ("x", "z", "y"), ("z", "y", "x"))
LEFT = (0, 0, 0, 3, 1, 1, 1, 4, 6, 2, 2, 2, 5)
RIGHT = (0, 1, 2, 3, 0, 1, 2, 3, 4, 0, 1, 2, 3)
PARTS = ((0, 4), (4, 5), (9, 4))


def params(semantics=None):
    if semantics is None:
        return pltpu.CompilerParams(vmem_limit_bytes=VMEM_LIMIT)
    return pltpu.CompilerParams(
        vmem_limit_bytes=VMEM_LIMIT, dimension_semantics=semantics
    )


def mm(a, b):
    return jnp.dot(a, b, preferred_element_type=F32)


def mm_nt(a, b):
    return lax.dot_general(a, b, NT, preferred_element_type=F32)


def group_sum(rows, expand):
    return lax.dot_general(rows, expand, NT, preferred_element_type=F32, precision=HIGH)


def spread(rows, expand):
    return jnp.dot(rows, expand, preferred_element_type=F32, precision=HIGH)


def expand_matrix(channels):
    per_group = channels // GROUPS
    return jnp.asarray(
        np.arange(channels)[None, :] // per_group == np.arange(GROUPS)[:, None], F32
    )


def shift_rows(value, down):
    count = value.shape[0]
    row = lax.broadcasted_iota(jnp.int32, value.shape, 0)
    if down == 1:
        return jnp.where(row == 0, 0.0, pltpu.roll(value, 1, 0))
    return jnp.where(row == count - 1, 0.0, pltpu.roll(value, count - 1, 0))


def cost(flops, nbytes, trans=0):
    return pl.CostEstimate(flops=int(flops), bytes_accessed=int(nbytes), transcendentals=int(trans))


def stats_kernel(x_ref, expand_ref, out_ref):
    images, cells, channels = x_ref.shape
    count = cells * (channels // GROUPS)
    expand = expand_ref[...]
    sums = jnp.concatenate(
        [jnp.sum(x_ref[n].astype(F32), axis=0, keepdims=True) for n in range(images)], axis=0
    )
    mean = group_sum(sums, expand) / count
    mean_c = spread(mean, expand)
    squares = []
    for n in range(images):
        d = x_ref[n].astype(F32) - mean_c[n : n + 1]
        squares.append(jnp.sum(d * d, axis=0, keepdims=True))
    m2 = group_sum(jnp.concatenate(squares, axis=0), expand)
    both = jnp.concatenate([mean, m2], axis=0)
    for s in range(out_ref.shape[0]):
        out_ref[s] = both


def local_stats(x, expand, strips):
    images = x.shape[0]
    return pl.pallas_call(
        stats_kernel,
        out_shape=jax.ShapeDtypeStruct((strips, 2 * images, GROUPS), F32),
        compiler_params=params(),
        name="local_stats",
    )(x, expand)


def upstream_kernel(up_ref, w_ref, g_ref):
    images = up_ref.shape[0]
    w = w_ref[...]
    hd = w.shape[0] // HEADS
    for n in range(images):
        g = mm_nt(w, up_ref[n])
        for h in range(HEADS):
            g_ref[n // 2, (n % 2) * HEADS + h, 0] = g[h * hd : (h + 1) * hd].astype(BF16)


def upstream_heads(up, w_out):
    images, cells, channels = up.shape
    return pl.pallas_call(
        upstream_kernel,
        out_shape=jax.ShapeDtypeStruct(
            (images // 2, 2 * HEADS, 1, channels // HEADS, cells), BF16
        ),
        compiler_params=params(),
        cost_estimate=cost(2 * images * cells * channels**2, 2.2e6),
        name="upstream_heads",
    )(up, w_out)


def forward_kernel(
    stats_ref,
    flags_ref,
    expand_ref,
    up_ref,
    x_ref,
    down_ref,
    vec_ref,
    conv_ref,
    wq_ref,
    wk_ref,
    wv_ref,
    hidden_ref,
    residual_ref,
    normed_ref,
    qkv_ref,
    chan_ref,
    acc_ref,
):
    step = pl.program_id(0)
    images, cells, channels = x_ref.shape
    hd = channels // HEADS

    @pl.when(step == 0)
    def _():
        strips = stats_ref.shape[0]
        count = cells * (channels // GROUPS)
        got = stats_ref[...]
        means = got[:, :images]
        mean = jnp.sum(means, axis=0) / strips
        off = means - mean[None]
        m2 = jnp.sum(got[:, images:], axis=0) + count * jnp.sum(off * off, axis=0)
        scale = lax.rsqrt(m2 / (count * strips) + EPSILON)
        expand = expand_ref[...]
        mean_c = spread(mean, expand)
        scale_c = spread(scale, expand)
        chan_ref[...] = jnp.concatenate([mean_c, scale_c], axis=0)
        gain = vec_ref[0:1]
        bias = vec_ref[1:2]
        for a, ref in enumerate((up_ref, x_ref, down_ref)):
            for n in range(images):
                u = (ref[n].astype(F32) - mean_c[n : n + 1]) * scale_c[n : n + 1]
                u = u * gain + bias
                h = u / (1.0 + jnp.exp(-u))
                if a != 1:
                    h = jnp.where(flags_ref[a // 2] > 0, h, 0.0)
                hidden_ref[a, n * cells : (n + 1) * cells] = h.astype(BF16)

    total = mm(hidden_ref[0], conv_ref[0, 0])
    total += mm(hidden_ref[1], conv_ref[1, 0])
    total += mm(hidden_ref[2], conv_ref[2, 0])

    @pl.when(step == 0)
    def _():
        for n in range(images):
            sl = slice(n * cells, (n + 1) * cells)
            acc_ref[sl] = shift_rows(total[sl], 1)

    @pl.when(step == 1)
    def _():
        acc_ref[...] += total

    @pl.when(step == 2)
    def _():
        factor = LOG2E / math.sqrt(hd)
        for n in range(images):
            sl = slice(n * cells, (n + 1) * cells)
            conv = acc_ref[sl] + shift_rows(total[sl], -1)
            residual = (x_ref[n].astype(F32) + conv + vec_ref[2:3]).astype(BF16)
            residual_ref[sl] = residual
            tokens = residual.astype(F32)
            dev = tokens - jnp.mean(tokens, axis=1, keepdims=True)
            scale = lax.rsqrt(jnp.mean(dev * dev, axis=1, keepdims=True) + EPSILON)
            normed_ref[sl] = (dev * scale * vec_ref[3:4] + vec_ref[4:5]).astype(BF16)
        normed = normed_ref[...]
        for t, ref in enumerate((wq_ref, wk_ref, wv_ref)):
            out = mm(normed, ref[...])
            if t == 0:
                out = out * factor
            for n in range(images):
                flipped = out[n * cells : (n + 1) * cells].T.astype(BF16)
                for h in range(HEADS):
                    qkv_ref[n // 2, (n % 2) * HEADS + h, t] = flipped[h * hd : (h + 1) * hd]


def forward(stats, flags, expand, up, x, down, vec, conv_weight, wq, wk, wv):
    images, cells, channels = x.shape
    tokens = images * cells
    hd = channels // HEADS
    full = lambda shape: pl.BlockSpec(shape, lambda b: (0,) * len(shape))
    square = (channels, channels)
    return pl.pallas_call(
        forward_kernel,
        grid=(3,),
        in_specs=[
            full(stats.shape),
            pl.BlockSpec(memory_space=pltpu.SMEM),
            full(expand.shape),
            full(x.shape),
            full(x.shape),
            full(x.shape),
            full(vec.shape),
            pl.BlockSpec((3, 1) + square, lambda b: (0, b, 0, 0)),
            full(square),
            full(square),
            full(square),
        ],
        out_specs=[
            full((3, tokens, channels)),
            full((tokens, channels)),
            full((tokens, channels)),
            full((images // 2, 2 * HEADS, 3, hd, cells)),
            full((2 * images, channels)),
        ],
        out_shape=[
            jax.ShapeDtypeStruct((3, tokens, channels), BF16),
            jax.ShapeDtypeStruct((tokens, channels), BF16),
            jax.ShapeDtypeStruct((tokens, channels), BF16),
            jax.ShapeDtypeStruct((images // 2, 2 * HEADS, 3, hd, cells), BF16),
            jax.ShapeDtypeStruct((2 * images, channels), F32),
        ],
        scratch_shapes=[pltpu.VMEM((tokens, channels), F32)],
        compiler_params=params(),
        cost_estimate=cost(24 * tokens * channels**2, 16e6, 1e6),
        name="forward_conv",
    )(stats, flags, expand, up, x, down, vec, conv_weight, wq, wk, wv)


def attention_kernel(
    qkv_ref, g_ref, out_ref, kt_ref, vt_ref, kn_ref, vn_ref, s_ref, e_ref, dk_ref, dv_ref
):
    step = pl.program_id(0)
    sources, _, hd, cells = qkv_ref.shape
    length = sources * cells
    wide = kn_ref.shape[1]
    block = s_ref.shape[1]
    per = block // cells
    chunk = min(KEY_CHUNK, length)
    chunks = length // chunk
    extra = vt_ref.shape[0] - hd

    @pl.when(step == 0)
    def _():
        ones_row = (lax.broadcasted_iota(jnp.int32, (extra, cells), 0) == 0).astype(F32)
        pad = jnp.zeros((wide - hd, cells), F32)
        row = lax.broadcasted_iota(jnp.int32, (wide - hd, cells), 0)
        ones_two = (row < 2).astype(F32)
        for s in range(sources):
            sl = slice(s * cells, (s + 1) * cells)
            k = qkv_ref[s, 1]
            v = qkv_ref[s, 2]
            kt_ref[:, sl] = k
            vt_ref[:hd, sl] = v
            vt_ref[hd:, sl] = ones_row.astype(BF16)
            kn_ref[sl] = jnp.concatenate([k.astype(F32), pad], axis=0).T.astype(BF16)
            vn_ref[sl] = jnp.concatenate([v.astype(F32), ones_two], axis=0).T.astype(BF16)
        dk_ref[...] = jnp.zeros_like(dk_ref)
        dv_ref[...] = jnp.zeros_like(dv_ref)

    base = step * per
    q = jnp.concatenate([qkv_ref[base + u, 0] for u in range(per)], axis=1).astype(F32)
    q_wide = jnp.concatenate([q, jnp.zeros((wide - hd, block), F32)], axis=0)
    q_t = q_wide.astype(BF16)
    q_n = q_wide.T.astype(BF16)
    top = None
    for c in range(chunks):
        sl = slice(c * chunk, (c + 1) * chunk)
        scores = mm(kn_ref[sl], q_t)
        s_ref[sl] = scores
        here = jnp.max(scores, axis=0, keepdims=True)
        top = here if top is None else jnp.maximum(top, here)
    acc = jnp.zeros((hd + extra, block), F32)
    for c in range(chunks):
        sl = slice(c * chunk, (c + 1) * chunk)
        e = jnp.exp2(s_ref[sl] - top).astype(BF16)
        e_ref[sl] = e
        acc += mm(vt_ref[:, sl], e)
    inverse = 1.0 / acc[hd : hd + 1]
    out = acc[:hd] * inverse
    g = jnp.concatenate([g_ref[base + u, 0] for u in range(per)], axis=1).astype(F32)
    g_scaled = (g * inverse).astype(BF16).astype(F32)
    delta = -jnp.sum(g_scaled * out, axis=0, keepdims=True)
    high = delta.astype(BF16).astype(F32)
    low = (delta - high).astype(BF16).astype(F32)
    row = lax.broadcasted_iota(jnp.int32, (wide - hd, block), 0)
    tail = jnp.where(row == 0, high, jnp.where(row == 1, low, 0.0))
    g_wide = jnp.concatenate([g_scaled, tail], axis=0)
    g_t = g_wide.astype(BF16)
    g_n = g_wide.T.astype(BF16)
    dq = jnp.zeros((hd, block), F32)
    for c in range(chunks):
        sl = slice(c * chunk, (c + 1) * chunk)
        e = e_ref[sl]
        ds = (e.astype(F32) * mm(vn_ref[sl], g_t)).astype(BF16)
        dq += mm(kt_ref[:, sl], ds)
        dk_ref[sl] += mm(ds, q_n)
        dv_ref[sl] += mm(e, g_n)
    out = out.astype(BF16)
    dq = (dq * (1.0 / math.sqrt(hd))).astype(BF16)
    for u in range(per):
        out_ref[base + u, 0] = out[:, u * cells : (u + 1) * cells]
        out_ref[base + u, 1] = dq[:, u * cells : (u + 1) * cells]

    @pl.when(step == pl.num_programs(0) - 1)
    def _():
        for s in range(sources):
            sl = slice(s * cells, (s + 1) * cells)
            out_ref[s, 2] = (dk_ref[sl].T[:hd] * (1.0 / LOG2E)).astype(BF16)
            out_ref[s, 3] = dv_ref[sl].T[:hd].astype(BF16)


def attention(qkv, g):
    sources, _, hd, cells = qkv.shape
    length = sources * cells
    block = QUERY_BLOCK
    wide = 128
    full = lambda shape: pl.BlockSpec(shape, lambda i: (0,) * len(shape))
    return pl.pallas_call(
        attention_kernel,
        grid=(length // block,),
        in_specs=[full(qkv.shape), full(g.shape)],
        out_specs=full((sources, 4, hd, cells)),
        out_shape=jax.ShapeDtypeStruct((sources, 4, hd, cells), BF16),
        scratch_shapes=[
            pltpu.VMEM((hd, length), BF16),
            pltpu.VMEM((hd + 16, length), BF16),
            pltpu.VMEM((length, wide), BF16),
            pltpu.VMEM((length, wide), BF16),
            pltpu.VMEM((length, block), F32),
            pltpu.VMEM((length, block), BF16),
            pltpu.VMEM((length, wide), F32),
            pltpu.VMEM((length, wide), F32),
        ],
        compiler_params=params(),
        cost_estimate=cost(12 * length * length * 256, 5e6, length * length),
        name="attention",
    )(qkv, g)


def tokens_kernel(
    got_ref,
    residual_ref,
    up_ref,
    vec_ref,
    wo_ref,
    wq_ref,
    wk_ref,
    wv_ref,
    block_out_ref,
    rg_ref,
    heads_ref,
    sums_ref,
):
    hd = got_ref.shape[2]
    cells = got_ref.shape[3]
    for n in range(2):
        for h in range(HEADS):
            for t in range(4):
                heads_ref[t, h * hd : (h + 1) * hd, n * cells : (n + 1) * cells] = got_ref[
                    n * HEADS + h, t
                ]
    residual = residual_ref[...].astype(F32)
    up = up_ref[...].astype(F32)
    mixed = mm(heads_ref[0].T, wo_ref[...])
    block_out_ref[...] = (residual + mixed + vec_ref[5:6]).astype(BF16)
    grad = mm_nt(heads_ref[1].T, wq_ref[...])
    grad += mm_nt(heads_ref[2].T, wk_ref[...])
    grad += mm_nt(heads_ref[3].T, wv_ref[...])
    dev = residual - jnp.mean(residual, axis=1, keepdims=True)
    scale = lax.rsqrt(jnp.mean(dev * dev, axis=1, keepdims=True) + EPSILON)
    standard = dev * scale
    scaled = grad * vec_ref[3:4]
    part = scale * (
        scaled
        - jnp.mean(scaled, axis=1, keepdims=True)
        - standard * jnp.mean(scaled * standard, axis=1, keepdims=True)
    )
    rg = (up + part).astype(BF16)
    rg_ref[...] = rg
    sums_ref[0:1] = jnp.sum(rg.astype(F32), axis=0, keepdims=True)
    sums_ref[1:2] = jnp.sum(grad * standard, axis=0, keepdims=True)
    sums_ref[2:3] = jnp.sum(grad, axis=0, keepdims=True)
    sums_ref[3:4] = jnp.sum(up, axis=0, keepdims=True)


def after_attention(got, residual, up, vec, wo, wq, wk, wv, part):
    channels = residual.shape[1]
    cells = got.shape[3]
    tokens = 2 * cells
    full = lambda shape: pl.BlockSpec(shape, lambda i: (0,) * len(shape))
    rows = pl.BlockSpec((tokens, channels), lambda i: (part, 0))
    square = (channels, channels)
    return pl.pallas_call(
        tokens_kernel,
        grid=(1,),
        in_specs=[full(got.shape), rows, rows, full(vec.shape)] + [full(square)] * 4,
        out_specs=[
            full((tokens, channels)),
            full((tokens, channels)),
            full((4, channels, tokens)),
            full((4, channels)),
        ],
        out_shape=[
            jax.ShapeDtypeStruct((tokens, channels), BF16),
            jax.ShapeDtypeStruct((tokens, channels), BF16),
            jax.ShapeDtypeStruct((4, channels, tokens), BF16),
            jax.ShapeDtypeStruct((4, channels), F32),
        ],
        compiler_params=params(),
        cost_estimate=cost(8 * tokens * channels**2, 7e6),
        name="after_attention",
    )(got, residual, up, vec, wo, wq, wk, wv)


def weights_kernel(
    gscale,
    cells,
    table_ref,
    perm_ref,
    hidden_ref,
    normed_ref,
    up_ref,
    rg0_ref,
    rg1_ref,
    heads0_ref,
    heads1_ref,
    mine_ref,
    send_ref,
    left_ref,
    right_ref,
):
    step = pl.program_id(0)
    half = rg0_ref.shape[0]
    tokens = 2 * half

    @pl.when(step == 0)
    def _():
        for b in range(3):
            for u, ref in enumerate((rg0_ref, rg1_ref)):
                pieces = []
                for n in range(half // cells):
                    piece = ref[n * cells : (n + 1) * cells].astype(F32)
                    if b == 0:
                        piece = shift_rows(piece, -1)
                    if b == 2:
                        piece = shift_rows(piece, 1)
                    pieces.append(piece.astype(BF16))
                rows = jnp.concatenate(pieces, axis=0)
                left_ref[b, :, u * half : (u + 1) * half] = mm_nt(perm_ref[b], rows).astype(BF16)
            for u, ref in enumerate((heads0_ref, heads1_ref)):
                left_ref[3 + b, :, u * half : (u + 1) * half] = mm(
                    perm_ref[b], ref[1 + b]
                ).astype(BF16)
            right_ref[b] = hidden_ref[b]
        left_ref[6] = mm_nt(perm_ref[1], up_ref[...]).astype(BF16)
        right_ref[3] = normed_ref[...]
        right_ref[4, :half] = heads0_ref[0].T
        right_ref[4, half:] = heads1_ref[0].T

    li = table_ref[0, step]
    ri = table_ref[1, step]
    out = (mm(left_ref[li], right_ref[ri]) * gscale).astype(BF16)
    rows = mine_ref.shape[1]
    mine_ref[0] = out[:rows]
    send_ref[0] = out[rows:]


def weight_grads(gscale, cells, perm, hidden, normed, up, rg0, rg1, heads0, heads1):
    tokens, channels = normed.shape
    entries = len(LEFT)
    table = jnp.asarray(np.array([LEFT, RIGHT]), jnp.int32)
    full = lambda shape: pl.BlockSpec(shape, lambda e, t: (0,) * len(shape))
    half = channels // 2
    out_spec = pl.BlockSpec((1, half, channels), lambda e, t: (e, 0, 0))
    out_type = jax.ShapeDtypeStruct((entries, half, channels), BF16)
    ins = (perm, hidden, normed, up, rg0, rg1, heads0, heads1)
    return pl.pallas_call(
        functools.partial(weights_kernel, gscale, cells),
        grid_spec=pltpu.PrefetchScalarGridSpec(
            num_scalar_prefetch=1,
            grid=(entries,),
            in_specs=[full(v.shape) for v in ins],
            out_specs=[out_spec, out_spec],
            scratch_shapes=[
                pltpu.VMEM((7, channels, tokens), BF16),
                pltpu.VMEM((5, tokens, channels), BF16),
            ],
        ),
        out_shape=[out_type, out_type],
        compiler_params=params(),
        cost_estimate=cost(2 * 20 * tokens * channels**2, 20e6),
        name="weight_grads",
    )(table, *ins)


def fold_kernel(count, ways, *refs):
    total = refs[0][0].astype(F32)
    for ref in refs[1:count]:
        total = total + ref[0].astype(F32)
    rows = total.shape[0] // ways
    for k, ref in enumerate(refs[count:]):
        ref[0] = total[k * rows : (k + 1) * rows].astype(ref.dtype)


def fold(values, first, entries, ways):
    _, rows, channels = values[0].shape
    specs = [
        pl.BlockSpec(
            (1, rows, channels),
            (lambda e: (e + first, 0, 0)) if v.shape[0] != entries else (lambda e: (e, 0, 0)),
        )
        for v in values
    ]
    cut = rows // ways
    return pl.pallas_call(
        functools.partial(fold_kernel, len(values), ways),
        grid=(entries,),
        in_specs=specs,
        out_specs=[pl.BlockSpec((1, cut, channels), lambda e: (e, 0, 0))] * ways,
        out_shape=[jax.ShapeDtypeStruct((entries, cut, channels), BF16)] * ways,
        compiler_params=params(),
        cost_estimate=cost(len(values) * entries * rows * channels, 2 * (len(values) + 1) * entries * rows * channels),
        name="fold",
    )(*values)


def coordinates(index):
    dp, strip = index // 16, index % 16
    return {
        "x": dp // 2,
        "z": (strip // 8) * 2 + dp % 2,
        "y": (strip // 2) % 4,
        "core": strip % 2,
    }


def device_index(place):
    dp = place["x"] * 2 + place["z"] % 2
    strip = (place["z"] // 2) * 8 + place["y"] * 2 + place["core"]
    return dp * 16 + strip


def ring_pairs(axis, offset):
    pairs = []
    for source in range(128):
        place = coordinates(source)
        place[axis] = (place[axis] + offset) % 4
        pairs.append((source, device_index(place)))
    return pairs


def core_pairs():
    return [(i, i ^ 1) for i in range(16)]


def row_order(channels, here):
    per = channels // 128
    row = jnp.arange(channels, dtype=jnp.int32)
    r = row % per
    k3 = (row // per) % 4
    k2 = (row // (per * 4)) % 4
    k1 = (row // (per * 16)) % 4
    flip = row // (per * 64)
    orders = []
    for order in ORDERS:
        place = {"core": (here["core"] + flip) % 2}
        for axis, k in zip(order, (k1, k2, k3)):
            place[axis] = (here[axis] + k) % 4
        orders.append(device_index(place) * per + r)
    return jnp.stack(orders)


def scatter_sum(mine, send):
    both = ("dp", "strip")
    got = lax.ppermute(send, "strip", core_pairs())
    sums = [fold((mine, got), first, count, 4) for first, count in PARTS]
    for stage in range(3):
        received = []
        for blocks, order in zip(sums, ORDERS):
            received.append(
                [blocks[0]]
                + [
                    lax.ppermute(blocks[k], both, ring_pairs(order[stage], k))
                    for k in range(1, 4)
                ]
            )
        if stage == 2:
            return [
                sum(value.astype(F32) for value in values) for values in received
            ]
        sums = [
            fold(tuple(values), 0, count, 4)
            for values, (_, count) in zip(received, PARTS)
        ]


def backward_kernel(
    expand_ref,
    up_ref,
    rg0_ref,
    rg1_ref,
    down_ref,
    x_ref,
    chan_ref,
    vec_ref,
    conv_ref,
    ag_ref,
    sums_ref,
    totals_ref,
    acc_ref,
):
    step = pl.program_id(0)
    images, cells, channels = x_ref.shape
    half = rg0_ref.shape[0]
    totals = mm_nt(down_ref[...], conv_ref[0, 0])
    totals += mm_nt(jnp.concatenate([rg0_ref[...], rg1_ref[...]], axis=0), conv_ref[1, 0])
    totals += mm_nt(up_ref[...], conv_ref[2, 0])

    @pl.when(step == 0)
    def _():
        for n in range(images):
            sl = slice(n * cells, (n + 1) * cells)
            acc_ref[sl] = shift_rows(totals[sl], -1)

    @pl.when(step == 1)
    def _():
        acc_ref[...] += totals

    @pl.when(step == 2)
    def _():
        gain = vec_ref[0:1]
        plain, weighted = [], []
        for n in range(images):
            sl = slice(n * cells, (n + 1) * cells)
            grad = acc_ref[sl] + shift_rows(totals[sl], 1)
            standard = (x_ref[n].astype(F32) - chan_ref[n : n + 1]) * chan_ref[
                images + n : images + n + 1
            ]
            u = standard * gain + vec_ref[1:2]
            sigma = 1.0 / (1.0 + jnp.exp(-u))
            ag = grad * (sigma * (1.0 + u * (1.0 - sigma)))
            ag_ref[sl] = ag
            plain.append(jnp.sum(ag, axis=0, keepdims=True))
            weighted.append(jnp.sum(ag * standard, axis=0, keepdims=True))
        plain = jnp.concatenate(plain, axis=0)
        weighted = jnp.concatenate(weighted, axis=0)
        sums_ref[0:1] = jnp.sum(weighted, axis=0, keepdims=True)
        sums_ref[1:2] = jnp.sum(plain, axis=0, keepdims=True)
        both = jnp.concatenate([plain * gain, weighted * gain], axis=0)
        totals_ref[...] = group_sum(both, expand_ref[...])


def backward(expand, up, rg0, rg1, down, x, chan, vec, conv_weight):
    images, cells, channels = x.shape
    tokens = images * cells
    full = lambda shape: pl.BlockSpec(shape, lambda b: (0,) * len(shape))
    return pl.pallas_call(
        backward_kernel,
        grid=(3,),
        in_specs=[
            full(expand.shape),
            full(up.shape),
            full(rg0.shape),
            full(rg1.shape),
            full(down.shape),
            full(x.shape),
            full(chan.shape),
            full(vec.shape),
            pl.BlockSpec((3, 1, channels, channels), lambda b: (0, b, 0, 0)),
        ],
        out_specs=[
            full((tokens, channels)),
            full((2, channels)),
            full((2 * images, GROUPS)),
        ],
        out_shape=[
            jax.ShapeDtypeStruct((tokens, channels), F32),
            jax.ShapeDtypeStruct((2, channels), F32),
            jax.ShapeDtypeStruct((2 * images, GROUPS), F32),
        ],
        scratch_shapes=[pltpu.VMEM((tokens, channels), F32)],
        compiler_params=params(),
        cost_estimate=cost(18 * tokens * channels**2, 12e6, 4e5),
        name="backward_conv",
    )(expand, up, rg0, rg1, down, x, chan, vec, conv_weight)


def input_kernel(totals_ref, expand_ref, rg0_ref, rg1_ref, ag_ref, x_ref, chan_ref, vec_ref, out_ref):
    images, cells, channels = x_ref.shape
    strips = totals_ref.shape[0]
    count = strips * cells * (channels // GROUPS)
    totals = jnp.sum(totals_ref[...], axis=0) / count
    spread_c = spread(totals, expand_ref[...])
    for n in range(images):
        sl = slice(n * cells, (n + 1) * cells)
        scale = chan_ref[images + n : images + n + 1]
        standard = (x_ref[n].astype(F32) - chan_ref[n : n + 1]) * scale
        part = scale * (
            ag_ref[sl] * vec_ref[0:1]
            - spread_c[n : n + 1]
            - standard * spread_c[images + n : images + n + 1]
        )
        rg_ref, m = (rg0_ref, n) if n < images // 2 else (rg1_ref, n - images // 2)
        rg = rg_ref[m * cells : (m + 1) * cells].astype(F32)
        out_ref[n] = (rg + part).astype(BF16)


def input_grad(totals, expand, rg0, rg1, ag, x, chan, vec):
    return pl.pallas_call(
        input_kernel,
        out_shape=jax.ShapeDtypeStruct(x.shape, BF16),
        compiler_params=params(),
        name="input_grad",
    )(totals, expand, rg0, rg1, ag, x, chan, vec)


def exchange(value, axis="strip"):
    return lax.all_to_all(value, axis, split_axis=0, concat_axis=0, tiled=True)


def neighbours(value):
    count = lax.axis_size("strip")
    before = lax.ppermute(value, "strip", [(i, i + 1) for i in range(count - 1)])
    after = lax.ppermute(value, "strip", [(i + 1, i) for i in range(count - 1)])
    return before, after


def on_device(
    block_in,
    upstream,
    gn_gain,
    gn_bias,
    conv_weight,
    conv_bias,
    ln_gain,
    ln_bias,
    w_query,
    w_key,
    w_value,
    w_out,
    out_bias,
):
    images, strip_rows, cells, channels = block_in.shape
    strips = lax.axis_size("strip")
    groups_dp = lax.axis_size("dp")
    me = lax.axis_index("strip")
    gscale = 1.0 / math.sqrt(cells * strips * images * groups_dp)
    x = block_in.reshape(images, cells, channels)
    up = upstream.reshape(images, cells, channels)
    up_rows = upstream.reshape(images * cells, channels)
    expand = expand_matrix(channels)
    zero = jnp.zeros_like(gn_gain)
    vec = jnp.stack([gn_gain, gn_bias, conv_bias, ln_gain, ln_bias, out_bias, zero, zero])
    flags = jnp.stack([me > 0, me < strips - 1]).astype(jnp.int32)
    here = coordinates(lax.axis_index("dp") * 16 + me)
    order = row_order(channels, here)
    perm = (order[:, :, None] == jnp.arange(channels, dtype=jnp.int32)).astype(BF16)

    x_above, x_below = neighbours(x)
    stats = exchange(local_stats(x, expand, strips))
    g = exchange_parts(upstream_heads(up, w_out))
    hidden, residual, normed, qkv, chan = forward(
        stats, flags, expand, x_above, x, x_below, vec, conv_weight, w_query, w_key, w_value
    )
    parts = images // 2
    got = [attention(exchange(qkv[c]), g[c]) for c in range(parts)]
    after = [
        after_attention(
            exchange(got[c]), residual, up_rows, vec, w_out, w_query, w_key, w_value, c
        )
        for c in range(parts)
    ]
    block_out = jnp.concatenate([a[0] for a in after], axis=0)
    (rg0, rg1), (heads0, heads1) = ([a[1] for a in after], [a[2] for a in after])
    above0, below0 = neighbours(rg0)
    above1, below1 = neighbours(rg1)
    mine, send = weight_grads(
        gscale, cells, perm, hidden, normed, up_rows, rg0, rg1, heads0, heads1
    )
    ag, gn_sums, totals = backward(
        expand,
        jnp.concatenate([above0, above1], axis=0),
        rg0,
        rg1,
        jnp.concatenate([below0, below1], axis=0),
        x,
        chan,
        vec,
        conv_weight,
    )
    vectors = gscale * jnp.concatenate([gn_sums, after[0][3] + after[1][3]], axis=0)
    count = vectors.shape[0]
    per = channels // (strips * groups_dp)
    spread_vectors = vectors.reshape(count, groups_dp, strips, per)
    spread_vectors = spread_vectors.transpose(2, 1, 0, 3).reshape(strips, groups_dp * count * per)
    flat = totals.reshape(1, -1)
    width = 512 - flat.shape[1] - spread_vectors.shape[1]
    payload = jnp.concatenate(
        [
            jnp.broadcast_to(flat, (strips, flat.shape[1])),
            spread_vectors,
            jnp.zeros((strips, width), F32),
        ],
        axis=1,
    )
    back = exchange(payload)
    all_totals = back[:, : flat.shape[1]].reshape((strips,) + totals.shape)
    grad_input = input_grad(all_totals, expand, rg0, rg1, ag, x, chan, vec)
    mid = jnp.sum(back[:, flat.shape[1] : flat.shape[1] + spread_vectors.shape[1]], axis=0)
    mid = exchange(mid.reshape(groups_dp, count * per), "dp")
    vector_shards = jnp.sum(mid, axis=0).reshape(count, per)

    p0, p1, p2 = scatter_sum(mine, send)
    conv_shard = jnp.stack([p0[:3], p1[:3], p2[:3]], axis=1).transpose(0, 1, 3, 2)
    shape = block_in.shape
    return (
        block_out.reshape(shape),
        grad_input.reshape(shape),
        conv_shard,
        p0[3].T,
        p1[3].T,
        p2[3].T,
        p1[4].T,
        vector_shards[0],
        vector_shards[1],
        vector_shards[2],
        vector_shards[3],
        vector_shards[4],
        vector_shards[5],
    )


def exchange_parts(value):
    return [exchange(value[c]) for c in range(value.shape[0])]


def solution(mesh):
    rows = P("dp", "strip", None, None)
    both = ("dp", "strip")
    in_specs = (rows, rows) + (P(),) * 11
    out_specs = (rows, rows, P(None, None, None, both)) + (P(None, both),) * 4 + (P(both),) * 6
    return jax.shard_map(
        on_device, mesh=mesh, in_specs=in_specs, out_specs=out_specs, check_vma=False
    )
```

```python
import functools
import math

import jax
import jax.numpy as jnp
import numpy as np
from jax import lax
from jax.experimental import pallas as pl
from jax.experimental.pallas import tpu as pltpu
from jax.sharding import PartitionSpec as P

HEADS = 8
GROUPS = 32
EPSILON = 1e-05
F32 = jnp.float32
BF16 = jnp.bfloat16
NT = (((1,), (1,)), ((), ()))
HIGH = lax.Precision.HIGHEST
VMEM_LIMIT = 56 * 1024 * 1024
LOG2E = math.log2(math.e)
QUERY_BLOCK = 512
KEY_CHUNK = 512
ORDERS = (("y", "x", "z"), ("x", "y", "z"), ("z", "x", "y"))
LEFT = (0, 0, 0, 3, 1, 1, 1, 4, 6, 2, 2, 2, 5)
RIGHT = (0, 1, 2, 3, 0, 1, 2, 3, 4, 0, 1, 2, 3)
LANES = 128
PARTS = ((0, 4), (4, 5), (9, 4))


def params(semantics=None):
    if semantics is None:
        return pltpu.CompilerParams(vmem_limit_bytes=VMEM_LIMIT)
    return pltpu.CompilerParams(
        vmem_limit_bytes=VMEM_LIMIT, dimension_semantics=semantics
    )


def mm(a, b):
    return jnp.dot(a, b, preferred_element_type=F32)


def mm_nt(a, b):
    return lax.dot_general(a, b, NT, preferred_element_type=F32)


def group_sum(rows, expand):
    return lax.dot_general(rows, expand, NT, preferred_element_type=F32, precision=HIGH)


def spread(rows, expand):
    return jnp.dot(rows, expand, preferred_element_type=F32, precision=HIGH)


def expand_matrix(channels):
    per_group = channels // GROUPS
    return jnp.asarray(
        np.arange(channels)[None, :] // per_group == np.arange(LANES)[:, None], F32
    )


def shift_rows(value, down):
    count = value.shape[0]
    row = lax.broadcasted_iota(jnp.int32, value.shape, 0)
    if down == 1:
        return jnp.where(row == 0, 0.0, pltpu.roll(value, 1, 0))
    return jnp.where(row == count - 1, 0.0, pltpu.roll(value, count - 1, 0))


def cost(flops, nbytes, trans=0):
    return pl.CostEstimate(flops=int(flops), bytes_accessed=int(nbytes), transcendentals=int(trans))


def stats_kernel(x_ref, expand_ref, out_ref):
    images, cells, channels = x_ref.shape
    count = cells * (channels // GROUPS)
    expand = expand_ref[...]
    sums = jnp.concatenate(
        [jnp.sum(x_ref[n].astype(F32), axis=0, keepdims=True) for n in range(images)], axis=0
    )
    mean = group_sum(sums, expand) / count
    mean_c = spread(mean, expand)
    squares = []
    for n in range(images):
        d = x_ref[n].astype(F32) - mean_c[n : n + 1]
        squares.append(jnp.sum(d * d, axis=0, keepdims=True))
    m2 = group_sum(jnp.concatenate(squares, axis=0), expand)
    both = jnp.concatenate([mean, m2], axis=0)
    for s in range(out_ref.shape[0]):
        out_ref[s] = both


def local_stats(x, expand, strips):
    images = x.shape[0]
    return pl.pallas_call(
        stats_kernel,
        out_shape=jax.ShapeDtypeStruct((strips, 2 * images, LANES), F32),
        compiler_params=params(),
        cost_estimate=cost(1e7, 7e5),
        name="local_stats",
    )(x, expand)


def upstream_kernel(up_ref, w_ref, g_ref):
    images = up_ref.shape[0]
    w = w_ref[...]
    hd = w.shape[0] // HEADS
    for n in range(images):
        g = mm_nt(w, up_ref[n])
        for h in range(HEADS):
            g_ref[n // 2, (n % 2) * HEADS + h] = g[h * hd : (h + 1) * hd].astype(BF16)


def upstream_heads(up, w_out):
    images, cells, channels = up.shape
    return pl.pallas_call(
        upstream_kernel,
        out_shape=jax.ShapeDtypeStruct((images // 2, 2 * HEADS, channels // HEADS, cells), BF16),
        compiler_params=params(),
        cost_estimate=cost(2 * images * cells * channels**2, 2.2e6),
        name="upstream_heads",
    )(up, w_out)


def forward_kernel(
    info_ref,
    stats_ref,
    expand_ref,
    x_ref,
    sib_ref,
    far_ref,
    up_ref,
    g_ref,
    vec_ref,
    conv_ref,
    wq_ref,
    wk_ref,
    wv_ref,
    hidden_ref,
    residual_ref,
    normed_ref,
    qkv0_ref,
    qkv1_ref,
    chan_ref,
    share_ref,
    acc_ref,
):
    step = pl.program_id(0)
    images, cells, channels = x_ref.shape
    hd = channels // HEADS

    @pl.when(step == 0)
    def _():
        strips = stats_ref.shape[0]
        count = cells * (channels // GROUPS)
        got = stats_ref[...]
        means = got[:, :images]
        mean = jnp.sum(means, axis=0) / strips
        off = means - mean[None]
        m2 = jnp.sum(got[:, images:], axis=0) + count * jnp.sum(off * off, axis=0)
        scale = lax.rsqrt(m2 / (count * strips) + EPSILON)
        expand = expand_ref[...]
        mean_c = spread(mean, expand)
        scale_c = spread(scale, expand)
        chan_ref[...] = jnp.concatenate([mean_c, scale_c], axis=0)
        gain = vec_ref[0:1]
        bias = vec_ref[1:2]
        core = info_ref[0]
        for a, ref in ((1, x_ref), (2 - 2 * core, sib_ref), (2 * core, far_ref)):
            for n in range(images):
                sl = slice(n * cells, (n + 1) * cells)
                u = (ref[n].astype(F32) - mean_c[n : n + 1]) * scale_c[n : n + 1]
                u = u * gain + bias
                h = u / (1.0 + jnp.exp(-u))
                if ref is far_ref:
                    h = jnp.where(info_ref[1] > 0, h, 0.0)
                    share_ref[0, sl] = h.astype(BF16)
                    share_ref[2, sl] = up_ref[n]
                hidden_ref[a, sl] = h.astype(BF16)

    total = mm(hidden_ref[0], conv_ref[0, 0])
    total += mm(hidden_ref[1], conv_ref[1, 0])
    total += mm(hidden_ref[2], conv_ref[2, 0])

    @pl.when(step == 0)
    def _():
        for n in range(images):
            sl = slice(n * cells, (n + 1) * cells)
            acc_ref[sl] = shift_rows(total[sl], 1)

    @pl.when(step == 1)
    def _():
        acc_ref[...] += total

    @pl.when(step == 2)
    def _():
        factor = LOG2E / math.sqrt(hd)
        for n in range(images):
            sl = slice(n * cells, (n + 1) * cells)
            conv = acc_ref[sl] + shift_rows(total[sl], -1)
            residual = (x_ref[n].astype(F32) + conv + vec_ref[2:3]).astype(BF16)
            residual_ref[sl] = residual
            tokens = residual.astype(F32)
            dev = tokens - jnp.mean(tokens, axis=1, keepdims=True)
            scale = lax.rsqrt(jnp.mean(dev * dev, axis=1, keepdims=True) + EPSILON)
            value = (dev * scale * vec_ref[3:4] + vec_ref[4:5]).astype(BF16)
            normed_ref[sl] = value
            share_ref[1, sl] = value
        normed = normed_ref[...]
        for t, ref in enumerate((wq_ref, wk_ref, wv_ref)):
            out = mm(normed, ref[...])
            if t == 0:
                out = out * factor
            for n in range(images):
                flipped = out[n * cells : (n + 1) * cells].T.astype(BF16)
                qkv_ref = (qkv0_ref, qkv1_ref)[n // 2]
                for h in range(HEADS):
                    qkv_ref[(n % 2) * HEADS + h, t] = flipped[h * hd : (h + 1) * hd]
        for c, qkv_ref in enumerate((qkv0_ref, qkv1_ref)):
            for i in range(2 * HEADS):
                qkv_ref[i, 3] = g_ref[c, i]


def forward(info, stats, expand, x, sib, far, up, g, vec, conv_weight, wq, wk, wv):
    images, cells, channels = x.shape
    tokens = images * cells
    hd = channels // HEADS
    full = lambda shape: pl.BlockSpec(shape, lambda b: (0,) * len(shape))
    square = (channels, channels)
    qkv_shape = (2 * HEADS, 4, hd, cells)
    return pl.pallas_call(
        forward_kernel,
        grid=(3,),
        in_specs=[pl.BlockSpec(memory_space=pltpu.SMEM)]
        + [full(v.shape) for v in (stats, expand, x, sib, far, up, g, vec)]
        + [
            pl.BlockSpec((3, 1) + square, lambda b: (0, b, 0, 0)),
            full(square),
            full(square),
            full(square),
        ],
        out_specs=[
            full((3, tokens, channels)),
            full((tokens, channels)),
            full((tokens, channels)),
            full(qkv_shape),
            full(qkv_shape),
            full((2 * images, channels)),
            full((3, tokens, channels)),
        ],
        out_shape=[
            jax.ShapeDtypeStruct((3, tokens, channels), BF16),
            jax.ShapeDtypeStruct((tokens, channels), BF16),
            jax.ShapeDtypeStruct((tokens, channels), BF16),
            jax.ShapeDtypeStruct(qkv_shape, BF16),
            jax.ShapeDtypeStruct(qkv_shape, BF16),
            jax.ShapeDtypeStruct((2 * images, channels), F32),
            jax.ShapeDtypeStruct((3, tokens, channels), BF16),
        ],
        scratch_shapes=[pltpu.VMEM((tokens, channels), F32)],
        compiler_params=params(),
        cost_estimate=cost(24 * tokens * channels**2, 20e6, 1e6),
        name="forward_conv",
    )(info, stats, expand, x, sib, far, up, g, vec, conv_weight, wq, wk, wv)


def together(*tasks):
    results = [None] * len(tasks)
    active = list(enumerate(tasks))
    while active:
        still = []
        for i, task in active:
            try:
                results[i] = next(task)
                still.append((i, task))
            except StopIteration:
                pass
        active = still
    return results


def attention_kernel(
    qkv_ref, out_ref, kt_ref, vt_ref, kn_ref, vn_ref, s_ref, e_ref, dk_ref, dv_ref
):
    step = pl.program_id(0)
    sources, _, hd, cells = qkv_ref.shape
    length = sources * cells
    wide = kn_ref.shape[1]
    block = s_ref.shape[2]
    per = block // cells
    spans = [slice(c, c + KEY_CHUNK) for c in range(0, length, KEY_CHUNK)]
    extra = vt_ref.shape[0] - hd

    @pl.when(step == 0)
    def _():
        ones_row = (lax.broadcasted_iota(jnp.int32, (extra, cells), 0) == 0).astype(F32)
        pad = jnp.zeros((wide - hd, cells), F32)
        row = lax.broadcasted_iota(jnp.int32, (wide - hd, cells), 0)
        ones_two = (row < 2).astype(F32)
        for s in range(sources):
            sl = slice(s * cells, (s + 1) * cells)
            k = qkv_ref[s, 1]
            v = qkv_ref[s, 2]
            kt_ref[:, sl] = k
            vt_ref[:hd, sl] = v
            vt_ref[hd:, sl] = ones_row.astype(BF16)
            kn_ref[sl] = jnp.concatenate([k.astype(F32), pad], axis=0).T.astype(BF16)
            vn_ref[sl] = jnp.concatenate([v.astype(F32), ones_two], axis=0).T.astype(BF16)
        dk_ref[...] = jnp.zeros_like(dk_ref)
        dv_ref[...] = jnp.zeros_like(dv_ref)

    bases = [(2 * step + b) * per for b in range(2)]

    def rows_of(b, t):
        return jnp.concatenate([qkv_ref[bases[b] + u, t] for u in range(per)], axis=1).astype(F32)

    def put(b, t, value):
        for u in range(per):
            out_ref[bases[b] + u, t] = value[:, u * cells : (u + 1) * cells].astype(BF16)

    def scores(b):
        q = jnp.concatenate([rows_of(b, 0), jnp.zeros((wide - hd, block), F32)], axis=0)
        q_t = q.astype(BF16)
        top = None
        for sl in spans:
            value = mm(kn_ref[sl], q_t)
            s_ref[b, sl] = value
            here = jnp.max(value, axis=0, keepdims=True)
            top = here if top is None else jnp.maximum(top, here)
            yield None
        yield top, q.T.astype(BF16)

    def attend(b, top):
        acc = jnp.zeros((hd + extra, block), F32)
        for sl in spans:
            e = jnp.exp2(s_ref[b, sl] - top).astype(BF16)
            e_ref[b, sl] = e
            acc += mm(vt_ref[:, sl], e)
            yield None
        yield acc

    def finish(b, acc):
        inverse = 1.0 / acc[hd : hd + 1]
        out = acc[:hd] * inverse
        put(b, 0, out)
        g = (rows_of(b, 3) * inverse).astype(BF16).astype(F32)
        delta = -jnp.sum(g * out, axis=0, keepdims=True)
        high = delta.astype(BF16).astype(F32)
        low = delta - high
        row = lax.broadcasted_iota(jnp.int32, (wide - hd, block), 0)
        tail = jnp.where(row == 0, high, jnp.where(row == 1, low, 0.0))
        g = jnp.concatenate([g, tail], axis=0)
        return g.astype(BF16), g.T.astype(BF16)

    def back(b, g_t, g_n, q_n):
        dq = jnp.zeros((hd, block), F32)
        for sl in spans:
            e = e_ref[b, sl]
            ds = (e.astype(F32) * mm(vn_ref[sl], g_t)).astype(BF16)
            dq += mm(kt_ref[:, sl], ds)
            dk_ref[sl] += mm(ds, q_n)
            dv_ref[sl] += mm(e, g_n)
            yield None
        put(b, 1, dq * (1.0 / math.sqrt(hd)))
        yield None

    ((top0, q0),) = together(scores(0))
    acc0, (top1, q1) = together(attend(0, top0), scores(1))
    _, acc1 = together(back(0, *finish(0, acc0), q0), attend(1, top1))
    together(back(1, *finish(1, acc1), q1))

    @pl.when(step == pl.num_programs(0) - 1)
    def _():
        for s in range(sources):
            sl = slice(s * cells, (s + 1) * cells)
            out_ref[s, 2] = (dk_ref[sl].T[:hd] * (1.0 / LOG2E)).astype(BF16)
            out_ref[s, 3] = dv_ref[sl].T[:hd].astype(BF16)


def attention(qkv):
    sources, _, hd, cells = qkv.shape
    length = sources * cells
    block = QUERY_BLOCK
    wide = 128
    full = lambda shape: pl.BlockSpec(shape, lambda i: (0,) * len(shape))
    return pl.pallas_call(
        attention_kernel,
        grid=(length // block // 2,),
        in_specs=[full(qkv.shape)],
        out_specs=full((sources, 4, hd, cells)),
        out_shape=jax.ShapeDtypeStruct((sources, 4, hd, cells), BF16),
        scratch_shapes=[
            pltpu.VMEM((hd, length), BF16),
            pltpu.VMEM((hd + 16, length), BF16),
            pltpu.VMEM((length, wide), BF16),
            pltpu.VMEM((length, wide), BF16),
            pltpu.VMEM((2, length, block), F32),
            pltpu.VMEM((2, length, block), BF16),
            pltpu.VMEM((length, wide), F32),
            pltpu.VMEM((length, wide), F32),
        ],
        compiler_params=params(),
        cost_estimate=cost(12 * length * length * 256, 5e6, length * length),
        name="attention",
    )(qkv)


def gather_heads(got_ref, t):
    return jnp.concatenate(
        [
            jnp.concatenate([got_ref[n * HEADS + h, t] for h in range(HEADS)], axis=0)
            for n in range(2)
        ],
        axis=1,
    )


def tokens_kernel(
    got_ref,
    residual_ref,
    up_ref,
    vec_ref,
    wo_ref,
    wq_ref,
    wk_ref,
    wv_ref,
    block_out_ref,
    rg_ref,
    sums_ref,
):
    residual = residual_ref[...].astype(F32)
    up = up_ref[...].astype(F32)
    mixed = mm(gather_heads(got_ref, 0).T, wo_ref[...])
    block_out_ref[...] = (residual + mixed + vec_ref[5:6]).astype(BF16)
    grad = mm_nt(gather_heads(got_ref, 1).T, wq_ref[...])
    grad += mm_nt(gather_heads(got_ref, 2).T, wk_ref[...])
    grad += mm_nt(gather_heads(got_ref, 3).T, wv_ref[...])
    dev = residual - jnp.mean(residual, axis=1, keepdims=True)
    scale = lax.rsqrt(jnp.mean(dev * dev, axis=1, keepdims=True) + EPSILON)
    standard = dev * scale
    scaled = grad * vec_ref[3:4]
    part = scale * (
        scaled
        - jnp.mean(scaled, axis=1, keepdims=True)
        - standard * jnp.mean(scaled * standard, axis=1, keepdims=True)
    )
    rg = (up + part).astype(BF16)
    rg_ref[...] = rg
    sums_ref[0:1] = jnp.sum(rg.astype(F32), axis=0, keepdims=True)
    sums_ref[1:2] = jnp.sum(grad * standard, axis=0, keepdims=True)
    sums_ref[2:3] = jnp.sum(grad, axis=0, keepdims=True)
    sums_ref[3:4] = jnp.sum(up, axis=0, keepdims=True)


def after_attention(got, residual, up, vec, wo, wq, wk, wv, part):
    channels = residual.shape[1]
    cells = got.shape[3]
    tokens = 2 * cells
    full = lambda shape: pl.BlockSpec(shape, lambda i: (0,) * len(shape))
    rows = pl.BlockSpec((tokens, channels), lambda i: (part, 0))
    square = (channels, channels)
    return pl.pallas_call(
        tokens_kernel,
        grid=(1,),
        in_specs=[full(got.shape), rows, rows, full(vec.shape)] + [full(square)] * 4,
        out_specs=[
            full((tokens, channels)),
            full((tokens, channels)),
            full((4, channels)),
        ],
        out_shape=[
            jax.ShapeDtypeStruct((tokens, channels), BF16),
            jax.ShapeDtypeStruct((tokens, channels), BF16),
            jax.ShapeDtypeStruct((4, channels), F32),
        ],
        compiler_params=params(),
        cost_estimate=cost(8 * tokens * channels**2, 7e6),
        name="after_attention",
    )(got, residual, up, vec, wo, wq, wk, wv)


def weights_kernel(
    gscale,
    cells,
    table_ref,
    info_ref,
    perm_ref,
    hidden_ref,
    share_ref,
    normed_ref,
    up_ref,
    rg0_ref,
    rg1_ref,
    rg0_sib_ref,
    rg1_sib_ref,
    got0_ref,
    got1_ref,
    got0_sib_ref,
    got1_sib_ref,
    *refs,
):
    outs, (left_ref, right_ref) = refs[:-2], refs[-2:]
    step = pl.program_id(0)
    half = rg0_ref.shape[0]
    tokens = 2 * half

    @pl.when(step == 0)
    def _():
        rgs = (rg0_ref, rg1_ref, rg0_sib_ref, rg1_sib_ref)
        gots = (got0_ref, got1_ref, got0_sib_ref, got1_sib_ref)
        for u in range(4):
            place = slice(u * half, (u + 1) * half)
            for b in range(3):
                pieces = []
                for n in range(half // cells):
                    piece = rgs[u][n * cells : (n + 1) * cells].astype(F32)
                    if b == 0:
                        piece = shift_rows(piece, -1)
                    if b == 2:
                        piece = shift_rows(piece, 1)
                    pieces.append(piece.astype(BF16))
                rows = jnp.concatenate(pieces, axis=0)
                left_ref[b, :, place] = mm_nt(perm_ref[b], rows).astype(BF16)
                left_ref[3 + b, :, place] = mm(
                    perm_ref[b], gather_heads(gots[u], 1 + b)
                ).astype(BF16)
            right_ref[4, place] = gather_heads(gots[u], 0).T
        left_ref[6, :, :tokens] = mm_nt(perm_ref[1], up_ref[...]).astype(BF16)
        left_ref[6, :, tokens:] = mm_nt(perm_ref[1], share_ref[2]).astype(BF16)
        right_ref[3, :tokens] = normed_ref[...]
        right_ref[3, tokens:] = share_ref[1]
        core = info_ref[0]
        for a in range(3):
            right_ref[a, :tokens] = hidden_ref[a]
        right_ref[1 + core, tokens:] = hidden_ref[2 - core]
        right_ref[core, tokens:] = hidden_ref[1 - core]
        right_ref[2 - 2 * core, tokens:] = share_ref[0]

    li = table_ref[0, step]
    ri = table_ref[1, step]
    out = (mm(left_ref[li], right_ref[ri]) * gscale).astype(BF16)
    rows = out.shape[0] // 4
    for p, (first, count) in enumerate(PARTS):

        @pl.when(jnp.logical_and(step >= first, step < first + count))
        def _():
            for k in range(4):
                outs[4 * p + k][0] = out[k * rows : (k + 1) * rows]


def weight_grads(gscale, cells, info, perm, ins):
    tokens, channels = ins[2].shape
    entries = len(LEFT)
    table = jnp.asarray(np.array([LEFT, RIGHT]), jnp.int32)
    full = lambda shape: pl.BlockSpec(shape, lambda e, t: (0,) * len(shape))
    rows = perm.shape[1] // 4
    out_specs, out_shape = [], []
    for first, count in PARTS:
        for _ in range(4):
            out_specs.append(
                pl.BlockSpec(
                    (1, rows, channels),
                    lambda e, t, first=first, count=count: (
                        jnp.clip(e - first, 0, count - 1),
                        0,
                        0,
                    ),
                )
            )
            out_shape.append(jax.ShapeDtypeStruct((count, rows, channels), BF16))
    outs = pl.pallas_call(
        functools.partial(weights_kernel, gscale, cells),
        grid_spec=pltpu.PrefetchScalarGridSpec(
            num_scalar_prefetch=1,
            grid=(entries,),
            in_specs=[pl.BlockSpec(memory_space=pltpu.SMEM), full(perm.shape)]
            + [full(v.shape) for v in ins],
            out_specs=out_specs,
            scratch_shapes=[
                pltpu.VMEM((7, perm.shape[1], 2 * tokens), BF16),
                pltpu.VMEM((5, 2 * tokens, channels), BF16),
            ],
        ),
        out_shape=out_shape,
        compiler_params=params(),
        cost_estimate=cost(2 * 20 * tokens * channels**2, 20e6),
        name="weight_grads",
    )(table, info, perm, *ins)
    return [outs[4 * p : 4 * p + 4] for p in range(3)]


def fold_first_kernel(*refs):
    ins, (own_ref, *sends) = refs[:12], refs[12:]
    for p, (first, count) in enumerate(PARTS):
        parts = ins[4 * p : 4 * p + 4]
        rows = parts[0].shape[1] // 4
        for e in range(count):
            total = parts[0][e].astype(F32)
            for ref in parts[1:]:
                total = total + ref[e].astype(F32)
            own_ref[first + e] = total[:rows]
            place, group = ((e, 0), (e, 1), (PARTS[0][1] + e, 0))[p]
            for k in range(1, 4):
                sends[3 * group + k - 1][place] = total[k * rows : (k + 1) * rows].astype(BF16)


def fold_second_kernel(*refs):
    own_in, got, (own_ref, *sends) = refs[0], refs[1:7], refs[7:]
    rows = own_in.shape[1] // 4
    for p, (first, count) in enumerate(PARTS):
        for e in range(count):
            place, group = ((e, 0), (e, 1), (PARTS[0][1] + e, 0))[p]
            total = own_in[first + e]
            for k in range(3):
                total = total + got[3 * group + k][place].astype(F32)
            own_ref[first + e] = total[:rows]
            place, group = ((e, 0), (PARTS[0][1] + e, 0), (e, 1))[p]
            for k in range(1, 4):
                sends[3 * group + k - 1][place] = total[k * rows : (k + 1) * rows].astype(BF16)


def fold_last_kernel(*refs):
    own_in, got, (conv_ref, q_ref, k_ref, v_ref, o_ref) = refs[0], refs[1:7], refs[7:]
    rows = own_in.shape[1]
    for p, (first, count) in enumerate(PARTS):
        for e in range(count):
            place, group = ((e, 0), (PARTS[0][1] + e, 0), (e, 1))[p]
            total = own_in[first + e]
            for k in range(3):
                total = total + got[3 * group + k][place].astype(F32)
            if e < 3:
                for r in range(rows):
                    conv_ref[e, r, p : p + 1] = total[r : r + 1]
            elif e == 3:
                (q_ref, k_ref, v_ref)[p][...] = total
            else:
                o_ref[...] = total


def fold_first(values):
    _, rows, channels = values[0].shape
    cut = rows // 4
    entries = len(LEFT)
    wide = PARTS[0][1] + PARTS[2][1]
    sizes = [wide] * 3 + [PARTS[1][1]] * 3
    return pl.pallas_call(
        fold_first_kernel,
        out_shape=[jax.ShapeDtypeStruct((entries, cut, channels), F32)]
        + [jax.ShapeDtypeStruct((s, cut, channels), BF16) for s in sizes],
        compiler_params=params(),
        cost_estimate=cost(4e6, 7e6),
        name="fold_first",
    )(*values)


def fold_second(values):
    entries, rows, channels = values[0].shape
    cut = rows // 4
    wide = PARTS[0][1] + PARTS[1][1]
    sizes = [wide] * 3 + [PARTS[2][1]] * 3
    return pl.pallas_call(
        fold_second_kernel,
        out_shape=[jax.ShapeDtypeStruct((entries, cut, channels), F32)]
        + [jax.ShapeDtypeStruct((s, cut, channels), BF16) for s in sizes],
        compiler_params=params(),
        cost_estimate=cost(1e6, 2e6),
        name="fold_second",
    )(*values)


def fold_last(values):
    _, rows, channels = values[0].shape
    return pl.pallas_call(
        fold_last_kernel,
        out_shape=[jax.ShapeDtypeStruct((3, rows, 3, channels), F32)]
        + [jax.ShapeDtypeStruct((rows, channels), F32)] * 4,
        compiler_params=params(),
        cost_estimate=cost(3e5, 7e5),
        name="fold_last",
    )(*values)


def coordinates(index):
    dp, strip = index // 16, index % 16
    return {
        "x": dp // 2,
        "z": (strip // 8) * 2 + dp % 2,
        "y": (strip // 2) % 4,
        "core": strip % 2,
    }


def device_index(place):
    dp = place["x"] * 2 + place["z"] % 2
    strip = (place["z"] // 2) * 8 + place["y"] * 2 + place["core"]
    return dp * 16 + strip


def ring_pairs(axis, offset):
    pairs = []
    for source in range(128):
        place = coordinates(source)
        place[axis] = (place[axis] + offset) % 4
        pairs.append((source, device_index(place)))
    return pairs


def row_order(channels, here):
    per = channels // 128
    row = jnp.arange(channels // 2, dtype=jnp.int32)
    r = row % per
    k3 = (row // per) % 4
    k2 = (row // (per * 4)) % 4
    k1 = row // (per * 16)
    orders = []
    for order in ORDERS:
        place = {"core": here["core"]}
        for axis, k in zip(order, (k1, k2, k3)):
            place[axis] = (here[axis] + k) % 4
        orders.append(device_index(place) * per + r)
    return jnp.stack(orders)


def ring_send(value, axis, offset):
    return lax.ppermute(value, ("dp", "strip"), ring_pairs(axis, offset))


def scatter_sum(blocks):
    values = []
    for p, order in enumerate(ORDERS):
        values.append(blocks[p][0])
        values += [ring_send(blocks[p][k], order[0], k) for k in range(1, 4)]
    own, *sends = fold_first(values)
    values = [own]
    for i, send in enumerate(sends):
        values.append(ring_send(send, ("x", "y")[i // 3], i % 3 + 1))
    own, *sends = fold_second(values)
    values = [own]
    for i, send in enumerate(sends):
        values.append(ring_send(send, ("z", "y")[i // 3], i % 3 + 1))
    return fold_last(values)


def backward_kernel(
    gscale,
    info_ref,
    expand_ref,
    rg_ref,
    sib_ref,
    far_ref,
    x_ref,
    chan_ref,
    vec_ref,
    conv_ref,
    *refs,
):
    last = len(refs) > 3
    if last:
        pick_ref, early_ref, sums0_ref, sums1_ref, ag_ref, payload_ref, acc_ref = refs
    else:
        ag_ref, out_ref, acc_ref = refs
    step = pl.program_id(0)
    images, cells, channels = x_ref.shape
    first = images if last else 0
    even = info_ref[0] == 0
    sib = sib_ref[...]
    far = far_ref[...]
    totals = mm_nt(jnp.where(even, sib, far), conv_ref[0, 0])
    totals += mm_nt(rg_ref[...], conv_ref[1, 0])
    totals += mm_nt(jnp.where(even, far, sib), conv_ref[2, 0])

    @pl.when(step == 0)
    def _():
        for n in range(images):
            sl = slice(n * cells, (n + 1) * cells)
            acc_ref[sl] = shift_rows(totals[sl], -1)

    @pl.when(step == 1)
    def _():
        acc_ref[...] += totals

    @pl.when(step == 2)
    def _():
        gain = vec_ref[0:1]
        plain, weighted = [], []
        for n in range(images):
            sl = slice(n * cells, (n + 1) * cells)
            grad = acc_ref[sl] + shift_rows(totals[sl], 1)
            m = first + n
            standard = (x_ref[n].astype(F32) - chan_ref[m : m + 1]) * chan_ref[
                2 * images + m : 2 * images + m + 1
            ]
            u = standard * gain + vec_ref[1:2]
            sigma = 1.0 / (1.0 + jnp.exp(-u))
            ag = grad * (sigma * (1.0 + u * (1.0 - sigma)))
            ag_ref[sl] = ag
            plain.append(jnp.sum(ag, axis=0, keepdims=True))
            weighted.append(jnp.sum(ag * standard, axis=0, keepdims=True))
        if not last:
            out_ref[...] = jnp.concatenate(plain + weighted, axis=0)
            return
        plain = [early_ref[n : n + 1] for n in range(images)] + plain
        weighted = [early_ref[images + n : images + n + 1] for n in range(images)] + weighted
        all_totals = group_sum(jnp.concatenate(plain + weighted, axis=0) * gain, expand_ref[...])
        sums = sums0_ref[...] + sums1_ref[...]
        vectors = gscale * jnp.concatenate(
            [sum(weighted), sum(plain), sums, jnp.zeros((2, channels), F32)], axis=0
        )
        pieces = []
        for _ in range(3):
            piece = vectors.astype(BF16)
            pieces.append(piece)
            vectors = vectors - piece.astype(F32)
        picked = [mm(piece, pick_ref[...]) for piece in pieces]
        picked = picked[0] + picked[1] + picked[2]
        for s in range(payload_ref.shape[0]):
            payload_ref[s] = all_totals + picked[:, s * LANES : (s + 1) * LANES]


def backward(gscale, info, expand, rg, sib, far, x, chan, vec, conv_weight, part, more=()):
    images, cells, channels = x.shape
    images = images // 2
    tokens = images * cells
    full = lambda shape: pl.BlockSpec(shape, lambda b: (0,) * len(shape))
    if more:
        out = (16, 4 * images, LANES)
    else:
        out = (2 * images, channels)
    return pl.pallas_call(
        functools.partial(backward_kernel, gscale),
        grid=(3,),
        in_specs=[pl.BlockSpec(memory_space=pltpu.SMEM)]
        + [full(v.shape) for v in (expand, rg, sib, far)]
        + [pl.BlockSpec((images, cells, channels), lambda b: (part, 0, 0))]
        + [full(v.shape) for v in (chan, vec)]
        + [pl.BlockSpec((3, 1, channels, channels), lambda b: (0, b, 0, 0))]
        + [full(v.shape) for v in more],
        out_specs=[full((tokens, channels)), full(out)],
        out_shape=[
            jax.ShapeDtypeStruct((tokens, channels), F32),
            jax.ShapeDtypeStruct(out, F32),
        ],
        scratch_shapes=[pltpu.VMEM((tokens, channels), F32)],
        compiler_params=params(),
        cost_estimate=cost(18 * tokens * channels**2, 10e6, 2e5),
        name="backward_conv",
    )(info, expand, rg, sib, far, x, chan, vec, conv_weight, *more)


def input_kernel(
    totals_ref, expand_ref, rg0_ref, rg1_ref, ag0_ref, ag1_ref, x_ref, chan_ref, vec_ref,
    out_ref, spread_ref
):
    images, cells, channels = x_ref.shape
    strips = totals_ref.shape[0]
    count = strips * cells * (channels // GROUPS)
    summed = jnp.sum(totals_ref[...], axis=0)
    for d in range(spread_ref.shape[0]):
        spread_ref[d] = summed
    spread_c = spread(summed / count, expand_ref[...])
    for n in range(images):
        u, m = n // 2, n % 2
        sl = slice(m * cells, (m + 1) * cells)
        scale = chan_ref[images + n : images + n + 1]
        standard = (x_ref[n].astype(F32) - chan_ref[n : n + 1]) * scale
        part = scale * (
            (ag0_ref, ag1_ref)[u][sl] * vec_ref[0:1]
            - spread_c[n : n + 1]
            - standard * spread_c[images + n : images + n + 1]
        )
        rg = (rg0_ref, rg1_ref)[u][sl].astype(F32)
        out_ref[n] = (rg + part).astype(BF16)


def input_grad(totals, expand, rg0, rg1, ag0, ag1, x, chan, vec, copies):
    return pl.pallas_call(
        input_kernel,
        out_shape=[
            jax.ShapeDtypeStruct(x.shape, BF16),
            jax.ShapeDtypeStruct((copies,) + totals.shape[1:], F32),
        ],
        compiler_params=params(),
        cost_estimate=cost(3e6, 4e6),
        name="input_grad",
    )(totals, expand, rg0, rg1, ag0, ag1, x, chan, vec)


def exchange(value, axis="strip"):
    return lax.all_to_all(value, axis, split_axis=0, concat_axis=0, tiled=True)


def core_mate(value):
    return lax.ppermute(value, "strip", [(i, i ^ 1) for i in range(16)])


def far_row(value):
    pairs = [(i, i + 1) for i in range(1, 15, 2)]
    return lax.ppermute(value, "strip", pairs + [(j, i) for i, j in pairs])


def pick_matrix(channels, groups_dp, strips):
    per = channels // (groups_dp * strips)
    pick = np.zeros((channels, strips * LANES), np.float32)
    for o in range(channels):
        device, r = divmod(o, per)
        dp, strip = divmod(device, strips)
        pick[o, strip * LANES + GROUPS + dp * per + r] = 1.0
    return jnp.asarray(pick, BF16)


def on_device(
    block_in,
    upstream,
    gn_gain,
    gn_bias,
    conv_weight,
    conv_bias,
    ln_gain,
    ln_bias,
    w_query,
    w_key,
    w_value,
    w_out,
    out_bias,
):
    images, strip_rows, cells, channels = block_in.shape
    strips = lax.axis_size("strip")
    groups_dp = lax.axis_size("dp")
    me = lax.axis_index("strip")
    me_dp = lax.axis_index("dp")
    gscale = 1.0 / math.sqrt(cells * strips * images * groups_dp)
    x = block_in.reshape(images, cells, channels)
    up = upstream.reshape(images, cells, channels)
    up_rows = upstream.reshape(images * cells, channels)
    expand = expand_matrix(channels)
    zero = jnp.zeros_like(gn_gain)
    vec = jnp.stack([gn_gain, gn_bias, conv_bias, ln_gain, ln_bias, out_bias, zero, zero])
    core = me % 2
    inside = jnp.where(core == 0, me > 0, me < strips - 1)
    info = jnp.stack([core, inside.astype(jnp.int32)]).astype(jnp.int32)
    here = coordinates(me_dp * 16 + me)
    order = row_order(channels, here)
    perm = (order[:, :, None] == jnp.arange(channels, dtype=jnp.int32)).astype(BF16)

    x_far = far_row(x)
    x_sib = core_mate(x)
    stats = exchange(local_stats(x, expand, strips))
    g = upstream_heads(up, w_out)
    hidden, residual, normed, qkv0, qkv1, chan, share = forward(
        info, stats, expand, x, x_sib, x_far, up, g, vec, conv_weight, w_query, w_key, w_value
    )
    got = [exchange(attention(exchange(qkv))) for qkv in (qkv0, qkv1)]
    share_sib = core_mate(share)
    got_sib = [core_mate(v) for v in got]
    after = [
        after_attention(got[c], residual, up_rows, vec, w_out, w_query, w_key, w_value, c)
        for c in range(2)
    ]
    block_out = jnp.concatenate([a[0] for a in after], axis=0)
    rg0, rg1 = [a[1] for a in after]
    rg0_sib, rg1_sib = core_mate(rg0), core_mate(rg1)
    rg0_far, rg1_far = far_row(rg0), far_row(rg1)
    common = (x, chan, vec, conv_weight)
    ag0, early = backward(gscale, info, expand, rg0, rg0_sib, rg0_far, *common, 0)
    blocks = weight_grads(
        gscale,
        cells,
        info,
        perm,
        (hidden, share_sib, normed, up_rows, rg0, rg1, rg0_sib, rg1_sib, *got, *got_sib),
    )
    pick = pick_matrix(channels, groups_dp, strips)
    ag1, payload = backward(
        gscale, info, expand, rg1, rg1_sib, rg1_far, *common, 1,
        (pick, early, after[0][2], after[1][2]),
    )
    grad_input, vectors = input_grad(
        exchange(payload), expand, rg0, rg1, ag0, ag1, x, chan, vec, groups_dp
    )
    conv_shard, q_shard, k_shard, v_shard, o_shard = scatter_sum(blocks)
    per = channels // (strips * groups_dp)
    vectors = jnp.sum(exchange(vectors, "dp"), axis=0)
    shards = lax.dynamic_slice_in_dim(vectors, GROUPS + me_dp * per, per, axis=1)
    shape = block_in.shape
    return (
        block_out.reshape(shape),
        grad_input.reshape(shape),
        conv_shard.transpose(0, 2, 3, 1),
        q_shard.T,
        k_shard.T,
        v_shard.T,
        o_shard.T,
        shards[0],
        shards[1],
        shards[2],
        shards[3],
        shards[4],
        shards[5],
    )


def solution(mesh):
    rows = P("dp", "strip", None, None)
    both = ("dp", "strip")
    in_specs = (rows, rows) + (P(),) * 11
    out_specs = (rows, rows, P(None, None, None, both)) + (P(None, both),) * 4 + (P(both),) * 6
    return jax.shard_map(
        on_device, mesh=mesh, in_specs=in_specs, out_specs=out_specs, check_vma=False
    )
```

```python
import functools
import math

import jax
import jax.numpy as jnp
import numpy as np
from jax import lax
from jax.experimental import pallas as pl
from jax.experimental.pallas import tpu as pltpu
from jax.sharding import PartitionSpec as P

HEADS = 8
GROUPS = 32
EPSILON = 1e-05
F32 = jnp.float32
BF16 = jnp.bfloat16
NT = (((1,), (1,)), ((), ()))
HIGH = lax.Precision.HIGHEST
VMEM_LIMIT = 56 * 1024 * 1024
LOG2E = math.log2(math.e)
QUERY_BLOCK = 512
KEY_CHUNK = 512
ORDERS = (("y", "x", "z"), ("x", "y", "z"), ("z", "x", "y"))
ENTRIES = 13
LANES = 128
PARTS = ((0, 4), (4, 5), (9, 4))


def params(semantics=None):
    if semantics is None:
        return pltpu.CompilerParams(vmem_limit_bytes=VMEM_LIMIT)
    return pltpu.CompilerParams(
        vmem_limit_bytes=VMEM_LIMIT, dimension_semantics=semantics
    )


def mm(a, b):
    return jnp.dot(a, b, preferred_element_type=F32)


def mm_nt(a, b):
    return lax.dot_general(a, b, NT, preferred_element_type=F32)


def group_sum(rows, expand):
    return lax.dot_general(rows, expand, NT, preferred_element_type=F32, precision=HIGH)


def spread(rows, expand):
    return jnp.dot(rows, expand, preferred_element_type=F32, precision=HIGH)


def expand_matrix(channels):
    per_group = channels // GROUPS
    return jnp.asarray(
        np.arange(channels)[None, :] // per_group == np.arange(LANES)[:, None], F32
    )


def shift_rows(value, down):
    count = value.shape[0]
    row = lax.broadcasted_iota(jnp.int32, value.shape, 0)
    if down == 1:
        return jnp.where(row == 0, 0.0, pltpu.roll(value, 1, 0))
    return jnp.where(row == count - 1, 0.0, pltpu.roll(value, count - 1, 0))


def cost(flops, nbytes, trans=0):
    return pl.CostEstimate(flops=int(flops), bytes_accessed=int(nbytes), transcendentals=int(trans))


def stats_kernel(x_ref, expand_ref, *refs):
    vectors, out_ref, vec_ref = refs[:-2], refs[-2], refs[-1]
    images, cells, channels = x_ref.shape
    count = cells * (channels // GROUPS)
    vec_ref[...] = jnp.zeros_like(vec_ref)
    for i, ref in enumerate(vectors):
        vec_ref[i : i + 1] = ref[...].reshape(1, channels)
    expand = expand_ref[...]
    sums = jnp.concatenate(
        [jnp.sum(x_ref[n].astype(F32), axis=0, keepdims=True) for n in range(images)], axis=0
    )
    mean = group_sum(sums, expand) / count
    mean_c = spread(mean, expand)
    squares = []
    for n in range(images):
        d = x_ref[n].astype(F32) - mean_c[n : n + 1]
        squares.append(jnp.sum(d * d, axis=0, keepdims=True))
    m2 = group_sum(jnp.concatenate(squares, axis=0), expand)
    both = jnp.concatenate([mean, m2], axis=0)
    for s in range(out_ref.shape[0]):
        out_ref[s] = both


def local_stats(x, expand, vectors, strips):
    images, _, channels = x.shape
    return pl.pallas_call(
        stats_kernel,
        out_shape=[
            jax.ShapeDtypeStruct((strips, 2 * images, LANES), F32),
            jax.ShapeDtypeStruct((8, channels), F32),
        ],
        compiler_params=params(),
        cost_estimate=cost(1e7, 7e5),
        name="local_stats",
    )(x, expand, *vectors)


def upstream_kernel(up_ref, w_ref, g_ref):
    images = up_ref.shape[0]
    w = w_ref[...]
    hd = w.shape[0] // HEADS
    for n in range(images):
        g = mm_nt(w, up_ref[n])
        for h in range(HEADS):
            g_ref[n // 2, (n % 2) * HEADS + h] = g[h * hd : (h + 1) * hd].astype(BF16)


def upstream_heads(up, w_out):
    images, cells, channels = up.shape
    return pl.pallas_call(
        upstream_kernel,
        out_shape=jax.ShapeDtypeStruct((images // 2, 2 * HEADS, channels // HEADS, cells), BF16),
        compiler_params=params(),
        cost_estimate=cost(2 * images * cells * channels**2, 2.2e6),
        name="upstream_heads",
    )(up, w_out)


def forward_kernel(
    info_ref,
    stats_ref,
    expand_ref,
    vec_ref,
    x_hbm,
    sib_hbm,
    far_hbm,
    g_hbm,
    conv_hbm,
    wq_hbm,
    wk_hbm,
    wv_hbm,
    hid_own_hbm,
    hid_sib_hbm,
    hid_far_hbm,
    residual_hbm,
    normed_hbm,
    qkv0_hbm,
    qkv1_hbm,
    chan_ref,
    x_ref,
    conv_ref,
    w_ref,
    hidden_ref,
    acc_ref,
    residual_ref,
    normed_ref,
    qkv_ref,
    in_sems,
    out_sems,
):
    _, images, cells, channels = x_ref.shape
    hd = channels // HEADS
    copy = pltpu.make_async_copy
    xs = [copy(h, x_ref.at[i], in_sems.at[i]) for i, h in enumerate((x_hbm, sib_hbm, far_hbm))]
    convs = [copy(conv_hbm.at[:, b], conv_ref.at[b], in_sems.at[3 + b]) for b in range(3)]
    ws = [copy(h, w_ref.at[i], in_sems.at[6 + i]) for i, h in enumerate((wq_hbm, wk_hbm, wv_hbm))]
    qkv_out = (qkv0_hbm, qkv1_hbm)
    gs = [copy(g_hbm.at[c], qkv_ref.at[c, :, 3], in_sems.at[9 + c]) for c in range(2)]
    for task in xs + convs + ws + gs:
        task.start()
    core = info_ref[0]
    strips = stats_ref.shape[0]
    count = cells * (channels // GROUPS)
    got = stats_ref[...]
    means = got[:, :images]
    mean = jnp.sum(means, axis=0) / strips
    off = means - mean[None]
    m2 = jnp.sum(got[:, images:], axis=0) + count * jnp.sum(off * off, axis=0)
    scale = lax.rsqrt(m2 / (count * strips) + EPSILON)
    expand = expand_ref[...]
    mean_c = spread(mean, expand)
    scale_c = spread(scale, expand)
    chan_ref[...] = jnp.concatenate([mean_c, scale_c], axis=0)
    gain = vec_ref[0:1]
    bias = vec_ref[1:2]
    outs = []
    for i, out_hbm in enumerate((hid_own_hbm, hid_sib_hbm, hid_far_hbm)):
        xs[i].wait()
        for n in range(images):
            factor_c = scale_c[n : n + 1] * gain
            u = (x_ref[i, n].astype(F32) - mean_c[n : n + 1]) * factor_c + bias
            h = u * (0.5 + 0.5 * jnp.tanh(0.5 * u))
            if i == 2:
                h = jnp.where(info_ref[1] > 0, h, 0.0)
            hidden_ref[i, n * cells : (n + 1) * cells] = h.astype(BF16)
        outs.append(copy(hidden_ref.at[i], out_hbm, out_sems.at[i]))
        outs[-1].start()

    above = 2 - core
    below = 1 + core
    for b in range(3):
        convs[b].wait()
        total = mm(hidden_ref[0], conv_ref[b, 1])
        total += mm(hidden_ref[above], conv_ref[b, 0])
        total += mm(hidden_ref[below], conv_ref[b, 2])
        if b == 1:
            acc_ref[...] += total
            continue
        for n in range(images):
            sl = slice(n * cells, (n + 1) * cells)
            if b == 0:
                acc_ref[sl] = shift_rows(total[sl], 1)
                continue
            conv = acc_ref[sl] + shift_rows(total[sl], -1)
            residual = (x_ref[0, n].astype(F32) + conv + vec_ref[2:3]).astype(BF16)
            residual_ref[sl] = residual
            tokens = residual.astype(F32)
            dev = tokens - jnp.mean(tokens, axis=1, keepdims=True)
            scale = lax.rsqrt(jnp.mean(dev * dev, axis=1, keepdims=True) + EPSILON)
            normed_ref[sl] = (dev * scale * vec_ref[3:4] + vec_ref[4:5]).astype(BF16)
    outs.append(copy(residual_ref, residual_hbm, out_sems.at[3]))
    outs.append(copy(normed_ref, normed_hbm, out_sems.at[4]))
    outs[-2].start()
    outs[-1].start()
    factor = LOG2E / math.sqrt(hd)
    for task in ws:
        task.wait()
    for c in range(2):
        rows = slice(2 * c * cells, 2 * (c + 1) * cells)
        for t in range(3):
            out = mm(normed_ref[rows], w_ref[t])
            if t == 0:
                out = out * factor
            for n in range(2):
                flipped = out[n * cells : (n + 1) * cells].T.astype(BF16)
                for h in range(HEADS):
                    qkv_ref[c, n * HEADS + h, t] = flipped[h * hd : (h + 1) * hd]
        gs[c].wait()
        outs.append(copy(qkv_ref.at[c], qkv_out[c], out_sems.at[5 + c]))
        outs[-1].start()
    for task in outs:
        task.wait()


def forward(info, stats, expand, vec, x, sib, far, g, conv_weight, wq, wk, wv):
    images, cells, channels = x.shape
    tokens = images * cells
    hd = channels // HEADS
    hbm = pl.BlockSpec(memory_space=pl.ANY)
    vmem = pl.BlockSpec(memory_space=pltpu.VMEM)
    row_type = jax.ShapeDtypeStruct((tokens, channels), BF16)
    qkv_type = jax.ShapeDtypeStruct((2 * HEADS, 4, hd, cells), BF16)
    return pl.pallas_call(
        forward_kernel,
        in_specs=[pl.BlockSpec(memory_space=pltpu.SMEM)] + [vmem] * 3 + [hbm] * 8,
        out_specs=[hbm] * 7 + [vmem],
        out_shape=[row_type] * 5
        + [qkv_type] * 2
        + [jax.ShapeDtypeStruct((2 * images, channels), F32)],
        scratch_shapes=[
            pltpu.VMEM((3, images, cells, channels), BF16),
            pltpu.VMEM((3, 3, channels, channels), BF16),
            pltpu.VMEM((3, channels, channels), BF16),
            pltpu.VMEM((3, tokens, channels), BF16),
            pltpu.VMEM((tokens, channels), F32),
            pltpu.VMEM((tokens, channels), BF16),
            pltpu.VMEM((tokens, channels), BF16),
            pltpu.VMEM((2, 2 * HEADS, 4, hd, cells), BF16),
            pltpu.SemaphoreType.DMA((11,)),
            pltpu.SemaphoreType.DMA((7,)),
        ],
        compiler_params=params(),
        cost_estimate=cost(24 * tokens * channels**2, 20e6, 1e6),
        name="forward_conv",
    )(info, stats, expand, vec, x, sib, far, g, conv_weight, wq, wk, wv)


def together(*tasks):
    results = [None] * len(tasks)
    active = list(enumerate(tasks))
    while active:
        still = []
        for i, task in active:
            try:
                results[i] = next(task)
                still.append((i, task))
            except StopIteration:
                pass
        active = still
    return results


def attention_kernel(
    qkv_ref, out_ref, kt_ref, vt_ref, kn_ref, vn_ref, s_ref, e_ref, dk_ref, dv_ref
):
    step = pl.program_id(0)
    sources, _, hd, cells = qkv_ref.shape
    length = sources * cells
    wide = kn_ref.shape[1]
    block = s_ref.shape[2]
    per = block // cells
    spans = [slice(c, c + KEY_CHUNK) for c in range(0, length, KEY_CHUNK)]
    extra = vt_ref.shape[0] - hd

    @pl.when(step == 0)
    def _():
        ones_row = (lax.broadcasted_iota(jnp.int32, (extra, cells), 0) == 0).astype(F32)
        pad = jnp.zeros((wide - hd, cells), F32)
        row = lax.broadcasted_iota(jnp.int32, (wide - hd, cells), 0)
        ones_two = (row < 2).astype(F32)
        for s in range(sources):
            sl = slice(s * cells, (s + 1) * cells)
            k = qkv_ref[s, 1]
            v = qkv_ref[s, 2]
            kt_ref[:, sl] = k
            vt_ref[:hd, sl] = v
            vt_ref[hd:, sl] = ones_row.astype(BF16)
            kn_ref[sl] = jnp.concatenate([k.astype(F32), pad], axis=0).T.astype(BF16)
            vn_ref[sl] = jnp.concatenate([v.astype(F32), ones_two], axis=0).T.astype(BF16)
        dk_ref[...] = jnp.zeros_like(dk_ref)
        dv_ref[...] = jnp.zeros_like(dv_ref)

    bases = [(2 * step + b) * per for b in range(2)]

    def rows_of(b, t):
        return jnp.concatenate([qkv_ref[bases[b] + u, t] for u in range(per)], axis=1).astype(F32)

    def put(b, t, value):
        for u in range(per):
            out_ref[bases[b] + u, t] = value[:, u * cells : (u + 1) * cells].astype(BF16)

    def scores(b):
        q = jnp.concatenate([rows_of(b, 0), jnp.zeros((wide - hd, block), F32)], axis=0)
        q_t = q.astype(BF16)
        top = None
        for sl in spans:
            value = mm(kn_ref[sl], q_t)
            s_ref[b, sl] = value
            here = jnp.max(value, axis=0, keepdims=True)
            top = here if top is None else jnp.maximum(top, here)
            yield None
        yield top, q.T.astype(BF16)

    def attend(b, top):
        acc = jnp.zeros((hd + extra, block), F32)
        for sl in spans:
            e = jnp.exp2(s_ref[b, sl] - top).astype(BF16)
            e_ref[b, sl] = e
            acc += mm(vt_ref[:, sl], e)
            yield None
        yield acc

    def finish(b, acc):
        inverse = 1.0 / acc[hd : hd + 1]
        out = acc[:hd] * inverse
        put(b, 0, out)
        g = (rows_of(b, 3) * inverse).astype(BF16).astype(F32)
        delta = -jnp.sum(g * out, axis=0, keepdims=True)
        high = delta.astype(BF16).astype(F32)
        low = delta - high
        row = lax.broadcasted_iota(jnp.int32, (wide - hd, block), 0)
        tail = jnp.where(row == 0, high, jnp.where(row == 1, low, 0.0))
        g = jnp.concatenate([g, tail], axis=0)
        return g.astype(BF16), g.T.astype(BF16)

    def back(b, g_t, g_n, q_n):
        dq = jnp.zeros((hd, block), F32)
        for sl in spans:
            e = e_ref[b, sl]
            ds = (e.astype(F32) * mm(vn_ref[sl], g_t)).astype(BF16)
            dq += mm(kt_ref[:, sl], ds)
            dk_ref[sl] += mm(ds, q_n)
            dv_ref[sl] += mm(e, g_n)
            yield None
        put(b, 1, dq * (1.0 / math.sqrt(hd)))
        yield None

    ((top0, q0),) = together(scores(0))
    acc0, (top1, q1) = together(attend(0, top0), scores(1))
    _, acc1 = together(back(0, *finish(0, acc0), q0), attend(1, top1))
    together(back(1, *finish(1, acc1), q1))

    @pl.when(step == pl.num_programs(0) - 1)
    def _():
        for s in range(sources):
            sl = slice(s * cells, (s + 1) * cells)
            out_ref[s, 2] = (dk_ref[sl].T[:hd] * (1.0 / LOG2E)).astype(BF16)
            out_ref[s, 3] = dv_ref[sl].T[:hd].astype(BF16)


def attention(qkv):
    sources, _, hd, cells = qkv.shape
    length = sources * cells
    block = QUERY_BLOCK
    wide = 128
    full = lambda shape: pl.BlockSpec(shape, lambda i: (0,) * len(shape))
    return pl.pallas_call(
        attention_kernel,
        grid=(length // block // 2,),
        in_specs=[full(qkv.shape)],
        out_specs=full((sources, 4, hd, cells)),
        out_shape=jax.ShapeDtypeStruct((sources, 4, hd, cells), BF16),
        scratch_shapes=[
            pltpu.VMEM((hd, length), BF16),
            pltpu.VMEM((hd + 16, length), BF16),
            pltpu.VMEM((length, wide), BF16),
            pltpu.VMEM((length, wide), BF16),
            pltpu.VMEM((2, length, block), F32),
            pltpu.VMEM((2, length, block), BF16),
            pltpu.VMEM((length, wide), F32),
            pltpu.VMEM((length, wide), F32),
        ],
        compiler_params=params(),
        cost_estimate=cost(12 * length * length * 256, 5e6, length * length),
        name="attention",
    )(qkv)


def gather_heads(got_ref, t):
    return jnp.concatenate(
        [
            jnp.concatenate([got_ref[n * HEADS + h, t] for h in range(HEADS)], axis=0)
            for n in range(2)
        ],
        axis=1,
    )


def tokens_kernel(
    got_ref,
    residual_ref,
    up_ref,
    vec_ref,
    wo_ref,
    wq_ref,
    wk_ref,
    wv_ref,
    block_out_ref,
    rg_ref,
    sums_ref,
):
    residual = residual_ref[...].astype(F32)
    up = up_ref[...].astype(F32)
    mixed = mm(gather_heads(got_ref, 0).T, wo_ref[...])
    block_out_ref[...] = (residual + mixed + vec_ref[5:6]).astype(BF16)
    grad = mm_nt(gather_heads(got_ref, 1).T, wq_ref[...])
    grad += mm_nt(gather_heads(got_ref, 2).T, wk_ref[...])
    grad += mm_nt(gather_heads(got_ref, 3).T, wv_ref[...])
    dev = residual - jnp.mean(residual, axis=1, keepdims=True)
    scale = lax.rsqrt(jnp.mean(dev * dev, axis=1, keepdims=True) + EPSILON)
    standard = dev * scale
    scaled = grad * vec_ref[3:4]
    part = scale * (
        scaled
        - jnp.mean(scaled, axis=1, keepdims=True)
        - standard * jnp.mean(scaled * standard, axis=1, keepdims=True)
    )
    rg = (up + part).astype(BF16)
    rg_ref[...] = rg
    sums_ref[0:1] = jnp.sum(rg.astype(F32), axis=0, keepdims=True)
    sums_ref[1:2] = jnp.sum(grad * standard, axis=0, keepdims=True)
    sums_ref[2:3] = jnp.sum(grad, axis=0, keepdims=True)
    sums_ref[3:4] = jnp.sum(up, axis=0, keepdims=True)


def after_attention(got, residual, up, vec, wo, wq, wk, wv, part):
    channels = residual.shape[1]
    cells = got.shape[3]
    tokens = 2 * cells
    full = lambda shape: pl.BlockSpec(shape, lambda i: (0,) * len(shape))
    rows = pl.BlockSpec((tokens, channels), lambda i: (part, 0))
    square = (channels, channels)
    return pl.pallas_call(
        tokens_kernel,
        grid=(1,),
        in_specs=[full(got.shape), rows, rows, full(vec.shape)] + [full(square)] * 4,
        out_specs=[
            full((tokens, channels)),
            full((tokens, channels)),
            full((4, channels)),
        ],
        out_shape=[
            jax.ShapeDtypeStruct((tokens, channels), BF16),
            jax.ShapeDtypeStruct((tokens, channels), BF16),
            jax.ShapeDtypeStruct((4, channels), F32),
        ],
        compiler_params=params(),
        cost_estimate=cost(8 * tokens * channels**2, 7e6),
        name="after_attention",
    )(got, residual, up, vec, wo, wq, wk, wv)


def weights_kernel(gscale, info_ref, perm_hbm, *refs):
    (
        own_hbm, sib_hbm, far_hbm, normed_hbm, normed_sib_hbm, up_hbm, up_sib_hbm,
        rg0_hbm, rg1_hbm, rg0_sib_hbm, rg1_sib_hbm,
        got0_hbm, got1_hbm, got0_sib_hbm, got1_sib_hbm,
        own_far_hbm,
    ) = refs[:16]
    outs_hbm = refs[16:22]
    perm_ref, rg_ref, got_ref, up_ref, left_ref, right_ref, out_ref = refs[22:29]
    in_sems, got_sems, out_sems = refs[29:]
    copy = pltpu.make_async_copy
    core = info_ref[0]
    half = rg_ref.shape[1]
    tokens = 2 * half
    cells = got_ref.shape[4]
    mine, other = pl.ds(0, tokens), pl.ds(tokens, tokens)
    perm_in = copy(perm_hbm, perm_ref, in_sems.at[0])
    rg_in = [
        copy(h, rg_ref.at[u], in_sems.at[1 + u])
        for u, h in enumerate((rg0_hbm, rg1_hbm, rg0_sib_hbm, rg1_sib_hbm))
    ]
    hidden_in = [
        copy(own_hbm, right_ref.at[1, mine], in_sems.at[5]),
        copy(sib_hbm, right_ref.at[2 - 2 * core, mine], in_sems.at[6]),
        copy(own_far_hbm, right_ref.at[2 * core, mine], in_sems.at[7]),
        copy(own_hbm, right_ref.at[2 * core, other], in_sems.at[8]),
        copy(sib_hbm, right_ref.at[1, other], in_sems.at[9]),
        copy(far_hbm, right_ref.at[2 - 2 * core, other], in_sems.at[10]),
    ]
    normed_in = [
        copy(normed_hbm, right_ref.at[3, mine], in_sems.at[11]),
        copy(normed_sib_hbm, right_ref.at[3, other], in_sems.at[12]),
    ]
    up_in = [
        copy(up_hbm, up_ref.at[mine], in_sems.at[13]),
        copy(up_sib_hbm, up_ref.at[other], in_sems.at[14]),
    ]
    gots = (got0_hbm, got1_hbm, got0_sib_hbm, got1_sib_hbm)
    got_in = [
        [copy(gots[u].at[:, t], got_ref.at[u, t], got_sems.at[u, t]) for u in range(4)]
        for t in range(4)
    ]
    order = [perm_in] + rg_in + hidden_in + got_in[1] + normed_in
    order += got_in[2] + got_in[0] + up_in + got_in[3]
    for task in order:
        task.start()

    def heads(u, t):
        return jnp.concatenate(
            [
                jnp.concatenate([got_ref[u, t, n * HEADS + h] for h in range(HEADS)], axis=0)
                for n in range(2)
            ],
            axis=1,
        )

    outs = []

    def emit(place, left, right):
        value = mm(left, right_ref[right])
        for i, p in enumerate(range(3) if place < 4 else (1,)):
            entry = PARTS[p][0] + place
            out_ref[entry] = (value[i * count : (i + 1) * count] * gscale).astype(BF16)
            rows = count // 2
            for k in range(2):
                outs.append(
                    copy(
                        out_ref.at[entry, pl.ds(k * rows, rows)],
                        outs_hbm[2 * p + k].at[place],
                        out_sems.at[entry, k],
                    )
                )
                outs[-1].start()

    def wait(tasks):
        for task in tasks:
            task.wait()

    count = perm_ref.shape[1]
    wait([perm_in] + rg_in)
    for p in range(3):
        rows = slice(p * count, (p + 1) * count)
        for u in range(4):
            pieces = []
            for n in range(half // cells):
                piece = rg_ref[u, n * cells : (n + 1) * cells]
                if p != 1:
                    piece = shift_rows(piece.astype(F32), p - 1).astype(BF16)
                pieces.append(piece)
            place = slice(u * half, (u + 1) * half)
            left_ref[0, rows, place] = mm_nt(
                perm_ref[p], jnp.concatenate(pieces, axis=0)
            ).astype(BF16)
    wait(hidden_in)
    for a in range(3):
        emit(a, left_ref[0], a)
    wait(got_in[1] + got_in[2] + got_in[3])
    for p in range(3):
        rows = slice(p * count, (p + 1) * count)
        for u in range(4):
            place = slice(u * half, (u + 1) * half)
            left_ref[1, rows, place] = mm(perm_ref[p], heads(u, 1 + p)).astype(BF16)
    wait(normed_in)
    emit(3, left_ref[1], 3)
    wait(got_in[0] + up_in)
    for u in range(4):
        right_ref[4, u * half : (u + 1) * half] = heads(u, 0).T
    emit(4, mm_nt(perm_ref[1], up_ref[...]).astype(BF16), 4)
    wait(outs)


def weight_grads(gscale, info, perm, ins):
    tokens, channels = ins[0].shape
    entries = ENTRIES
    rows = perm.shape[1] // 2
    hbm = pl.BlockSpec(memory_space=pl.ANY)
    out_shape = []
    for _, count in PARTS:
        out_shape += [jax.ShapeDtypeStruct((count, rows, channels), BF16)] * 2
    outs = pl.pallas_call(
        functools.partial(weights_kernel, gscale),
        in_specs=[pl.BlockSpec(memory_space=pltpu.SMEM)] + [hbm] * (1 + len(ins)),
        out_specs=[hbm] * 6,
        out_shape=out_shape,
        scratch_shapes=[
            pltpu.VMEM(perm.shape, BF16),
            pltpu.VMEM((4, tokens // 2, channels), BF16),
            pltpu.VMEM((4, 4) + ins[-2].shape[:1] + ins[-2].shape[2:], BF16),
            pltpu.VMEM((2 * tokens, channels), BF16),
            pltpu.VMEM((2, 3 * perm.shape[1], 2 * tokens), BF16),
            pltpu.VMEM((5, 2 * tokens, channels), BF16),
            pltpu.VMEM((entries, 2 * rows, channels), BF16),
            pltpu.SemaphoreType.DMA((15,)),
            pltpu.SemaphoreType.DMA((4, 4)),
            pltpu.SemaphoreType.DMA((entries, 2)),
        ],
        compiler_params=params(),
        cost_estimate=cost(2 * 20 * tokens * channels**2, 20e6),
        name="weight_grads",
    )(info, perm, *ins)
    return [outs[2 * p : 2 * p + 2] for p in range(3)]


def fold_half_kernel(*refs):
    for p in range(3):
        mine, got, own_ref, send_ref = refs[2 * p], refs[2 * p + 1], refs[6 + 2 * p], refs[7 + 2 * p]
        rows = own_ref.shape[1]
        total = mine[...].astype(F32) + got[...].astype(F32)
        own_ref[...] = total[:, :rows].astype(BF16)
        send_ref[...] = total[:, rows:].astype(BF16)


def fold_half(values):
    shapes = []
    for value in values:
        count, rows, channels = value.shape
        shapes.append(jax.ShapeDtypeStruct((count, rows // 2, channels), BF16))
    return pl.pallas_call(
        fold_half_kernel,
        out_shape=shapes,
        compiler_params=params(),
        cost_estimate=cost(4e6, 8e6),
        name="fold_half",
    )(*values)


def fold_first_kernel(*refs):
    ins, (own_ref, *sends) = refs[:6], refs[6:]
    for p, (first, count) in enumerate(PARTS):
        rows = ins[0].shape[1] // 4
        for e in range(count):
            total = ins[2 * p][e].astype(F32) + ins[2 * p + 1][e].astype(F32)
            own_ref[first + e] = total[:rows]
            place, group = ((e, 0), (e, 1), (PARTS[0][1] + e, 0))[p]
            for k in range(1, 4):
                sends[3 * group + k - 1][place] = total[k * rows : (k + 1) * rows].astype(BF16)


def fold_second_kernel(*refs):
    own_in, got, (own_ref, *sends) = refs[0], refs[1:7], refs[7:]
    rows = own_in.shape[1] // 4
    for p, (first, count) in enumerate(PARTS):
        for e in range(count):
            place, group = ((e, 0), (e, 1), (PARTS[0][1] + e, 0))[p]
            total = own_in[first + e]
            for k in range(3):
                total = total + got[3 * group + k][place].astype(F32)
            own_ref[first + e] = total[:rows]
            place, group = ((e, 0), (PARTS[0][1] + e, 0), (e, 1))[p]
            for k in range(1, 4):
                sends[3 * group + k - 1][place] = total[k * rows : (k + 1) * rows].astype(BF16)


def fold_last_kernel(*refs):
    own_in, got, (conv_ref, q_ref, k_ref, v_ref, o_ref) = refs[0], refs[1:7], refs[7:]
    rows = own_in.shape[1]
    for p, (first, count) in enumerate(PARTS):
        for e in range(count):
            place, group = ((e, 0), (PARTS[0][1] + e, 0), (e, 1))[p]
            total = own_in[first + e]
            for k in range(3):
                total = total + got[3 * group + k][place].astype(F32)
            if e < 3:
                for r in range(rows):
                    conv_ref[e, r, p : p + 1] = total[r : r + 1]
            elif e == 3:
                (q_ref, k_ref, v_ref)[p][...] = total
            else:
                o_ref[...] = total


def fold_first(values):
    _, rows, channels = values[0].shape
    cut = rows // 4
    entries = ENTRIES
    wide = PARTS[0][1] + PARTS[2][1]
    sizes = [wide] * 3 + [PARTS[1][1]] * 3
    return pl.pallas_call(
        fold_first_kernel,
        out_shape=[jax.ShapeDtypeStruct((entries, cut, channels), F32)]
        + [jax.ShapeDtypeStruct((s, cut, channels), BF16) for s in sizes],
        compiler_params=params(),
        cost_estimate=cost(4e6, 7e6),
        name="fold_first",
    )(*values)


def fold_second(values):
    entries, rows, channels = values[0].shape
    cut = rows // 4
    wide = PARTS[0][1] + PARTS[1][1]
    sizes = [wide] * 3 + [PARTS[2][1]] * 3
    return pl.pallas_call(
        fold_second_kernel,
        out_shape=[jax.ShapeDtypeStruct((entries, cut, channels), F32)]
        + [jax.ShapeDtypeStruct((s, cut, channels), BF16) for s in sizes],
        compiler_params=params(),
        cost_estimate=cost(1e6, 2e6),
        name="fold_second",
    )(*values)


def fold_last(values):
    _, rows, channels = values[0].shape
    return pl.pallas_call(
        fold_last_kernel,
        out_shape=[jax.ShapeDtypeStruct((3, rows, 3, channels), F32)]
        + [jax.ShapeDtypeStruct((rows, channels), F32)] * 4,
        compiler_params=params(),
        cost_estimate=cost(3e5, 7e5),
        name="fold_last",
    )(*values)


def coordinates(index):
    dp, strip = index // 16, index % 16
    return {
        "x": dp // 2,
        "z": (strip // 8) * 2 + dp % 2,
        "y": (strip // 2) % 4,
        "core": strip % 2,
    }


def device_index(place):
    dp = place["x"] * 2 + place["z"] % 2
    strip = (place["z"] // 2) * 8 + place["y"] * 2 + place["core"]
    return dp * 16 + strip


def ring_pairs(axis, offset):
    pairs = []
    for source in range(128):
        place = coordinates(source)
        place[axis] = (place[axis] + offset) % 4
        pairs.append((source, device_index(place)))
    return pairs


def row_order(channels, here):
    per = channels // 128
    row = jnp.arange(channels // 2, dtype=jnp.int32)
    r = row % per
    k3 = (row // per) % 4
    k2 = (row // (per * 4)) % 4
    k1 = row // (per * 16)
    flip = (k1 // 2) ^ (3 * (k1 % 2))
    orders = []
    for order in ORDERS:
        place = {"core": here["core"], order[0]: here[order[0]] ^ flip}
        for axis, k in zip(order[1:], (k2, k3)):
            place[axis] = (here[axis] + k) % 4
        orders.append(device_index(place) * per + r)
    return jnp.stack(orders)


def ring_send(value, axis, offset):
    return lax.ppermute(value, ("dp", "strip"), ring_pairs(axis, offset))


def pair_send(value, axis, flip):
    pairs = []
    for source in range(128):
        place = coordinates(source)
        place[axis] = place[axis] ^ flip
        pairs.append((source, device_index(place)))
    return lax.ppermute(value, ("dp", "strip"), pairs)


def scatter_sum(blocks):
    for flip, join in ((1, fold_half), (3, fold_first)):
        values = []
        for (own, send), order in zip(blocks, ORDERS):
            values += [own, pair_send(send, order[0], flip)]
        joined = join(values)
        blocks = [joined[2 * p : 2 * p + 2] for p in range(3)]
    own, *sends = joined
    values = [own]
    for i, send in enumerate(sends):
        values.append(ring_send(send, ("x", "y")[i // 3], i % 3 + 1))
    own, *sends = fold_second(values)
    values = [own]
    for i, send in enumerate(sends):
        values.append(ring_send(send, ("z", "y")[i // 3], i % 3 + 1))
    return fold_last(values)


def backward_kernel(
    gscale,
    info_ref,
    expand_ref,
    rg_ref,
    sib_ref,
    far_ref,
    x_ref,
    chan_ref,
    vec_ref,
    conv_ref,
    *refs,
):
    last = len(refs) > 3
    if last:
        pick_ref, early_ref, sums0_ref, sums1_ref, ag_ref, payload_ref, acc_ref = refs
    else:
        ag_ref, out_ref, acc_ref = refs
    step = pl.program_id(0)
    images, cells, channels = x_ref.shape
    first = images if last else 0
    even = info_ref[0] == 0
    sib = sib_ref[...]
    far = far_ref[...]
    totals = mm_nt(jnp.where(even, sib, far), conv_ref[0, 0])
    totals += mm_nt(rg_ref[...], conv_ref[1, 0])
    totals += mm_nt(jnp.where(even, far, sib), conv_ref[2, 0])

    @pl.when(step == 0)
    def _():
        for n in range(images):
            sl = slice(n * cells, (n + 1) * cells)
            acc_ref[sl] = shift_rows(totals[sl], -1)

    @pl.when(step == 1)
    def _():
        acc_ref[...] += totals

    @pl.when(step == 2)
    def _():
        gain = vec_ref[0:1]
        plain, weighted = [], []
        for n in range(images):
            sl = slice(n * cells, (n + 1) * cells)
            grad = acc_ref[sl] + shift_rows(totals[sl], 1)
            m = first + n
            standard = (x_ref[n].astype(F32) - chan_ref[m : m + 1]) * chan_ref[
                2 * images + m : 2 * images + m + 1
            ]
            u = standard * gain + vec_ref[1:2]
            sigma = 1.0 / (1.0 + jnp.exp(-u))
            ag = grad * (sigma * (1.0 + u * (1.0 - sigma)))
            ag_ref[sl] = ag
            plain.append(jnp.sum(ag, axis=0, keepdims=True))
            weighted.append(jnp.sum(ag * standard, axis=0, keepdims=True))
        if not last:
            out_ref[...] = jnp.concatenate(plain + weighted, axis=0)
            return
        plain = [early_ref[n : n + 1] for n in range(images)] + plain
        weighted = [early_ref[images + n : images + n + 1] for n in range(images)] + weighted
        all_totals = group_sum(jnp.concatenate(plain + weighted, axis=0) * gain, expand_ref[...])
        sums = sums0_ref[...] + sums1_ref[...]
        vectors = gscale * jnp.concatenate(
            [sum(weighted), sum(plain), sums, jnp.zeros((2, channels), F32)], axis=0
        )
        pieces = []
        for _ in range(3):
            piece = vectors.astype(BF16)
            pieces.append(piece)
            vectors = vectors - piece.astype(F32)
        picked = [mm(piece, pick_ref[...]) for piece in pieces]
        picked = picked[0] + picked[1] + picked[2]
        for s in range(payload_ref.shape[0]):
            payload_ref[s] = all_totals + picked[:, s * LANES : (s + 1) * LANES]


def backward(gscale, info, expand, rg, sib, far, x, chan, vec, conv_weight, part, more=()):
    images, cells, channels = x.shape
    images = images // 2
    tokens = images * cells
    full = lambda shape: pl.BlockSpec(shape, lambda b: (0,) * len(shape))
    if more:
        out = (16, 4 * images, LANES)
    else:
        out = (2 * images, channels)
    return pl.pallas_call(
        functools.partial(backward_kernel, gscale),
        grid=(3,),
        in_specs=[pl.BlockSpec(memory_space=pltpu.SMEM)]
        + [full(v.shape) for v in (expand, rg, sib, far)]
        + [pl.BlockSpec((images, cells, channels), lambda b: (part, 0, 0))]
        + [full(v.shape) for v in (chan, vec)]
        + [pl.BlockSpec((3, 1, channels, channels), lambda b: (0, b, 0, 0))]
        + [full(v.shape) for v in more],
        out_specs=[full((tokens, channels)), full(out)],
        out_shape=[
            jax.ShapeDtypeStruct((tokens, channels), F32),
            jax.ShapeDtypeStruct(out, F32),
        ],
        scratch_shapes=[pltpu.VMEM((tokens, channels), F32)],
        compiler_params=params(),
        cost_estimate=cost(18 * tokens * channels**2, 10e6, 2e5),
        name="backward_conv",
    )(info, expand, rg, sib, far, x, chan, vec, conv_weight, *more)


def input_kernel(
    totals_ref, expand_ref, rg0_ref, rg1_ref, ag0_ref, ag1_ref, x_ref, chan_ref, vec_ref,
    out_ref, spread_ref
):
    images, cells, channels = x_ref.shape
    strips = totals_ref.shape[0]
    count = strips * cells * (channels // GROUPS)
    summed = jnp.sum(totals_ref[...], axis=0)
    for d in range(spread_ref.shape[0]):
        spread_ref[d] = summed
    spread_c = spread(summed / count, expand_ref[...])
    for n in range(images):
        u, m = n // 2, n % 2
        sl = slice(m * cells, (m + 1) * cells)
        scale = chan_ref[images + n : images + n + 1]
        standard = (x_ref[n].astype(F32) - chan_ref[n : n + 1]) * scale
        part = scale * (
            (ag0_ref, ag1_ref)[u][sl] * vec_ref[0:1]
            - spread_c[n : n + 1]
            - standard * spread_c[images + n : images + n + 1]
        )
        rg = (rg0_ref, rg1_ref)[u][sl].astype(F32)
        out_ref[n] = (rg + part).astype(BF16)


def input_grad(totals, expand, rg0, rg1, ag0, ag1, x, chan, vec, copies):
    return pl.pallas_call(
        input_kernel,
        out_shape=[
            jax.ShapeDtypeStruct(x.shape, BF16),
            jax.ShapeDtypeStruct((copies,) + totals.shape[1:], F32),
        ],
        compiler_params=params(),
        cost_estimate=cost(3e6, 4e6),
        name="input_grad",
    )(totals, expand, rg0, rg1, ag0, ag1, x, chan, vec)


def exchange(value, axis="strip"):
    return lax.all_to_all(value, axis, split_axis=0, concat_axis=0, tiled=True)


def core_mate(value):
    return lax.ppermute(value, "strip", [(i, i ^ 1) for i in range(16)])


def far_row(value):
    pairs = [(i, i + 1) for i in range(1, 15, 2)]
    return lax.ppermute(value, "strip", pairs + [(j, i) for i, j in pairs])


def pick_matrix(channels, groups_dp, strips):
    per = channels // (groups_dp * strips)
    pick = np.zeros((channels, strips * LANES), np.float32)
    for o in range(channels):
        device, r = divmod(o, per)
        dp, strip = divmod(device, strips)
        pick[o, strip * LANES + GROUPS + dp * per + r] = 1.0
    return jnp.asarray(pick, BF16)


def on_device(
    block_in,
    upstream,
    gn_gain,
    gn_bias,
    conv_weight,
    conv_bias,
    ln_gain,
    ln_bias,
    w_query,
    w_key,
    w_value,
    w_out,
    out_bias,
):
    images, strip_rows, cells, channels = block_in.shape
    strips = lax.axis_size("strip")
    groups_dp = lax.axis_size("dp")
    me = lax.axis_index("strip")
    me_dp = lax.axis_index("dp")
    gscale = 1.0 / math.sqrt(cells * strips * images * groups_dp)
    x = block_in.reshape(images, cells, channels)
    up = upstream.reshape(images, cells, channels)
    up_rows = upstream.reshape(images * cells, channels)
    expand = expand_matrix(channels)
    core = me % 2
    inside = jnp.where(core == 0, me > 0, me < strips - 1)
    info = jnp.stack([core, inside.astype(jnp.int32)]).astype(jnp.int32)
    here = coordinates(me_dp * 16 + me)
    order = row_order(channels, here)
    perm = (order[:, :, None] == jnp.arange(channels, dtype=jnp.int32)).astype(BF16)

    x_far = far_row(x)
    x_sib = core_mate(x)
    up_sib = core_mate(up_rows)
    stats, vec = local_stats(
        x, expand, (gn_gain, gn_bias, conv_bias, ln_gain, ln_bias, out_bias), strips
    )
    stats = exchange(stats)
    g = upstream_heads(up, w_out)
    hid_own, hid_sib, hid_far, residual, normed, qkv0, qkv1, chan = forward(
        info, stats, expand, vec, x, x_sib, x_far, g, conv_weight, w_query, w_key, w_value
    )
    hid_far_sib = core_mate(hid_far)
    normed_sib = core_mate(normed)
    got0, got1 = [exchange(attention(exchange(qkv))) for qkv in (qkv0, qkv1)]
    got0_sib = core_mate(got0)
    shared = (residual, up_rows, vec, w_out, w_query, w_key, w_value)
    common = (x, chan, vec, conv_weight)
    block_out0, rg0, sums0 = after_attention(got0, *shared, 0)
    rg0_sib, rg0_far = core_mate(rg0), far_row(rg0)
    ag0, early = backward(gscale, info, expand, rg0, rg0_sib, rg0_far, *common, 0)
    got1, ag0, early = lax.optimization_barrier((got1, ag0, early))
    got1_sib = core_mate(got1)
    block_out1, rg1, sums1 = after_attention(got1, *shared, 1)
    rg1_sib, rg1_far = core_mate(rg1), far_row(rg1)
    block_out = jnp.concatenate([block_out0, block_out1], axis=0)
    blocks = weight_grads(
        gscale,
        info,
        perm,
        (
            hid_own, hid_sib, hid_far_sib, normed, normed_sib, up_rows, up_sib,
            rg0, rg1, rg0_sib, rg1_sib, got0, got1, got0_sib, got1_sib, hid_far,
        ),
    )
    pick = pick_matrix(channels, groups_dp, strips)
    ag1, payload = backward(
        gscale, info, expand, rg1, rg1_sib, rg1_far, *common, 1,
        (pick, early, sums0, sums1),
    )
    grad_input, vectors = input_grad(
        exchange(payload), expand, rg0, rg1, ag0, ag1, x, chan, vec, groups_dp
    )
    conv_shard, q_shard, k_shard, v_shard, o_shard = scatter_sum(blocks)
    per = channels // (strips * groups_dp)
    vectors = jnp.sum(exchange(vectors, "dp"), axis=0)
    shards = lax.dynamic_slice_in_dim(vectors, GROUPS + me_dp * per, per, axis=1)
    shape = block_in.shape
    return (
        block_out.reshape(shape),
        grad_input.reshape(shape),
        conv_shard.transpose(0, 2, 3, 1),
        q_shard.T,
        k_shard.T,
        v_shard.T,
        o_shard.T,
        shards[0],
        shards[1],
        shards[2],
        shards[3],
        shards[4],
        shards[5],
    )


def solution(mesh):
    rows = P("dp", "strip", None, None)
    both = ("dp", "strip")
    in_specs = (rows, rows) + (P(),) * 11
    out_specs = (rows, rows, P(None, None, None, both)) + (P(None, both),) * 4 + (P(both),) * 6
    return jax.shard_map(
        on_device, mesh=mesh, in_specs=in_specs, out_specs=out_specs, check_vma=False
    )
```

```python
import functools
import math

import jax
import jax.numpy as jnp
import numpy as np
from jax import lax
from jax.experimental import pallas as pl
from jax.experimental.pallas import tpu as pltpu
from jax.sharding import PartitionSpec as P

HEADS = 8
GROUPS = 32
EPSILON = 1e-05
F32 = jnp.float32
BF16 = jnp.bfloat16
NT = (((1,), (1,)), ((), ()))
HIGH = lax.Precision.HIGHEST
VMEM_LIMIT = 56 * 1024 * 1024
LOG2E = math.log2(math.e)
QUERY_BLOCK = 1024
KEY_CHUNK = 512
ORDERS = (("y", "x", "z"), ("x", "y", "z"), ("z", "x", "y"))
ENTRIES = 13
LANES = 128
PARTS = ((0, 4), (4, 5), (9, 4))


def params(semantics=None):
    if semantics is None:
        return pltpu.CompilerParams(vmem_limit_bytes=VMEM_LIMIT)
    return pltpu.CompilerParams(
        vmem_limit_bytes=VMEM_LIMIT, dimension_semantics=semantics
    )


def mm(a, b):
    return jnp.dot(a, b, preferred_element_type=F32)


def mm_nt(a, b):
    return lax.dot_general(a, b, NT, preferred_element_type=F32)


def group_sum(rows, expand):
    return lax.dot_general(rows, expand, NT, preferred_element_type=F32, precision=HIGH)


def spread(rows, expand):
    return jnp.dot(rows, expand, preferred_element_type=F32, precision=HIGH)


def expand_matrix(channels):
    per_group = channels // GROUPS
    return jnp.asarray(
        np.arange(channels)[None, :] // per_group == np.arange(LANES)[:, None], F32
    )


def shift_rows(value, down):
    count = value.shape[0]
    row = lax.broadcasted_iota(jnp.int32, value.shape, 0)
    if down == 1:
        return jnp.where(row == 0, 0.0, pltpu.roll(value, 1, 0))
    return jnp.where(row == count - 1, 0.0, pltpu.roll(value, count - 1, 0))


def cost(flops, nbytes, trans=0):
    return pl.CostEstimate(flops=int(flops), bytes_accessed=int(nbytes), transcendentals=int(trans))


def stats_kernel(x_ref, expand_ref, *refs):
    vectors, out_ref, vec_ref = refs[:-2], refs[-2], refs[-1]
    images, cells, channels = x_ref.shape
    count = cells * (channels // GROUPS)
    vec_ref[...] = jnp.zeros_like(vec_ref)
    for i, ref in enumerate(vectors):
        vec_ref[i : i + 1] = ref[...].reshape(1, channels)
    expand = expand_ref[...]
    sums = jnp.concatenate(
        [jnp.sum(x_ref[n].astype(F32), axis=0, keepdims=True) for n in range(images)], axis=0
    )
    mean = group_sum(sums, expand) / count
    mean_c = spread(mean, expand)
    squares = []
    for n in range(images):
        d = x_ref[n].astype(F32) - mean_c[n : n + 1]
        squares.append(jnp.sum(d * d, axis=0, keepdims=True))
    m2 = group_sum(jnp.concatenate(squares, axis=0), expand)
    both = jnp.concatenate([mean, m2], axis=0)
    for s in range(out_ref.shape[0]):
        out_ref[s] = both


def local_stats(x, expand, vectors, strips):
    images, _, channels = x.shape
    return pl.pallas_call(
        stats_kernel,
        out_shape=[
            jax.ShapeDtypeStruct((strips, 2 * images, LANES), F32),
            jax.ShapeDtypeStruct((8, channels), F32),
        ],
        compiler_params=params(),
        cost_estimate=cost(1e7, 7e5),
        name="local_stats",
    )(x, expand, *vectors)


def upstream_kernel(up_ref, w_ref, g_ref):
    images = up_ref.shape[0]
    w = w_ref[...]
    hd = w.shape[0] // HEADS
    for n in range(images):
        g = mm_nt(w, up_ref[n])
        for h in range(HEADS):
            g_ref[n // 2, (n % 2) * HEADS + h] = g[h * hd : (h + 1) * hd].astype(BF16)


def upstream_heads(up, w_out):
    images, cells, channels = up.shape
    return pl.pallas_call(
        upstream_kernel,
        out_shape=jax.ShapeDtypeStruct((images // 2, 2 * HEADS, channels // HEADS, cells), BF16),
        compiler_params=params(),
        cost_estimate=cost(2 * images * cells * channels**2, 2.2e6),
        name="upstream_heads",
    )(up, w_out)


def forward_kernel(
    info_ref,
    stats_ref,
    expand_ref,
    vec_ref,
    x_hbm,
    sib_hbm,
    far_hbm,
    g_hbm,
    conv_hbm,
    wq_hbm,
    wk_hbm,
    wv_hbm,
    hid_own_hbm,
    hid_sib_hbm,
    hid_far_hbm,
    residual_hbm,
    normed_hbm,
    qkv0_hbm,
    qkv1_hbm,
    chan_ref,
    x_ref,
    conv_ref,
    w_ref,
    hidden_ref,
    acc_ref,
    residual_ref,
    normed_ref,
    qkv_ref,
    in_sems,
    out_sems,
):
    _, images, cells, channels = x_ref.shape
    hd = channels // HEADS
    copy = pltpu.make_async_copy
    xs = [copy(h, x_ref.at[i], in_sems.at[i]) for i, h in enumerate((x_hbm, sib_hbm, far_hbm))]
    convs = [copy(conv_hbm.at[:, b], conv_ref.at[b], in_sems.at[3 + b]) for b in range(3)]
    ws = [copy(h, w_ref.at[i], in_sems.at[6 + i]) for i, h in enumerate((wq_hbm, wk_hbm, wv_hbm))]
    qkv_out = (qkv0_hbm, qkv1_hbm)
    gs = [copy(g_hbm.at[c], qkv_ref.at[c, :, 3], in_sems.at[9 + c]) for c in range(2)]
    for task in xs + convs + ws + gs:
        task.start()
    core = info_ref[0]
    strips = stats_ref.shape[0]
    count = cells * (channels // GROUPS)
    got = stats_ref[...]
    means = got[:, :images]
    mean = jnp.sum(means, axis=0) / strips
    off = means - mean[None]
    m2 = jnp.sum(got[:, images:], axis=0) + count * jnp.sum(off * off, axis=0)
    scale = lax.rsqrt(m2 / (count * strips) + EPSILON)
    expand = expand_ref[...]
    mean_c = spread(mean, expand)
    scale_c = spread(scale, expand)
    chan_ref[...] = jnp.concatenate([mean_c, scale_c], axis=0)
    gain = vec_ref[0:1]
    bias = vec_ref[1:2]
    outs = []
    for i, out_hbm in enumerate((hid_own_hbm, hid_sib_hbm, hid_far_hbm)):
        xs[i].wait()
        for n in range(images):
            factor_c = scale_c[n : n + 1] * gain
            u = (x_ref[i, n].astype(F32) - mean_c[n : n + 1]) * factor_c + bias
            h = u * (0.5 + 0.5 * jnp.tanh(0.5 * u))
            if i == 2:
                h = jnp.where(info_ref[1] > 0, h, 0.0)
            hidden_ref[i, n * cells : (n + 1) * cells] = h.astype(BF16)
        outs.append(copy(hidden_ref.at[i], out_hbm, out_sems.at[i]))
        outs[-1].start()

    above = 2 - core
    below = 1 + core
    for b in range(3):
        convs[b].wait()
        total = mm(hidden_ref[0], conv_ref[b, 1])
        total += mm(hidden_ref[above], conv_ref[b, 0])
        total += mm(hidden_ref[below], conv_ref[b, 2])
        if b == 1:
            acc_ref[...] += total
            continue
        for n in range(images):
            sl = slice(n * cells, (n + 1) * cells)
            if b == 0:
                acc_ref[sl] = shift_rows(total[sl], 1)
                continue
            conv = acc_ref[sl] + shift_rows(total[sl], -1)
            residual = (x_ref[0, n].astype(F32) + conv + vec_ref[2:3]).astype(BF16)
            residual_ref[sl] = residual
            tokens = residual.astype(F32)
            dev = tokens - jnp.mean(tokens, axis=1, keepdims=True)
            scale = lax.rsqrt(jnp.mean(dev * dev, axis=1, keepdims=True) + EPSILON)
            normed_ref[sl] = (dev * scale * vec_ref[3:4] + vec_ref[4:5]).astype(BF16)
    outs.append(copy(residual_ref, residual_hbm, out_sems.at[3]))
    outs.append(copy(normed_ref, normed_hbm, out_sems.at[4]))
    outs[-2].start()
    outs[-1].start()
    factor = LOG2E / math.sqrt(hd)
    for task in ws:
        task.wait()
    for c in range(2):
        rows = slice(2 * c * cells, 2 * (c + 1) * cells)
        for t in range(3):
            out = mm(normed_ref[rows], w_ref[t])
            if t == 0:
                out = out * factor
            for n in range(2):
                flipped = out[n * cells : (n + 1) * cells].T.astype(BF16)
                for h in range(HEADS):
                    qkv_ref[c, n * HEADS + h, t] = flipped[h * hd : (h + 1) * hd]
        gs[c].wait()
        outs.append(copy(qkv_ref.at[c], qkv_out[c], out_sems.at[5 + c]))
        outs[-1].start()
    for task in outs:
        task.wait()


def forward(info, stats, expand, vec, x, sib, far, g, conv_weight, wq, wk, wv):
    images, cells, channels = x.shape
    tokens = images * cells
    hd = channels // HEADS
    hbm = pl.BlockSpec(memory_space=pl.ANY)
    vmem = pl.BlockSpec(memory_space=pltpu.VMEM)
    row_type = jax.ShapeDtypeStruct((tokens, channels), BF16)
    qkv_type = jax.ShapeDtypeStruct((2 * HEADS, 4, hd, cells), BF16)
    return pl.pallas_call(
        forward_kernel,
        in_specs=[pl.BlockSpec(memory_space=pltpu.SMEM)] + [vmem] * 3 + [hbm] * 8,
        out_specs=[hbm] * 7 + [vmem],
        out_shape=[row_type] * 5
        + [qkv_type] * 2
        + [jax.ShapeDtypeStruct((2 * images, channels), F32)],
        scratch_shapes=[
            pltpu.VMEM((3, images, cells, channels), BF16),
            pltpu.VMEM((3, 3, channels, channels), BF16),
            pltpu.VMEM((3, channels, channels), BF16),
            pltpu.VMEM((3, tokens, channels), BF16),
            pltpu.VMEM((tokens, channels), F32),
            pltpu.VMEM((tokens, channels), BF16),
            pltpu.VMEM((tokens, channels), BF16),
            pltpu.VMEM((2, 2 * HEADS, 4, hd, cells), BF16),
            pltpu.SemaphoreType.DMA((11,)),
            pltpu.SemaphoreType.DMA((7,)),
        ],
        compiler_params=params(),
        cost_estimate=cost(24 * tokens * channels**2, 20e6, 1e6),
        name="forward_conv",
    )(info, stats, expand, vec, x, sib, far, g, conv_weight, wq, wk, wv)


def together(*tasks):
    results = [None] * len(tasks)
    active = list(enumerate(tasks))
    while active:
        still = []
        for i, task in active:
            try:
                results[i] = next(task)
                still.append((i, task))
            except StopIteration:
                pass
        active = still
    return results


def attention_kernel(
    qkv_ref, out_ref, kt_ref, vt_ref, kn_ref, vn_ref, s_ref, e_ref, dk_ref, dv_ref
):
    step = pl.program_id(0)
    sources, _, hd, cells = qkv_ref.shape
    length = sources * cells
    wide = kn_ref.shape[1]
    block = s_ref.shape[2]
    per = block // cells
    spans = [slice(c, c + KEY_CHUNK) for c in range(0, length, KEY_CHUNK)]
    extra = vt_ref.shape[0] - hd

    @pl.when(step == 0)
    def _():
        ones_row = (lax.broadcasted_iota(jnp.int32, (extra, cells), 0) == 0).astype(F32)
        pad = jnp.zeros((wide - hd, cells), F32)
        row = lax.broadcasted_iota(jnp.int32, (wide - hd, cells), 0)
        ones_two = (row < 2).astype(F32)
        for s in range(sources):
            sl = slice(s * cells, (s + 1) * cells)
            k = qkv_ref[s, 1]
            v = qkv_ref[s, 2]
            kt_ref[:, sl] = k
            vt_ref[:hd, sl] = v
            vt_ref[hd:, sl] = ones_row.astype(BF16)
            kn_ref[sl] = jnp.concatenate([k.astype(F32), pad], axis=0).T.astype(BF16)
            vn_ref[sl] = jnp.concatenate([v.astype(F32), ones_two], axis=0).T.astype(BF16)
        dk_ref[...] = jnp.zeros_like(dk_ref)
        dv_ref[...] = jnp.zeros_like(dv_ref)

    bases = [(2 * step + b) * per for b in range(2)]

    def rows_of(b, t):
        return jnp.concatenate([qkv_ref[bases[b] + u, t] for u in range(per)], axis=1).astype(F32)

    def put(b, t, value):
        for u in range(per):
            out_ref[bases[b] + u, t] = value[:, u * cells : (u + 1) * cells].astype(BF16)

    def scores(b):
        q = jnp.concatenate([rows_of(b, 0), jnp.zeros((wide - hd, block), F32)], axis=0)
        q_t = q.astype(BF16)
        top = None
        for sl in spans:
            value = mm(kn_ref[sl], q_t)
            s_ref[b, sl] = value
            here = jnp.max(value, axis=0, keepdims=True)
            top = here if top is None else jnp.maximum(top, here)
            yield None
        yield top, q.T.astype(BF16)

    def attend(b, top):
        acc = jnp.zeros((hd + extra, block), F32)
        for sl in spans:
            e = jnp.exp2(s_ref[b, sl] - top).astype(BF16)
            e_ref[b, sl] = e
            acc += mm(vt_ref[:, sl], e)
            yield None
        yield acc

    def finish(b, acc):
        inverse = 1.0 / acc[hd : hd + 1]
        out = acc[:hd] * inverse
        put(b, 0, out)
        g = (rows_of(b, 3) * inverse).astype(BF16).astype(F32)
        delta = -jnp.sum(g * out, axis=0, keepdims=True)
        high = delta.astype(BF16).astype(F32)
        low = delta - high
        row = lax.broadcasted_iota(jnp.int32, (wide - hd, block), 0)
        tail = jnp.where(row == 0, high, jnp.where(row == 1, low, 0.0))
        g = jnp.concatenate([g, tail], axis=0)
        return g.astype(BF16), g.T.astype(BF16)

    def back(b, g_t, g_n, q_n):
        dq = jnp.zeros((hd, block), F32)
        for sl in spans:
            e = e_ref[b, sl]
            ds = (e.astype(F32) * mm(vn_ref[sl], g_t)).astype(BF16)
            dq += mm(kt_ref[:, sl], ds)
            dk_ref[sl] += mm(ds, q_n)
            dv_ref[sl] += mm(e, g_n)
            yield None
        put(b, 1, dq * (1.0 / math.sqrt(hd)))
        yield None

    ((top0, q0),) = together(scores(0))
    acc0, (top1, q1) = together(attend(0, top0), scores(1))
    _, acc1 = together(back(0, *finish(0, acc0), q0), attend(1, top1))
    together(back(1, *finish(1, acc1), q1))

    @pl.when(step == pl.num_programs(0) - 1)
    def _():
        for s in range(sources):
            sl = slice(s * cells, (s + 1) * cells)
            out_ref[s, 2] = (dk_ref[sl].T[:hd] * (1.0 / LOG2E)).astype(BF16)
            out_ref[s, 3] = dv_ref[sl].T[:hd].astype(BF16)


def attention(qkv):
    sources, _, hd, cells = qkv.shape
    length = sources * cells
    block = QUERY_BLOCK
    wide = 128
    full = lambda shape: pl.BlockSpec(shape, lambda i: (0,) * len(shape))
    return pl.pallas_call(
        attention_kernel,
        grid=(length // block // 2,),
        in_specs=[full(qkv.shape)],
        out_specs=full((sources, 4, hd, cells)),
        out_shape=jax.ShapeDtypeStruct((sources, 4, hd, cells), BF16),
        scratch_shapes=[
            pltpu.VMEM((hd, length), BF16),
            pltpu.VMEM((hd + 16, length), BF16),
            pltpu.VMEM((length, wide), BF16),
            pltpu.VMEM((length, wide), BF16),
            pltpu.VMEM((2, length, block), F32),
            pltpu.VMEM((2, length, block), BF16),
            pltpu.VMEM((length, wide), F32),
            pltpu.VMEM((length, wide), F32),
        ],
        compiler_params=params(),
        cost_estimate=cost(12 * length * length * 256, 5e6, length * length),
        name="attention",
    )(qkv)


def gather_heads(got_ref, t):
    return jnp.concatenate(
        [
            jnp.concatenate([got_ref[n * HEADS + h, t] for h in range(HEADS)], axis=0)
            for n in range(2)
        ],
        axis=1,
    )


def tokens_kernel(
    got_ref,
    residual_ref,
    up_ref,
    vec_ref,
    wo_ref,
    wq_ref,
    wk_ref,
    wv_ref,
    block_out_ref,
    rg_ref,
    sums_ref,
):
    residual = residual_ref[...].astype(F32)
    up = up_ref[...].astype(F32)
    mixed = mm(gather_heads(got_ref, 0).T, wo_ref[...])
    block_out_ref[...] = (residual + mixed + vec_ref[5:6]).astype(BF16)
    grad = mm_nt(gather_heads(got_ref, 1).T, wq_ref[...])
    grad += mm_nt(gather_heads(got_ref, 2).T, wk_ref[...])
    grad += mm_nt(gather_heads(got_ref, 3).T, wv_ref[...])
    dev = residual - jnp.mean(residual, axis=1, keepdims=True)
    scale = lax.rsqrt(jnp.mean(dev * dev, axis=1, keepdims=True) + EPSILON)
    standard = dev * scale
    scaled = grad * vec_ref[3:4]
    part = scale * (
        scaled
        - jnp.mean(scaled, axis=1, keepdims=True)
        - standard * jnp.mean(scaled * standard, axis=1, keepdims=True)
    )
    rg = (up + part).astype(BF16)
    rg_ref[...] = rg
    sums_ref[0:1] = jnp.sum(rg.astype(F32), axis=0, keepdims=True)
    sums_ref[1:2] = jnp.sum(grad * standard, axis=0, keepdims=True)
    sums_ref[2:3] = jnp.sum(grad, axis=0, keepdims=True)
    sums_ref[3:4] = jnp.sum(up, axis=0, keepdims=True)


def after_attention(got, residual, up, vec, wo, wq, wk, wv, part):
    channels = residual.shape[1]
    cells = got.shape[3]
    tokens = 2 * cells
    full = lambda shape: pl.BlockSpec(shape, lambda i: (0,) * len(shape))
    rows = pl.BlockSpec((tokens, channels), lambda i: (part, 0))
    square = (channels, channels)
    return pl.pallas_call(
        tokens_kernel,
        grid=(1,),
        in_specs=[full(got.shape), rows, rows, full(vec.shape)] + [full(square)] * 4,
        out_specs=[
            full((tokens, channels)),
            full((tokens, channels)),
            full((4, channels)),
        ],
        out_shape=[
            jax.ShapeDtypeStruct((tokens, channels), BF16),
            jax.ShapeDtypeStruct((tokens, channels), BF16),
            jax.ShapeDtypeStruct((4, channels), F32),
        ],
        compiler_params=params(),
        cost_estimate=cost(8 * tokens * channels**2, 7e6),
        name="after_attention",
    )(got, residual, up, vec, wo, wq, wk, wv)


def weights_kernel(gscale, info_ref, perm_hbm, *refs):
    (
        own_hbm, sib_hbm, far_hbm, normed_hbm, normed_sib_hbm, up_hbm, up_sib_hbm,
        rg0_hbm, rg1_hbm, rg0_sib_hbm, rg1_sib_hbm,
        got0_hbm, got1_hbm, got0_sib_hbm, got1_sib_hbm,
        own_far_hbm,
    ) = refs[:16]
    outs_hbm = refs[16:22]
    perm_ref, rg_ref, got_ref, up_ref, left_ref, right_ref, out_ref = refs[22:29]
    in_sems, got_sems, out_sems = refs[29:]
    copy = pltpu.make_async_copy
    core = info_ref[0]
    half = rg_ref.shape[1]
    tokens = 2 * half
    cells = got_ref.shape[4]
    mine, other = pl.ds(0, tokens), pl.ds(tokens, tokens)
    perm_in = copy(perm_hbm, perm_ref, in_sems.at[0])
    rg_in = [
        copy(h, rg_ref.at[u], in_sems.at[1 + u])
        for u, h in enumerate((rg0_hbm, rg1_hbm, rg0_sib_hbm, rg1_sib_hbm))
    ]
    hidden_in = [
        copy(own_hbm, right_ref.at[1, mine], in_sems.at[5]),
        copy(sib_hbm, right_ref.at[2 - 2 * core, mine], in_sems.at[6]),
        copy(own_far_hbm, right_ref.at[2 * core, mine], in_sems.at[7]),
        copy(own_hbm, right_ref.at[2 * core, other], in_sems.at[8]),
        copy(sib_hbm, right_ref.at[1, other], in_sems.at[9]),
        copy(far_hbm, right_ref.at[2 - 2 * core, other], in_sems.at[10]),
    ]
    normed_in = [
        copy(normed_hbm, right_ref.at[3, mine], in_sems.at[11]),
        copy(normed_sib_hbm, right_ref.at[3, other], in_sems.at[12]),
    ]
    up_in = [
        copy(up_hbm, up_ref.at[mine], in_sems.at[13]),
        copy(up_sib_hbm, up_ref.at[other], in_sems.at[14]),
    ]
    gots = (got0_hbm, got1_hbm, got0_sib_hbm, got1_sib_hbm)
    got_in = [
        [copy(gots[u].at[:, t], got_ref.at[u, t], got_sems.at[u, t]) for u in range(4)]
        for t in range(4)
    ]
    order = [perm_in] + rg_in + hidden_in + got_in[1] + normed_in
    order += got_in[2] + got_in[0] + up_in + got_in[3]
    for task in order:
        task.start()

    def heads(u, t):
        return jnp.concatenate(
            [
                jnp.concatenate([got_ref[u, t, n * HEADS + h] for h in range(HEADS)], axis=0)
                for n in range(2)
            ],
            axis=1,
        )

    outs = []

    def emit(place, left, right):
        value = mm(left, right_ref[right])
        for i, p in enumerate(range(3) if place < 4 else (1,)):
            entry = PARTS[p][0] + place
            out_ref[entry] = (value[i * count : (i + 1) * count] * gscale).astype(BF16)
            rows = count // 2
            for k in range(2):
                outs.append(
                    copy(
                        out_ref.at[entry, pl.ds(k * rows, rows)],
                        outs_hbm[2 * p + k].at[place],
                        out_sems.at[entry, k],
                    )
                )
                outs[-1].start()

    def wait(tasks):
        for task in tasks:
            task.wait()

    count = perm_ref.shape[1]
    wait([perm_in] + rg_in)
    for p in range(3):
        rows = slice(p * count, (p + 1) * count)
        for u in range(4):
            pieces = []
            for n in range(half // cells):
                piece = rg_ref[u, n * cells : (n + 1) * cells]
                if p != 1:
                    piece = shift_rows(piece.astype(F32), p - 1).astype(BF16)
                pieces.append(piece)
            place = slice(u * half, (u + 1) * half)
            left_ref[0, rows, place] = mm_nt(
                perm_ref[p], jnp.concatenate(pieces, axis=0)
            ).astype(BF16)
    wait(hidden_in)
    for a in range(3):
        emit(a, left_ref[0], a)
    wait(got_in[1] + got_in[2] + got_in[3])
    for p in range(3):
        rows = slice(p * count, (p + 1) * count)
        for u in range(4):
            place = slice(u * half, (u + 1) * half)
            left_ref[1, rows, place] = mm(perm_ref[p], heads(u, 1 + p)).astype(BF16)
    wait(normed_in)
    emit(3, left_ref[1], 3)
    wait(got_in[0] + up_in)
    for u in range(4):
        right_ref[4, u * half : (u + 1) * half] = heads(u, 0).T
    emit(4, mm_nt(perm_ref[1], up_ref[...]).astype(BF16), 4)
    wait(outs)


def weight_grads(gscale, info, perm, ins):
    tokens, channels = ins[0].shape
    entries = ENTRIES
    rows = perm.shape[1] // 2
    hbm = pl.BlockSpec(memory_space=pl.ANY)
    out_shape = []
    for _, count in PARTS:
        out_shape += [jax.ShapeDtypeStruct((count, rows, channels), BF16)] * 2
    outs = pl.pallas_call(
        functools.partial(weights_kernel, gscale),
        in_specs=[pl.BlockSpec(memory_space=pltpu.SMEM)] + [hbm] * (1 + len(ins)),
        out_specs=[hbm] * 6,
        out_shape=out_shape,
        scratch_shapes=[
            pltpu.VMEM(perm.shape, BF16),
            pltpu.VMEM((4, tokens // 2, channels), BF16),
            pltpu.VMEM((4, 4) + ins[-2].shape[:1] + ins[-2].shape[2:], BF16),
            pltpu.VMEM((2 * tokens, channels), BF16),
            pltpu.VMEM((2, 3 * perm.shape[1], 2 * tokens), BF16),
            pltpu.VMEM((5, 2 * tokens, channels), BF16),
            pltpu.VMEM((entries, 2 * rows, channels), BF16),
            pltpu.SemaphoreType.DMA((15,)),
            pltpu.SemaphoreType.DMA((4, 4)),
            pltpu.SemaphoreType.DMA((entries, 2)),
        ],
        compiler_params=params(),
        cost_estimate=cost(2 * 20 * tokens * channels**2, 20e6),
        name="weight_grads",
    )(info, perm, *ins)
    return [outs[2 * p : 2 * p + 2] for p in range(3)]


def fold_half_kernel(*refs):
    for p in range(3):
        mine, got, own_ref, send_ref = refs[2 * p], refs[2 * p + 1], refs[6 + 2 * p], refs[7 + 2 * p]
        rows = own_ref.shape[1]
        total = mine[...].astype(F32) + got[...].astype(F32)
        own_ref[...] = total[:, :rows].astype(BF16)
        send_ref[...] = total[:, rows:].astype(BF16)


def fold_half(values):
    shapes = []
    for value in values:
        count, rows, channels = value.shape
        shapes.append(jax.ShapeDtypeStruct((count, rows // 2, channels), BF16))
    return pl.pallas_call(
        fold_half_kernel,
        out_shape=shapes,
        compiler_params=params(),
        cost_estimate=cost(4e6, 8e6),
        name="fold_half",
    )(*values)


def fold_first_kernel(*refs):
    ins, (own_ref, *sends) = refs[:6], refs[6:]
    for p, (first, count) in enumerate(PARTS):
        rows = ins[0].shape[1] // 4
        for e in range(count):
            total = ins[2 * p][e].astype(F32) + ins[2 * p + 1][e].astype(F32)
            own_ref[first + e] = total[:rows]
            place, group = ((e, 0), (e, 1), (PARTS[0][1] + e, 0))[p]
            for k in range(1, 4):
                sends[3 * group + k - 1][place] = total[k * rows : (k + 1) * rows].astype(BF16)


def fold_second_kernel(*refs):
    own_in, got, (own_ref, *sends) = refs[0], refs[1:7], refs[7:]
    rows = own_in.shape[1] // 4
    for p, (first, count) in enumerate(PARTS):
        for e in range(count):
            place, group = ((e, 0), (e, 1), (PARTS[0][1] + e, 0))[p]
            total = own_in[first + e]
            for k in range(3):
                total = total + got[3 * group + k][place].astype(F32)
            own_ref[first + e] = total[:rows]
            place, group = ((e, 0), (PARTS[0][1] + e, 0), (e, 1))[p]
            for k in range(1, 4):
                sends[3 * group + k - 1][place] = total[k * rows : (k + 1) * rows].astype(BF16)


def fold_last_kernel(*refs):
    own_in, got, (conv_ref, q_ref, k_ref, v_ref, o_ref) = refs[0], refs[1:7], refs[7:]
    rows = own_in.shape[1]
    for p, (first, count) in enumerate(PARTS):
        for e in range(count):
            place, group = ((e, 0), (PARTS[0][1] + e, 0), (e, 1))[p]
            total = own_in[first + e]
            for k in range(3):
                total = total + got[3 * group + k][place].astype(F32)
            if e < 3:
                for r in range(rows):
                    conv_ref[e, r, p : p + 1] = total[r : r + 1]
            elif e == 3:
                (q_ref, k_ref, v_ref)[p][...] = total
            else:
                o_ref[...] = total


def fold_first(values):
    _, rows, channels = values[0].shape
    cut = rows // 4
    entries = ENTRIES
    wide = PARTS[0][1] + PARTS[2][1]
    sizes = [wide] * 3 + [PARTS[1][1]] * 3
    return pl.pallas_call(
        fold_first_kernel,
        out_shape=[jax.ShapeDtypeStruct((entries, cut, channels), F32)]
        + [jax.ShapeDtypeStruct((s, cut, channels), BF16) for s in sizes],
        compiler_params=params(),
        cost_estimate=cost(4e6, 7e6),
        name="fold_first",
    )(*values)


def fold_second(values):
    entries, rows, channels = values[0].shape
    cut = rows // 4
    wide = PARTS[0][1] + PARTS[1][1]
    sizes = [wide] * 3 + [PARTS[2][1]] * 3
    return pl.pallas_call(
        fold_second_kernel,
        out_shape=[jax.ShapeDtypeStruct((entries, cut, channels), F32)]
        + [jax.ShapeDtypeStruct((s, cut, channels), BF16) for s in sizes],
        compiler_params=params(),
        cost_estimate=cost(1e6, 2e6),
        name="fold_second",
    )(*values)


def fold_last(values):
    _, rows, channels = values[0].shape
    return pl.pallas_call(
        fold_last_kernel,
        out_shape=[jax.ShapeDtypeStruct((3, rows, 3, channels), F32)]
        + [jax.ShapeDtypeStruct((rows, channels), F32)] * 4,
        compiler_params=params(),
        cost_estimate=cost(3e5, 7e5),
        name="fold_last",
    )(*values)


def coordinates(index):
    dp, strip = index // 16, index % 16
    return {
        "x": dp // 2,
        "z": (strip // 8) * 2 + dp % 2,
        "y": (strip // 2) % 4,
        "core": strip % 2,
    }


def device_index(place):
    dp = place["x"] * 2 + place["z"] % 2
    strip = (place["z"] // 2) * 8 + place["y"] * 2 + place["core"]
    return dp * 16 + strip


def ring_pairs(axis, offset):
    pairs = []
    for source in range(128):
        place = coordinates(source)
        place[axis] = (place[axis] + offset) % 4
        pairs.append((source, device_index(place)))
    return pairs


def row_order(channels, here):
    per = channels // 128
    row = jnp.arange(channels // 2, dtype=jnp.int32)
    r = row % per
    k3 = (row // per) % 4
    k2 = (row // (per * 4)) % 4
    k1 = row // (per * 16)
    flip = (k1 // 2) ^ (3 * (k1 % 2))
    orders = []
    for order in ORDERS:
        place = {"core": here["core"], order[0]: here[order[0]] ^ flip}
        for axis, k in zip(order[1:], (k2, k3)):
            place[axis] = (here[axis] + k) % 4
        orders.append(device_index(place) * per + r)
    return jnp.stack(orders)


def ring_send(value, axis, offset):
    return lax.ppermute(value, ("dp", "strip"), ring_pairs(axis, offset))


def pair_send(value, axis, flip):
    pairs = []
    for source in range(128):
        place = coordinates(source)
        place[axis] = place[axis] ^ flip
        pairs.append((source, device_index(place)))
    return lax.ppermute(value, ("dp", "strip"), pairs)


def ring_sum(joined):
    own, *sends = joined
    values = [own]
    for i, send in enumerate(sends):
        values.append(ring_send(send, ("x", "y")[i // 3], i % 3 + 1))
    own, *sends = fold_second(values)
    values = [own]
    for i, send in enumerate(sends):
        values.append(ring_send(send, ("z", "y")[i // 3], i % 3 + 1))
    return fold_last(values)


def backward_kernel(
    gscale,
    info_ref,
    expand_ref,
    pick_ref,
    rg0_ref,
    rg1_ref,
    sib0_ref,
    sib1_ref,
    far0_ref,
    far1_ref,
    sums0_ref,
    sums1_ref,
    x_ref,
    chan_ref,
    vec_ref,
    conv_ref,
    ag_ref,
    payload_ref,
    rows_ref,
    acc_ref,
):
    step = pl.program_id(0)
    images, cells, channels = x_ref.shape
    half = rg0_ref.shape[0]

    @pl.when(step == 0)
    def _():
        core = info_ref[0]
        rows_ref[1, :half] = rg0_ref[...]
        rows_ref[1, half:] = rg1_ref[...]
        rows_ref[2 * core, :half] = sib0_ref[...]
        rows_ref[2 * core, half:] = sib1_ref[...]
        rows_ref[2 - 2 * core, :half] = far0_ref[...]
        rows_ref[2 - 2 * core, half:] = far1_ref[...]

    total = mm_nt(rows_ref[0], conv_ref[0, 0])
    total += mm_nt(rows_ref[1], conv_ref[1, 0])
    total += mm_nt(rows_ref[2], conv_ref[2, 0])

    @pl.when(step == 0)
    def _():
        for n in range(images):
            sl = slice(n * cells, (n + 1) * cells)
            acc_ref[sl] = shift_rows(total[sl], -1)

    @pl.when(step == 1)
    def _():
        acc_ref[...] += total

    @pl.when(step == 2)
    def _():
        gain = vec_ref[0:1]
        plain, weighted = [], []
        for n in range(images):
            sl = slice(n * cells, (n + 1) * cells)
            grad = acc_ref[sl] + shift_rows(total[sl], 1)
            standard = (x_ref[n].astype(F32) - chan_ref[n : n + 1]) * chan_ref[
                images + n : images + n + 1
            ]
            u = standard * gain + vec_ref[1:2]
            sigma = 0.5 + 0.5 * jnp.tanh(0.5 * u)
            ag = grad * (sigma * (1.0 + u * (1.0 - sigma)))
            ag_ref[sl] = ag
            plain.append(jnp.sum(ag, axis=0, keepdims=True))
            weighted.append(jnp.sum(ag * standard, axis=0, keepdims=True))
        all_totals = group_sum(jnp.concatenate(plain + weighted, axis=0) * gain, expand_ref[...])
        sums = sums0_ref[...] + sums1_ref[...]
        vectors = gscale * jnp.concatenate(
            [sum(weighted), sum(plain), sums, jnp.zeros((2, channels), F32)], axis=0
        )
        pieces = []
        for _ in range(3):
            piece = vectors.astype(BF16)
            pieces.append(piece.astype(F32))
            vectors = vectors - pieces[-1]
        picked = mm(jnp.concatenate(pieces, axis=0).astype(BF16), pick_ref[...])
        count = vectors.shape[0]
        picked = picked[:count] + picked[count : 2 * count] + picked[2 * count :]
        for s in range(payload_ref.shape[0]):
            payload_ref[s] = all_totals + picked[:, s * LANES : (s + 1) * LANES]


def backward(gscale, info, expand, pick, rows, sums, x, chan, vec, conv_weight):
    images, cells, channels = x.shape
    tokens = images * cells
    full = lambda shape: pl.BlockSpec(shape, lambda b: (0,) * len(shape))
    payload = (pick.shape[1] // LANES, 2 * images, LANES)
    ins = (expand, pick, *rows, *sums, x, chan, vec)
    return pl.pallas_call(
        functools.partial(backward_kernel, gscale),
        grid=(3,),
        in_specs=[pl.BlockSpec(memory_space=pltpu.SMEM)]
        + [full(v.shape) for v in ins]
        + [pl.BlockSpec((3, 1, channels, channels), lambda b: (0, b, 0, 0))],
        out_specs=[full((tokens, channels)), full(payload)],
        out_shape=[
            jax.ShapeDtypeStruct((tokens, channels), F32),
            jax.ShapeDtypeStruct(payload, F32),
        ],
        scratch_shapes=[
            pltpu.VMEM((3, tokens, channels), BF16),
            pltpu.VMEM((tokens, channels), F32),
        ],
        compiler_params=params(),
        cost_estimate=cost(18 * tokens * channels**2, 12e6, 4e5),
        name="backward_conv",
    )(info, *ins, conv_weight)


def input_kernel(
    totals_ref, expand_ref, rg0_ref, rg1_ref, ag_ref, x_ref, chan_ref, vec_ref,
    out_ref, spread_ref
):
    images, cells, channels = x_ref.shape
    strips = totals_ref.shape[0]
    count = strips * cells * (channels // GROUPS)
    summed = jnp.sum(totals_ref[...], axis=0)
    for d in range(spread_ref.shape[0]):
        spread_ref[d] = summed
    spread_c = spread(summed / count, expand_ref[...])
    for n in range(images):
        u, m = n // 2, n % 2
        sl = slice(m * cells, (m + 1) * cells)
        scale = chan_ref[images + n : images + n + 1]
        standard = (x_ref[n].astype(F32) - chan_ref[n : n + 1]) * scale
        part = scale * (
            ag_ref[n * cells : (n + 1) * cells] * vec_ref[0:1]
            - spread_c[n : n + 1]
            - standard * spread_c[images + n : images + n + 1]
        )
        rg = (rg0_ref, rg1_ref)[u][sl].astype(F32)
        out_ref[n] = (rg + part).astype(BF16)


def input_grad(totals, expand, rg0, rg1, ag, x, chan, vec, copies):
    return pl.pallas_call(
        input_kernel,
        out_shape=[
            jax.ShapeDtypeStruct(x.shape, BF16),
            jax.ShapeDtypeStruct((copies,) + totals.shape[1:], F32),
        ],
        compiler_params=params(),
        cost_estimate=cost(3e6, 4e6),
        name="input_grad",
    )(totals, expand, rg0, rg1, ag, x, chan, vec)


def exchange(value, axis="strip"):
    return lax.all_to_all(value, axis, split_axis=0, concat_axis=0, tiled=True)


def core_mate(value):
    return lax.ppermute(value, "strip", [(i, i ^ 1) for i in range(16)])


def far_row(value):
    pairs = [(i, i + 1) for i in range(1, 15, 2)]
    return lax.ppermute(value, "strip", pairs + [(j, i) for i, j in pairs])


def pick_matrix(channels, groups_dp, strips):
    per = channels // (groups_dp * strips)
    pick = np.zeros((channels, strips * LANES), np.float32)
    for o in range(channels):
        device, r = divmod(o, per)
        dp, strip = divmod(device, strips)
        pick[o, strip * LANES + GROUPS + dp * per + r] = 1.0
    return jnp.asarray(pick, BF16)


def on_device(
    block_in,
    upstream,
    gn_gain,
    gn_bias,
    conv_weight,
    conv_bias,
    ln_gain,
    ln_bias,
    w_query,
    w_key,
    w_value,
    w_out,
    out_bias,
):
    images, strip_rows, cells, channels = block_in.shape
    strips = lax.axis_size("strip")
    groups_dp = lax.axis_size("dp")
    me = lax.axis_index("strip")
    me_dp = lax.axis_index("dp")
    gscale = 1.0 / math.sqrt(cells * strips * images * groups_dp)
    x = block_in.reshape(images, cells, channels)
    up = upstream.reshape(images, cells, channels)
    up_rows = upstream.reshape(images * cells, channels)
    expand = expand_matrix(channels)
    core = me % 2
    inside = jnp.where(core == 0, me > 0, me < strips - 1)
    info = jnp.stack([core, inside.astype(jnp.int32)]).astype(jnp.int32)
    here = coordinates(me_dp * 16 + me)
    order = row_order(channels, here)
    perm = (order[:, :, None] == jnp.arange(channels, dtype=jnp.int32)).astype(BF16)
    perm, info = lax.optimization_barrier((perm, info))

    x_far = far_row(x)
    x_sib = core_mate(x)
    up_sib = core_mate(up_rows)
    stats, vec = local_stats(
        x, expand, (gn_gain, gn_bias, conv_bias, ln_gain, ln_bias, out_bias), strips
    )
    stats = exchange(stats)
    g = upstream_heads(up, w_out)
    hid_own, hid_sib, hid_far, residual, normed, qkv0, qkv1, chan = forward(
        info, stats, expand, vec, x, x_sib, x_far, g, conv_weight, w_query, w_key, w_value
    )
    hid_far_sib = core_mate(hid_far)
    normed_sib = core_mate(normed)
    got0, got1 = [exchange(attention(exchange(qkv))) for qkv in (qkv0, qkv1)]
    got0_sib = core_mate(got0)
    shared = (residual, up_rows, vec, w_out, w_query, w_key, w_value)
    block_out0, rg0, sums0 = after_attention(got0, *shared, 0)
    rg0_sib, rg0_far = core_mate(rg0), far_row(rg0)
    got1, rg0 = lax.optimization_barrier((got1, rg0))
    got1_sib = core_mate(got1)
    block_out1, rg1, sums1 = after_attention(got1, *shared, 1)
    rg1_sib, rg1_far = core_mate(rg1), far_row(rg1)
    block_out = jnp.concatenate([block_out0, block_out1], axis=0)
    blocks = weight_grads(
        gscale,
        info,
        perm,
        (
            hid_own, hid_sib, hid_far_sib, normed, normed_sib, up_rows, up_sib,
            rg0, rg1, rg0_sib, rg1_sib, got0, got1, got0_sib, got1_sib, hid_far,
        ),
    )
    pick = pick_matrix(channels, groups_dp, strips)
    sends = [pair_send(blocks[p][1], ORDERS[p][0], 1) for p in range(3)]
    ag, payload = backward(
        gscale,
        info,
        expand,
        pick,
        (rg0, rg1, rg0_sib, rg1_sib, rg0_far, rg1_far),
        (sums0, sums1),
        x,
        chan,
        vec,
        conv_weight,
    )
    sends, payload = lax.optimization_barrier((sends, payload))
    halves = fold_half([v for p in range(3) for v in (blocks[p][0], sends[p])])
    totals = exchange(payload)
    sends = [pair_send(halves[2 * p + 1], ORDERS[p][0], 3) for p in range(3)]
    grad_input, vectors = input_grad(totals, expand, rg0, rg1, ag, x, chan, vec, groups_dp)
    sends, vectors = lax.optimization_barrier((sends, vectors))
    conv_shard, q_shard, k_shard, v_shard, o_shard = ring_sum(
        fold_first([v for p in range(3) for v in (halves[2 * p], sends[p])])
    )
    per = channels // (strips * groups_dp)
    vectors = jnp.sum(exchange(vectors, "dp"), axis=0)
    shards = lax.dynamic_slice_in_dim(vectors, GROUPS + me_dp * per, per, axis=1)
    shape = block_in.shape
    return (
        block_out.reshape(shape),
        grad_input.reshape(shape),
        conv_shard.transpose(0, 2, 3, 1),
        q_shard.T,
        k_shard.T,
        v_shard.T,
        o_shard.T,
        shards[0],
        shards[1],
        shards[2],
        shards[3],
        shards[4],
        shards[5],
    )


def solution(mesh):
    rows = P("dp", "strip", None, None)
    both = ("dp", "strip")
    in_specs = (rows, rows) + (P(),) * 11
    out_specs = (rows, rows, P(None, None, None, both)) + (P(None, both),) * 4 + (P(both),) * 6
    return jax.shard_map(
        on_device, mesh=mesh, in_specs=in_specs, out_specs=out_specs, check_vma=False
    )
```

```python
import functools
import math

import jax
import jax.numpy as jnp
import numpy as np
from jax import lax
from jax.experimental import pallas as pl
from jax.experimental.pallas import tpu as pltpu
from jax.sharding import PartitionSpec as P

HEADS = 8
GROUPS = 32
EPSILON = 1e-05
F32 = jnp.float32
BF16 = jnp.bfloat16
NT = (((1,), (1,)), ((), ()))
HIGH = lax.Precision.HIGHEST
VMEM_LIMIT = 56 * 1024 * 1024
LOG2E = math.log2(math.e)
QUERY_BLOCK = 1024
KEY_CHUNK = 512
ORDERS = (("y", "x", "z"), ("x", "y", "z"), ("z", "x", "y"))
ENTRIES = 13
LANES = 128
PARTS = ((0, 4), (4, 5), (9, 4))


def params(semantics=None):
    if semantics is None:
        return pltpu.CompilerParams(vmem_limit_bytes=VMEM_LIMIT)
    return pltpu.CompilerParams(
        vmem_limit_bytes=VMEM_LIMIT, dimension_semantics=semantics
    )


def mm(a, b):
    return jnp.dot(a, b, preferred_element_type=F32)


def mm_nt(a, b):
    return lax.dot_general(a, b, NT, preferred_element_type=F32)


def group_sum(rows, expand):
    return lax.dot_general(rows, expand, NT, preferred_element_type=F32, precision=HIGH)


def spread(rows, expand):
    return jnp.dot(rows, expand, preferred_element_type=F32, precision=HIGH)


def expand_matrix(channels):
    per_group = channels // GROUPS
    return jnp.asarray(
        np.arange(channels)[None, :] // per_group == np.arange(LANES)[:, None], F32
    )


def shift_rows(value, down):
    count = value.shape[0]
    row = lax.broadcasted_iota(jnp.int32, value.shape, 0)
    if down == 1:
        return jnp.where(row == 0, 0.0, pltpu.roll(value, 1, 0))
    return jnp.where(row == count - 1, 0.0, pltpu.roll(value, count - 1, 0))


def cost(flops, nbytes, trans=0):
    return pl.CostEstimate(flops=int(flops), bytes_accessed=int(nbytes), transcendentals=int(trans))


def stats_kernel(x_ref, expand_ref, *refs):
    vectors, out_ref, vec_ref = refs[:-2], refs[-2], refs[-1]
    images, cells, channels = x_ref.shape
    count = cells * (channels // GROUPS)
    vec_ref[...] = jnp.zeros_like(vec_ref)
    for i, ref in enumerate(vectors):
        vec_ref[i : i + 1] = ref[...].reshape(1, channels)
    expand = expand_ref[...]
    sums = jnp.concatenate(
        [jnp.sum(x_ref[n].astype(F32), axis=0, keepdims=True) for n in range(images)], axis=0
    )
    mean = group_sum(sums, expand) / count
    mean_c = spread(mean, expand)
    squares = []
    for n in range(images):
        d = x_ref[n].astype(F32) - mean_c[n : n + 1]
        squares.append(jnp.sum(d * d, axis=0, keepdims=True))
    m2 = group_sum(jnp.concatenate(squares, axis=0), expand)
    both = jnp.concatenate([mean, m2], axis=0)
    for s in range(out_ref.shape[0]):
        out_ref[s] = both


def local_stats(x, expand, vectors, strips):
    images, _, channels = x.shape
    return pl.pallas_call(
        stats_kernel,
        out_shape=[
            jax.ShapeDtypeStruct((strips, 2 * images, LANES), F32),
            jax.ShapeDtypeStruct((8, channels), F32),
        ],
        compiler_params=params(),
        cost_estimate=cost(1e7, 7e5),
        name="local_stats",
    )(x, expand, *vectors)


def upstream_kernel(up_ref, w_ref, g_ref):
    images = up_ref.shape[0]
    w = w_ref[...]
    hd = w.shape[0] // HEADS
    for n in range(images):
        g = mm_nt(w, up_ref[n])
        for h in range(HEADS):
            g_ref[n // 2, (n % 2) * HEADS + h] = g[h * hd : (h + 1) * hd].astype(BF16)


def upstream_heads(up, w_out):
    images, cells, channels = up.shape
    return pl.pallas_call(
        upstream_kernel,
        out_shape=jax.ShapeDtypeStruct((images // 2, 2 * HEADS, channels // HEADS, cells), BF16),
        compiler_params=params(),
        cost_estimate=cost(2 * images * cells * channels**2, 2.2e6),
        name="upstream_heads",
    )(up, w_out)


def forward_kernel(
    info_ref,
    stats_ref,
    expand_ref,
    vec_ref,
    x_hbm,
    sib_hbm,
    far_hbm,
    g_hbm,
    conv_hbm,
    wq_hbm,
    wk_hbm,
    wv_hbm,
    hid_own_hbm,
    hid_sib_hbm,
    hid_far_hbm,
    residual_hbm,
    normed_hbm,
    qkv0_hbm,
    qkv1_hbm,
    chan_ref,
    x_ref,
    conv_ref,
    w_ref,
    hidden_ref,
    acc_ref,
    residual_ref,
    normed_ref,
    qkv_ref,
    in_sems,
    out_sems,
):
    _, images, cells, channels = x_ref.shape
    hd = channels // HEADS
    copy = pltpu.make_async_copy
    xs = [copy(h, x_ref.at[i], in_sems.at[i]) for i, h in enumerate((x_hbm, sib_hbm, far_hbm))]
    convs = [copy(conv_hbm.at[:, b], conv_ref.at[b], in_sems.at[3 + b]) for b in range(3)]
    ws = [copy(h, w_ref.at[i], in_sems.at[6 + i]) for i, h in enumerate((wq_hbm, wk_hbm, wv_hbm))]
    qkv_out = (qkv0_hbm, qkv1_hbm)
    gs = [copy(g_hbm.at[c], qkv_ref.at[c, :, 3], in_sems.at[9 + c]) for c in range(2)]
    for task in xs + convs + ws + gs:
        task.start()
    core = info_ref[0]
    strips = stats_ref.shape[0]
    count = cells * (channels // GROUPS)
    got = stats_ref[...]
    means = got[:, :images]
    mean = jnp.sum(means, axis=0) / strips
    off = means - mean[None]
    m2 = jnp.sum(got[:, images:], axis=0) + count * jnp.sum(off * off, axis=0)
    scale = lax.rsqrt(m2 / (count * strips) + EPSILON)
    expand = expand_ref[...]
    mean_c = spread(mean, expand)
    scale_c = spread(scale, expand)
    chan_ref[...] = jnp.concatenate([mean_c, scale_c], axis=0)
    gain = vec_ref[0:1]
    bias = vec_ref[1:2]
    outs = []
    for i, out_hbm in enumerate((hid_own_hbm, hid_sib_hbm, hid_far_hbm)):
        xs[i].wait()
        for n in range(images):
            factor_c = scale_c[n : n + 1] * gain
            u = (x_ref[i, n].astype(F32) - mean_c[n : n + 1]) * factor_c + bias
            h = u * (0.5 + 0.5 * jnp.tanh(0.5 * u))
            if i == 2:
                h = jnp.where(info_ref[1] > 0, h, 0.0)
            hidden_ref[i, n * cells : (n + 1) * cells] = h.astype(BF16)
        outs.append(copy(hidden_ref.at[i], out_hbm, out_sems.at[i]))
        outs[-1].start()

    above = 2 - core
    below = 1 + core
    for b in range(3):
        convs[b].wait()
        total = mm(hidden_ref[0], conv_ref[b, 1])
        total += mm(hidden_ref[above], conv_ref[b, 0])
        total += mm(hidden_ref[below], conv_ref[b, 2])
        if b == 1:
            acc_ref[...] += total
            continue
        for n in range(images):
            sl = slice(n * cells, (n + 1) * cells)
            if b == 0:
                acc_ref[sl] = shift_rows(total[sl], 1)
                continue
            conv = acc_ref[sl] + shift_rows(total[sl], -1)
            residual = (x_ref[0, n].astype(F32) + conv + vec_ref[2:3]).astype(BF16)
            residual_ref[sl] = residual
            tokens = residual.astype(F32)
            dev = tokens - jnp.mean(tokens, axis=1, keepdims=True)
            scale = lax.rsqrt(jnp.mean(dev * dev, axis=1, keepdims=True) + EPSILON)
            normed_ref[sl] = (dev * scale * vec_ref[3:4] + vec_ref[4:5]).astype(BF16)
    outs.append(copy(residual_ref, residual_hbm, out_sems.at[3]))
    outs.append(copy(normed_ref, normed_hbm, out_sems.at[4]))
    outs[-2].start()
    outs[-1].start()
    factor = LOG2E / math.sqrt(hd)
    for task in ws:
        task.wait()
    for c in range(2):
        rows = slice(2 * c * cells, 2 * (c + 1) * cells)
        for t in range(3):
            out = mm(normed_ref[rows], w_ref[t])
            if t == 0:
                out = out * factor
            for n in range(2):
                flipped = out[n * cells : (n + 1) * cells].T.astype(BF16)
                for h in range(HEADS):
                    qkv_ref[c, n * HEADS + h, t] = flipped[h * hd : (h + 1) * hd]
        gs[c].wait()
        outs.append(copy(qkv_ref.at[c], qkv_out[c], out_sems.at[5 + c]))
        outs[-1].start()
    for task in outs:
        task.wait()


def forward(info, stats, expand, vec, x, sib, far, g, conv_weight, wq, wk, wv):
    images, cells, channels = x.shape
    tokens = images * cells
    hd = channels // HEADS
    hbm = pl.BlockSpec(memory_space=pl.ANY)
    vmem = pl.BlockSpec(memory_space=pltpu.VMEM)
    row_type = jax.ShapeDtypeStruct((tokens, channels), BF16)
    qkv_type = jax.ShapeDtypeStruct((2 * HEADS, 4, hd, cells), BF16)
    return pl.pallas_call(
        forward_kernel,
        in_specs=[pl.BlockSpec(memory_space=pltpu.SMEM)] + [vmem] * 3 + [hbm] * 8,
        out_specs=[hbm] * 7 + [vmem],
        out_shape=[row_type] * 5
        + [qkv_type] * 2
        + [jax.ShapeDtypeStruct((2 * images, channels), F32)],
        scratch_shapes=[
            pltpu.VMEM((3, images, cells, channels), BF16),
            pltpu.VMEM((3, 3, channels, channels), BF16),
            pltpu.VMEM((3, channels, channels), BF16),
            pltpu.VMEM((3, tokens, channels), BF16),
            pltpu.VMEM((tokens, channels), F32),
            pltpu.VMEM((tokens, channels), BF16),
            pltpu.VMEM((tokens, channels), BF16),
            pltpu.VMEM((2, 2 * HEADS, 4, hd, cells), BF16),
            pltpu.SemaphoreType.DMA((11,)),
            pltpu.SemaphoreType.DMA((7,)),
        ],
        compiler_params=params(),
        cost_estimate=cost(24 * tokens * channels**2, 20e6, 1e6),
        name="forward_conv",
    )(info, stats, expand, vec, x, sib, far, g, conv_weight, wq, wk, wv)


def together(*tasks):
    results = [None] * len(tasks)
    active = list(enumerate(tasks))
    while active:
        still = []
        for i, task in active:
            try:
                results[i] = next(task)
                still.append((i, task))
            except StopIteration:
                pass
        active = still
    return results


def attention_kernel(
    qkv_ref, out_ref, kt_ref, vt_ref, kn_ref, vn_ref, s_ref, e_ref, dk_ref, dv_ref
):
    step = pl.program_id(0)
    sources, _, hd, cells = qkv_ref.shape
    length = sources * cells
    wide = kn_ref.shape[1]
    block = s_ref.shape[2]
    per = block // cells
    spans = [slice(c, c + KEY_CHUNK) for c in range(0, length, KEY_CHUNK)]
    extra = vt_ref.shape[0] - hd

    @pl.when(step == 0)
    def _():
        ones_row = (lax.broadcasted_iota(jnp.int32, (extra, cells), 0) == 0).astype(F32)
        pad = jnp.zeros((wide - hd, cells), F32)
        row = lax.broadcasted_iota(jnp.int32, (wide - hd, cells), 0)
        ones_two = (row < 2).astype(F32)
        for s in range(sources):
            sl = slice(s * cells, (s + 1) * cells)
            k = qkv_ref[s, 1]
            v = qkv_ref[s, 2]
            kt_ref[:, sl] = k
            vt_ref[:hd, sl] = v
            vt_ref[hd:, sl] = ones_row.astype(BF16)
            kn_ref[sl] = jnp.concatenate([k.astype(F32), pad], axis=0).T.astype(BF16)
            vn_ref[sl] = jnp.concatenate([v.astype(F32), ones_two], axis=0).T.astype(BF16)
        dk_ref[...] = jnp.zeros_like(dk_ref)
        dv_ref[...] = jnp.zeros_like(dv_ref)

    bases = [(2 * step + b) * per for b in range(2)]

    def rows_of(b, t):
        return jnp.concatenate([qkv_ref[bases[b] + u, t] for u in range(per)], axis=1).astype(F32)

    def put(b, t, value):
        for u in range(per):
            out_ref[bases[b] + u, t] = value[:, u * cells : (u + 1) * cells].astype(BF16)

    def scores(b):
        q = jnp.concatenate([rows_of(b, 0), jnp.zeros((wide - hd, block), F32)], axis=0)
        q_t = q.astype(BF16)
        top = None
        for sl in spans:
            value = mm(kn_ref[sl], q_t)
            s_ref[b, sl] = value
            here = jnp.max(value, axis=0, keepdims=True)
            top = here if top is None else jnp.maximum(top, here)
            yield None
        yield top, q.T.astype(BF16)

    def attend(b, top):
        acc = jnp.zeros((hd + extra, block), F32)
        for sl in spans:
            e = jnp.exp2(s_ref[b, sl] - top).astype(BF16)
            e_ref[b, sl] = e
            acc += mm(vt_ref[:, sl], e)
            yield None
        yield acc

    def finish(b, acc):
        inverse = 1.0 / acc[hd : hd + 1]
        out = acc[:hd] * inverse
        put(b, 0, out)
        g = (rows_of(b, 3) * inverse).astype(BF16).astype(F32)
        delta = -jnp.sum(g * out, axis=0, keepdims=True)
        high = delta.astype(BF16).astype(F32)
        low = delta - high
        row = lax.broadcasted_iota(jnp.int32, (wide - hd, block), 0)
        tail = jnp.where(row == 0, high, jnp.where(row == 1, low, 0.0))
        g = jnp.concatenate([g, tail], axis=0)
        return g.astype(BF16), g.T.astype(BF16)

    def back(b, g_t, g_n, q_n):
        dq = jnp.zeros((hd, block), F32)
        for sl in spans:
            e = e_ref[b, sl]
            ds = (e.astype(F32) * mm(vn_ref[sl], g_t)).astype(BF16)
            dq += mm(kt_ref[:, sl], ds)
            dk_ref[sl] += mm(ds, q_n)
            dv_ref[sl] += mm(e, g_n)
            yield None
        put(b, 1, dq * (1.0 / math.sqrt(hd)))
        yield None

    ((top0, q0),) = together(scores(0))
    acc0, (top1, q1) = together(attend(0, top0), scores(1))
    _, acc1 = together(back(0, *finish(0, acc0), q0), attend(1, top1))
    together(back(1, *finish(1, acc1), q1))

    @pl.when(step == pl.num_programs(0) - 1)
    def _():
        for s in range(sources):
            sl = slice(s * cells, (s + 1) * cells)
            out_ref[s, 2] = (dk_ref[sl].T[:hd] * (1.0 / LOG2E)).astype(BF16)
            out_ref[s, 3] = dv_ref[sl].T[:hd].astype(BF16)


def attention(qkv):
    sources, _, hd, cells = qkv.shape
    length = sources * cells
    block = QUERY_BLOCK
    wide = 128
    full = lambda shape: pl.BlockSpec(shape, lambda i: (0,) * len(shape))
    return pl.pallas_call(
        attention_kernel,
        grid=(length // block // 2,),
        in_specs=[full(qkv.shape)],
        out_specs=full((sources, 4, hd, cells)),
        out_shape=jax.ShapeDtypeStruct((sources, 4, hd, cells), BF16),
        scratch_shapes=[
            pltpu.VMEM((hd, length), BF16),
            pltpu.VMEM((hd + 16, length), BF16),
            pltpu.VMEM((length, wide), BF16),
            pltpu.VMEM((length, wide), BF16),
            pltpu.VMEM((2, length, block), F32),
            pltpu.VMEM((2, length, block), BF16),
            pltpu.VMEM((length, wide), F32),
            pltpu.VMEM((length, wide), F32),
        ],
        compiler_params=params(),
        cost_estimate=cost(12 * length * length * 256, 5e6, length * length),
        name="attention",
    )(qkv)


def gather_heads(got_ref, t):
    return jnp.concatenate(
        [
            jnp.concatenate([got_ref[n * HEADS + h, t] for h in range(HEADS)], axis=0)
            for n in range(2)
        ],
        axis=1,
    )


def tokens_kernel(
    got_ref,
    residual_ref,
    up_ref,
    vec_ref,
    wo_ref,
    wq_ref,
    wk_ref,
    wv_ref,
    block_out_ref,
    rg_ref,
    sums_ref,
):
    residual = residual_ref[...].astype(F32)
    up = up_ref[...].astype(F32)
    mixed = mm(gather_heads(got_ref, 0).T, wo_ref[...])
    block_out_ref[...] = (residual + mixed + vec_ref[5:6]).astype(BF16)
    grad = mm_nt(gather_heads(got_ref, 1).T, wq_ref[...])
    grad += mm_nt(gather_heads(got_ref, 2).T, wk_ref[...])
    grad += mm_nt(gather_heads(got_ref, 3).T, wv_ref[...])
    dev = residual - jnp.mean(residual, axis=1, keepdims=True)
    scale = lax.rsqrt(jnp.mean(dev * dev, axis=1, keepdims=True) + EPSILON)
    standard = dev * scale
    scaled = grad * vec_ref[3:4]
    part = scale * (
        scaled
        - jnp.mean(scaled, axis=1, keepdims=True)
        - standard * jnp.mean(scaled * standard, axis=1, keepdims=True)
    )
    rg = (up + part).astype(BF16)
    rg_ref[...] = rg
    sums_ref[0:1] = jnp.sum(rg.astype(F32), axis=0, keepdims=True)
    sums_ref[1:2] = jnp.sum(grad * standard, axis=0, keepdims=True)
    sums_ref[2:3] = jnp.sum(grad, axis=0, keepdims=True)
    sums_ref[3:4] = jnp.sum(up, axis=0, keepdims=True)


def after_attention(got, residual, up, vec, wo, wq, wk, wv, part):
    channels = residual.shape[1]
    cells = got.shape[3]
    tokens = 2 * cells
    full = lambda shape: pl.BlockSpec(shape, lambda i: (0,) * len(shape))
    rows = pl.BlockSpec((tokens, channels), lambda i: (part, 0))
    square = (channels, channels)
    return pl.pallas_call(
        tokens_kernel,
        grid=(1,),
        in_specs=[full(got.shape), rows, rows, full(vec.shape)] + [full(square)] * 4,
        out_specs=[
            full((tokens, channels)),
            full((tokens, channels)),
            full((4, channels)),
        ],
        out_shape=[
            jax.ShapeDtypeStruct((tokens, channels), BF16),
            jax.ShapeDtypeStruct((tokens, channels), BF16),
            jax.ShapeDtypeStruct((4, channels), F32),
        ],
        compiler_params=params(),
        cost_estimate=cost(8 * tokens * channels**2, 7e6),
        name="after_attention",
    )(got, residual, up, vec, wo, wq, wk, wv)


def wait_all(tasks):
    for task in tasks:
        task.wait()


def emitter(gscale, outs_hbm, part_ref, out_ref, out_sems, outs):
    def emit(entry, p, place, value):
        value = value * gscale
        if part_ref is not None:
            value = value + part_ref[entry].astype(F32)
        out_ref[entry] = value.astype(BF16)
        if part_ref is None:
            targets = [(out_ref.at[entry], outs_hbm[0].at[entry])]
        else:
            rows = value.shape[0] // 2
            targets = [
                (out_ref.at[entry, pl.ds(k * rows, rows)], outs_hbm[2 * p + k].at[place])
                for k in range(2)
            ]
        for k, (source, target) in enumerate(targets):
            outs.append(pltpu.make_async_copy(source, target, out_sems.at[entry, k]))
            outs[-1].start()

    return emit


def proj_kernel(gscale, part, last, *refs):
    perm_hbm, got_hbm, got_sib_hbm, normed_hbm, normed_sib_hbm, up_hbm, up_sib_hbm = refs[:7]
    inputs = 8 if last else 7
    part_hbm = refs[7] if last else None
    outs_hbm, scratch = refs[inputs:-10], refs[-10:]
    perm_ref, got_ref, up_ref, left_ref, normed_ref, att_ref, part_ref, out_ref = scratch[:8]
    in_sems, out_sems = scratch[8:]
    copy = pltpu.make_async_copy
    half = normed_ref.shape[0] // 2
    rows = pl.ds(part * half, half)
    places = [pl.ds(u * half, half) for u in range(2)]
    got_in = [
        [
            copy(h.at[:, t], got_ref.at[u, t], in_sems.at[2 * t + u])
            for u, h in enumerate((got_hbm, got_sib_hbm))
        ]
        for t in range(4)
    ]
    perm_in = [copy(perm_hbm, perm_ref, in_sems.at[8])]
    normed_in = [
        copy(h.at[rows], normed_ref.at[places[u]], in_sems.at[9 + u])
        for u, h in enumerate((normed_hbm, normed_sib_hbm))
    ]
    up_in = [
        copy(h.at[rows], up_ref.at[places[u]], in_sems.at[11 + u])
        for u, h in enumerate((up_hbm, up_sib_hbm))
    ]
    part_in = [copy(part_hbm, part_ref, in_sems.at[13])] if last else []
    for tasks in (perm_in, got_in[1], got_in[2], got_in[3], normed_in, part_in, got_in[0], up_in):
        for task in tasks:
            task.start()

    def heads(u, t):
        return jnp.concatenate(
            [
                jnp.concatenate([got_ref[u, t, n * HEADS + h] for h in range(HEADS)], axis=0)
                for n in range(2)
            ],
            axis=1,
        )

    outs = []
    emit = emitter(gscale, outs_hbm, part_ref if last else None, out_ref, out_sems, outs)
    count = perm_ref.shape[1]
    wait_all(perm_in)
    for p in range(3):
        wait_all(got_in[1 + p])
        for u in range(2):
            left_ref[p * count : (p + 1) * count, u * half : (u + 1) * half] = mm(
                perm_ref[p], heads(u, 1 + p)
            ).astype(BF16)
    wait_all(normed_in + part_in)
    value = mm(left_ref[...], normed_ref[...])
    for p in range(3):
        emit(p, p, 3, value[p * count : (p + 1) * count])
    wait_all(got_in[0] + up_in)
    for u in range(2):
        att_ref[u * half : (u + 1) * half] = heads(u, 0).T
    emit(3, 1, 4, mm(mm_nt(perm_ref[1], up_ref[...]).astype(BF16), att_ref[...]))
    wait_all(outs)


def conv_kernel(gscale, part, last, *refs):
    info_ref, perm_hbm, rg_hbm, rg_sib_hbm, own_hbm, sib_hbm, far_hbm, far_sib_hbm = refs[:8]
    inputs = 15 if last else 8
    part_hbm = refs[8] if last else None
    outs_hbm, scratch = refs[inputs:-8], refs[-8:]
    perm_ref, rg_ref, left_ref, right_ref, part_ref, out_ref, in_sems, out_sems = scratch
    copy = pltpu.make_async_copy
    core = info_ref[0]
    half = rg_ref.shape[1]
    rows = pl.ds(part * half, half)
    mine, other = pl.ds(0, half), pl.ds(half, half)
    first_in = [
        copy(perm_hbm, perm_ref, in_sems.at[0]),
        copy(rg_hbm, rg_ref.at[0], in_sems.at[1]),
        copy(rg_sib_hbm, rg_ref.at[1], in_sems.at[2]),
    ]
    hidden_in = [
        copy(own_hbm.at[rows], right_ref.at[1, mine], in_sems.at[3]),
        copy(sib_hbm.at[rows], right_ref.at[2 - 2 * core, mine], in_sems.at[4]),
        copy(far_hbm.at[rows], right_ref.at[2 * core, mine], in_sems.at[5]),
        copy(own_hbm.at[rows], right_ref.at[2 * core, other], in_sems.at[6]),
        copy(sib_hbm.at[rows], right_ref.at[1, other], in_sems.at[7]),
        copy(far_sib_hbm.at[rows], right_ref.at[2 - 2 * core, other], in_sems.at[8]),
    ]
    part_in = [copy(part_hbm, part_ref, in_sems.at[9])] if last else []
    for task in first_in + hidden_in + part_in:
        task.start()
    outs = []
    emit = emitter(gscale, outs_hbm, part_ref if last else None, out_ref, out_sems, outs)
    count = perm_ref.shape[1]
    cells = half // 2
    wait_all(first_in)
    for p in range(3):
        for u in range(2):
            pieces = []
            for n in range(2):
                piece = rg_ref[u, n * cells : (n + 1) * cells]
                if p != 1:
                    piece = shift_rows(piece.astype(F32), p - 1).astype(BF16)
                pieces.append(piece)
            left_ref[p * count : (p + 1) * count, u * half : (u + 1) * half] = mm_nt(
                perm_ref[p], jnp.concatenate(pieces, axis=0)
            ).astype(BF16)
    wait_all(hidden_in + part_in)
    for a in range(3):
        value = mm(left_ref[...], right_ref[a])
        for p in range(3):
            emit(3 * p + a, p, a, value[p * count : (p + 1) * count])
    wait_all(outs)


def part_types(channels, rows):
    types = []
    for _, count in PARTS:
        types += [jax.ShapeDtypeStruct((count, rows // 2, channels), BF16)] * 2
    return types


def proj_grads(gscale, part, perm, ins, partial=None):
    channels = perm.shape[2]
    rows = perm.shape[1]
    got = ins[0]
    tokens = 4 * got.shape[3]
    last = partial is not None
    whole = jax.ShapeDtypeStruct((4, rows, channels), BF16)
    hbm = pl.BlockSpec(memory_space=pl.ANY)
    args = (perm, *ins) + ((partial,) if last else ())
    out_shape = part_types(channels, rows) if last else [whole]
    outs = pl.pallas_call(
        functools.partial(proj_kernel, gscale, part, last),
        in_specs=[hbm] * len(args),
        out_specs=[hbm] * len(out_shape),
        out_shape=out_shape,
        scratch_shapes=[
            pltpu.VMEM(perm.shape, BF16),
            pltpu.VMEM((2, 4) + got.shape[:1] + got.shape[2:], BF16),
            pltpu.VMEM((tokens, channels), BF16),
            pltpu.VMEM((3 * rows, tokens), BF16),
            pltpu.VMEM((tokens, channels), BF16),
            pltpu.VMEM((tokens, channels), BF16),
            pltpu.VMEM(whole.shape, BF16),
            pltpu.VMEM(whole.shape, BF16),
            pltpu.SemaphoreType.DMA((14,)),
            pltpu.SemaphoreType.DMA((4, 2)),
        ],
        compiler_params=params(),
        cost_estimate=cost(16 * rows * tokens * channels, 9e6),
        name="proj_grads",
    )(*args)
    return list(outs) if last else outs[0]


def conv_grads(gscale, part, info, perm, ins, partial=None, parts=()):
    channels = perm.shape[2]
    rows = perm.shape[1]
    tokens = 2 * ins[0].shape[0]
    last = partial is not None
    whole = jax.ShapeDtypeStruct((9, rows, channels), BF16)
    hbm = pl.BlockSpec(memory_space=pl.ANY)
    args = (info, perm, *ins) + ((partial, *parts) if last else ())
    out_shape = part_types(channels, rows) if last else [whole]
    outs = pl.pallas_call(
        functools.partial(conv_kernel, gscale, part, last),
        in_specs=[pl.BlockSpec(memory_space=pltpu.SMEM)] + [hbm] * (len(args) - 1),
        out_specs=[hbm] * len(out_shape),
        out_shape=out_shape,
        input_output_aliases={9 + i: i for i in range(6)} if last else {},
        scratch_shapes=[
            pltpu.VMEM(perm.shape, BF16),
            pltpu.VMEM((2, tokens // 2, channels), BF16),
            pltpu.VMEM((3 * rows, tokens), BF16),
            pltpu.VMEM((3, tokens, channels), BF16),
            pltpu.VMEM(whole.shape, BF16),
            pltpu.VMEM(whole.shape, BF16),
            pltpu.SemaphoreType.DMA((10,)),
            pltpu.SemaphoreType.DMA((9, 2)),
        ],
        compiler_params=params(),
        cost_estimate=cost(24 * rows * tokens * channels, 12e6),
        name="conv_grads",
    )(*args)
    return [list(outs[2 * p : 2 * p + 2]) for p in range(3)] if last else outs[0]


def fold_half_kernel(*refs):
    for p in range(3):
        mine, got, own_ref, send_ref = refs[2 * p], refs[2 * p + 1], refs[6 + 2 * p], refs[7 + 2 * p]
        rows = own_ref.shape[1]
        total = mine[...].astype(F32) + got[...].astype(F32)
        own_ref[...] = total[:, :rows].astype(BF16)
        send_ref[...] = total[:, rows:].astype(BF16)


def fold_half(values):
    shapes = []
    for value in values:
        count, rows, channels = value.shape
        shapes.append(jax.ShapeDtypeStruct((count, rows // 2, channels), BF16))
    return pl.pallas_call(
        fold_half_kernel,
        out_shape=shapes,
        compiler_params=params(),
        cost_estimate=cost(4e6, 8e6),
        name="fold_half",
    )(*values)


def fold_first_kernel(*refs):
    ins, (own_ref, *sends) = refs[:6], refs[6:]
    for p, (first, count) in enumerate(PARTS):
        rows = ins[0].shape[1] // 4
        for e in range(count):
            total = ins[2 * p][e].astype(F32) + ins[2 * p + 1][e].astype(F32)
            own_ref[first + e] = total[:rows]
            place, group = ((e, 0), (e, 1), (PARTS[0][1] + e, 0))[p]
            for k in range(1, 4):
                sends[3 * group + k - 1][place] = total[k * rows : (k + 1) * rows].astype(BF16)


def fold_second_kernel(*refs):
    own_in, got, (own_ref, *sends) = refs[0], refs[1:7], refs[7:]
    rows = own_in.shape[1] // 4
    for p, (first, count) in enumerate(PARTS):
        for e in range(count):
            place, group = ((e, 0), (e, 1), (PARTS[0][1] + e, 0))[p]
            total = own_in[first + e]
            for k in range(3):
                total = total + got[3 * group + k][place].astype(F32)
            own_ref[first + e] = total[:rows]
            place, group = ((e, 0), (PARTS[0][1] + e, 0), (e, 1))[p]
            for k in range(1, 4):
                sends[3 * group + k - 1][place] = total[k * rows : (k + 1) * rows].astype(BF16)


def fold_last_kernel(*refs):
    own_in, got, (conv_ref, q_ref, k_ref, v_ref, o_ref) = refs[0], refs[1:7], refs[7:]
    rows = own_in.shape[1]
    for p, (first, count) in enumerate(PARTS):
        for e in range(count):
            place, group = ((e, 0), (PARTS[0][1] + e, 0), (e, 1))[p]
            total = own_in[first + e]
            for k in range(3):
                total = total + got[3 * group + k][place].astype(F32)
            if e < 3:
                for r in range(rows):
                    conv_ref[e, r, p : p + 1] = total[r : r + 1]
            elif e == 3:
                (q_ref, k_ref, v_ref)[p][...] = total
            else:
                o_ref[...] = total


def fold_first(values):
    _, rows, channels = values[0].shape
    cut = rows // 4
    entries = ENTRIES
    wide = PARTS[0][1] + PARTS[2][1]
    sizes = [wide] * 3 + [PARTS[1][1]] * 3
    return pl.pallas_call(
        fold_first_kernel,
        out_shape=[jax.ShapeDtypeStruct((entries, cut, channels), F32)]
        + [jax.ShapeDtypeStruct((s, cut, channels), BF16) for s in sizes],
        compiler_params=params(),
        cost_estimate=cost(4e6, 7e6),
        name="fold_first",
    )(*values)


def fold_second(values):
    entries, rows, channels = values[0].shape
    cut = rows // 4
    wide = PARTS[0][1] + PARTS[1][1]
    sizes = [wide] * 3 + [PARTS[2][1]] * 3
    return pl.pallas_call(
        fold_second_kernel,
        out_shape=[jax.ShapeDtypeStruct((entries, cut, channels), F32)]
        + [jax.ShapeDtypeStruct((s, cut, channels), BF16) for s in sizes],
        compiler_params=params(),
        cost_estimate=cost(1e6, 2e6),
        name="fold_second",
    )(*values)


def fold_last(values):
    _, rows, channels = values[0].shape
    return pl.pallas_call(
        fold_last_kernel,
        out_shape=[jax.ShapeDtypeStruct((3, rows, 3, channels), F32)]
        + [jax.ShapeDtypeStruct((rows, channels), F32)] * 4,
        compiler_params=params(),
        cost_estimate=cost(3e5, 7e5),
        name="fold_last",
    )(*values)


def coordinates(index):
    dp, strip = index // 16, index % 16
    return {
        "x": dp // 2,
        "z": (strip // 8) * 2 + dp % 2,
        "y": (strip // 2) % 4,
        "core": strip % 2,
    }


def device_index(place):
    dp = place["x"] * 2 + place["z"] % 2
    strip = (place["z"] // 2) * 8 + place["y"] * 2 + place["core"]
    return dp * 16 + strip


def ring_pairs(axis, offset):
    pairs = []
    for source in range(128):
        place = coordinates(source)
        place[axis] = (place[axis] + offset) % 4
        pairs.append((source, device_index(place)))
    return pairs


def row_order(channels, here):
    per = channels // 128
    row = jnp.arange(channels // 2, dtype=jnp.int32)
    r = row % per
    k3 = (row // per) % 4
    k2 = (row // (per * 4)) % 4
    k1 = row // (per * 16)
    flip = (k1 // 2) ^ (3 * (k1 % 2))
    orders = []
    for order in ORDERS:
        place = {"core": here["core"], order[0]: here[order[0]] ^ flip}
        for axis, k in zip(order[1:], (k2, k3)):
            place[axis] = (here[axis] + k) % 4
        orders.append(device_index(place) * per + r)
    return jnp.stack(orders)


def ring_send(value, axis, offset):
    return lax.ppermute(value, ("dp", "strip"), ring_pairs(axis, offset))


def pair_send(value, axis, flip):
    pairs = []
    for source in range(128):
        place = coordinates(source)
        place[axis] = place[axis] ^ flip
        pairs.append((source, device_index(place)))
    return lax.ppermute(value, ("dp", "strip"), pairs)


def ring_sum(joined):
    own, *sends = joined
    values = [own]
    for i, send in enumerate(sends):
        values.append(ring_send(send, ("x", "y")[i // 3], i % 3 + 1))
    own, *sends = fold_second(values)
    values = [own]
    for i, send in enumerate(sends):
        values.append(ring_send(send, ("z", "y")[i // 3], i % 3 + 1))
    return fold_last(values)


def backward_kernel(
    gscale,
    info_ref,
    expand_ref,
    pick_ref,
    rg0_ref,
    rg1_ref,
    sib0_ref,
    sib1_ref,
    far0_ref,
    far1_ref,
    sums0_ref,
    sums1_ref,
    x_ref,
    chan_ref,
    vec_ref,
    conv_ref,
    ag_ref,
    payload_ref,
    rows_ref,
    acc_ref,
):
    step = pl.program_id(0)
    images, cells, channels = x_ref.shape
    half = rg0_ref.shape[0]

    @pl.when(step == 0)
    def _():
        core = info_ref[0]
        rows_ref[1, :half] = rg0_ref[...]
        rows_ref[1, half:] = rg1_ref[...]
        rows_ref[2 * core, :half] = sib0_ref[...]
        rows_ref[2 * core, half:] = sib1_ref[...]
        rows_ref[2 - 2 * core, :half] = far0_ref[...]
        rows_ref[2 - 2 * core, half:] = far1_ref[...]

    total = mm_nt(rows_ref[0], conv_ref[0, 0])
    total += mm_nt(rows_ref[1], conv_ref[1, 0])
    total += mm_nt(rows_ref[2], conv_ref[2, 0])

    @pl.when(step == 0)
    def _():
        for n in range(images):
            sl = slice(n * cells, (n + 1) * cells)
            acc_ref[sl] = shift_rows(total[sl], -1)

    @pl.when(step == 1)
    def _():
        acc_ref[...] += total

    @pl.when(step == 2)
    def _():
        gain = vec_ref[0:1]
        plain, weighted = [], []
        for n in range(images):
            sl = slice(n * cells, (n + 1) * cells)
            grad = acc_ref[sl] + shift_rows(total[sl], 1)
            standard = (x_ref[n].astype(F32) - chan_ref[n : n + 1]) * chan_ref[
                images + n : images + n + 1
            ]
            u = standard * gain + vec_ref[1:2]
            sigma = 0.5 + 0.5 * jnp.tanh(0.5 * u)
            ag = grad * (sigma * (1.0 + u * (1.0 - sigma)))
            ag_ref[sl] = ag
            plain.append(jnp.sum(ag, axis=0, keepdims=True))
            weighted.append(jnp.sum(ag * standard, axis=0, keepdims=True))
        all_totals = group_sum(jnp.concatenate(plain + weighted, axis=0) * gain, expand_ref[...])
        sums = sums0_ref[...] + sums1_ref[...]
        vectors = gscale * jnp.concatenate(
            [sum(weighted), sum(plain), sums, jnp.zeros((2, channels), F32)], axis=0
        )
        pieces = []
        for _ in range(3):
            piece = vectors.astype(BF16)
            pieces.append(piece.astype(F32))
            vectors = vectors - pieces[-1]
        picked = mm(jnp.concatenate(pieces, axis=0).astype(BF16), pick_ref[...])
        count = vectors.shape[0]
        picked = picked[:count] + picked[count : 2 * count] + picked[2 * count :]
        for s in range(payload_ref.shape[0]):
            payload_ref[s] = all_totals + picked[:, s * LANES : (s + 1) * LANES]


def backward(gscale, info, expand, pick, rows, sums, x, chan, vec, conv_weight):
    images, cells, channels = x.shape
    tokens = images * cells
    full = lambda shape: pl.BlockSpec(shape, lambda b: (0,) * len(shape))
    payload = (pick.shape[1] // LANES, 2 * images, LANES)
    ins = (expand, pick, *rows, *sums, x, chan, vec)
    return pl.pallas_call(
        functools.partial(backward_kernel, gscale),
        grid=(3,),
        in_specs=[pl.BlockSpec(memory_space=pltpu.SMEM)]
        + [full(v.shape) for v in ins]
        + [pl.BlockSpec((3, 1, channels, channels), lambda b: (0, b, 0, 0))],
        out_specs=[full((tokens, channels)), full(payload)],
        out_shape=[
            jax.ShapeDtypeStruct((tokens, channels), F32),
            jax.ShapeDtypeStruct(payload, F32),
        ],
        scratch_shapes=[
            pltpu.VMEM((3, tokens, channels), BF16),
            pltpu.VMEM((tokens, channels), F32),
        ],
        compiler_params=params(),
        cost_estimate=cost(18 * tokens * channels**2, 12e6, 4e5),
        name="backward_conv",
    )(info, *ins, conv_weight)


def input_kernel(
    totals_ref, expand_ref, rg0_ref, rg1_ref, ag_ref, x_ref, chan_ref, vec_ref,
    out_ref, spread_ref
):
    images, cells, channels = x_ref.shape
    strips = totals_ref.shape[0]
    count = strips * cells * (channels // GROUPS)
    summed = jnp.sum(totals_ref[...], axis=0)
    for d in range(spread_ref.shape[0]):
        spread_ref[d] = summed
    spread_c = spread(summed / count, expand_ref[...])
    for n in range(images):
        u, m = n // 2, n % 2
        sl = slice(m * cells, (m + 1) * cells)
        scale = chan_ref[images + n : images + n + 1]
        standard = (x_ref[n].astype(F32) - chan_ref[n : n + 1]) * scale
        part = scale * (
            ag_ref[n * cells : (n + 1) * cells] * vec_ref[0:1]
            - spread_c[n : n + 1]
            - standard * spread_c[images + n : images + n + 1]
        )
        rg = (rg0_ref, rg1_ref)[u][sl].astype(F32)
        out_ref[n] = (rg + part).astype(BF16)


def input_grad(totals, expand, rg0, rg1, ag, x, chan, vec, copies):
    return pl.pallas_call(
        input_kernel,
        out_shape=[
            jax.ShapeDtypeStruct(x.shape, BF16),
            jax.ShapeDtypeStruct((copies,) + totals.shape[1:], F32),
        ],
        compiler_params=params(),
        cost_estimate=cost(3e6, 4e6),
        name="input_grad",
    )(totals, expand, rg0, rg1, ag, x, chan, vec)


def exchange(value, axis="strip"):
    return lax.all_to_all(value, axis, split_axis=0, concat_axis=0, tiled=True)


def core_mate(value):
    return lax.ppermute(value, "strip", [(i, i ^ 1) for i in range(16)])


def far_row(value):
    pairs = [(i, i + 1) for i in range(1, 15, 2)]
    return lax.ppermute(value, "strip", pairs + [(j, i) for i, j in pairs])


def pick_matrix(channels, groups_dp, strips):
    per = channels // (groups_dp * strips)
    pick = np.zeros((channels, strips * LANES), np.float32)
    for o in range(channels):
        device, r = divmod(o, per)
        dp, strip = divmod(device, strips)
        pick[o, strip * LANES + GROUPS + dp * per + r] = 1.0
    return jnp.asarray(pick, BF16)


def on_device(
    block_in,
    upstream,
    gn_gain,
    gn_bias,
    conv_weight,
    conv_bias,
    ln_gain,
    ln_bias,
    w_query,
    w_key,
    w_value,
    w_out,
    out_bias,
):
    images, strip_rows, cells, channels = block_in.shape
    strips = lax.axis_size("strip")
    groups_dp = lax.axis_size("dp")
    me = lax.axis_index("strip")
    me_dp = lax.axis_index("dp")
    gscale = 1.0 / math.sqrt(cells * strips * images * groups_dp)
    x = block_in.reshape(images, cells, channels)
    up = upstream.reshape(images, cells, channels)
    up_rows = upstream.reshape(images * cells, channels)
    expand = expand_matrix(channels)
    core = me % 2
    inside = jnp.where(core == 0, me > 0, me < strips - 1)
    info = jnp.stack([core, inside.astype(jnp.int32)]).astype(jnp.int32)
    here = coordinates(me_dp * 16 + me)
    order = row_order(channels, here)
    perm = (order[:, :, None] == jnp.arange(channels, dtype=jnp.int32)).astype(BF16)
    perm, info = lax.optimization_barrier((perm, info))

    x_far = far_row(x)
    x_sib = core_mate(x)
    up_sib = core_mate(up_rows)
    stats, vec = local_stats(
        x, expand, (gn_gain, gn_bias, conv_bias, ln_gain, ln_bias, out_bias), strips
    )
    stats = exchange(stats)
    g = upstream_heads(up, w_out)
    hid_own, hid_sib, hid_far, residual, normed, qkv0, qkv1, chan = forward(
        info, stats, expand, vec, x, x_sib, x_far, g, conv_weight, w_query, w_key, w_value
    )
    hid_far_sib = core_mate(hid_far)
    normed_sib = core_mate(normed)
    got0, got1 = [exchange(attention(exchange(qkv))) for qkv in (qkv0, qkv1)]
    got0_sib = core_mate(got0)
    shared = (residual, up_rows, vec, w_out, w_query, w_key, w_value)
    block_out0, rg0, sums0 = after_attention(got0, *shared, 0)
    rg0_sib, rg0_far = core_mate(rg0), far_row(rg0)
    rows_in = (normed, normed_sib, up_rows, up_sib)
    hidden_in = (hid_own, hid_sib, hid_far, hid_far_sib)
    proj_part = proj_grads(gscale, 0, perm, (got0, got0_sib, *rows_in))
    conv_part = conv_grads(gscale, 0, info, perm, (rg0, rg0_sib, *hidden_in))
    got1, proj_part, conv_part, rg0_far = lax.optimization_barrier(
        (got1, proj_part, conv_part, rg0_far)
    )
    got1_sib = core_mate(got1)
    block_out1, rg1, sums1 = after_attention(got1, *shared, 1)
    rg1_sib, rg1_far = core_mate(rg1), far_row(rg1)
    block_out = jnp.concatenate([block_out0, block_out1], axis=0)
    blocks = proj_grads(gscale, 1, perm, (got1, got1_sib, *rows_in), proj_part)
    rg1_sib, rg1_far, blocks = lax.optimization_barrier((rg1_sib, rg1_far, blocks))
    blocks = conv_grads(gscale, 1, info, perm, (rg1, rg1_sib, *hidden_in), conv_part, blocks)
    pick = pick_matrix(channels, groups_dp, strips)
    sends = [pair_send(blocks[p][1], ORDERS[p][0], 1) for p in range(3)]
    ag, payload = backward(
        gscale,
        info,
        expand,
        pick,
        (rg0, rg1, rg0_sib, rg1_sib, rg0_far, rg1_far),
        (sums0, sums1),
        x,
        chan,
        vec,
        conv_weight,
    )
    totals = exchange(payload)
    sends, totals = lax.optimization_barrier((sends, totals))
    halves = fold_half([v for p in range(3) for v in (blocks[p][0], sends[p])])
    sends = [pair_send(halves[2 * p + 1], ORDERS[p][0], 3) for p in range(3)]
    grad_input, vectors = input_grad(totals, expand, rg0, rg1, ag, x, chan, vec, groups_dp)
    vectors = exchange(vectors, "dp")
    sends, vectors = lax.optimization_barrier((sends, vectors))
    conv_shard, q_shard, k_shard, v_shard, o_shard = ring_sum(
        fold_first([v for p in range(3) for v in (halves[2 * p], sends[p])])
    )
    per = channels // (strips * groups_dp)
    vectors = jnp.sum(vectors, axis=0)
    shards = lax.dynamic_slice_in_dim(vectors, GROUPS + me_dp * per, per, axis=1)
    shape = block_in.shape
    return (
        block_out.reshape(shape),
        grad_input.reshape(shape),
        conv_shard.transpose(0, 2, 3, 1),
        q_shard.T,
        k_shard.T,
        v_shard.T,
        o_shard.T,
        shards[0],
        shards[1],
        shards[2],
        shards[3],
        shards[4],
        shards[5],
    )


def solution(mesh):
    rows = P("dp", "strip", None, None)
    both = ("dp", "strip")
    in_specs = (rows, rows) + (P(),) * 11
    out_specs = (rows, rows, P(None, None, None, both)) + (P(None, both),) * 4 + (P(both),) * 6
    return jax.shard_map(
        on_device, mesh=mesh, in_specs=in_specs, out_specs=out_specs, check_vma=False
    )
```

```python
import functools
import math

import jax
import jax.numpy as jnp
import numpy as np
from jax import lax
from jax.experimental import pallas as pl
from jax.experimental.pallas import tpu as pltpu
from jax.sharding import PartitionSpec as P

HEADS = 8
GROUPS = 32
EPSILON = 1e-05
F32 = jnp.float32
BF16 = jnp.bfloat16
NT = (((1,), (1,)), ((), ()))
HIGH = lax.Precision.HIGHEST
VMEM_LIMIT = 56 * 1024 * 1024
LOG2E = math.log2(math.e)
QUERY_BLOCK = 1024
KEY_CHUNK = 512
ORDERS = (("y", "x", "z"), ("x", "y", "z"), ("z", "x", "y"))
ENTRIES = 13
LANES = 128
PARTS = ((0, 4), (4, 5), (9, 4))


def params(semantics=None):
    if semantics is None:
        return pltpu.CompilerParams(vmem_limit_bytes=VMEM_LIMIT)
    return pltpu.CompilerParams(
        vmem_limit_bytes=VMEM_LIMIT, dimension_semantics=semantics
    )


def mm(a, b):
    return jnp.dot(a, b, preferred_element_type=F32)


def mm_nt(a, b):
    return lax.dot_general(a, b, NT, preferred_element_type=F32)


def group_sum(rows, expand):
    return lax.dot_general(rows, expand, NT, preferred_element_type=F32, precision=HIGH)


def spread(rows, expand):
    return jnp.dot(rows, expand, preferred_element_type=F32, precision=HIGH)


def expand_matrix(channels):
    per_group = channels // GROUPS
    return jnp.asarray(
        np.arange(channels)[None, :] // per_group == np.arange(LANES)[:, None], F32
    )


def shift_rows(value, down):
    count = value.shape[0]
    row = lax.broadcasted_iota(jnp.int32, value.shape, 0)
    if down == 1:
        return jnp.where(row == 0, 0.0, pltpu.roll(value, 1, 0))
    return jnp.where(row == count - 1, 0.0, pltpu.roll(value, count - 1, 0))


def cost(flops, nbytes, trans=0):
    return pl.CostEstimate(flops=int(flops), bytes_accessed=int(nbytes), transcendentals=int(trans))


def stats_kernel(x_ref, expand_ref, *refs):
    vectors, out_ref, vec_ref = refs[:-2], refs[-2], refs[-1]
    images, cells, channels = x_ref.shape
    count = cells * (channels // GROUPS)
    vec_ref[...] = jnp.zeros_like(vec_ref)
    for i, ref in enumerate(vectors):
        vec_ref[i : i + 1] = ref[...].reshape(1, channels)
    expand = expand_ref[...]
    sums = jnp.concatenate(
        [jnp.sum(x_ref[n].astype(F32), axis=0, keepdims=True) for n in range(images)], axis=0
    )
    mean = group_sum(sums, expand) / count
    mean_c = spread(mean, expand)
    squares = []
    for n in range(images):
        d = x_ref[n].astype(F32) - mean_c[n : n + 1]
        squares.append(jnp.sum(d * d, axis=0, keepdims=True))
    m2 = group_sum(jnp.concatenate(squares, axis=0), expand)
    both = jnp.concatenate([mean, m2], axis=0)
    for s in range(out_ref.shape[0]):
        out_ref[s] = both


def local_stats(x, expand, vectors, strips):
    images, _, channels = x.shape
    return pl.pallas_call(
        stats_kernel,
        out_shape=[
            jax.ShapeDtypeStruct((strips, 2 * images, LANES), F32),
            jax.ShapeDtypeStruct((8, channels), F32),
        ],
        compiler_params=params(),
        cost_estimate=cost(1e7, 7e5),
        name="local_stats",
    )(x, expand, *vectors)


def upstream_kernel(up_ref, w_ref, g_ref):
    images = up_ref.shape[0]
    w = w_ref[...]
    hd = w.shape[0] // HEADS
    for n in range(images):
        g = mm_nt(w, up_ref[n])
        for h in range(HEADS):
            g_ref[n // 2, (n % 2) * HEADS + h] = g[h * hd : (h + 1) * hd].astype(BF16)


def upstream_heads(up, w_out):
    images, cells, channels = up.shape
    return pl.pallas_call(
        upstream_kernel,
        out_shape=jax.ShapeDtypeStruct((images // 2, 2 * HEADS, channels // HEADS, cells), BF16),
        compiler_params=params(),
        cost_estimate=cost(2 * images * cells * channels**2, 2.2e6),
        name="upstream_heads",
    )(up, w_out)


def forward_kernel(
    part,
    info_ref,
    stats_ref,
    expand_ref,
    vec_ref,
    x_hbm,
    sib_hbm,
    far_hbm,
    g_hbm,
    conv_hbm,
    wq_hbm,
    wk_hbm,
    wv_hbm,
    hid_own_hbm,
    hid_sib_hbm,
    hid_far_hbm,
    residual_hbm,
    normed_hbm,
    qkv_hbm,
    chan_ref,
    x_ref,
    conv_ref,
    w_ref,
    hidden_ref,
    acc_ref,
    residual_ref,
    normed_ref,
    qkv_ref,
    in_sems,
    out_sems,
):
    _, images, cells, channels = x_ref.shape
    all_images = x_hbm.shape[0]
    hd = channels // HEADS
    copy = pltpu.make_async_copy
    chosen = pl.ds(part * images, images)
    xs = [
        copy(h.at[chosen], x_ref.at[i], in_sems.at[i])
        for i, h in enumerate((x_hbm, sib_hbm, far_hbm))
    ]
    convs = [copy(conv_hbm.at[:, b], conv_ref.at[b], in_sems.at[3 + b]) for b in range(3)]
    ws = [copy(h, w_ref.at[i], in_sems.at[6 + i]) for i, h in enumerate((wq_hbm, wk_hbm, wv_hbm))]
    g_in = copy(g_hbm.at[part], qkv_ref.at[:, 3], in_sems.at[9])
    for task in xs + convs + ws + [g_in]:
        task.start()
    core = info_ref[0]
    strips = stats_ref.shape[0]
    count = cells * (channels // GROUPS)
    got = stats_ref[...]
    means = got[:, :all_images]
    mean = jnp.sum(means, axis=0) / strips
    off = means - mean[None]
    m2 = jnp.sum(got[:, all_images:], axis=0) + count * jnp.sum(off * off, axis=0)
    scale = lax.rsqrt(m2 / (count * strips) + EPSILON)
    both = spread(jnp.concatenate([mean, scale], axis=0), expand_ref[...])
    chan_ref[...] = both
    gain = vec_ref[0:1]
    bias = vec_ref[1:2]
    outs = []
    for i, out_hbm in enumerate((hid_own_hbm, hid_sib_hbm, hid_far_hbm)):
        xs[i].wait()
        for n in range(images):
            m = part * images + n
            factor_c = both[all_images + m : all_images + m + 1] * gain
            u = (x_ref[i, n].astype(F32) - both[m : m + 1]) * factor_c + bias
            h = u * (0.5 + 0.5 * jnp.tanh(0.5 * u))
            if i == 2:
                h = jnp.where(info_ref[1] > 0, h, 0.0)
            hidden_ref[i, n * cells : (n + 1) * cells] = h.astype(BF16)
        outs.append(copy(hidden_ref.at[i], out_hbm, out_sems.at[i]))
        outs[-1].start()

    above = 2 - core
    below = 1 + core
    for b in range(3):
        convs[b].wait()
        total = mm(hidden_ref[0], conv_ref[b, 1])
        total += mm(hidden_ref[above], conv_ref[b, 0])
        total += mm(hidden_ref[below], conv_ref[b, 2])
        if b == 1:
            acc_ref[...] += total
            continue
        for n in range(images):
            sl = slice(n * cells, (n + 1) * cells)
            if b == 0:
                acc_ref[sl] = shift_rows(total[sl], 1)
                continue
            conv = acc_ref[sl] + shift_rows(total[sl], -1)
            residual = (x_ref[0, n].astype(F32) + conv + vec_ref[2:3]).astype(BF16)
            residual_ref[sl] = residual
            tokens = residual.astype(F32)
            dev = tokens - jnp.mean(tokens, axis=1, keepdims=True)
            scale = lax.rsqrt(jnp.mean(dev * dev, axis=1, keepdims=True) + EPSILON)
            normed_ref[sl] = (dev * scale * vec_ref[3:4] + vec_ref[4:5]).astype(BF16)
    outs.append(copy(residual_ref, residual_hbm, out_sems.at[3]))
    outs.append(copy(normed_ref, normed_hbm, out_sems.at[4]))
    outs[-2].start()
    outs[-1].start()
    factor = LOG2E / math.sqrt(hd)
    for t in range(3):
        ws[t].wait()
        out = mm(normed_ref[...], w_ref[t])
        if t == 0:
            out = out * factor
        for n in range(images):
            flipped = out[n * cells : (n + 1) * cells].T.astype(BF16)
            for h in range(HEADS):
                qkv_ref[n * HEADS + h, t] = flipped[h * hd : (h + 1) * hd]
    g_in.wait()
    outs.append(copy(qkv_ref, qkv_hbm, out_sems.at[5]))
    outs[-1].start()
    for task in outs:
        task.wait()


def forward(part, info, stats, expand, vec, x, sib, far, g, conv_weight, wq, wk, wv):
    images, cells, channels = x.shape
    half = images // 2
    tokens = half * cells
    hd = channels // HEADS
    hbm = pl.BlockSpec(memory_space=pl.ANY)
    vmem = pl.BlockSpec(memory_space=pltpu.VMEM)
    row_type = jax.ShapeDtypeStruct((tokens, channels), BF16)
    qkv_shape = (half * HEADS, 4, hd, cells)
    return pl.pallas_call(
        functools.partial(forward_kernel, part),
        in_specs=[pl.BlockSpec(memory_space=pltpu.SMEM)] + [vmem] * 3 + [hbm] * 8,
        out_specs=[hbm] * 6 + [vmem],
        out_shape=[row_type] * 5
        + [
            jax.ShapeDtypeStruct(qkv_shape, BF16),
            jax.ShapeDtypeStruct((2 * images, channels), F32),
        ],
        scratch_shapes=[
            pltpu.VMEM((3, half, cells, channels), BF16),
            pltpu.VMEM((3, 3, channels, channels), BF16),
            pltpu.VMEM((3, channels, channels), BF16),
            pltpu.VMEM((3, tokens, channels), BF16),
            pltpu.VMEM((tokens, channels), F32),
            pltpu.VMEM((tokens, channels), BF16),
            pltpu.VMEM((tokens, channels), BF16),
            pltpu.VMEM(qkv_shape, BF16),
            pltpu.SemaphoreType.DMA((10,)),
            pltpu.SemaphoreType.DMA((6,)),
        ],
        compiler_params=params(),
        cost_estimate=cost(24 * tokens * channels**2, 16e6, 5e5),
        name="forward_conv",
    )(info, stats, expand, vec, x, sib, far, g, conv_weight, wq, wk, wv)


def together(*tasks):
    results = [None] * len(tasks)
    active = list(enumerate(tasks))
    while active:
        still = []
        for i, task in active:
            try:
                results[i] = next(task)
                still.append((i, task))
            except StopIteration:
                pass
        active = still
    return results


def attention_kernel(
    qkv_ref, out_ref, kt_ref, vt_ref, kn_ref, vn_ref, s_ref, e_ref, dk_ref, dv_ref
):
    step = pl.program_id(0)
    sources, _, hd, cells = qkv_ref.shape
    length = sources * cells
    wide = kn_ref.shape[1]
    block = s_ref.shape[2]
    per = block // cells
    spans = [slice(c, c + KEY_CHUNK) for c in range(0, length, KEY_CHUNK)]
    extra = vt_ref.shape[0] - hd

    @pl.when(step == 0)
    def _():
        ones_row = (lax.broadcasted_iota(jnp.int32, (extra, cells), 0) == 0).astype(F32)
        pad = jnp.zeros((wide - hd, cells), F32)
        row = lax.broadcasted_iota(jnp.int32, (wide - hd, cells), 0)
        ones_two = (row < 2).astype(F32)
        for s in range(sources):
            sl = slice(s * cells, (s + 1) * cells)
            k = qkv_ref[s, 1]
            v = qkv_ref[s, 2]
            kt_ref[:, sl] = k
            vt_ref[:hd, sl] = v
            vt_ref[hd:, sl] = ones_row.astype(BF16)
            kn_ref[sl] = jnp.concatenate([k.astype(F32), pad], axis=0).T.astype(BF16)
            vn_ref[sl] = jnp.concatenate([v.astype(F32), ones_two], axis=0).T.astype(BF16)
        dk_ref[...] = jnp.zeros_like(dk_ref)
        dv_ref[...] = jnp.zeros_like(dv_ref)

    bases = [(2 * step + b) * per for b in range(2)]

    def rows_of(b, t):
        return jnp.concatenate([qkv_ref[bases[b] + u, t] for u in range(per)], axis=1).astype(F32)

    def put(b, t, value):
        for u in range(per):
            out_ref[bases[b] + u, t] = value[:, u * cells : (u + 1) * cells].astype(BF16)

    def scores(b):
        q = jnp.concatenate([rows_of(b, 0), jnp.zeros((wide - hd, block), F32)], axis=0)
        q_t = q.astype(BF16)
        top = None
        for sl in spans:
            value = mm(kn_ref[sl], q_t)
            s_ref[b, sl] = value
            here = jnp.max(value, axis=0, keepdims=True)
            top = here if top is None else jnp.maximum(top, here)
            yield None
        yield top, q.T.astype(BF16)

    def attend(b, top):
        acc = jnp.zeros((hd + extra, block), F32)
        for sl in spans:
            e = jnp.exp2(s_ref[b, sl] - top).astype(BF16)
            e_ref[b, sl] = e
            acc += mm(vt_ref[:, sl], e)
            yield None
        yield acc

    def finish(b, acc):
        inverse = 1.0 / acc[hd : hd + 1]
        out = acc[:hd] * inverse
        put(b, 0, out)
        g = (rows_of(b, 3) * inverse).astype(BF16).astype(F32)
        delta = -jnp.sum(g * out, axis=0, keepdims=True)
        high = delta.astype(BF16).astype(F32)
        low = delta - high
        row = lax.broadcasted_iota(jnp.int32, (wide - hd, block), 0)
        tail = jnp.where(row == 0, high, jnp.where(row == 1, low, 0.0))
        g = jnp.concatenate([g, tail], axis=0)
        return g.astype(BF16), g.T.astype(BF16)

    def back(b, g_t, g_n, q_n):
        dq = jnp.zeros((hd, block), F32)
        for sl in spans:
            e = e_ref[b, sl]
            ds = (e.astype(F32) * mm(vn_ref[sl], g_t)).astype(BF16)
            dq += mm(kt_ref[:, sl], ds)
            dk_ref[sl] += mm(ds, q_n)
            dv_ref[sl] += mm(e, g_n)
            yield None
        put(b, 1, dq * (1.0 / math.sqrt(hd)))
        yield None

    ((top0, q0),) = together(scores(0))
    acc0, (top1, q1) = together(attend(0, top0), scores(1))
    _, acc1 = together(back(0, *finish(0, acc0), q0), attend(1, top1))
    together(back(1, *finish(1, acc1), q1))

    @pl.when(step == pl.num_programs(0) - 1)
    def _():
        for s in range(sources):
            sl = slice(s * cells, (s + 1) * cells)
            out_ref[s, 2] = (dk_ref[sl].T[:hd] * (1.0 / LOG2E)).astype(BF16)
            out_ref[s, 3] = dv_ref[sl].T[:hd].astype(BF16)


def attention(qkv):
    sources, _, hd, cells = qkv.shape
    length = sources * cells
    block = QUERY_BLOCK
    wide = 128
    full = lambda shape: pl.BlockSpec(shape, lambda i: (0,) * len(shape))
    return pl.pallas_call(
        attention_kernel,
        grid=(length // block // 2,),
        in_specs=[full(qkv.shape)],
        out_specs=full((sources, 4, hd, cells)),
        out_shape=jax.ShapeDtypeStruct((sources, 4, hd, cells), BF16),
        scratch_shapes=[
            pltpu.VMEM((hd, length), BF16),
            pltpu.VMEM((hd + 16, length), BF16),
            pltpu.VMEM((length, wide), BF16),
            pltpu.VMEM((length, wide), BF16),
            pltpu.VMEM((2, length, block), F32),
            pltpu.VMEM((2, length, block), BF16),
            pltpu.VMEM((length, wide), F32),
            pltpu.VMEM((length, wide), F32),
        ],
        compiler_params=params(),
        cost_estimate=cost(12 * length * length * 256, 5e6, length * length),
        name="attention",
    )(qkv)


def gather_heads(got_ref, t):
    return jnp.concatenate(
        [
            jnp.concatenate([got_ref[n * HEADS + h, t] for h in range(HEADS)], axis=0)
            for n in range(2)
        ],
        axis=1,
    )


def tokens_kernel(
    got_ref,
    residual_ref,
    up_ref,
    vec_ref,
    wo_ref,
    wq_ref,
    wk_ref,
    wv_ref,
    block_out_ref,
    rg_ref,
    sums_ref,
):
    residual = residual_ref[...].astype(F32)
    up = up_ref[...].astype(F32)
    mixed = mm(gather_heads(got_ref, 0).T, wo_ref[...])
    block_out_ref[...] = (residual + mixed + vec_ref[5:6]).astype(BF16)
    grad = mm_nt(gather_heads(got_ref, 1).T, wq_ref[...])
    grad += mm_nt(gather_heads(got_ref, 2).T, wk_ref[...])
    grad += mm_nt(gather_heads(got_ref, 3).T, wv_ref[...])
    dev = residual - jnp.mean(residual, axis=1, keepdims=True)
    scale = lax.rsqrt(jnp.mean(dev * dev, axis=1, keepdims=True) + EPSILON)
    standard = dev * scale
    scaled = grad * vec_ref[3:4]
    part = scale * (
        scaled
        - jnp.mean(scaled, axis=1, keepdims=True)
        - standard * jnp.mean(scaled * standard, axis=1, keepdims=True)
    )
    rg = (up + part).astype(BF16)
    rg_ref[...] = rg
    sums_ref[0:1] = jnp.sum(rg.astype(F32), axis=0, keepdims=True)
    sums_ref[1:2] = jnp.sum(grad * standard, axis=0, keepdims=True)
    sums_ref[2:3] = jnp.sum(grad, axis=0, keepdims=True)
    sums_ref[3:4] = jnp.sum(up, axis=0, keepdims=True)


def after_attention(got, residual, up, vec, wo, wq, wk, wv, part):
    channels = residual.shape[1]
    cells = got.shape[3]
    tokens = 2 * cells
    full = lambda shape: pl.BlockSpec(shape, lambda i: (0,) * len(shape))
    rows = pl.BlockSpec((tokens, channels), lambda i: (part, 0))
    square = (channels, channels)
    return pl.pallas_call(
        tokens_kernel,
        grid=(1,),
        in_specs=[full(got.shape), full(residual.shape), rows, full(vec.shape)]
        + [full(square)] * 4,
        out_specs=[
            full((tokens, channels)),
            full((tokens, channels)),
            full((4, channels)),
        ],
        out_shape=[
            jax.ShapeDtypeStruct((tokens, channels), BF16),
            jax.ShapeDtypeStruct((tokens, channels), BF16),
            jax.ShapeDtypeStruct((4, channels), F32),
        ],
        compiler_params=params(),
        cost_estimate=cost(8 * tokens * channels**2, 7e6),
        name="after_attention",
    )(got, residual, up, vec, wo, wq, wk, wv)


def wait_all(tasks):
    for task in tasks:
        task.wait()


def emitter(gscale, outs_hbm, part_ref, out_ref, out_sems, outs):
    def emit(entry, p, place, value):
        value = value * gscale
        if part_ref is not None:
            value = value + part_ref[entry].astype(F32)
        out_ref[entry] = value.astype(BF16)
        if part_ref is None:
            targets = [(out_ref.at[entry], outs_hbm[0].at[entry])]
        else:
            rows = value.shape[0] // 2
            targets = [
                (out_ref.at[entry, pl.ds(k * rows, rows)], outs_hbm[2 * p + k].at[place])
                for k in range(2)
            ]
        for k, (source, target) in enumerate(targets):
            outs.append(pltpu.make_async_copy(source, target, out_sems.at[entry, k]))
            outs[-1].start()

    return emit


def proj_kernel(gscale, part, last, *refs):
    perm_hbm, got_hbm, got_sib_hbm, normed_hbm, normed_sib_hbm, up_hbm, up_sib_hbm = refs[:7]
    inputs = 8 if last else 7
    part_hbm = refs[7] if last else None
    outs_hbm, scratch = refs[inputs:-10], refs[-10:]
    perm_ref, got_ref, up_ref, left_ref, normed_ref, att_ref, part_ref, out_ref = scratch[:8]
    in_sems, out_sems = scratch[8:]
    copy = pltpu.make_async_copy
    half = normed_ref.shape[0] // 2
    rows = pl.ds(part * half, half)
    places = [pl.ds(u * half, half) for u in range(2)]
    got_in = [
        [
            copy(h.at[:, t], got_ref.at[u, t], in_sems.at[2 * t + u])
            for u, h in enumerate((got_hbm, got_sib_hbm))
        ]
        for t in range(4)
    ]
    perm_in = [copy(perm_hbm, perm_ref, in_sems.at[8])]
    normed_in = [
        copy(h, normed_ref.at[places[u]], in_sems.at[9 + u])
        for u, h in enumerate((normed_hbm, normed_sib_hbm))
    ]
    up_in = [
        copy(h.at[rows], up_ref.at[places[u]], in_sems.at[11 + u])
        for u, h in enumerate((up_hbm, up_sib_hbm))
    ]
    part_in = [copy(part_hbm, part_ref, in_sems.at[13])] if last else []
    for tasks in (perm_in, got_in[1], got_in[2], got_in[3], normed_in, part_in, got_in[0], up_in):
        for task in tasks:
            task.start()

    def heads(u, t):
        return jnp.concatenate(
            [
                jnp.concatenate([got_ref[u, t, n * HEADS + h] for h in range(HEADS)], axis=0)
                for n in range(2)
            ],
            axis=1,
        )

    outs = []
    emit = emitter(gscale, outs_hbm, part_ref if last else None, out_ref, out_sems, outs)
    count = perm_ref.shape[1]
    wait_all(perm_in)
    for p in range(3):
        wait_all(got_in[1 + p])
        for u in range(2):
            left_ref[p * count : (p + 1) * count, u * half : (u + 1) * half] = mm(
                perm_ref[p], heads(u, 1 + p)
            ).astype(BF16)
    wait_all(normed_in + part_in)
    value = mm(left_ref[...], normed_ref[...])
    for p in range(3):
        emit(p, p, 3, value[p * count : (p + 1) * count])
    wait_all(got_in[0] + up_in)
    for u in range(2):
        att_ref[u * half : (u + 1) * half] = heads(u, 0).T
    emit(3, 1, 4, mm(mm_nt(perm_ref[1], up_ref[...]).astype(BF16), att_ref[...]))
    wait_all(outs)


def conv_kernel(gscale, last, *refs):
    info_ref, perm_hbm, rg_hbm, rg_sib_hbm, own_hbm, sib_hbm, far_hbm, far_sib_hbm = refs[:8]
    inputs = 15 if last else 8
    part_hbm = refs[8] if last else None
    outs_hbm, scratch = refs[inputs:-8], refs[-8:]
    perm_ref, rg_ref, left_ref, right_ref, part_ref, out_ref, in_sems, out_sems = scratch
    copy = pltpu.make_async_copy
    core = info_ref[0]
    half = rg_ref.shape[1]
    mine, other = pl.ds(0, half), pl.ds(half, half)
    first_in = [
        copy(perm_hbm, perm_ref, in_sems.at[0]),
        copy(rg_hbm, rg_ref.at[0], in_sems.at[1]),
        copy(rg_sib_hbm, rg_ref.at[1], in_sems.at[2]),
    ]
    hidden_in = [
        copy(own_hbm, right_ref.at[1, mine], in_sems.at[3]),
        copy(sib_hbm, right_ref.at[2 - 2 * core, mine], in_sems.at[4]),
        copy(far_hbm, right_ref.at[2 * core, mine], in_sems.at[5]),
        copy(own_hbm, right_ref.at[2 * core, other], in_sems.at[6]),
        copy(sib_hbm, right_ref.at[1, other], in_sems.at[7]),
        copy(far_sib_hbm, right_ref.at[2 - 2 * core, other], in_sems.at[8]),
    ]
    part_in = [copy(part_hbm, part_ref, in_sems.at[9])] if last else []
    for task in first_in + hidden_in + part_in:
        task.start()
    outs = []
    emit = emitter(gscale, outs_hbm, part_ref if last else None, out_ref, out_sems, outs)
    count = perm_ref.shape[1]
    cells = half // 2
    wait_all(first_in)
    for p in range(3):
        for u in range(2):
            pieces = []
            for n in range(2):
                piece = rg_ref[u, n * cells : (n + 1) * cells]
                if p != 1:
                    piece = shift_rows(piece.astype(F32), p - 1).astype(BF16)
                pieces.append(piece)
            left_ref[p * count : (p + 1) * count, u * half : (u + 1) * half] = mm_nt(
                perm_ref[p], jnp.concatenate(pieces, axis=0)
            ).astype(BF16)
    wait_all(hidden_in + part_in)
    for a in range(3):
        value = mm(left_ref[...], right_ref[a])
        for p in range(3):
            emit(3 * p + a, p, a, value[p * count : (p + 1) * count])
    wait_all(outs)


def part_types(channels, rows):
    types = []
    for _, count in PARTS:
        types += [jax.ShapeDtypeStruct((count, rows // 2, channels), BF16)] * 2
    return types


def proj_grads(gscale, part, perm, ins, partial=None):
    channels = perm.shape[2]
    rows = perm.shape[1]
    got = ins[0]
    tokens = 4 * got.shape[3]
    last = partial is not None
    whole = jax.ShapeDtypeStruct((4, rows, channels), BF16)
    hbm = pl.BlockSpec(memory_space=pl.ANY)
    args = (perm, *ins) + ((partial,) if last else ())
    out_shape = part_types(channels, rows) if last else [whole]
    outs = pl.pallas_call(
        functools.partial(proj_kernel, gscale, part, last),
        in_specs=[hbm] * len(args),
        out_specs=[hbm] * len(out_shape),
        out_shape=out_shape,
        scratch_shapes=[
            pltpu.VMEM(perm.shape, BF16),
            pltpu.VMEM((2, 4) + got.shape[:1] + got.shape[2:], BF16),
            pltpu.VMEM((tokens, channels), BF16),
            pltpu.VMEM((3 * rows, tokens), BF16),
            pltpu.VMEM((tokens, channels), BF16),
            pltpu.VMEM((tokens, channels), BF16),
            pltpu.VMEM(whole.shape, BF16),
            pltpu.VMEM(whole.shape, BF16),
            pltpu.SemaphoreType.DMA((14,)),
            pltpu.SemaphoreType.DMA((4, 2)),
        ],
        compiler_params=params(),
        cost_estimate=cost(16 * rows * tokens * channels, 9e6),
        name="proj_grads",
    )(*args)
    return list(outs) if last else outs[0]


def conv_grads(gscale, info, perm, ins, partial=None, parts=()):
    channels = perm.shape[2]
    rows = perm.shape[1]
    tokens = 2 * ins[0].shape[0]
    last = partial is not None
    whole = jax.ShapeDtypeStruct((9, rows, channels), BF16)
    hbm = pl.BlockSpec(memory_space=pl.ANY)
    args = (info, perm, *ins) + ((partial, *parts) if last else ())
    out_shape = part_types(channels, rows) if last else [whole]
    outs = pl.pallas_call(
        functools.partial(conv_kernel, gscale, last),
        in_specs=[pl.BlockSpec(memory_space=pltpu.SMEM)] + [hbm] * (len(args) - 1),
        out_specs=[hbm] * len(out_shape),
        out_shape=out_shape,
        input_output_aliases={9 + i: i for i in range(6)} if last else {},
        scratch_shapes=[
            pltpu.VMEM(perm.shape, BF16),
            pltpu.VMEM((2, tokens // 2, channels), BF16),
            pltpu.VMEM((3 * rows, tokens), BF16),
            pltpu.VMEM((3, tokens, channels), BF16),
            pltpu.VMEM(whole.shape, BF16),
            pltpu.VMEM(whole.shape, BF16),
            pltpu.SemaphoreType.DMA((10,)),
            pltpu.SemaphoreType.DMA((9, 2)),
        ],
        compiler_params=params(),
        cost_estimate=cost(24 * rows * tokens * channels, 12e6),
        name="conv_grads",
    )(*args)
    return [list(outs[2 * p : 2 * p + 2]) for p in range(3)] if last else outs[0]


def fold_half_kernel(*refs):
    for p in range(3):
        mine, got, own_ref, send_ref = refs[2 * p], refs[2 * p + 1], refs[6 + 2 * p], refs[7 + 2 * p]
        rows = own_ref.shape[1]
        total = mine[...].astype(F32) + got[...].astype(F32)
        own_ref[...] = total[:, :rows].astype(BF16)
        send_ref[...] = total[:, rows:].astype(BF16)


def fold_half(values):
    shapes = []
    for value in values:
        count, rows, channels = value.shape
        shapes.append(jax.ShapeDtypeStruct((count, rows // 2, channels), BF16))
    return pl.pallas_call(
        fold_half_kernel,
        out_shape=shapes,
        compiler_params=params(),
        cost_estimate=cost(4e6, 8e6),
        name="fold_half",
    )(*values)


def fold_first_kernel(*refs):
    ins, (own_ref, *sends) = refs[:6], refs[6:]
    for p, (first, count) in enumerate(PARTS):
        rows = ins[0].shape[1] // 4
        for e in range(count):
            total = ins[2 * p][e].astype(F32) + ins[2 * p + 1][e].astype(F32)
            own_ref[first + e] = total[:rows]
            place, group = ((e, 0), (e, 1), (PARTS[0][1] + e, 0))[p]
            for k in range(1, 4):
                sends[3 * group + k - 1][place] = total[k * rows : (k + 1) * rows].astype(BF16)


def fold_second_kernel(*refs):
    own_in, got, (own_ref, *sends) = refs[0], refs[1:7], refs[7:]
    rows = own_in.shape[1] // 4
    for p, (first, count) in enumerate(PARTS):
        for e in range(count):
            place, group = ((e, 0), (e, 1), (PARTS[0][1] + e, 0))[p]
            total = own_in[first + e]
            for k in range(3):
                total = total + got[3 * group + k][place].astype(F32)
            own_ref[first + e] = total[:rows]
            place, group = ((e, 0), (PARTS[0][1] + e, 0), (e, 1))[p]
            for k in range(1, 4):
                sends[3 * group + k - 1][place] = total[k * rows : (k + 1) * rows].astype(BF16)


def fold_last_kernel(*refs):
    own_in, got, (conv_ref, q_ref, k_ref, v_ref, o_ref) = refs[0], refs[1:7], refs[7:]
    rows = own_in.shape[1]
    for p, (first, count) in enumerate(PARTS):
        for e in range(count):
            place, group = ((e, 0), (PARTS[0][1] + e, 0), (e, 1))[p]
            total = own_in[first + e]
            for k in range(3):
                total = total + got[3 * group + k][place].astype(F32)
            if e < 3:
                for r in range(rows):
                    conv_ref[e, r, p : p + 1] = total[r : r + 1]
            elif e == 3:
                (q_ref, k_ref, v_ref)[p][...] = total
            else:
                o_ref[...] = total


def fold_first(values):
    _, rows, channels = values[0].shape
    cut = rows // 4
    entries = ENTRIES
    wide = PARTS[0][1] + PARTS[2][1]
    sizes = [wide] * 3 + [PARTS[1][1]] * 3
    return pl.pallas_call(
        fold_first_kernel,
        out_shape=[jax.ShapeDtypeStruct((entries, cut, channels), F32)]
        + [jax.ShapeDtypeStruct((s, cut, channels), BF16) for s in sizes],
        compiler_params=params(),
        cost_estimate=cost(4e6, 7e6),
        name="fold_first",
    )(*values)


def fold_second(values):
    entries, rows, channels = values[0].shape
    cut = rows // 4
    wide = PARTS[0][1] + PARTS[1][1]
    sizes = [wide] * 3 + [PARTS[2][1]] * 3
    return pl.pallas_call(
        fold_second_kernel,
        out_shape=[jax.ShapeDtypeStruct((entries, cut, channels), F32)]
        + [jax.ShapeDtypeStruct((s, cut, channels), BF16) for s in sizes],
        compiler_params=params(),
        cost_estimate=cost(1e6, 2e6),
        name="fold_second",
    )(*values)


def fold_last(values):
    _, rows, channels = values[0].shape
    return pl.pallas_call(
        fold_last_kernel,
        out_shape=[jax.ShapeDtypeStruct((3, rows, 3, channels), F32)]
        + [jax.ShapeDtypeStruct((rows, channels), F32)] * 4,
        compiler_params=params(),
        cost_estimate=cost(3e5, 7e5),
        name="fold_last",
    )(*values)


def coordinates(index):
    dp, strip = index // 16, index % 16
    return {
        "x": dp // 2,
        "z": (strip // 8) * 2 + dp % 2,
        "y": (strip // 2) % 4,
        "core": strip % 2,
    }


def device_index(place):
    dp = place["x"] * 2 + place["z"] % 2
    strip = (place["z"] // 2) * 8 + place["y"] * 2 + place["core"]
    return dp * 16 + strip


def ring_pairs(axis, offset):
    pairs = []
    for source in range(128):
        place = coordinates(source)
        place[axis] = (place[axis] + offset) % 4
        pairs.append((source, device_index(place)))
    return pairs


def row_order(channels, here):
    per = channels // 128
    row = jnp.arange(channels // 2, dtype=jnp.int32)
    r = row % per
    k3 = (row // per) % 4
    k2 = (row // (per * 4)) % 4
    k1 = row // (per * 16)
    flip = (k1 // 2) ^ (3 * (k1 % 2))
    orders = []
    for order in ORDERS:
        place = {"core": here["core"], order[0]: here[order[0]] ^ flip}
        for axis, k in zip(order[1:], (k2, k3)):
            place[axis] = (here[axis] + k) % 4
        orders.append(device_index(place) * per + r)
    return jnp.stack(orders)


def ring_send(value, axis, offset):
    return lax.ppermute(value, ("dp", "strip"), ring_pairs(axis, offset))


def pair_send(value, axis, flip):
    pairs = []
    for source in range(128):
        place = coordinates(source)
        place[axis] = place[axis] ^ flip
        pairs.append((source, device_index(place)))
    return lax.ppermute(value, ("dp", "strip"), pairs)


def ring_sum(joined):
    own, *sends = joined
    values = [own]
    for i, send in enumerate(sends):
        values.append(ring_send(send, ("x", "y")[i // 3], i % 3 + 1))
    own, *sends = fold_second(values)
    values = [own]
    for i, send in enumerate(sends):
        values.append(ring_send(send, ("z", "y")[i // 3], i % 3 + 1))
    return fold_last(values)


def backward_kernel(
    gscale,
    info_ref,
    expand_ref,
    sums0_ref,
    sums1_ref,
    chan_ref,
    vec_ref,
    pick_hbm,
    rg0_hbm,
    rg1_hbm,
    sib0_hbm,
    sib1_hbm,
    far0_hbm,
    far1_hbm,
    x_hbm,
    conv_hbm,
    ag_hbm,
    payload_ref,
    pick_ref,
    rows_ref,
    x_ref,
    conv_ref,
    acc_ref,
    in_sems,
    out_sems,
):
    images, cells, channels = x_ref.shape
    half = images * cells // 2
    copy = pltpu.make_async_copy
    core = info_ref[0]
    first, second = pl.ds(0, half), pl.ds(half, half)
    rows_in = [
        copy(h, rows_ref.at[place, rows], in_sems.at[i])
        for i, (h, place, rows) in enumerate(
            (
                (rg0_hbm, 1, first),
                (rg1_hbm, 1, second),
                (sib0_hbm, 2 * core, first),
                (sib1_hbm, 2 * core, second),
                (far0_hbm, 2 - 2 * core, first),
                (far1_hbm, 2 - 2 * core, second),
            )
        )
    ]
    convs = [copy(conv_hbm.at[:, b], conv_ref.at[b], in_sems.at[6 + b]) for b in range(3)]
    x_in = copy(x_hbm, x_ref, in_sems.at[9])
    pick_in = copy(pick_hbm, pick_ref, in_sems.at[10])
    for task in rows_in + convs + [x_in, pick_in]:
        task.start()
    wait_all(rows_in)
    gain = vec_ref[0:1]
    plain, weighted, outs = [], [], []
    for b in range(3):
        convs[b].wait()
        total = mm_nt(rows_ref[0], conv_ref[b, 0])
        total += mm_nt(rows_ref[1], conv_ref[b, 1])
        total += mm_nt(rows_ref[2], conv_ref[b, 2])
        if b == 1:
            acc_ref[...] += total
            continue
        if b == 2:
            x_in.wait()
        for n in range(images):
            sl = slice(n * cells, (n + 1) * cells)
            if b == 0:
                acc_ref[sl] = shift_rows(total[sl], -1)
                continue
            grad = acc_ref[sl] + shift_rows(total[sl], 1)
            standard = (x_ref[n].astype(F32) - chan_ref[n : n + 1]) * chan_ref[
                images + n : images + n + 1
            ]
            u = standard * gain + vec_ref[1:2]
            sigma = 0.5 + 0.5 * jnp.tanh(0.5 * u)
            ag = grad * (sigma * (1.0 + u * (1.0 - sigma)))
            acc_ref[sl] = ag
            rows = pl.ds(n * cells, cells)
            outs.append(copy(acc_ref.at[rows], ag_hbm.at[rows], out_sems.at[n]))
            outs[-1].start()
            plain.append(jnp.sum(ag, axis=0, keepdims=True))
            weighted.append(jnp.sum(ag * standard, axis=0, keepdims=True))
    all_totals = group_sum(jnp.concatenate(plain + weighted, axis=0) * gain, expand_ref[...])
    sums = sums0_ref[...] + sums1_ref[...]
    vectors = gscale * jnp.concatenate(
        [sum(weighted), sum(plain), sums, jnp.zeros((2, channels), F32)], axis=0
    )
    pieces = []
    for _ in range(3):
        piece = vectors.astype(BF16)
        pieces.append(piece.astype(F32))
        vectors = vectors - pieces[-1]
    pick_in.wait()
    picked = mm(jnp.concatenate(pieces, axis=0).astype(BF16), pick_ref[...])
    count = vectors.shape[0]
    picked = picked[:count] + picked[count : 2 * count] + picked[2 * count :]
    for s in range(payload_ref.shape[0]):
        payload_ref[s] = all_totals + picked[:, s * LANES : (s + 1) * LANES]
    wait_all(outs)


def backward(gscale, info, expand, pick, rows, sums, x, chan, vec, conv_weight):
    images, cells, channels = x.shape
    tokens = images * cells
    payload = (pick.shape[1] // LANES, 2 * images, LANES)
    hbm = pl.BlockSpec(memory_space=pl.ANY)
    vmem = pl.BlockSpec(memory_space=pltpu.VMEM)
    return pl.pallas_call(
        functools.partial(backward_kernel, gscale),
        in_specs=[pl.BlockSpec(memory_space=pltpu.SMEM)] + [vmem] * 5 + [hbm] * 9,
        out_specs=[hbm, vmem],
        out_shape=[
            jax.ShapeDtypeStruct((tokens, channels), F32),
            jax.ShapeDtypeStruct(payload, F32),
        ],
        scratch_shapes=[
            pltpu.VMEM(pick.shape, BF16),
            pltpu.VMEM((3, tokens, channels), BF16),
            pltpu.VMEM(x.shape, BF16),
            pltpu.VMEM((3, 3, channels, channels), BF16),
            pltpu.VMEM((tokens, channels), F32),
            pltpu.SemaphoreType.DMA((11,)),
            pltpu.SemaphoreType.DMA((images,)),
        ],
        compiler_params=params(),
        cost_estimate=cost(18 * tokens * channels**2, 12e6, 4e5),
        name="backward_conv",
    )(info, expand, *sums, chan, vec, pick, *rows, x, conv_weight)


def input_kernel(
    totals_ref, expand_ref, rg0_ref, rg1_ref, ag_ref, x_ref, chan_ref, vec_ref,
    out_ref, spread_ref
):
    images, cells, channels = x_ref.shape
    strips = totals_ref.shape[0]
    count = strips * cells * (channels // GROUPS)
    summed = jnp.sum(totals_ref[...], axis=0)
    for d in range(spread_ref.shape[0]):
        spread_ref[d] = summed
    spread_c = spread(summed / count, expand_ref[...])
    for n in range(images):
        u, m = n // 2, n % 2
        sl = slice(m * cells, (m + 1) * cells)
        scale = chan_ref[images + n : images + n + 1]
        standard = (x_ref[n].astype(F32) - chan_ref[n : n + 1]) * scale
        part = scale * (
            ag_ref[n * cells : (n + 1) * cells] * vec_ref[0:1]
            - spread_c[n : n + 1]
            - standard * spread_c[images + n : images + n + 1]
        )
        rg = (rg0_ref, rg1_ref)[u][sl].astype(F32)
        out_ref[n] = (rg + part).astype(BF16)


def input_grad(totals, expand, rg0, rg1, ag, x, chan, vec, copies):
    return pl.pallas_call(
        input_kernel,
        out_shape=[
            jax.ShapeDtypeStruct(x.shape, BF16),
            jax.ShapeDtypeStruct((copies,) + totals.shape[1:], F32),
        ],
        compiler_params=params(),
        cost_estimate=cost(3e6, 4e6),
        name="input_grad",
    )(totals, expand, rg0, rg1, ag, x, chan, vec)


def exchange(value, axis="strip"):
    return lax.all_to_all(value, axis, split_axis=0, concat_axis=0, tiled=True)


def core_mate(value):
    return lax.ppermute(value, "strip", [(i, i ^ 1) for i in range(16)])


def far_row(value):
    pairs = [(i, i + 1) for i in range(1, 15, 2)]
    return lax.ppermute(value, "strip", pairs + [(j, i) for i, j in pairs])


def pick_matrix(channels, groups_dp, strips):
    per = channels // (groups_dp * strips)
    pick = np.zeros((channels, strips * LANES), np.float32)
    for o in range(channels):
        device, r = divmod(o, per)
        dp, strip = divmod(device, strips)
        pick[o, strip * LANES + GROUPS + dp * per + r] = 1.0
    return jnp.asarray(pick, BF16)


def on_device(
    block_in,
    upstream,
    gn_gain,
    gn_bias,
    conv_weight,
    conv_bias,
    ln_gain,
    ln_bias,
    w_query,
    w_key,
    w_value,
    w_out,
    out_bias,
):
    images, strip_rows, cells, channels = block_in.shape
    strips = lax.axis_size("strip")
    groups_dp = lax.axis_size("dp")
    me = lax.axis_index("strip")
    me_dp = lax.axis_index("dp")
    gscale = 1.0 / math.sqrt(cells * strips * images * groups_dp)
    x = block_in.reshape(images, cells, channels)
    up = upstream.reshape(images, cells, channels)
    up_rows = upstream.reshape(images * cells, channels)
    expand = expand_matrix(channels)
    core = me % 2
    inside = jnp.where(core == 0, me > 0, me < strips - 1)
    info = jnp.stack([core, inside.astype(jnp.int32)]).astype(jnp.int32)
    here = coordinates(me_dp * 16 + me)
    order = row_order(channels, here)
    perm = (order[:, :, None] == jnp.arange(channels, dtype=jnp.int32)).astype(BF16)
    perm, info = lax.optimization_barrier((perm, info))

    x_far = far_row(x)
    x_sib = core_mate(x)
    up_sib = core_mate(up_rows)
    stats, vec = local_stats(
        x, expand, (gn_gain, gn_bias, conv_bias, ln_gain, ln_bias, out_bias), strips
    )
    stats = exchange(stats)
    g = upstream_heads(up, w_out)
    halves = [
        forward(
            c, info, stats, expand, vec, x, x_sib, x_far, g, conv_weight, w_query, w_key, w_value
        )
        for c in range(2)
    ]
    hidden = [h[:3] for h in halves]
    (residual0, normed0, qkv0, chan), (residual1, normed1, qkv1, _) = [h[3:] for h in halves]
    normed0_sib, normed1_sib = core_mate(normed0), core_mate(normed1)
    hid_far_sib = [core_mate(h[2]) for h in hidden]
    qkv0, qkv1 = lax.optimization_barrier((exchange(qkv0), qkv1))
    att0 = attention(qkv0)
    att0, qkv1 = lax.optimization_barrier((att0, exchange(qkv1)))
    got0 = exchange(att0)
    got1 = exchange(attention(qkv1))
    got0_sib = core_mate(got0)
    shared = (up_rows, vec, w_out, w_query, w_key, w_value)
    block_out0, rg0, sums0 = after_attention(got0, residual0, *shared, 0)
    rg0_sib, rg0_far = core_mate(rg0), far_row(rg0)
    proj_part = proj_grads(
        gscale, 0, perm, (got0, got0_sib, normed0, normed0_sib, up_rows, up_sib)
    )
    conv_part = conv_grads(gscale, info, perm, (rg0, rg0_sib, *hidden[0], hid_far_sib[0]))
    got1, proj_part, conv_part, rg0_far = lax.optimization_barrier(
        (got1, proj_part, conv_part, rg0_far)
    )
    got1_sib = core_mate(got1)
    block_out1, rg1, sums1 = after_attention(got1, residual1, *shared, 1)
    rg1_sib, rg1_far = core_mate(rg1), far_row(rg1)
    block_out = jnp.concatenate([block_out0, block_out1], axis=0)
    blocks = proj_grads(
        gscale, 1, perm, (got1, got1_sib, normed1, normed1_sib, up_rows, up_sib), proj_part
    )
    rg1_sib, rg1_far, blocks = lax.optimization_barrier((rg1_sib, rg1_far, blocks))
    blocks = conv_grads(
        gscale, info, perm, (rg1, rg1_sib, *hidden[1], hid_far_sib[1]), conv_part, blocks
    )
    pick = pick_matrix(channels, groups_dp, strips)
    sends = [pair_send(blocks[p][1], ORDERS[p][0], 1) for p in range(3)]
    ag, payload = backward(
        gscale,
        info,
        expand,
        pick,
        (rg0, rg1, rg0_sib, rg1_sib, rg0_far, rg1_far),
        (sums0, sums1),
        x,
        chan,
        vec,
        conv_weight,
    )
    totals = exchange(payload)
    sends, totals = lax.optimization_barrier((sends, totals))
    halves = fold_half([v for p in range(3) for v in (blocks[p][0], sends[p])])
    sends = [pair_send(halves[2 * p + 1], ORDERS[p][0], 3) for p in range(3)]
    grad_input, vectors = input_grad(totals, expand, rg0, rg1, ag, x, chan, vec, groups_dp)
    vectors = exchange(vectors, "dp")
    sends, vectors = lax.optimization_barrier((sends, vectors))
    conv_shard, q_shard, k_shard, v_shard, o_shard = ring_sum(
        fold_first([v for p in range(3) for v in (halves[2 * p], sends[p])])
    )
    per = channels // (strips * groups_dp)
    vectors = jnp.sum(vectors, axis=0)
    shards = lax.dynamic_slice_in_dim(vectors, GROUPS + me_dp * per, per, axis=1)
    shape = block_in.shape
    return (
        block_out.reshape(shape),
        grad_input.reshape(shape),
        conv_shard.transpose(0, 2, 3, 1),
        q_shard.T,
        k_shard.T,
        v_shard.T,
        o_shard.T,
        shards[0],
        shards[1],
        shards[2],
        shards[3],
        shards[4],
        shards[5],
    )


def solution(mesh):
    rows = P("dp", "strip", None, None)
    both = ("dp", "strip")
    in_specs = (rows, rows) + (P(),) * 11
    out_specs = (rows, rows, P(None, None, None, both)) + (P(None, both),) * 4 + (P(both),) * 6
    return jax.shard_map(
        on_device, mesh=mesh, in_specs=in_specs, out_specs=out_specs, check_vma=False
    )
```

```python
import functools
import math

import jax
import jax.numpy as jnp
import numpy as np
from jax import lax
from jax.experimental import pallas as pl
from jax.experimental.pallas import tpu as pltpu
from jax.sharding import PartitionSpec as P

HEADS = 8
GROUPS = 32
EPSILON = 1e-05
F32 = jnp.float32
BF16 = jnp.bfloat16
NT = (((1,), (1,)), ((), ()))
HIGH = lax.Precision.HIGHEST
VMEM_LIMIT = 56 * 1024 * 1024
LOG2E = math.log2(math.e)
QUERY_BLOCK = 1024
KEY_CHUNK = 512
ORDERS = (("y", "x", "z"), ("x", "y", "z"), ("z", "x", "y"))
ENTRIES = 13
LANES = 128
PARTS = ((0, 4), (4, 5), (9, 4))


def params(semantics=None):
    if semantics is None:
        return pltpu.CompilerParams(vmem_limit_bytes=VMEM_LIMIT)
    return pltpu.CompilerParams(
        vmem_limit_bytes=VMEM_LIMIT, dimension_semantics=semantics
    )


def mm(a, b):
    return jnp.dot(a, b, preferred_element_type=F32)


def mm_nt(a, b):
    return lax.dot_general(a, b, NT, preferred_element_type=F32)


def group_sum(rows, expand):
    return lax.dot_general(rows, expand, NT, preferred_element_type=F32, precision=HIGH)


def spread(rows, expand):
    return jnp.dot(rows, expand, preferred_element_type=F32, precision=HIGH)


def expand_matrix(channels):
    per_group = channels // GROUPS
    return jnp.asarray(
        np.arange(channels)[None, :] // per_group == np.arange(LANES)[:, None], F32
    )


def shift_rows(value, down):
    count = value.shape[0]
    row = lax.broadcasted_iota(jnp.int32, value.shape, 0)
    if down == 1:
        return jnp.where(row == 0, 0.0, pltpu.roll(value, 1, 0))
    return jnp.where(row == count - 1, 0.0, pltpu.roll(value, count - 1, 0))


def cost(flops, nbytes, trans=0):
    return pl.CostEstimate(flops=int(flops), bytes_accessed=int(nbytes), transcendentals=int(trans))


def stats_kernel(x_ref, expand_ref, *refs):
    vectors, out_ref, vec_ref = refs[:-2], refs[-2], refs[-1]
    images, cells, channels = x_ref.shape
    count = cells * (channels // GROUPS)
    vec_ref[...] = jnp.zeros_like(vec_ref)
    for i, ref in enumerate(vectors):
        vec_ref[i : i + 1] = ref[...].reshape(1, channels)
    expand = expand_ref[...]
    sums = jnp.concatenate(
        [jnp.sum(x_ref[n].astype(F32), axis=0, keepdims=True) for n in range(images)], axis=0
    )
    mean = group_sum(sums, expand) / count
    mean_c = spread(mean, expand)
    squares = []
    for n in range(images):
        d = x_ref[n].astype(F32) - mean_c[n : n + 1]
        squares.append(jnp.sum(d * d, axis=0, keepdims=True))
    m2 = group_sum(jnp.concatenate(squares, axis=0), expand)
    both = jnp.concatenate([mean, m2], axis=0)
    for s in range(out_ref.shape[0]):
        out_ref[s] = both


def local_stats(x, expand, vectors, strips):
    images, _, channels = x.shape
    return pl.pallas_call(
        stats_kernel,
        out_shape=[
            jax.ShapeDtypeStruct((strips, 2 * images, LANES), F32),
            jax.ShapeDtypeStruct((8, channels), F32),
        ],
        compiler_params=params(),
        cost_estimate=cost(1e7, 7e5),
        name="local_stats",
    )(x, expand, *vectors)


def upstream_kernel(up_ref, w_ref, g_ref):
    images = up_ref.shape[0]
    w = w_ref[...]
    hd = w.shape[0] // HEADS
    for n in range(images):
        g = mm_nt(w, up_ref[n])
        for h in range(HEADS):
            g_ref[n // 2, (n % 2) * HEADS + h] = g[h * hd : (h + 1) * hd].astype(BF16)


def upstream_heads(up, w_out):
    images, cells, channels = up.shape
    return pl.pallas_call(
        upstream_kernel,
        out_shape=jax.ShapeDtypeStruct((images // 2, 2 * HEADS, channels // HEADS, cells), BF16),
        compiler_params=params(),
        cost_estimate=cost(2 * images * cells * channels**2, 2.2e6),
        name="upstream_heads",
    )(up, w_out)


def forward_kernel(
    info_ref,
    stats_ref,
    expand_ref,
    vec_ref,
    x_hbm,
    sib_hbm,
    far_hbm,
    g_hbm,
    conv_hbm,
    wq_hbm,
    wk_hbm,
    wv_hbm,
    hid_own_hbm,
    hid_sib_hbm,
    hid_far_hbm,
    residual_hbm,
    normed_hbm,
    qkv0_hbm,
    qkv1_hbm,
    chan_ref,
    x_ref,
    conv_ref,
    w_ref,
    hidden_ref,
    acc_ref,
    residual_ref,
    normed_ref,
    qkv_ref,
    in_sems,
    out_sems,
):
    _, images, cells, channels = x_ref.shape
    hd = channels // HEADS
    copy = pltpu.make_async_copy
    xs = [copy(h, x_ref.at[i], in_sems.at[i]) for i, h in enumerate((x_hbm, sib_hbm, far_hbm))]
    convs = [copy(conv_hbm.at[:, b], conv_ref.at[b], in_sems.at[3 + b]) for b in range(3)]
    ws = [copy(h, w_ref.at[i], in_sems.at[6 + i]) for i, h in enumerate((wq_hbm, wk_hbm, wv_hbm))]
    qkv_out = (qkv0_hbm, qkv1_hbm)
    gs = [copy(g_hbm.at[c], qkv_ref.at[c, :, 3], in_sems.at[9 + c]) for c in range(2)]
    for task in xs + convs + ws + gs:
        task.start()
    core = info_ref[0]
    strips = stats_ref.shape[0]
    count = cells * (channels // GROUPS)
    got = stats_ref[...]
    means = got[:, :images]
    mean = jnp.sum(means, axis=0) / strips
    off = means - mean[None]
    m2 = jnp.sum(got[:, images:], axis=0) + count * jnp.sum(off * off, axis=0)
    scale = lax.rsqrt(m2 / (count * strips) + EPSILON)
    expand = expand_ref[...]
    mean_c = spread(mean, expand)
    scale_c = spread(scale, expand)
    chan_ref[...] = jnp.concatenate([mean_c, scale_c], axis=0)
    gain = vec_ref[0:1]
    bias = vec_ref[1:2]
    outs = []
    for i, out_hbm in enumerate((hid_own_hbm, hid_sib_hbm, hid_far_hbm)):
        xs[i].wait()
        for n in range(images):
            factor_c = scale_c[n : n + 1] * gain
            u = (x_ref[i, n].astype(F32) - mean_c[n : n + 1]) * factor_c + bias
            h = u * (0.5 + 0.5 * jnp.tanh(0.5 * u))
            if i == 2:
                h = jnp.where(info_ref[1] > 0, h, 0.0)
            hidden_ref[i, n * cells : (n + 1) * cells] = h.astype(BF16)
        outs.append(copy(hidden_ref.at[i], out_hbm, out_sems.at[i]))
        outs[-1].start()

    above = 2 - core
    below = 1 + core
    for b in range(3):
        convs[b].wait()
        total = mm(hidden_ref[0], conv_ref[b, 1])
        total += mm(hidden_ref[above], conv_ref[b, 0])
        total += mm(hidden_ref[below], conv_ref[b, 2])
        if b == 1:
            acc_ref[...] += total
            continue
        for n in range(images):
            sl = slice(n * cells, (n + 1) * cells)
            if b == 0:
                acc_ref[sl] = shift_rows(total[sl], 1)
                continue
            conv = acc_ref[sl] + shift_rows(total[sl], -1)
            residual = (x_ref[0, n].astype(F32) + conv + vec_ref[2:3]).astype(BF16)
            residual_ref[sl] = residual
            tokens = residual.astype(F32)
            dev = tokens - jnp.mean(tokens, axis=1, keepdims=True)
            scale = lax.rsqrt(jnp.mean(dev * dev, axis=1, keepdims=True) + EPSILON)
            normed_ref[sl] = (dev * scale * vec_ref[3:4] + vec_ref[4:5]).astype(BF16)
    outs.append(copy(residual_ref, residual_hbm, out_sems.at[3]))
    outs.append(copy(normed_ref, normed_hbm, out_sems.at[4]))
    outs[-2].start()
    outs[-1].start()
    factor = LOG2E / math.sqrt(hd)
    for task in ws:
        task.wait()
    for c in range(2):
        rows = slice(2 * c * cells, 2 * (c + 1) * cells)
        for t in range(3):
            out = mm(normed_ref[rows], w_ref[t])
            if t == 0:
                out = out * factor
            for n in range(2):
                flipped = out[n * cells : (n + 1) * cells].T.astype(BF16)
                for h in range(HEADS):
                    qkv_ref[c, n * HEADS + h, t] = flipped[h * hd : (h + 1) * hd]
        gs[c].wait()
        outs.append(copy(qkv_ref.at[c], qkv_out[c], out_sems.at[5 + c]))
        outs[-1].start()
    for task in outs:
        task.wait()


def forward(info, stats, expand, vec, x, sib, far, g, conv_weight, wq, wk, wv):
    images, cells, channels = x.shape
    tokens = images * cells
    hd = channels // HEADS
    hbm = pl.BlockSpec(memory_space=pl.ANY)
    vmem = pl.BlockSpec(memory_space=pltpu.VMEM)
    row_type = jax.ShapeDtypeStruct((tokens, channels), BF16)
    qkv_type = jax.ShapeDtypeStruct((2 * HEADS, 4, hd, cells), BF16)
    return pl.pallas_call(
        forward_kernel,
        in_specs=[pl.BlockSpec(memory_space=pltpu.SMEM)] + [vmem] * 3 + [hbm] * 8,
        out_specs=[hbm] * 7 + [vmem],
        out_shape=[row_type] * 5
        + [qkv_type] * 2
        + [jax.ShapeDtypeStruct((2 * images, channels), F32)],
        scratch_shapes=[
            pltpu.VMEM((3, images, cells, channels), BF16),
            pltpu.VMEM((3, 3, channels, channels), BF16),
            pltpu.VMEM((3, channels, channels), BF16),
            pltpu.VMEM((3, tokens, channels), BF16),
            pltpu.VMEM((tokens, channels), F32),
            pltpu.VMEM((tokens, channels), BF16),
            pltpu.VMEM((tokens, channels), BF16),
            pltpu.VMEM((2, 2 * HEADS, 4, hd, cells), BF16),
            pltpu.SemaphoreType.DMA((11,)),
            pltpu.SemaphoreType.DMA((7,)),
        ],
        compiler_params=params(),
        cost_estimate=cost(24 * tokens * channels**2, 20e6, 1e6),
        name="forward_conv",
    )(info, stats, expand, vec, x, sib, far, g, conv_weight, wq, wk, wv)


def together(*tasks):
    results = [None] * len(tasks)
    active = list(enumerate(tasks))
    while active:
        still = []
        for i, task in active:
            try:
                results[i] = next(task)
                still.append((i, task))
            except StopIteration:
                pass
        active = still
    return results


def attention_kernel(
    qkv_ref, out_ref, kt_ref, vt_ref, kn_ref, vn_ref, s_ref, e_ref, dk_ref, dv_ref
):
    step = pl.program_id(0)
    sources, _, hd, cells = qkv_ref.shape
    length = sources * cells
    wide = kn_ref.shape[1]
    block = s_ref.shape[2]
    per = block // cells
    spans = [slice(c, c + KEY_CHUNK) for c in range(0, length, KEY_CHUNK)]
    extra = vt_ref.shape[0] - hd

    @pl.when(step == 0)
    def _():
        ones_row = (lax.broadcasted_iota(jnp.int32, (extra, cells), 0) == 0).astype(F32)
        pad = jnp.zeros((wide - hd, cells), F32)
        row = lax.broadcasted_iota(jnp.int32, (wide - hd, cells), 0)
        ones_two = (row < 2).astype(F32)
        for s in range(sources):
            sl = slice(s * cells, (s + 1) * cells)
            k = qkv_ref[s, 1]
            v = qkv_ref[s, 2]
            kt_ref[:, sl] = k
            vt_ref[:hd, sl] = v
            vt_ref[hd:, sl] = ones_row.astype(BF16)
            kn_ref[sl] = jnp.concatenate([k.astype(F32), pad], axis=0).T.astype(BF16)
            vn_ref[sl] = jnp.concatenate([v.astype(F32), ones_two], axis=0).T.astype(BF16)
        dk_ref[...] = jnp.zeros_like(dk_ref)
        dv_ref[...] = jnp.zeros_like(dv_ref)

    bases = [(2 * step + b) * per for b in range(2)]

    def rows_of(b, t):
        return jnp.concatenate([qkv_ref[bases[b] + u, t] for u in range(per)], axis=1).astype(F32)

    def put(b, t, value):
        for u in range(per):
            out_ref[bases[b] + u, t] = value[:, u * cells : (u + 1) * cells].astype(BF16)

    def scores(b):
        q = jnp.concatenate([rows_of(b, 0), jnp.zeros((wide - hd, block), F32)], axis=0)
        q_t = q.astype(BF16)
        top = None
        for sl in spans:
            value = mm(kn_ref[sl], q_t)
            s_ref[b, sl] = value
            here = jnp.max(value, axis=0, keepdims=True)
            top = here if top is None else jnp.maximum(top, here)
            yield None
        yield top, q.T.astype(BF16)

    def attend(b, top):
        acc = jnp.zeros((hd + extra, block), F32)
        for sl in spans:
            e = jnp.exp2(s_ref[b, sl] - top).astype(BF16)
            e_ref[b, sl] = e
            acc += mm(vt_ref[:, sl], e)
            yield None
        yield acc

    def finish(b, acc):
        inverse = 1.0 / acc[hd : hd + 1]
        out = acc[:hd] * inverse
        put(b, 0, out)
        g = (rows_of(b, 3) * inverse).astype(BF16).astype(F32)
        delta = -jnp.sum(g * out, axis=0, keepdims=True)
        high = delta.astype(BF16).astype(F32)
        low = delta - high
        row = lax.broadcasted_iota(jnp.int32, (wide - hd, block), 0)
        tail = jnp.where(row == 0, high, jnp.where(row == 1, low, 0.0))
        g = jnp.concatenate([g, tail], axis=0)
        return g.astype(BF16), g.T.astype(BF16)

    def back(b, g_t, g_n, q_n):
        dq = jnp.zeros((hd, block), F32)
        for sl in spans:
            e = e_ref[b, sl]
            ds = (e.astype(F32) * mm(vn_ref[sl], g_t)).astype(BF16)
            dq += mm(kt_ref[:, sl], ds)
            dk_ref[sl] += mm(ds, q_n)
            dv_ref[sl] += mm(e, g_n)
            yield None
        put(b, 1, dq * (1.0 / math.sqrt(hd)))
        yield None

    ((top0, q0),) = together(scores(0))
    acc0, (top1, q1) = together(attend(0, top0), scores(1))
    _, acc1 = together(back(0, *finish(0, acc0), q0), attend(1, top1))
    together(back(1, *finish(1, acc1), q1))

    @pl.when(step == pl.num_programs(0) - 1)
    def _():
        for s in range(sources):
            sl = slice(s * cells, (s + 1) * cells)
            out_ref[s, 2] = (dk_ref[sl].T[:hd] * (1.0 / LOG2E)).astype(BF16)
            out_ref[s, 3] = dv_ref[sl].T[:hd].astype(BF16)


def attention(qkv):
    sources, _, hd, cells = qkv.shape
    length = sources * cells
    block = QUERY_BLOCK
    wide = 128
    full = lambda shape: pl.BlockSpec(shape, lambda i: (0,) * len(shape))
    return pl.pallas_call(
        attention_kernel,
        grid=(length // block // 2,),
        in_specs=[full(qkv.shape)],
        out_specs=full((sources, 4, hd, cells)),
        out_shape=jax.ShapeDtypeStruct((sources, 4, hd, cells), BF16),
        scratch_shapes=[
            pltpu.VMEM((hd, length), BF16),
            pltpu.VMEM((hd + 16, length), BF16),
            pltpu.VMEM((length, wide), BF16),
            pltpu.VMEM((length, wide), BF16),
            pltpu.VMEM((2, length, block), F32),
            pltpu.VMEM((2, length, block), BF16),
            pltpu.VMEM((length, wide), F32),
            pltpu.VMEM((length, wide), F32),
        ],
        compiler_params=params(),
        cost_estimate=cost(12 * length * length * 256, 5e6, length * length),
        name="attention",
    )(qkv)


def gather_heads(got_ref, t):
    return jnp.concatenate(
        [
            jnp.concatenate([got_ref[n * HEADS + h, t] for h in range(HEADS)], axis=0)
            for n in range(2)
        ],
        axis=1,
    )


def tokens_kernel(
    got_ref,
    residual_ref,
    up_ref,
    vec_ref,
    wo_ref,
    wq_ref,
    wk_ref,
    wv_ref,
    block_out_ref,
    rg_ref,
    sums_ref,
):
    residual = residual_ref[...].astype(F32)
    up = up_ref[...].astype(F32)
    mixed = mm(gather_heads(got_ref, 0).T, wo_ref[...])
    block_out_ref[...] = (residual + mixed + vec_ref[5:6]).astype(BF16)
    grad = mm_nt(gather_heads(got_ref, 1).T, wq_ref[...])
    grad += mm_nt(gather_heads(got_ref, 2).T, wk_ref[...])
    grad += mm_nt(gather_heads(got_ref, 3).T, wv_ref[...])
    dev = residual - jnp.mean(residual, axis=1, keepdims=True)
    scale = lax.rsqrt(jnp.mean(dev * dev, axis=1, keepdims=True) + EPSILON)
    standard = dev * scale
    scaled = grad * vec_ref[3:4]
    part = scale * (
        scaled
        - jnp.mean(scaled, axis=1, keepdims=True)
        - standard * jnp.mean(scaled * standard, axis=1, keepdims=True)
    )
    rg = (up + part).astype(BF16)
    rg_ref[...] = rg
    sums_ref[0:1] = jnp.sum(rg.astype(F32), axis=0, keepdims=True)
    sums_ref[1:2] = jnp.sum(grad * standard, axis=0, keepdims=True)
    sums_ref[2:3] = jnp.sum(grad, axis=0, keepdims=True)
    sums_ref[3:4] = jnp.sum(up, axis=0, keepdims=True)


def after_attention(got, residual, up, vec, wo, wq, wk, wv, part):
    channels = residual.shape[1]
    cells = got.shape[3]
    tokens = 2 * cells
    full = lambda shape: pl.BlockSpec(shape, lambda i: (0,) * len(shape))
    rows = pl.BlockSpec((tokens, channels), lambda i: (part, 0))
    square = (channels, channels)
    return pl.pallas_call(
        tokens_kernel,
        grid=(1,),
        in_specs=[full(got.shape), rows, rows, full(vec.shape)] + [full(square)] * 4,
        out_specs=[
            full((tokens, channels)),
            full((tokens, channels)),
            full((4, channels)),
        ],
        out_shape=[
            jax.ShapeDtypeStruct((tokens, channels), BF16),
            jax.ShapeDtypeStruct((tokens, channels), BF16),
            jax.ShapeDtypeStruct((4, channels), F32),
        ],
        compiler_params=params(),
        cost_estimate=cost(8 * tokens * channels**2, 7e6),
        name="after_attention",
    )(got, residual, up, vec, wo, wq, wk, wv)


def wait_all(tasks):
    for task in tasks:
        task.wait()


def emitter(gscale, outs_hbm, part_ref, out_ref, out_sems, outs):
    def emit(entry, p, place, value):
        value = value * gscale
        if part_ref is not None:
            value = value + part_ref[entry].astype(F32)
        out_ref[entry] = value.astype(BF16)
        if part_ref is None:
            targets = [(out_ref.at[entry], outs_hbm[0].at[entry])]
        else:
            rows = value.shape[0] // 2
            targets = [
                (out_ref.at[entry, pl.ds(k * rows, rows)], outs_hbm[2 * p + k].at[place])
                for k in range(2)
            ]
        for k, (source, target) in enumerate(targets):
            outs.append(pltpu.make_async_copy(source, target, out_sems.at[entry, k]))
            outs[-1].start()

    return emit


def proj_kernel(gscale, part, last, *refs):
    perm_hbm, got_hbm, got_sib_hbm, normed_hbm, normed_sib_hbm, up_hbm, up_sib_hbm = refs[:7]
    inputs = 8 if last else 7
    part_hbm = refs[7] if last else None
    outs_hbm, scratch = refs[inputs:-10], refs[-10:]
    perm_ref, got_ref, up_ref, left_ref, normed_ref, att_ref, part_ref, out_ref = scratch[:8]
    in_sems, out_sems = scratch[8:]
    copy = pltpu.make_async_copy
    half = normed_ref.shape[0] // 2
    rows = pl.ds(part * half, half)
    places = [pl.ds(u * half, half) for u in range(2)]
    got_in = [
        [
            copy(h.at[:, t], got_ref.at[u, t], in_sems.at[2 * t + u])
            for u, h in enumerate((got_hbm, got_sib_hbm))
        ]
        for t in range(4)
    ]
    perm_in = [copy(perm_hbm, perm_ref, in_sems.at[8])]
    normed_in = [
        copy(h.at[rows], normed_ref.at[places[u]], in_sems.at[9 + u])
        for u, h in enumerate((normed_hbm, normed_sib_hbm))
    ]
    up_in = [
        copy(h.at[rows], up_ref.at[places[u]], in_sems.at[11 + u])
        for u, h in enumerate((up_hbm, up_sib_hbm))
    ]
    part_in = [copy(part_hbm, part_ref, in_sems.at[13])] if last else []
    for tasks in (perm_in, got_in[1], got_in[2], got_in[3], normed_in, part_in, got_in[0], up_in):
        for task in tasks:
            task.start()

    def heads(u, t):
        return jnp.concatenate(
            [
                jnp.concatenate([got_ref[u, t, n * HEADS + h] for h in range(HEADS)], axis=0)
                for n in range(2)
            ],
            axis=1,
        )

    outs = []
    emit = emitter(gscale, outs_hbm, part_ref if last else None, out_ref, out_sems, outs)
    count = perm_ref.shape[1]
    wait_all(perm_in)
    for p in range(3):
        wait_all(got_in[1 + p])
        for u in range(2):
            left_ref[p * count : (p + 1) * count, u * half : (u + 1) * half] = mm(
                perm_ref[p], heads(u, 1 + p)
            ).astype(BF16)
    wait_all(normed_in + part_in)
    value = mm(left_ref[...], normed_ref[...])
    for p in range(3):
        emit(p, p, 3, value[p * count : (p + 1) * count])
    wait_all(got_in[0] + up_in)
    for u in range(2):
        att_ref[u * half : (u + 1) * half] = heads(u, 0).T
    emit(3, 1, 4, mm(mm_nt(perm_ref[1], up_ref[...]).astype(BF16), att_ref[...]))
    wait_all(outs)


def conv_kernel(gscale, part, last, *refs):
    info_ref, perm_hbm, rg_hbm, rg_sib_hbm, own_hbm, sib_hbm, far_hbm, far_sib_hbm = refs[:8]
    inputs = 15 if last else 8
    part_hbm = refs[8] if last else None
    outs_hbm, scratch = refs[inputs:-8], refs[-8:]
    perm_ref, rg_ref, left_ref, right_ref, part_ref, out_ref, in_sems, out_sems = scratch
    copy = pltpu.make_async_copy
    core = info_ref[0]
    half = rg_ref.shape[1]
    rows = pl.ds(part * half, half)
    mine, other = pl.ds(0, half), pl.ds(half, half)
    first_in = [
        copy(perm_hbm, perm_ref, in_sems.at[0]),
        copy(rg_hbm, rg_ref.at[0], in_sems.at[1]),
        copy(rg_sib_hbm, rg_ref.at[1], in_sems.at[2]),
    ]
    hidden_in = [
        copy(own_hbm.at[rows], right_ref.at[1, mine], in_sems.at[3]),
        copy(sib_hbm.at[rows], right_ref.at[2 - 2 * core, mine], in_sems.at[4]),
        copy(far_hbm.at[rows], right_ref.at[2 * core, mine], in_sems.at[5]),
        copy(own_hbm.at[rows], right_ref.at[2 * core, other], in_sems.at[6]),
        copy(sib_hbm.at[rows], right_ref.at[1, other], in_sems.at[7]),
        copy(far_sib_hbm.at[rows], right_ref.at[2 - 2 * core, other], in_sems.at[8]),
    ]
    part_in = [copy(part_hbm, part_ref, in_sems.at[9])] if last else []
    for task in first_in + hidden_in + part_in:
        task.start()
    outs = []
    emit = emitter(gscale, outs_hbm, part_ref if last else None, out_ref, out_sems, outs)
    count = perm_ref.shape[1]
    cells = half // 2
    wait_all(first_in)
    for p in range(3):
        for u in range(2):
            pieces = []
            for n in range(2):
                piece = rg_ref[u, n * cells : (n + 1) * cells]
                if p != 1:
                    piece = shift_rows(piece.astype(F32), p - 1).astype(BF16)
                pieces.append(piece)
            left_ref[p * count : (p + 1) * count, u * half : (u + 1) * half] = mm_nt(
                perm_ref[p], jnp.concatenate(pieces, axis=0)
            ).astype(BF16)
    wait_all(hidden_in + part_in)
    for a in range(3):
        value = mm(left_ref[...], right_ref[a])
        for p in range(3):
            emit(3 * p + a, p, a, value[p * count : (p + 1) * count])
    wait_all(outs)


def part_types(channels, rows):
    types = []
    for _, count in PARTS:
        types += [jax.ShapeDtypeStruct((count, rows // 2, channels), BF16)] * 2
    return types


def proj_grads(gscale, part, perm, ins, partial=None):
    channels = perm.shape[2]
    rows = perm.shape[1]
    got = ins[0]
    tokens = 4 * got.shape[3]
    last = partial is not None
    whole = jax.ShapeDtypeStruct((4, rows, channels), BF16)
    hbm = pl.BlockSpec(memory_space=pl.ANY)
    args = (perm, *ins) + ((partial,) if last else ())
    out_shape = part_types(channels, rows) if last else [whole]
    outs = pl.pallas_call(
        functools.partial(proj_kernel, gscale, part, last),
        in_specs=[hbm] * len(args),
        out_specs=[hbm] * len(out_shape),
        out_shape=out_shape,
        scratch_shapes=[
            pltpu.VMEM(perm.shape, BF16),
            pltpu.VMEM((2, 4) + got.shape[:1] + got.shape[2:], BF16),
            pltpu.VMEM((tokens, channels), BF16),
            pltpu.VMEM((3 * rows, tokens), BF16),
            pltpu.VMEM((tokens, channels), BF16),
            pltpu.VMEM((tokens, channels), BF16),
            pltpu.VMEM(whole.shape, BF16),
            pltpu.VMEM(whole.shape, BF16),
            pltpu.SemaphoreType.DMA((14,)),
            pltpu.SemaphoreType.DMA((4, 2)),
        ],
        compiler_params=params(),
        cost_estimate=cost(16 * rows * tokens * channels, 9e6),
        name="proj_grads",
    )(*args)
    return list(outs) if last else outs[0]


def conv_grads(gscale, part, info, perm, ins, partial=None, parts=()):
    channels = perm.shape[2]
    rows = perm.shape[1]
    tokens = 2 * ins[0].shape[0]
    last = partial is not None
    whole = jax.ShapeDtypeStruct((9, rows, channels), BF16)
    hbm = pl.BlockSpec(memory_space=pl.ANY)
    args = (info, perm, *ins) + ((partial, *parts) if last else ())
    out_shape = part_types(channels, rows) if last else [whole]
    outs = pl.pallas_call(
        functools.partial(conv_kernel, gscale, part, last),
        in_specs=[pl.BlockSpec(memory_space=pltpu.SMEM)] + [hbm] * (len(args) - 1),
        out_specs=[hbm] * len(out_shape),
        out_shape=out_shape,
        input_output_aliases={9 + i: i for i in range(6)} if last else {},
        scratch_shapes=[
            pltpu.VMEM(perm.shape, BF16),
            pltpu.VMEM((2, tokens // 2, channels), BF16),
            pltpu.VMEM((3 * rows, tokens), BF16),
            pltpu.VMEM((3, tokens, channels), BF16),
            pltpu.VMEM(whole.shape, BF16),
            pltpu.VMEM(whole.shape, BF16),
            pltpu.SemaphoreType.DMA((10,)),
            pltpu.SemaphoreType.DMA((9, 2)),
        ],
        compiler_params=params(),
        cost_estimate=cost(24 * rows * tokens * channels, 12e6),
        name="conv_grads",
    )(*args)
    return [list(outs[2 * p : 2 * p + 2]) for p in range(3)] if last else outs[0]


def fold_half_kernel(*refs):
    for p in range(3):
        mine, got, own_ref, send_ref = refs[2 * p], refs[2 * p + 1], refs[6 + 2 * p], refs[7 + 2 * p]
        rows = own_ref.shape[1]
        total = mine[...].astype(F32) + got[...].astype(F32)
        own_ref[...] = total[:, :rows].astype(BF16)
        send_ref[...] = total[:, rows:].astype(BF16)


def fold_half(values):
    shapes = []
    for value in values:
        count, rows, channels = value.shape
        shapes.append(jax.ShapeDtypeStruct((count, rows // 2, channels), BF16))
    return pl.pallas_call(
        fold_half_kernel,
        out_shape=shapes,
        compiler_params=params(),
        cost_estimate=cost(4e6, 8e6),
        name="fold_half",
    )(*values)


def fold_first_kernel(*refs):
    ins, (own_ref, *sends) = refs[:6], refs[6:]
    for p, (first, count) in enumerate(PARTS):
        rows = ins[0].shape[1] // 4
        for e in range(count):
            total = ins[2 * p][e].astype(F32) + ins[2 * p + 1][e].astype(F32)
            own_ref[first + e] = total[:rows]
            place, group = ((e, 0), (e, 1), (PARTS[0][1] + e, 0))[p]
            for k in range(1, 4):
                sends[3 * group + k - 1][place] = total[k * rows : (k + 1) * rows].astype(BF16)


def fold_second_kernel(*refs):
    own_in, got, (own_ref, *sends) = refs[0], refs[1:7], refs[7:]
    rows = own_in.shape[1] // 4
    for p, (first, count) in enumerate(PARTS):
        for e in range(count):
            place, group = ((e, 0), (e, 1), (PARTS[0][1] + e, 0))[p]
            total = own_in[first + e]
            for k in range(3):
                total = total + got[3 * group + k][place].astype(F32)
            own_ref[first + e] = total[:rows]
            place, group = ((e, 0), (PARTS[0][1] + e, 0), (e, 1))[p]
            for k in range(1, 4):
                sends[3 * group + k - 1][place] = total[k * rows : (k + 1) * rows].astype(BF16)


def fold_last_kernel(*refs):
    own_in, got, (conv_ref, q_ref, k_ref, v_ref, o_ref) = refs[0], refs[1:7], refs[7:]
    rows = own_in.shape[1]
    for p, (first, count) in enumerate(PARTS):
        for e in range(count):
            place, group = ((e, 0), (PARTS[0][1] + e, 0), (e, 1))[p]
            total = own_in[first + e]
            for k in range(3):
                total = total + got[3 * group + k][place].astype(F32)
            if e < 3:
                for r in range(rows):
                    conv_ref[e, r, p : p + 1] = total[r : r + 1]
            elif e == 3:
                (q_ref, k_ref, v_ref)[p][...] = total
            else:
                o_ref[...] = total


def fold_first(values):
    _, rows, channels = values[0].shape
    cut = rows // 4
    entries = ENTRIES
    wide = PARTS[0][1] + PARTS[2][1]
    sizes = [wide] * 3 + [PARTS[1][1]] * 3
    return pl.pallas_call(
        fold_first_kernel,
        out_shape=[jax.ShapeDtypeStruct((entries, cut, channels), F32)]
        + [jax.ShapeDtypeStruct((s, cut, channels), BF16) for s in sizes],
        compiler_params=params(),
        cost_estimate=cost(4e6, 7e6),
        name="fold_first",
    )(*values)


def fold_second(values):
    entries, rows, channels = values[0].shape
    cut = rows // 4
    wide = PARTS[0][1] + PARTS[1][1]
    sizes = [wide] * 3 + [PARTS[2][1]] * 3
    return pl.pallas_call(
        fold_second_kernel,
        out_shape=[jax.ShapeDtypeStruct((entries, cut, channels), F32)]
        + [jax.ShapeDtypeStruct((s, cut, channels), BF16) for s in sizes],
        compiler_params=params(),
        cost_estimate=cost(1e6, 2e6),
        name="fold_second",
    )(*values)


def fold_last(values):
    _, rows, channels = values[0].shape
    return pl.pallas_call(
        fold_last_kernel,
        out_shape=[jax.ShapeDtypeStruct((3, rows, 3, channels), F32)]
        + [jax.ShapeDtypeStruct((rows, channels), F32)] * 4,
        compiler_params=params(),
        cost_estimate=cost(3e5, 7e5),
        name="fold_last",
    )(*values)


def coordinates(index):
    dp, strip = index // 16, index % 16
    return {
        "x": dp // 2,
        "z": (strip // 8) * 2 + dp % 2,
        "y": (strip // 2) % 4,
        "core": strip % 2,
    }


def device_index(place):
    dp = place["x"] * 2 + place["z"] % 2
    strip = (place["z"] // 2) * 8 + place["y"] * 2 + place["core"]
    return dp * 16 + strip


def ring_pairs(axis, offset):
    pairs = []
    for source in range(128):
        place = coordinates(source)
        place[axis] = (place[axis] + offset) % 4
        pairs.append((source, device_index(place)))
    return pairs


def row_order(channels, here):
    per = channels // 128
    row = jnp.arange(channels // 2, dtype=jnp.int32)
    r = row % per
    k3 = (row // per) % 4
    k2 = (row // (per * 4)) % 4
    k1 = row // (per * 16)
    flip = (k1 // 2) ^ (3 * (k1 % 2))
    orders = []
    for order in ORDERS:
        place = {"core": here["core"], order[0]: here[order[0]] ^ flip}
        for axis, k in zip(order[1:], (k2, k3)):
            place[axis] = (here[axis] + k) % 4
        orders.append(device_index(place) * per + r)
    return jnp.stack(orders)


def ring_send(value, axis, offset):
    return lax.ppermute(value, ("dp", "strip"), ring_pairs(axis, offset))


def pair_send(value, axis, flip):
    pairs = []
    for source in range(128):
        place = coordinates(source)
        place[axis] = place[axis] ^ flip
        pairs.append((source, device_index(place)))
    return lax.ppermute(value, ("dp", "strip"), pairs)


def ring_sum(joined):
    own, *sends = joined
    values = [own]
    for i, send in enumerate(sends):
        values.append(ring_send(send, ("x", "y")[i // 3], i % 3 + 1))
    own, *sends = fold_second(values)
    values = [own]
    for i, send in enumerate(sends):
        values.append(ring_send(send, ("z", "y")[i // 3], i % 3 + 1))
    return fold_last(values)


def backward_kernel(
    gscale,
    info_ref,
    expand_ref,
    pick_ref,
    rg0_ref,
    rg1_ref,
    sib0_ref,
    sib1_ref,
    far0_ref,
    far1_ref,
    sums0_ref,
    sums1_ref,
    x_ref,
    chan_ref,
    vec_ref,
    conv_ref,
    ag_ref,
    payload_ref,
    rows_ref,
    acc_ref,
):
    step = pl.program_id(0)
    images, cells, channels = x_ref.shape
    half = rg0_ref.shape[0]

    @pl.when(step == 0)
    def _():
        core = info_ref[0]
        rows_ref[1, :half] = rg0_ref[...]
        rows_ref[1, half:] = rg1_ref[...]
        rows_ref[2 * core, :half] = sib0_ref[...]
        rows_ref[2 * core, half:] = sib1_ref[...]
        rows_ref[2 - 2 * core, :half] = far0_ref[...]
        rows_ref[2 - 2 * core, half:] = far1_ref[...]

    total = mm_nt(rows_ref[0], conv_ref[0, 0])
    total += mm_nt(rows_ref[1], conv_ref[1, 0])
    total += mm_nt(rows_ref[2], conv_ref[2, 0])

    @pl.when(step == 0)
    def _():
        for n in range(images):
            sl = slice(n * cells, (n + 1) * cells)
            acc_ref[sl] = shift_rows(total[sl], -1)

    @pl.when(step == 1)
    def _():
        acc_ref[...] += total

    @pl.when(step == 2)
    def _():
        gain = vec_ref[0:1]
        plain, weighted = [], []
        for n in range(images):
            sl = slice(n * cells, (n + 1) * cells)
            grad = acc_ref[sl] + shift_rows(total[sl], 1)
            standard = (x_ref[n].astype(F32) - chan_ref[n : n + 1]) * chan_ref[
                images + n : images + n + 1
            ]
            u = standard * gain + vec_ref[1:2]
            sigma = 0.5 + 0.5 * jnp.tanh(0.5 * u)
            ag = grad * (sigma * (1.0 + u * (1.0 - sigma)))
            ag_ref[sl] = ag
            plain.append(jnp.sum(ag, axis=0, keepdims=True))
            weighted.append(jnp.sum(ag * standard, axis=0, keepdims=True))
        all_totals = group_sum(jnp.concatenate(plain + weighted, axis=0) * gain, expand_ref[...])
        sums = sums0_ref[...] + sums1_ref[...]
        vectors = gscale * jnp.concatenate(
            [sum(weighted), sum(plain), sums, jnp.zeros((2, channels), F32)], axis=0
        )
        pieces = []
        for _ in range(3):
            piece = vectors.astype(BF16)
            pieces.append(piece.astype(F32))
            vectors = vectors - pieces[-1]
        picked = mm(jnp.concatenate(pieces, axis=0).astype(BF16), pick_ref[...])
        count = vectors.shape[0]
        picked = picked[:count] + picked[count : 2 * count] + picked[2 * count :]
        for s in range(payload_ref.shape[0]):
            payload_ref[s] = all_totals + picked[:, s * LANES : (s + 1) * LANES]


def backward(gscale, info, expand, pick, rows, sums, x, chan, vec, conv_weight):
    images, cells, channels = x.shape
    tokens = images * cells
    full = lambda shape: pl.BlockSpec(shape, lambda b: (0,) * len(shape))
    payload = (pick.shape[1] // LANES, 2 * images, LANES)
    ins = (expand, pick, *rows, *sums, x, chan, vec)
    return pl.pallas_call(
        functools.partial(backward_kernel, gscale),
        grid=(3,),
        in_specs=[pl.BlockSpec(memory_space=pltpu.SMEM)]
        + [full(v.shape) for v in ins]
        + [pl.BlockSpec((3, 1, channels, channels), lambda b: (0, b, 0, 0))],
        out_specs=[full((tokens, channels)), full(payload)],
        out_shape=[
            jax.ShapeDtypeStruct((tokens, channels), F32),
            jax.ShapeDtypeStruct(payload, F32),
        ],
        scratch_shapes=[
            pltpu.VMEM((3, tokens, channels), BF16),
            pltpu.VMEM((tokens, channels), F32),
        ],
        compiler_params=params(),
        cost_estimate=cost(18 * tokens * channels**2, 12e6, 4e5),
        name="backward_conv",
    )(info, *ins, conv_weight)


def input_kernel(
    totals_ref, expand_ref, rg0_ref, rg1_ref, ag_ref, x_ref, chan_ref, vec_ref,
    out_ref, spread_ref
):
    images, cells, channels = x_ref.shape
    strips = totals_ref.shape[0]
    count = strips * cells * (channels // GROUPS)
    summed = jnp.sum(totals_ref[...], axis=0)
    for d in range(spread_ref.shape[0]):
        spread_ref[d] = summed
    spread_c = spread(summed / count, expand_ref[...])
    for n in range(images):
        u, m = n // 2, n % 2
        sl = slice(m * cells, (m + 1) * cells)
        scale = chan_ref[images + n : images + n + 1]
        standard = (x_ref[n].astype(F32) - chan_ref[n : n + 1]) * scale
        part = scale * (
            ag_ref[n * cells : (n + 1) * cells] * vec_ref[0:1]
            - spread_c[n : n + 1]
            - standard * spread_c[images + n : images + n + 1]
        )
        rg = (rg0_ref, rg1_ref)[u][sl].astype(F32)
        out_ref[n] = (rg + part).astype(BF16)


def input_grad(totals, expand, rg0, rg1, ag, x, chan, vec, copies):
    return pl.pallas_call(
        input_kernel,
        out_shape=[
            jax.ShapeDtypeStruct(x.shape, BF16),
            jax.ShapeDtypeStruct((copies,) + totals.shape[1:], F32),
        ],
        compiler_params=params(),
        cost_estimate=cost(3e6, 4e6),
        name="input_grad",
    )(totals, expand, rg0, rg1, ag, x, chan, vec)


def exchange(value, axis="strip"):
    return lax.all_to_all(value, axis, split_axis=0, concat_axis=0, tiled=True)


def core_mate(value):
    return lax.ppermute(value, "strip", [(i, i ^ 1) for i in range(16)])


def far_row(value):
    pairs = [(i, i + 1) for i in range(1, 15, 2)]
    return lax.ppermute(value, "strip", pairs + [(j, i) for i, j in pairs])


def pick_matrix(channels, groups_dp, strips):
    per = channels // (groups_dp * strips)
    pick = np.zeros((channels, strips * LANES), np.float32)
    for o in range(channels):
        device, r = divmod(o, per)
        dp, strip = divmod(device, strips)
        pick[o, strip * LANES + GROUPS + dp * per + r] = 1.0
    return jnp.asarray(pick, BF16)


def on_device(
    block_in,
    upstream,
    gn_gain,
    gn_bias,
    conv_weight,
    conv_bias,
    ln_gain,
    ln_bias,
    w_query,
    w_key,
    w_value,
    w_out,
    out_bias,
):
    images, strip_rows, cells, channels = block_in.shape
    strips = lax.axis_size("strip")
    groups_dp = lax.axis_size("dp")
    me = lax.axis_index("strip")
    me_dp = lax.axis_index("dp")
    gscale = 1.0 / math.sqrt(cells * strips * images * groups_dp)
    x = block_in.reshape(images, cells, channels)
    up = upstream.reshape(images, cells, channels)
    up_rows = upstream.reshape(images * cells, channels)
    expand = expand_matrix(channels)
    core = me % 2
    inside = jnp.where(core == 0, me > 0, me < strips - 1)
    info = jnp.stack([core, inside.astype(jnp.int32)]).astype(jnp.int32)
    here = coordinates(me_dp * 16 + me)
    order = row_order(channels, here)
    perm = (order[:, :, None] == jnp.arange(channels, dtype=jnp.int32)).astype(BF16)
    perm, info = lax.optimization_barrier((perm, info))

    x_far = far_row(x)
    x_sib = core_mate(x)
    up_sib = core_mate(up_rows)
    stats, vec = local_stats(
        x, expand, (gn_gain, gn_bias, conv_bias, ln_gain, ln_bias, out_bias), strips
    )
    stats = exchange(stats)
    g = upstream_heads(up, w_out)
    hid_own, hid_sib, hid_far, residual, normed, qkv0, qkv1, chan = forward(
        info, stats, expand, vec, x, x_sib, x_far, g, conv_weight, w_query, w_key, w_value
    )
    hid_far_sib = core_mate(hid_far)
    normed_sib = core_mate(normed)
    att0, qkv1 = lax.optimization_barrier((attention(exchange(qkv0)), exchange(qkv1)))
    got0, att1 = lax.optimization_barrier((exchange(att0), attention(qkv1)))
    got1 = exchange(att1)
    got0_sib = core_mate(got0)
    shared = (residual, up_rows, vec, w_out, w_query, w_key, w_value)
    block_out0, rg0, sums0 = after_attention(got0, *shared, 0)
    rg0_sib, rg0_far = core_mate(rg0), far_row(rg0)
    rows_in = (normed, normed_sib, up_rows, up_sib)
    hidden_in = (hid_own, hid_sib, hid_far, hid_far_sib)
    proj_part = proj_grads(gscale, 0, perm, (got0, got0_sib, *rows_in))
    conv_part = conv_grads(gscale, 0, info, perm, (rg0, rg0_sib, *hidden_in))
    got1, proj_part, conv_part, rg0_far = lax.optimization_barrier(
        (got1, proj_part, conv_part, rg0_far)
    )
    got1_sib = core_mate(got1)
    block_out1, rg1, sums1 = after_attention(got1, *shared, 1)
    rg1_sib, rg1_far = core_mate(rg1), far_row(rg1)
    block_out = jnp.concatenate([block_out0, block_out1], axis=0)
    blocks = proj_grads(gscale, 1, perm, (got1, got1_sib, *rows_in), proj_part)
    rg1_sib, rg1_far, blocks = lax.optimization_barrier((rg1_sib, rg1_far, blocks))
    blocks = conv_grads(gscale, 1, info, perm, (rg1, rg1_sib, *hidden_in), conv_part, blocks)
    pick = pick_matrix(channels, groups_dp, strips)
    sends = [pair_send(blocks[p][1], ORDERS[p][0], 1) for p in range(3)]
    ag, payload = backward(
        gscale,
        info,
        expand,
        pick,
        (rg0, rg1, rg0_sib, rg1_sib, rg0_far, rg1_far),
        (sums0, sums1),
        x,
        chan,
        vec,
        conv_weight,
    )
    sends, payload = lax.optimization_barrier((sends, payload))
    halves = fold_half([v for p in range(3) for v in (blocks[p][0], sends[p])])
    halves, totals = lax.optimization_barrier((halves, exchange(payload)))
    sends = [pair_send(halves[2 * p + 1], ORDERS[p][0], 3) for p in range(3)]
    grad_input, vectors = input_grad(totals, expand, rg0, rg1, ag, x, chan, vec, groups_dp)
    sends, vectors = lax.optimization_barrier((sends, vectors))
    joined = fold_first([v for p in range(3) for v in (halves[2 * p], sends[p])])
    joined, vectors = lax.optimization_barrier((joined, exchange(vectors, "dp")))
    conv_shard, q_shard, k_shard, v_shard, o_shard = ring_sum(joined)
    per = channels // (strips * groups_dp)
    vectors = jnp.sum(vectors, axis=0)
    shards = lax.dynamic_slice_in_dim(vectors, GROUPS + me_dp * per, per, axis=1)
    shape = block_in.shape
    return (
        block_out.reshape(shape),
        grad_input.reshape(shape),
        conv_shard.transpose(0, 2, 3, 1),
        q_shard.T,
        k_shard.T,
        v_shard.T,
        o_shard.T,
        shards[0],
        shards[1],
        shards[2],
        shards[3],
        shards[4],
        shards[5],
    )


def solution(mesh):
    rows = P("dp", "strip", None, None)
    both = ("dp", "strip")
    in_specs = (rows, rows) + (P(),) * 11
    out_specs = (rows, rows, P(None, None, None, both)) + (P(None, both),) * 4 + (P(both),) * 6
    return jax.shard_map(
        on_device, mesh=mesh, in_specs=in_specs, out_specs=out_specs, check_vma=False
    )
```

```python
import functools
import math

import jax
import jax.numpy as jnp
import numpy as np
from jax import lax
from jax.experimental import pallas as pl
from jax.experimental.pallas import tpu as pltpu
from jax.sharding import PartitionSpec as P

HEADS = 8
GROUPS = 32
EPSILON = 1e-05
F32 = jnp.float32
BF16 = jnp.bfloat16
NT = (((1,), (1,)), ((), ()))
HIGH = lax.Precision.HIGHEST
VMEM_LIMIT = 56 * 1024 * 1024
LOG2E = math.log2(math.e)
QUERY_BLOCK = 1024
KEY_CHUNK = 512
ORDERS = (("y", "x", "z"), ("x", "y", "z"), ("z", "x", "y"))
ENTRIES = 13
LANES = 128
PARTS = ((0, 4), (4, 5), (9, 4))


def params(semantics=None):
    if semantics is None:
        return pltpu.CompilerParams(vmem_limit_bytes=VMEM_LIMIT)
    return pltpu.CompilerParams(
        vmem_limit_bytes=VMEM_LIMIT, dimension_semantics=semantics
    )


def mm(a, b):
    return jnp.dot(a, b, preferred_element_type=F32)


def mm_nt(a, b):
    return lax.dot_general(a, b, NT, preferred_element_type=F32)


def group_sum(rows, expand):
    return lax.dot_general(rows, expand, NT, preferred_element_type=F32, precision=HIGH)


def spread(rows, expand):
    return jnp.dot(rows, expand, preferred_element_type=F32, precision=HIGH)


def expand_matrix(channels):
    per_group = channels // GROUPS
    return jnp.asarray(
        np.arange(channels)[None, :] // per_group == np.arange(LANES)[:, None], F32
    )


def shift_rows(value, down):
    count = value.shape[0]
    row = lax.broadcasted_iota(jnp.int32, value.shape, 0)
    if down == 1:
        return jnp.where(row == 0, 0.0, pltpu.roll(value, 1, 0))
    return jnp.where(row == count - 1, 0.0, pltpu.roll(value, count - 1, 0))


def cost(flops, nbytes, trans=0):
    return pl.CostEstimate(flops=int(flops), bytes_accessed=int(nbytes), transcendentals=int(trans))


def stats_kernel(x_ref, expand_ref, *refs):
    vectors, out_ref, vec_ref = refs[:-2], refs[-2], refs[-1]
    images, cells, channels = x_ref.shape
    count = cells * (channels // GROUPS)
    vec_ref[...] = jnp.zeros_like(vec_ref)
    for i, ref in enumerate(vectors):
        vec_ref[i : i + 1] = ref[...].reshape(1, channels)
    expand = expand_ref[...]
    sums = jnp.concatenate(
        [jnp.sum(x_ref[n].astype(F32), axis=0, keepdims=True) for n in range(images)], axis=0
    )
    mean = group_sum(sums, expand) / count
    mean_c = spread(mean, expand)
    squares = []
    for n in range(images):
        d = x_ref[n].astype(F32) - mean_c[n : n + 1]
        squares.append(jnp.sum(d * d, axis=0, keepdims=True))
    m2 = group_sum(jnp.concatenate(squares, axis=0), expand)
    both = jnp.concatenate([mean, m2], axis=0)
    for s in range(out_ref.shape[0]):
        out_ref[s] = both


def local_stats(x, expand, vectors, strips):
    images, _, channels = x.shape
    return pl.pallas_call(
        stats_kernel,
        out_shape=[
            jax.ShapeDtypeStruct((strips, 2 * images, LANES), F32),
            jax.ShapeDtypeStruct((8, channels), F32),
        ],
        compiler_params=params(),
        cost_estimate=cost(1e7, 7e5),
        name="local_stats",
    )(x, expand, *vectors)


def upstream_kernel(up_ref, w_ref, g_ref):
    images = up_ref.shape[0]
    w = w_ref[...]
    hd = w.shape[0] // HEADS
    for n in range(images):
        g = mm_nt(w, up_ref[n])
        for h in range(HEADS):
            g_ref[n // 2, (n % 2) * HEADS + h] = g[h * hd : (h + 1) * hd].astype(BF16)


def upstream_heads(up, w_out):
    images, cells, channels = up.shape
    return pl.pallas_call(
        upstream_kernel,
        out_shape=jax.ShapeDtypeStruct((images // 2, 2 * HEADS, channels // HEADS, cells), BF16),
        compiler_params=params(),
        cost_estimate=cost(2 * images * cells * channels**2, 2.2e6),
        name="upstream_heads",
    )(up, w_out)


def forward_kernel(
    info_ref,
    stats_ref,
    expand_ref,
    vec_ref,
    x_hbm,
    sib_hbm,
    far_hbm,
    g_hbm,
    conv_hbm,
    wq_hbm,
    wk_hbm,
    wv_hbm,
    hid_own_hbm,
    hid_sib_hbm,
    hid_far_hbm,
    residual_hbm,
    normed_hbm,
    qkv0_hbm,
    qkv1_hbm,
    chan_ref,
    x_ref,
    conv_ref,
    w_ref,
    hidden_ref,
    acc_ref,
    residual_ref,
    normed_ref,
    qkv_ref,
    in_sems,
    out_sems,
):
    _, images, cells, channels = x_ref.shape
    hd = channels // HEADS
    copy = pltpu.make_async_copy
    xs = [copy(h, x_ref.at[i], in_sems.at[i]) for i, h in enumerate((x_hbm, sib_hbm, far_hbm))]
    convs = [copy(conv_hbm.at[:, b], conv_ref.at[b], in_sems.at[3 + b]) for b in range(3)]
    ws = [copy(h, w_ref.at[i], in_sems.at[6 + i]) for i, h in enumerate((wq_hbm, wk_hbm, wv_hbm))]
    qkv_out = (qkv0_hbm, qkv1_hbm)
    gs = [copy(g_hbm.at[c], qkv_ref.at[c, :, 3], in_sems.at[9 + c]) for c in range(2)]
    for task in xs + convs + ws + gs:
        task.start()
    core = info_ref[0]
    strips = stats_ref.shape[0]
    count = cells * (channels // GROUPS)
    got = stats_ref[...]
    means = got[:, :images]
    mean = jnp.sum(means, axis=0) / strips
    off = means - mean[None]
    m2 = jnp.sum(got[:, images:], axis=0) + count * jnp.sum(off * off, axis=0)
    scale = lax.rsqrt(m2 / (count * strips) + EPSILON)
    expand = expand_ref[...]
    mean_c = spread(mean, expand)
    scale_c = spread(scale, expand)
    chan_ref[...] = jnp.concatenate([mean_c, scale_c], axis=0)
    gain = vec_ref[0:1]
    bias = vec_ref[1:2]
    outs = []
    for i, out_hbm in enumerate((hid_own_hbm, hid_sib_hbm, hid_far_hbm)):
        xs[i].wait()
        for n in range(images):
            factor_c = scale_c[n : n + 1] * gain
            u = (x_ref[i, n].astype(F32) - mean_c[n : n + 1]) * factor_c + bias
            h = u * (0.5 + 0.5 * jnp.tanh(0.5 * u))
            if i == 2:
                h = jnp.where(info_ref[1] > 0, h, 0.0)
            hidden_ref[i, n * cells : (n + 1) * cells] = h.astype(BF16)
        outs.append(copy(hidden_ref.at[i], out_hbm, out_sems.at[i]))
        outs[-1].start()

    above = 2 - core
    below = 1 + core
    for b in range(3):
        convs[b].wait()
        total = mm(hidden_ref[0], conv_ref[b, 1])
        total += mm(hidden_ref[above], conv_ref[b, 0])
        total += mm(hidden_ref[below], conv_ref[b, 2])
        if b == 1:
            acc_ref[...] += total
            continue
        for n in range(images):
            sl = slice(n * cells, (n + 1) * cells)
            if b == 0:
                acc_ref[sl] = shift_rows(total[sl], 1)
                continue
            conv = acc_ref[sl] + shift_rows(total[sl], -1)
            residual = (x_ref[0, n].astype(F32) + conv + vec_ref[2:3]).astype(BF16)
            residual_ref[sl] = residual
            tokens = residual.astype(F32)
            dev = tokens - jnp.mean(tokens, axis=1, keepdims=True)
            scale = lax.rsqrt(jnp.mean(dev * dev, axis=1, keepdims=True) + EPSILON)
            normed_ref[sl] = (dev * scale * vec_ref[3:4] + vec_ref[4:5]).astype(BF16)
    outs.append(copy(residual_ref, residual_hbm, out_sems.at[3]))
    outs.append(copy(normed_ref, normed_hbm, out_sems.at[4]))
    outs[-2].start()
    outs[-1].start()
    factor = LOG2E / math.sqrt(hd)
    for task in ws:
        task.wait()
    for c in range(2):
        rows = slice(2 * c * cells, 2 * (c + 1) * cells)
        for t in range(3):
            out = mm(normed_ref[rows], w_ref[t])
            if t == 0:
                out = out * factor
            for n in range(2):
                flipped = out[n * cells : (n + 1) * cells].T.astype(BF16)
                for h in range(HEADS):
                    qkv_ref[c, n * HEADS + h, t] = flipped[h * hd : (h + 1) * hd]
        gs[c].wait()
        outs.append(copy(qkv_ref.at[c], qkv_out[c], out_sems.at[5 + c]))
        outs[-1].start()
    for task in outs:
        task.wait()


def forward(info, stats, expand, vec, x, sib, far, g, conv_weight, wq, wk, wv):
    images, cells, channels = x.shape
    tokens = images * cells
    hd = channels // HEADS
    hbm = pl.BlockSpec(memory_space=pl.ANY)
    vmem = pl.BlockSpec(memory_space=pltpu.VMEM)
    row_type = jax.ShapeDtypeStruct((tokens, channels), BF16)
    qkv_type = jax.ShapeDtypeStruct((2 * HEADS, 4, hd, cells), BF16)
    return pl.pallas_call(
        forward_kernel,
        in_specs=[pl.BlockSpec(memory_space=pltpu.SMEM)] + [vmem] * 3 + [hbm] * 8,
        out_specs=[hbm] * 7 + [vmem],
        out_shape=[row_type] * 5
        + [qkv_type] * 2
        + [jax.ShapeDtypeStruct((2 * images, channels), F32)],
        scratch_shapes=[
            pltpu.VMEM((3, images, cells, channels), BF16),
            pltpu.VMEM((3, 3, channels, channels), BF16),
            pltpu.VMEM((3, channels, channels), BF16),
            pltpu.VMEM((3, tokens, channels), BF16),
            pltpu.VMEM((tokens, channels), F32),
            pltpu.VMEM((tokens, channels), BF16),
            pltpu.VMEM((tokens, channels), BF16),
            pltpu.VMEM((2, 2 * HEADS, 4, hd, cells), BF16),
            pltpu.SemaphoreType.DMA((11,)),
            pltpu.SemaphoreType.DMA((7,)),
        ],
        compiler_params=params(),
        cost_estimate=cost(24 * tokens * channels**2, 20e6, 1e6),
        name="forward_conv",
    )(info, stats, expand, vec, x, sib, far, g, conv_weight, wq, wk, wv)


def together(*tasks):
    results = [None] * len(tasks)
    active = list(enumerate(tasks))
    while active:
        still = []
        for i, task in active:
            try:
                results[i] = next(task)
                still.append((i, task))
            except StopIteration:
                pass
        active = still
    return results


def attention_kernel(
    qkv_ref, out_ref, kt_ref, vt_ref, kn_ref, vn_ref, s_ref, e_ref, dk_ref, dv_ref
):
    step = pl.program_id(0)
    sources, _, hd, cells = qkv_ref.shape
    length = sources * cells
    wide = kn_ref.shape[1]
    block = s_ref.shape[2]
    per = block // cells
    spans = [slice(c, c + KEY_CHUNK) for c in range(0, length, KEY_CHUNK)]
    extra = vt_ref.shape[0] - hd

    @pl.when(step == 0)
    def _():
        ones_row = (lax.broadcasted_iota(jnp.int32, (extra, cells), 0) == 0).astype(F32)
        pad = jnp.zeros((wide - hd, cells), F32)
        row = lax.broadcasted_iota(jnp.int32, (wide - hd, cells), 0)
        ones_two = (row < 2).astype(F32)
        for s in range(sources):
            sl = slice(s * cells, (s + 1) * cells)
            k = qkv_ref[s, 1]
            v = qkv_ref[s, 2]
            kt_ref[:, sl] = k
            vt_ref[:hd, sl] = v
            vt_ref[hd:, sl] = ones_row.astype(BF16)
            kn_ref[sl] = jnp.concatenate([k.astype(F32), pad], axis=0).T.astype(BF16)
            vn_ref[sl] = jnp.concatenate([v.astype(F32), ones_two], axis=0).T.astype(BF16)
        dk_ref[...] = jnp.zeros_like(dk_ref)
        dv_ref[...] = jnp.zeros_like(dv_ref)

    bases = [(2 * step + b) * per for b in range(2)]

    def rows_of(b, t):
        return jnp.concatenate([qkv_ref[bases[b] + u, t] for u in range(per)], axis=1).astype(F32)

    def put(b, t, value):
        for u in range(per):
            out_ref[bases[b] + u, t] = value[:, u * cells : (u + 1) * cells].astype(BF16)

    def scores(b):
        q = jnp.concatenate([rows_of(b, 0), jnp.zeros((wide - hd, block), F32)], axis=0)
        q_t = q.astype(BF16)
        top = None
        for sl in spans:
            value = mm(kn_ref[sl], q_t)
            s_ref[b, sl] = value
            here = jnp.max(value, axis=0, keepdims=True)
            top = here if top is None else jnp.maximum(top, here)
            yield None
        yield top, q.T.astype(BF16)

    def attend(b, top):
        acc = jnp.zeros((hd + extra, block), F32)
        for sl in spans:
            e = jnp.exp2(s_ref[b, sl] - top).astype(BF16)
            e_ref[b, sl] = e
            acc += mm(vt_ref[:, sl], e)
            yield None
        yield acc

    def finish(b, acc):
        inverse = 1.0 / acc[hd : hd + 1]
        out = acc[:hd] * inverse
        put(b, 0, out)
        g = (rows_of(b, 3) * inverse).astype(BF16).astype(F32)
        delta = -jnp.sum(g * out, axis=0, keepdims=True)
        high = delta.astype(BF16).astype(F32)
        low = delta - high
        row = lax.broadcasted_iota(jnp.int32, (wide - hd, block), 0)
        tail = jnp.where(row == 0, high, jnp.where(row == 1, low, 0.0))
        g = jnp.concatenate([g, tail], axis=0)
        return g.astype(BF16), g.T.astype(BF16)

    def back(b, g_t, g_n, q_n):
        dq = jnp.zeros((hd, block), F32)
        for sl in spans:
            e = e_ref[b, sl]
            ds = (e.astype(F32) * mm(vn_ref[sl], g_t)).astype(BF16)
            dq += mm(kt_ref[:, sl], ds)
            dk_ref[sl] += mm(ds, q_n)
            dv_ref[sl] += mm(e, g_n)
            yield None
        put(b, 1, dq * (1.0 / math.sqrt(hd)))
        yield None

    ((top0, q0),) = together(scores(0))
    acc0, (top1, q1) = together(attend(0, top0), scores(1))
    _, acc1 = together(back(0, *finish(0, acc0), q0), attend(1, top1))
    together(back(1, *finish(1, acc1), q1))

    @pl.when(step == pl.num_programs(0) - 1)
    def _():
        for s in range(sources):
            sl = slice(s * cells, (s + 1) * cells)
            out_ref[s, 2] = (dk_ref[sl].T[:hd] * (1.0 / LOG2E)).astype(BF16)
            out_ref[s, 3] = dv_ref[sl].T[:hd].astype(BF16)


def attention(qkv):
    sources, _, hd, cells = qkv.shape
    length = sources * cells
    block = QUERY_BLOCK
    wide = 128
    full = lambda shape: pl.BlockSpec(shape, lambda i: (0,) * len(shape))
    return pl.pallas_call(
        attention_kernel,
        grid=(length // block // 2,),
        in_specs=[full(qkv.shape)],
        out_specs=full((sources, 4, hd, cells)),
        out_shape=jax.ShapeDtypeStruct((sources, 4, hd, cells), BF16),
        scratch_shapes=[
            pltpu.VMEM((hd, length), BF16),
            pltpu.VMEM((hd + 16, length), BF16),
            pltpu.VMEM((length, wide), BF16),
            pltpu.VMEM((length, wide), BF16),
            pltpu.VMEM((2, length, block), F32),
            pltpu.VMEM((2, length, block), BF16),
            pltpu.VMEM((length, wide), F32),
            pltpu.VMEM((length, wide), F32),
        ],
        compiler_params=params(),
        cost_estimate=cost(12 * length * length * 256, 5e6, length * length),
        name="attention",
    )(qkv)


def gather_heads(got_ref, t):
    return jnp.concatenate(
        [
            jnp.concatenate([got_ref[n * HEADS + h, t] for h in range(HEADS)], axis=0)
            for n in range(2)
        ],
        axis=1,
    )


def tokens_kernel(
    got_ref,
    residual_ref,
    up_ref,
    vec_ref,
    wo_ref,
    wq_ref,
    wk_ref,
    wv_ref,
    block_out_ref,
    rg_ref,
    sums_ref,
):
    residual = residual_ref[...].astype(F32)
    up = up_ref[...].astype(F32)
    mixed = mm(gather_heads(got_ref, 0).T, wo_ref[...])
    block_out_ref[...] = (residual + mixed + vec_ref[5:6]).astype(BF16)
    grad = mm_nt(gather_heads(got_ref, 1).T, wq_ref[...])
    grad += mm_nt(gather_heads(got_ref, 2).T, wk_ref[...])
    grad += mm_nt(gather_heads(got_ref, 3).T, wv_ref[...])
    dev = residual - jnp.mean(residual, axis=1, keepdims=True)
    scale = lax.rsqrt(jnp.mean(dev * dev, axis=1, keepdims=True) + EPSILON)
    standard = dev * scale
    scaled = grad * vec_ref[3:4]
    part = scale * (
        scaled
        - jnp.mean(scaled, axis=1, keepdims=True)
        - standard * jnp.mean(scaled * standard, axis=1, keepdims=True)
    )
    rg = (up + part).astype(BF16)
    rg_ref[...] = rg
    sums_ref[0:1] = jnp.sum(rg.astype(F32), axis=0, keepdims=True)
    sums_ref[1:2] = jnp.sum(grad * standard, axis=0, keepdims=True)
    sums_ref[2:3] = jnp.sum(grad, axis=0, keepdims=True)
    sums_ref[3:4] = jnp.sum(up, axis=0, keepdims=True)


def after_attention(got, residual, up, vec, wo, wq, wk, wv, part):
    channels = residual.shape[1]
    cells = got.shape[3]
    tokens = 2 * cells
    full = lambda shape: pl.BlockSpec(shape, lambda i: (0,) * len(shape))
    rows = pl.BlockSpec((tokens, channels), lambda i: (part, 0))
    square = (channels, channels)
    return pl.pallas_call(
        tokens_kernel,
        grid=(1,),
        in_specs=[full(got.shape), rows, rows, full(vec.shape)] + [full(square)] * 4,
        out_specs=[
            full((tokens, channels)),
            full((tokens, channels)),
            full((4, channels)),
        ],
        out_shape=[
            jax.ShapeDtypeStruct((tokens, channels), BF16),
            jax.ShapeDtypeStruct((tokens, channels), BF16),
            jax.ShapeDtypeStruct((4, channels), F32),
        ],
        compiler_params=params(),
        cost_estimate=cost(8 * tokens * channels**2, 7e6),
        name="after_attention",
    )(got, residual, up, vec, wo, wq, wk, wv)


def wait_all(tasks):
    for task in tasks:
        task.wait()


def emitter(gscale, outs_hbm, part_ref, out_ref, out_sems, outs):
    def emit(entry, p, place, value):
        value = value * gscale
        if part_ref is not None:
            value = value + part_ref[entry].astype(F32)
        out_ref[entry] = value.astype(BF16)
        if part_ref is None:
            targets = [(out_ref.at[entry], outs_hbm[0].at[entry])]
        else:
            rows = value.shape[0] // 2
            targets = [
                (out_ref.at[entry, pl.ds(k * rows, rows)], outs_hbm[2 * p + k].at[place])
                for k in range(2)
            ]
        for k, (source, target) in enumerate(targets):
            outs.append(pltpu.make_async_copy(source, target, out_sems.at[entry, k]))
            outs[-1].start()

    return emit


def proj_kernel(gscale, part, last, *refs):
    perm_hbm, got_hbm, got_sib_hbm, normed_hbm, normed_sib_hbm, up_hbm, up_sib_hbm = refs[:7]
    inputs = 8 if last else 7
    part_hbm = refs[7] if last else None
    outs_hbm, scratch = refs[inputs:-10], refs[-10:]
    perm_ref, got_ref, up_ref, left_ref, normed_ref, att_ref, part_ref, out_ref = scratch[:8]
    in_sems, out_sems = scratch[8:]
    copy = pltpu.make_async_copy
    half = normed_ref.shape[0] // 2
    rows = pl.ds(part * half, half)
    places = [pl.ds(u * half, half) for u in range(2)]
    got_in = [
        [
            copy(h.at[:, t], got_ref.at[u, t], in_sems.at[2 * t + u])
            for u, h in enumerate((got_hbm, got_sib_hbm))
        ]
        for t in range(4)
    ]
    perm_in = [copy(perm_hbm, perm_ref, in_sems.at[8])]
    normed_in = [
        copy(h.at[rows], normed_ref.at[places[u]], in_sems.at[9 + u])
        for u, h in enumerate((normed_hbm, normed_sib_hbm))
    ]
    up_in = [
        copy(h.at[rows], up_ref.at[places[u]], in_sems.at[11 + u])
        for u, h in enumerate((up_hbm, up_sib_hbm))
    ]
    part_in = [copy(part_hbm, part_ref, in_sems.at[13])] if last else []
    for tasks in (perm_in, got_in[1], got_in[2], got_in[3], normed_in, part_in, got_in[0], up_in):
        for task in tasks:
            task.start()

    def heads(u, t):
        return jnp.concatenate(
            [
                jnp.concatenate([got_ref[u, t, n * HEADS + h] for h in range(HEADS)], axis=0)
                for n in range(2)
            ],
            axis=1,
        )

    outs = []
    emit = emitter(gscale, outs_hbm, part_ref if last else None, out_ref, out_sems, outs)
    count = perm_ref.shape[1]
    wait_all(perm_in)
    for p in range(3):
        wait_all(got_in[1 + p])
        for u in range(2):
            left_ref[p * count : (p + 1) * count, u * half : (u + 1) * half] = mm(
                perm_ref[p], heads(u, 1 + p)
            ).astype(BF16)
    wait_all(normed_in + part_in)
    value = mm(left_ref[...], normed_ref[...])
    for p in range(3):
        emit(p, p, 3, value[p * count : (p + 1) * count])
    wait_all(got_in[0] + up_in)
    for u in range(2):
        att_ref[u * half : (u + 1) * half] = heads(u, 0).T
    emit(3, 1, 4, mm(mm_nt(perm_ref[1], up_ref[...]).astype(BF16), att_ref[...]))
    wait_all(outs)


def conv_kernel(gscale, part, last, *refs):
    info_ref, perm_hbm, rg_hbm, rg_sib_hbm, own_hbm, sib_hbm, far_hbm, far_sib_hbm = refs[:8]
    inputs = 15 if last else 8
    part_hbm = refs[8] if last else None
    outs_hbm, scratch = refs[inputs:-8], refs[-8:]
    perm_ref, rg_ref, left_ref, right_ref, part_ref, out_ref, in_sems, out_sems = scratch
    copy = pltpu.make_async_copy
    core = info_ref[0]
    half = rg_ref.shape[1]
    rows = pl.ds(part * half, half)
    mine, other = pl.ds(0, half), pl.ds(half, half)
    first_in = [
        copy(perm_hbm, perm_ref, in_sems.at[0]),
        copy(rg_hbm, rg_ref.at[0], in_sems.at[1]),
        copy(rg_sib_hbm, rg_ref.at[1], in_sems.at[2]),
    ]
    hidden_in = [
        copy(own_hbm.at[rows], right_ref.at[1, mine], in_sems.at[3]),
        copy(sib_hbm.at[rows], right_ref.at[2 - 2 * core, mine], in_sems.at[4]),
        copy(far_hbm.at[rows], right_ref.at[2 * core, mine], in_sems.at[5]),
        copy(own_hbm.at[rows], right_ref.at[2 * core, other], in_sems.at[6]),
        copy(sib_hbm.at[rows], right_ref.at[1, other], in_sems.at[7]),
        copy(far_sib_hbm.at[rows], right_ref.at[2 - 2 * core, other], in_sems.at[8]),
    ]
    part_in = [copy(part_hbm, part_ref, in_sems.at[9])] if last else []
    for task in first_in + hidden_in + part_in:
        task.start()
    outs = []
    emit = emitter(gscale, outs_hbm, part_ref if last else None, out_ref, out_sems, outs)
    count = perm_ref.shape[1]
    cells = half // 2
    wait_all(first_in)
    for p in range(3):
        for u in range(2):
            pieces = []
            for n in range(2):
                piece = rg_ref[u, n * cells : (n + 1) * cells]
                if p != 1:
                    piece = shift_rows(piece.astype(F32), p - 1).astype(BF16)
                pieces.append(piece)
            left_ref[p * count : (p + 1) * count, u * half : (u + 1) * half] = mm_nt(
                perm_ref[p], jnp.concatenate(pieces, axis=0)
            ).astype(BF16)
    wait_all(hidden_in + part_in)
    for a in range(3):
        value = mm(left_ref[...], right_ref[a])
        for p in range(3):
            emit(3 * p + a, p, a, value[p * count : (p + 1) * count])
    wait_all(outs)


def part_types(channels, rows):
    types = []
    for _, count in PARTS:
        types += [jax.ShapeDtypeStruct((count, rows // 2, channels), BF16)] * 2
    return types


def proj_grads(gscale, part, perm, ins, partial=None):
    channels = perm.shape[2]
    rows = perm.shape[1]
    got = ins[0]
    tokens = 4 * got.shape[3]
    last = partial is not None
    whole = jax.ShapeDtypeStruct((4, rows, channels), BF16)
    hbm = pl.BlockSpec(memory_space=pl.ANY)
    args = (perm, *ins) + ((partial,) if last else ())
    out_shape = part_types(channels, rows) if last else [whole]
    outs = pl.pallas_call(
        functools.partial(proj_kernel, gscale, part, last),
        in_specs=[hbm] * len(args),
        out_specs=[hbm] * len(out_shape),
        out_shape=out_shape,
        scratch_shapes=[
            pltpu.VMEM(perm.shape, BF16),
            pltpu.VMEM((2, 4) + got.shape[:1] + got.shape[2:], BF16),
            pltpu.VMEM((tokens, channels), BF16),
            pltpu.VMEM((3 * rows, tokens), BF16),
            pltpu.VMEM((tokens, channels), BF16),
            pltpu.VMEM((tokens, channels), BF16),
            pltpu.VMEM(whole.shape, BF16),
            pltpu.VMEM(whole.shape, BF16),
            pltpu.SemaphoreType.DMA((14,)),
            pltpu.SemaphoreType.DMA((4, 2)),
        ],
        compiler_params=params(),
        cost_estimate=cost(16 * rows * tokens * channels, 9e6),
        name="proj_grads",
    )(*args)
    return list(outs) if last else outs[0]


def conv_grads(gscale, part, info, perm, ins, partial=None, parts=()):
    channels = perm.shape[2]
    rows = perm.shape[1]
    tokens = 2 * ins[0].shape[0]
    last = partial is not None
    whole = jax.ShapeDtypeStruct((9, rows, channels), BF16)
    hbm = pl.BlockSpec(memory_space=pl.ANY)
    args = (info, perm, *ins) + ((partial, *parts) if last else ())
    out_shape = part_types(channels, rows) if last else [whole]
    outs = pl.pallas_call(
        functools.partial(conv_kernel, gscale, part, last),
        in_specs=[pl.BlockSpec(memory_space=pltpu.SMEM)] + [hbm] * (len(args) - 1),
        out_specs=[hbm] * len(out_shape),
        out_shape=out_shape,
        input_output_aliases={9 + i: i for i in range(6)} if last else {},
        scratch_shapes=[
            pltpu.VMEM(perm.shape, BF16),
            pltpu.VMEM((2, tokens // 2, channels), BF16),
            pltpu.VMEM((3 * rows, tokens), BF16),
            pltpu.VMEM((3, tokens, channels), BF16),
            pltpu.VMEM(whole.shape, BF16),
            pltpu.VMEM(whole.shape, BF16),
            pltpu.SemaphoreType.DMA((10,)),
            pltpu.SemaphoreType.DMA((9, 2)),
        ],
        compiler_params=params(),
        cost_estimate=cost(24 * rows * tokens * channels, 12e6),
        name="conv_grads",
    )(*args)
    return [list(outs[2 * p : 2 * p + 2]) for p in range(3)] if last else outs[0]


def fold_half_kernel(*refs):
    for p in range(3):
        mine, got, own_ref, send_ref = refs[2 * p], refs[2 * p + 1], refs[6 + 2 * p], refs[7 + 2 * p]
        rows = own_ref.shape[1]
        total = mine[...].astype(F32) + got[...].astype(F32)
        own_ref[...] = total[:, :rows].astype(BF16)
        send_ref[...] = total[:, rows:].astype(BF16)


def fold_half(values):
    shapes = []
    for value in values:
        count, rows, channels = value.shape
        shapes.append(jax.ShapeDtypeStruct((count, rows // 2, channels), BF16))
    return pl.pallas_call(
        fold_half_kernel,
        out_shape=shapes,
        compiler_params=params(),
        cost_estimate=cost(4e6, 8e6),
        name="fold_half",
    )(*values)


def fold_first_kernel(*refs):
    ins, (own_ref, *sends) = refs[:6], refs[6:]
    for p, (first, count) in enumerate(PARTS):
        rows = ins[0].shape[1] // 4
        for e in range(count):
            total = ins[2 * p][e].astype(F32) + ins[2 * p + 1][e].astype(F32)
            own_ref[first + e] = total[:rows]
            place, group = ((e, 0), (e, 1), (PARTS[0][1] + e, 0))[p]
            for k in range(1, 4):
                sends[3 * group + k - 1][place] = total[k * rows : (k + 1) * rows].astype(BF16)


def fold_second_kernel(*refs):
    own_in, got, (own_ref, *sends) = refs[0], refs[1:7], refs[7:]
    rows = own_in.shape[1] // 4
    for p, (first, count) in enumerate(PARTS):
        for e in range(count):
            place, group = ((e, 0), (e, 1), (PARTS[0][1] + e, 0))[p]
            total = own_in[first + e]
            for k in range(3):
                total = total + got[3 * group + k][place].astype(F32)
            own_ref[first + e] = total[:rows]
            place, group = ((e, 0), (PARTS[0][1] + e, 0), (e, 1))[p]
            for k in range(1, 4):
                sends[3 * group + k - 1][place] = total[k * rows : (k + 1) * rows].astype(BF16)


def fold_last_kernel(*refs):
    own_in, got, (conv_ref, q_ref, k_ref, v_ref, o_ref) = refs[0], refs[1:7], refs[7:]
    rows = own_in.shape[1]
    for p, (first, count) in enumerate(PARTS):
        for e in range(count):
            place, group = ((e, 0), (PARTS[0][1] + e, 0), (e, 1))[p]
            total = own_in[first + e]
            for k in range(3):
                total = total + got[3 * group + k][place].astype(F32)
            if e < 3:
                for r in range(rows):
                    conv_ref[e, r, p : p + 1] = total[r : r + 1]
            elif e == 3:
                (q_ref, k_ref, v_ref)[p][...] = total
            else:
                o_ref[...] = total


def fold_first(values):
    _, rows, channels = values[0].shape
    cut = rows // 4
    entries = ENTRIES
    wide = PARTS[0][1] + PARTS[2][1]
    sizes = [wide] * 3 + [PARTS[1][1]] * 3
    return pl.pallas_call(
        fold_first_kernel,
        out_shape=[jax.ShapeDtypeStruct((entries, cut, channels), F32)]
        + [jax.ShapeDtypeStruct((s, cut, channels), BF16) for s in sizes],
        compiler_params=params(),
        cost_estimate=cost(4e6, 7e6),
        name="fold_first",
    )(*values)


def fold_second(values):
    entries, rows, channels = values[0].shape
    cut = rows // 4
    wide = PARTS[0][1] + PARTS[1][1]
    sizes = [wide] * 3 + [PARTS[2][1]] * 3
    return pl.pallas_call(
        fold_second_kernel,
        out_shape=[jax.ShapeDtypeStruct((entries, cut, channels), F32)]
        + [jax.ShapeDtypeStruct((s, cut, channels), BF16) for s in sizes],
        compiler_params=params(),
        cost_estimate=cost(1e6, 2e6),
        name="fold_second",
    )(*values)


def fold_last(values):
    _, rows, channels = values[0].shape
    return pl.pallas_call(
        fold_last_kernel,
        out_shape=[jax.ShapeDtypeStruct((3, rows, 3, channels), F32)]
        + [jax.ShapeDtypeStruct((rows, channels), F32)] * 4,
        compiler_params=params(),
        cost_estimate=cost(3e5, 7e5),
        name="fold_last",
    )(*values)


def coordinates(index):
    dp, strip = index // 16, index % 16
    return {
        "x": dp // 2,
        "z": (strip // 8) * 2 + dp % 2,
        "y": (strip // 2) % 4,
        "core": strip % 2,
    }


def device_index(place):
    dp = place["x"] * 2 + place["z"] % 2
    strip = (place["z"] // 2) * 8 + place["y"] * 2 + place["core"]
    return dp * 16 + strip


def ring_pairs(axis, offset):
    pairs = []
    for source in range(128):
        place = coordinates(source)
        place[axis] = (place[axis] + offset) % 4
        pairs.append((source, device_index(place)))
    return pairs


def row_order(channels, here):
    per = channels // 128
    row = jnp.arange(channels // 2, dtype=jnp.int32)
    r = row % per
    k3 = (row // per) % 4
    k2 = (row // (per * 4)) % 4
    k1 = row // (per * 16)
    flip = (k1 // 2) ^ (3 * (k1 % 2))
    orders = []
    for order in ORDERS:
        place = {"core": here["core"], order[0]: here[order[0]] ^ flip}
        for axis, k in zip(order[1:], (k2, k3)):
            place[axis] = (here[axis] + k) % 4
        orders.append(device_index(place) * per + r)
    return jnp.stack(orders)


def ring_send(value, axis, offset):
    return lax.ppermute(value, ("dp", "strip"), ring_pairs(axis, offset))


def pair_send(value, axis, flip):
    pairs = []
    for source in range(128):
        place = coordinates(source)
        place[axis] = place[axis] ^ flip
        pairs.append((source, device_index(place)))
    return lax.ppermute(value, ("dp", "strip"), pairs)


def ring_sum(joined):
    own, *sends = joined
    values = [own]
    for i, send in enumerate(sends):
        values.append(ring_send(send, ("x", "y")[i // 3], i % 3 + 1))
    own, *sends = fold_second(values)
    values = [own]
    for i, send in enumerate(sends):
        values.append(ring_send(send, ("z", "y")[i // 3], i % 3 + 1))
    return fold_last(values)


def backward_kernel(
    gscale,
    info_ref,
    expand_ref,
    pick_ref,
    rg0_ref,
    rg1_ref,
    sib0_ref,
    sib1_ref,
    far0_ref,
    far1_ref,
    sums0_ref,
    sums1_ref,
    x_ref,
    chan_ref,
    vec_ref,
    conv_ref,
    ag_ref,
    payload_ref,
    rows_ref,
    acc_ref,
):
    step = pl.program_id(0)
    images, cells, channels = x_ref.shape
    half = rg0_ref.shape[0]

    @pl.when(step == 0)
    def _():
        core = info_ref[0]
        rows_ref[1, :half] = rg0_ref[...]
        rows_ref[1, half:] = rg1_ref[...]
        rows_ref[2 * core, :half] = sib0_ref[...]
        rows_ref[2 * core, half:] = sib1_ref[...]
        rows_ref[2 - 2 * core, :half] = far0_ref[...]
        rows_ref[2 - 2 * core, half:] = far1_ref[...]

    total = mm_nt(rows_ref[0], conv_ref[0, 0])
    total += mm_nt(rows_ref[1], conv_ref[1, 0])
    total += mm_nt(rows_ref[2], conv_ref[2, 0])

    @pl.when(step == 0)
    def _():
        for n in range(images):
            sl = slice(n * cells, (n + 1) * cells)
            acc_ref[sl] = shift_rows(total[sl], -1)

    @pl.when(step == 1)
    def _():
        acc_ref[...] += total

    @pl.when(step == 2)
    def _():
        gain = vec_ref[0:1]
        plain, weighted = [], []
        for n in range(images):
            sl = slice(n * cells, (n + 1) * cells)
            grad = acc_ref[sl] + shift_rows(total[sl], 1)
            standard = (x_ref[n].astype(F32) - chan_ref[n : n + 1]) * chan_ref[
                images + n : images + n + 1
            ]
            u = standard * gain + vec_ref[1:2]
            sigma = 0.5 + 0.5 * jnp.tanh(0.5 * u)
            ag = grad * (sigma * (1.0 + u * (1.0 - sigma)))
            ag_ref[sl] = ag
            plain.append(jnp.sum(ag, axis=0, keepdims=True))
            weighted.append(jnp.sum(ag * standard, axis=0, keepdims=True))
        all_totals = group_sum(jnp.concatenate(plain + weighted, axis=0) * gain, expand_ref[...])
        sums = sums0_ref[...] + sums1_ref[...]
        vectors = gscale * jnp.concatenate(
            [sum(weighted), sum(plain), sums, jnp.zeros((2, channels), F32)], axis=0
        )
        pieces = []
        for _ in range(3):
            piece = vectors.astype(BF16)
            pieces.append(piece.astype(F32))
            vectors = vectors - pieces[-1]
        picked = mm(jnp.concatenate(pieces, axis=0).astype(BF16), pick_ref[...])
        count = vectors.shape[0]
        picked = picked[:count] + picked[count : 2 * count] + picked[2 * count :]
        for s in range(payload_ref.shape[0]):
            payload_ref[s] = all_totals + picked[:, s * LANES : (s + 1) * LANES]


def backward(gscale, info, expand, pick, rows, sums, x, chan, vec, conv_weight):
    images, cells, channels = x.shape
    tokens = images * cells
    full = lambda shape: pl.BlockSpec(shape, lambda b: (0,) * len(shape))
    payload = (pick.shape[1] // LANES, 2 * images, LANES)
    ins = (expand, pick, *rows, *sums, x, chan, vec)
    return pl.pallas_call(
        functools.partial(backward_kernel, gscale),
        grid=(3,),
        in_specs=[pl.BlockSpec(memory_space=pltpu.SMEM)]
        + [full(v.shape) for v in ins]
        + [pl.BlockSpec((3, 1, channels, channels), lambda b: (0, b, 0, 0))],
        out_specs=[full((tokens, channels)), full(payload)],
        out_shape=[
            jax.ShapeDtypeStruct((tokens, channels), F32),
            jax.ShapeDtypeStruct(payload, F32),
        ],
        scratch_shapes=[
            pltpu.VMEM((3, tokens, channels), BF16),
            pltpu.VMEM((tokens, channels), F32),
        ],
        compiler_params=params(),
        cost_estimate=cost(18 * tokens * channels**2, 12e6, 4e5),
        name="backward_conv",
    )(info, *ins, conv_weight)


def input_kernel(
    totals_ref, expand_ref, rg0_ref, rg1_ref, ag_ref, x_ref, chan_ref, vec_ref,
    out_ref, spread_ref
):
    images, cells, channels = x_ref.shape
    strips = totals_ref.shape[0]
    count = strips * cells * (channels // GROUPS)
    summed = jnp.sum(totals_ref[...], axis=0)
    for d in range(spread_ref.shape[0]):
        spread_ref[d] = summed
    spread_c = spread(summed / count, expand_ref[...])
    for n in range(images):
        u, m = n // 2, n % 2
        sl = slice(m * cells, (m + 1) * cells)
        scale = chan_ref[images + n : images + n + 1]
        standard = (x_ref[n].astype(F32) - chan_ref[n : n + 1]) * scale
        part = scale * (
            ag_ref[n * cells : (n + 1) * cells] * vec_ref[0:1]
            - spread_c[n : n + 1]
            - standard * spread_c[images + n : images + n + 1]
        )
        rg = (rg0_ref, rg1_ref)[u][sl].astype(F32)
        out_ref[n] = (rg + part).astype(BF16)


def input_grad(totals, expand, rg0, rg1, ag, x, chan, vec, copies):
    return pl.pallas_call(
        input_kernel,
        out_shape=[
            jax.ShapeDtypeStruct(x.shape, BF16),
            jax.ShapeDtypeStruct((copies,) + totals.shape[1:], F32),
        ],
        compiler_params=params(),
        cost_estimate=cost(3e6, 4e6),
        name="input_grad",
    )(totals, expand, rg0, rg1, ag, x, chan, vec)


def exchange(value, axis="strip"):
    return lax.all_to_all(value, axis, split_axis=0, concat_axis=0, tiled=True)


def core_mate(value):
    return lax.ppermute(value, "strip", [(i, i ^ 1) for i in range(16)])


def far_row(value):
    pairs = [(i, i + 1) for i in range(1, 15, 2)]
    return lax.ppermute(value, "strip", pairs + [(j, i) for i, j in pairs])


def pick_matrix(channels, groups_dp, strips):
    per = channels // (groups_dp * strips)
    pick = np.zeros((channels, strips * LANES), np.float32)
    for o in range(channels):
        device, r = divmod(o, per)
        dp, strip = divmod(device, strips)
        pick[o, strip * LANES + GROUPS + dp * per + r] = 1.0
    return jnp.asarray(pick, BF16)


def on_device(
    block_in,
    upstream,
    gn_gain,
    gn_bias,
    conv_weight,
    conv_bias,
    ln_gain,
    ln_bias,
    w_query,
    w_key,
    w_value,
    w_out,
    out_bias,
):
    images, strip_rows, cells, channels = block_in.shape
    strips = lax.axis_size("strip")
    groups_dp = lax.axis_size("dp")
    me = lax.axis_index("strip")
    me_dp = lax.axis_index("dp")
    gscale = 1.0 / math.sqrt(cells * strips * images * groups_dp)
    x = block_in.reshape(images, cells, channels)
    up = upstream.reshape(images, cells, channels)
    up_rows = upstream.reshape(images * cells, channels)
    expand = expand_matrix(channels)
    core = me % 2
    inside = jnp.where(core == 0, me > 0, me < strips - 1)
    info = jnp.stack([core, inside.astype(jnp.int32)]).astype(jnp.int32)
    here = coordinates(me_dp * 16 + me)
    order = row_order(channels, here)
    perm = (order[:, :, None] == jnp.arange(channels, dtype=jnp.int32)).astype(BF16)
    perm, info = lax.optimization_barrier((perm, info))

    x_far = far_row(x)
    x_sib = core_mate(x)
    up_sib = core_mate(up_rows)
    stats, vec = local_stats(
        x, expand, (gn_gain, gn_bias, conv_bias, ln_gain, ln_bias, out_bias), strips
    )
    stats = exchange(stats)
    g = upstream_heads(up, w_out)
    hid_own, hid_sib, hid_far, residual, normed, qkv0, qkv1, chan = forward(
        info, stats, expand, vec, x, x_sib, x_far, g, conv_weight, w_query, w_key, w_value
    )
    hid_far_sib = core_mate(hid_far)
    normed_sib = core_mate(normed)
    att0, qkv1 = lax.optimization_barrier((attention(exchange(qkv0)), exchange(qkv1)))
    got0, att1 = lax.optimization_barrier((exchange(att0), attention(qkv1)))
    got1 = exchange(att1)
    got0_sib = core_mate(got0)
    shared = (residual, up_rows, vec, w_out, w_query, w_key, w_value)
    block_out0, rg0, sums0 = after_attention(got0, *shared, 0)
    rg0_sib, rg0_far = core_mate(rg0), far_row(rg0)
    rows_in = (normed, normed_sib, up_rows, up_sib)
    hidden_in = (hid_own, hid_sib, hid_far, hid_far_sib)
    proj_part = proj_grads(gscale, 0, perm, (got0, got0_sib, *rows_in))
    conv_part = conv_grads(gscale, 0, info, perm, (rg0, rg0_sib, *hidden_in))
    got1, proj_part, conv_part, rg0_far = lax.optimization_barrier(
        (got1, proj_part, conv_part, rg0_far)
    )
    got1_sib = core_mate(got1)
    block_out1, rg1, sums1 = after_attention(got1, *shared, 1)
    rg1_sib, rg1_far = core_mate(rg1), far_row(rg1)
    block_out = jnp.concatenate([block_out0, block_out1], axis=0)
    blocks = proj_grads(gscale, 1, perm, (got1, got1_sib, *rows_in), proj_part)
    rg1_sib, rg1_far, blocks = lax.optimization_barrier((rg1_sib, rg1_far, blocks))
    blocks = conv_grads(gscale, 1, info, perm, (rg1, rg1_sib, *hidden_in), conv_part, blocks)
    pick = pick_matrix(channels, groups_dp, strips)
    sends = [pair_send(blocks[p][1], ORDERS[p][0], 1) for p in range(3)]
    ag, payload = backward(
        gscale,
        info,
        expand,
        pick,
        (rg0, rg1, rg0_sib, rg1_sib, rg0_far, rg1_far),
        (sums0, sums1),
        x,
        chan,
        vec,
        conv_weight,
    )
    sends, ag = lax.optimization_barrier((sends, ag))
    halves = fold_half([v for p in range(3) for v in (blocks[p][0], sends[p])])
    halves, totals = lax.optimization_barrier((halves, exchange(payload)))
    sends = [pair_send(halves[2 * p + 1], ORDERS[p][0], 3) for p in range(3)]
    grad_input, vectors = input_grad(totals, expand, rg0, rg1, ag, x, chan, vec, groups_dp)
    sends, grad_input = lax.optimization_barrier((sends, grad_input))
    joined = fold_first([v for p in range(3) for v in (halves[2 * p], sends[p])])
    joined, vectors = lax.optimization_barrier((joined, exchange(vectors, "dp")))
    conv_shard, q_shard, k_shard, v_shard, o_shard = ring_sum(joined)
    per = channels // (strips * groups_dp)
    vectors = jnp.sum(vectors, axis=0)
    shards = lax.dynamic_slice_in_dim(vectors, GROUPS + me_dp * per, per, axis=1)
    shape = block_in.shape
    return (
        block_out.reshape(shape),
        grad_input.reshape(shape),
        conv_shard.transpose(0, 2, 3, 1),
        q_shard.T,
        k_shard.T,
        v_shard.T,
        o_shard.T,
        shards[0],
        shards[1],
        shards[2],
        shards[3],
        shards[4],
        shards[5],
    )


def solution(mesh):
    rows = P("dp", "strip", None, None)
    both = ("dp", "strip")
    in_specs = (rows, rows) + (P(),) * 11
    out_specs = (rows, rows, P(None, None, None, both)) + (P(None, both),) * 4 + (P(both),) * 6
    return jax.shard_map(
        on_device, mesh=mesh, in_specs=in_specs, out_specs=out_specs, check_vma=False
    )
```

```python
import functools
import math

import jax
import jax.numpy as jnp
import numpy as np
from jax import lax
from jax.experimental import pallas as pl
from jax.experimental.pallas import tpu as pltpu
from jax.sharding import PartitionSpec as P

HEADS = 8
GROUPS = 32
EPSILON = 1e-05
F32 = jnp.float32
BF16 = jnp.bfloat16
NT = (((1,), (1,)), ((), ()))
HIGH = lax.Precision.HIGHEST
VMEM_LIMIT = 56 * 1024 * 1024
LOG2E = math.log2(math.e)
QUERY_BLOCK = 1024
KEY_CHUNK = 512
ORDERS = (("y", "x", "z"), ("x", "y", "z"), ("z", "x", "y"))
ENTRIES = 13
LANES = 128
PARTS = ((0, 4), (4, 5), (9, 4))


def params(semantics=None):
    if semantics is None:
        return pltpu.CompilerParams(vmem_limit_bytes=VMEM_LIMIT)
    return pltpu.CompilerParams(
        vmem_limit_bytes=VMEM_LIMIT, dimension_semantics=semantics
    )


def mm(a, b):
    return jnp.dot(a, b, preferred_element_type=F32)


def mm_nt(a, b):
    return lax.dot_general(a, b, NT, preferred_element_type=F32)


def group_sum(rows, expand):
    return lax.dot_general(rows, expand, NT, preferred_element_type=F32, precision=HIGH)


def spread(rows, expand):
    return jnp.dot(rows, expand, preferred_element_type=F32, precision=HIGH)


def expand_matrix(channels):
    per_group = channels // GROUPS
    return jnp.asarray(
        np.arange(channels)[None, :] // per_group == np.arange(LANES)[:, None], F32
    )


def shift_rows(value, down):
    count = value.shape[0]
    row = lax.broadcasted_iota(jnp.int32, value.shape, 0)
    if down == 1:
        return jnp.where(row == 0, 0.0, pltpu.roll(value, 1, 0))
    return jnp.where(row == count - 1, 0.0, pltpu.roll(value, count - 1, 0))


def cost(flops, nbytes, trans=0):
    return pl.CostEstimate(flops=int(flops), bytes_accessed=int(nbytes), transcendentals=int(trans))


def stats_kernel(x_ref, expand_ref, *refs):
    vectors, out_ref, vec_ref = refs[:-2], refs[-2], refs[-1]
    images, cells, channels = x_ref.shape
    count = cells * (channels // GROUPS)
    vec_ref[...] = jnp.zeros_like(vec_ref)
    for i, ref in enumerate(vectors):
        vec_ref[i : i + 1] = ref[...].reshape(1, channels)
    expand = expand_ref[...]
    sums = jnp.concatenate(
        [jnp.sum(x_ref[n].astype(F32), axis=0, keepdims=True) for n in range(images)], axis=0
    )
    mean = group_sum(sums, expand) / count
    mean_c = spread(mean, expand)
    squares = []
    for n in range(images):
        d = x_ref[n].astype(F32) - mean_c[n : n + 1]
        squares.append(jnp.sum(d * d, axis=0, keepdims=True))
    m2 = group_sum(jnp.concatenate(squares, axis=0), expand)
    both = jnp.concatenate([mean, m2], axis=0)
    for s in range(out_ref.shape[0]):
        out_ref[s] = both


def local_stats(x, expand, vectors, strips):
    images, _, channels = x.shape
    return pl.pallas_call(
        stats_kernel,
        out_shape=[
            jax.ShapeDtypeStruct((strips, 2 * images, LANES), F32),
            jax.ShapeDtypeStruct((8, channels), F32),
        ],
        compiler_params=params(),
        cost_estimate=cost(1e7, 7e5),
        name="local_stats",
    )(x, expand, *vectors)


def upstream_kernel(up_ref, w_ref, g_ref):
    images = up_ref.shape[0]
    w = w_ref[...]
    hd = w.shape[0] // HEADS
    for n in range(images):
        g = mm_nt(w, up_ref[n])
        for h in range(HEADS):
            g_ref[n // 2, (n % 2) * HEADS + h] = g[h * hd : (h + 1) * hd].astype(BF16)


def upstream_heads(up, w_out):
    images, cells, channels = up.shape
    return pl.pallas_call(
        upstream_kernel,
        out_shape=jax.ShapeDtypeStruct((images // 2, 2 * HEADS, channels // HEADS, cells), BF16),
        compiler_params=params(),
        cost_estimate=cost(2 * images * cells * channels**2, 2.2e6),
        name="upstream_heads",
    )(up, w_out)


def forward_kernel(
    info_ref,
    stats_ref,
    expand_ref,
    vec_ref,
    x_hbm,
    sib_hbm,
    far_hbm,
    g_hbm,
    conv_hbm,
    wq_hbm,
    wk_hbm,
    wv_hbm,
    hid_own_hbm,
    hid_sib_hbm,
    hid_far_hbm,
    residual_hbm,
    normed_hbm,
    qkv0_hbm,
    qkv1_hbm,
    chan_ref,
    x_ref,
    conv_ref,
    w_ref,
    hidden_ref,
    acc_ref,
    residual_ref,
    normed_ref,
    qkv_ref,
    in_sems,
    out_sems,
):
    _, images, cells, channels = x_ref.shape
    hd = channels // HEADS
    copy = pltpu.make_async_copy
    xs = [copy(h, x_ref.at[i], in_sems.at[i]) for i, h in enumerate((x_hbm, sib_hbm, far_hbm))]
    convs = [copy(conv_hbm.at[:, b], conv_ref.at[b], in_sems.at[3 + b]) for b in range(3)]
    ws = [copy(h, w_ref.at[i], in_sems.at[6 + i]) for i, h in enumerate((wq_hbm, wk_hbm, wv_hbm))]
    qkv_out = (qkv0_hbm, qkv1_hbm)
    gs = [copy(g_hbm.at[c], qkv_ref.at[c, :, 3], in_sems.at[9 + c]) for c in range(2)]
    for task in xs + convs + ws + gs:
        task.start()
    core = info_ref[0]
    strips = stats_ref.shape[0]
    count = cells * (channels // GROUPS)
    got = stats_ref[...]
    means = got[:, :images]
    mean = jnp.sum(means, axis=0) / strips
    off = means - mean[None]
    m2 = jnp.sum(got[:, images:], axis=0) + count * jnp.sum(off * off, axis=0)
    scale = lax.rsqrt(m2 / (count * strips) + EPSILON)
    expand = expand_ref[...]
    mean_c = spread(mean, expand)
    scale_c = spread(scale, expand)
    chan_ref[...] = jnp.concatenate([mean_c, scale_c], axis=0)
    gain = vec_ref[0:1]
    bias = vec_ref[1:2]
    outs = []
    for i, out_hbm in enumerate((hid_own_hbm, hid_sib_hbm, hid_far_hbm)):
        xs[i].wait()
        for n in range(images):
            factor_c = scale_c[n : n + 1] * gain
            u = (x_ref[i, n].astype(F32) - mean_c[n : n + 1]) * factor_c + bias
            h = u * (0.5 + 0.5 * jnp.tanh(0.5 * u))
            if i == 2:
                h = jnp.where(info_ref[1] > 0, h, 0.0)
            hidden_ref[i, n * cells : (n + 1) * cells] = h.astype(BF16)
        outs.append(copy(hidden_ref.at[i], out_hbm, out_sems.at[i]))
        outs[-1].start()

    above = 2 - core
    below = 1 + core
    for b in range(3):
        convs[b].wait()
        total = mm(hidden_ref[0], conv_ref[b, 1])
        total += mm(hidden_ref[above], conv_ref[b, 0])
        total += mm(hidden_ref[below], conv_ref[b, 2])
        if b == 1:
            acc_ref[...] += total
            continue
        for n in range(images):
            sl = slice(n * cells, (n + 1) * cells)
            if b == 0:
                acc_ref[sl] = shift_rows(total[sl], 1)
                continue
            conv = acc_ref[sl] + shift_rows(total[sl], -1)
            residual = (x_ref[0, n].astype(F32) + conv + vec_ref[2:3]).astype(BF16)
            residual_ref[sl] = residual
            tokens = residual.astype(F32)
            dev = tokens - jnp.mean(tokens, axis=1, keepdims=True)
            scale = lax.rsqrt(jnp.mean(dev * dev, axis=1, keepdims=True) + EPSILON)
            normed_ref[sl] = (dev * scale * vec_ref[3:4] + vec_ref[4:5]).astype(BF16)
    outs.append(copy(residual_ref, residual_hbm, out_sems.at[3]))
    outs.append(copy(normed_ref, normed_hbm, out_sems.at[4]))
    outs[-2].start()
    outs[-1].start()
    factor = LOG2E / math.sqrt(hd)
    for task in ws:
        task.wait()
    for c in range(2):
        rows = slice(2 * c * cells, 2 * (c + 1) * cells)
        for t in range(3):
            out = mm(normed_ref[rows], w_ref[t])
            if t == 0:
                out = out * factor
            for n in range(2):
                flipped = out[n * cells : (n + 1) * cells].T.astype(BF16)
                for h in range(HEADS):
                    qkv_ref[c, n * HEADS + h, t] = flipped[h * hd : (h + 1) * hd]
        gs[c].wait()
        outs.append(copy(qkv_ref.at[c], qkv_out[c], out_sems.at[5 + c]))
        outs[-1].start()
    for task in outs:
        task.wait()


def forward(info, stats, expand, vec, x, sib, far, g, conv_weight, wq, wk, wv):
    images, cells, channels = x.shape
    tokens = images * cells
    hd = channels // HEADS
    hbm = pl.BlockSpec(memory_space=pl.ANY)
    vmem = pl.BlockSpec(memory_space=pltpu.VMEM)
    row_type = jax.ShapeDtypeStruct((tokens, channels), BF16)
    qkv_type = jax.ShapeDtypeStruct((2 * HEADS, 4, hd, cells), BF16)
    return pl.pallas_call(
        forward_kernel,
        in_specs=[pl.BlockSpec(memory_space=pltpu.SMEM)] + [vmem] * 3 + [hbm] * 8,
        out_specs=[hbm] * 7 + [vmem],
        out_shape=[row_type] * 5
        + [qkv_type] * 2
        + [jax.ShapeDtypeStruct((2 * images, channels), F32)],
        scratch_shapes=[
            pltpu.VMEM((3, images, cells, channels), BF16),
            pltpu.VMEM((3, 3, channels, channels), BF16),
            pltpu.VMEM((3, channels, channels), BF16),
            pltpu.VMEM((3, tokens, channels), BF16),
            pltpu.VMEM((tokens, channels), F32),
            pltpu.VMEM((tokens, channels), BF16),
            pltpu.VMEM((tokens, channels), BF16),
            pltpu.VMEM((2, 2 * HEADS, 4, hd, cells), BF16),
            pltpu.SemaphoreType.DMA((11,)),
            pltpu.SemaphoreType.DMA((7,)),
        ],
        compiler_params=params(),
        cost_estimate=cost(24 * tokens * channels**2, 20e6, 1e6),
        name="forward_conv",
    )(info, stats, expand, vec, x, sib, far, g, conv_weight, wq, wk, wv)


def together(*tasks):
    results = [None] * len(tasks)
    active = list(enumerate(tasks))
    while active:
        still = []
        for i, task in active:
            try:
                results[i] = next(task)
                still.append((i, task))
            except StopIteration:
                pass
        active = still
    return results


def attention_kernel(
    qkv_ref, out_ref, kt_ref, vt_ref, kn_ref, vn_ref, s_ref, e_ref, dk_ref, dv_ref
):
    step = pl.program_id(0)
    sources, _, hd, cells = qkv_ref.shape
    length = sources * cells
    wide = kn_ref.shape[1]
    block = s_ref.shape[2]
    per = block // cells
    spans = [slice(c, c + KEY_CHUNK) for c in range(0, length, KEY_CHUNK)]
    extra = vt_ref.shape[0] - hd

    @pl.when(step == 0)
    def _():
        ones_row = (lax.broadcasted_iota(jnp.int32, (extra, cells), 0) == 0).astype(F32)
        pad = jnp.zeros((wide - hd, cells), F32)
        row = lax.broadcasted_iota(jnp.int32, (wide - hd, cells), 0)
        ones_two = (row < 2).astype(F32)
        for s in range(sources):
            sl = slice(s * cells, (s + 1) * cells)
            k = qkv_ref[s, 1]
            v = qkv_ref[s, 2]
            kt_ref[:, sl] = k
            vt_ref[:hd, sl] = v
            vt_ref[hd:, sl] = ones_row.astype(BF16)
            kn_ref[sl] = jnp.concatenate([k.astype(F32), pad], axis=0).T.astype(BF16)
            vn_ref[sl] = jnp.concatenate([v.astype(F32), ones_two], axis=0).T.astype(BF16)
        dk_ref[...] = jnp.zeros_like(dk_ref)
        dv_ref[...] = jnp.zeros_like(dv_ref)

    bases = [(2 * step + b) * per for b in range(2)]

    def rows_of(b, t):
        return jnp.concatenate([qkv_ref[bases[b] + u, t] for u in range(per)], axis=1).astype(F32)

    def put(b, t, value):
        for u in range(per):
            out_ref[bases[b] + u, t] = value[:, u * cells : (u + 1) * cells].astype(BF16)

    def scores(b):
        q = jnp.concatenate([rows_of(b, 0), jnp.zeros((wide - hd, block), F32)], axis=0)
        q_t = q.astype(BF16)
        top = None
        for sl in spans:
            value = mm(kn_ref[sl], q_t)
            s_ref[b, sl] = value
            here = jnp.max(value, axis=0, keepdims=True)
            top = here if top is None else jnp.maximum(top, here)
            yield None
        yield top, q.T.astype(BF16)

    def attend(b, top):
        acc = jnp.zeros((hd + extra, block), F32)
        for sl in spans:
            e = jnp.exp2(s_ref[b, sl] - top).astype(BF16)
            e_ref[b, sl] = e
            acc += mm(vt_ref[:, sl], e)
            yield None
        yield acc

    def finish(b, acc):
        inverse = 1.0 / acc[hd : hd + 1]
        out = acc[:hd] * inverse
        put(b, 0, out)
        g = (rows_of(b, 3) * inverse).astype(BF16).astype(F32)
        delta = -jnp.sum(g * out, axis=0, keepdims=True)
        high = delta.astype(BF16).astype(F32)
        low = delta - high
        row = lax.broadcasted_iota(jnp.int32, (wide - hd, block), 0)
        tail = jnp.where(row == 0, high, jnp.where(row == 1, low, 0.0))
        g = jnp.concatenate([g, tail], axis=0)
        return g.astype(BF16), g.T.astype(BF16)

    def back(b, g_t, g_n, q_n):
        dq = jnp.zeros((hd, block), F32)
        for sl in spans:
            e = e_ref[b, sl]
            ds = (e.astype(F32) * mm(vn_ref[sl], g_t)).astype(BF16)
            dq += mm(kt_ref[:, sl], ds)
            dk_ref[sl] += mm(ds, q_n)
            dv_ref[sl] += mm(e, g_n)
            yield None
        put(b, 1, dq * (1.0 / math.sqrt(hd)))
        yield None

    ((top0, q0),) = together(scores(0))
    acc0, (top1, q1) = together(attend(0, top0), scores(1))
    _, acc1 = together(back(0, *finish(0, acc0), q0), attend(1, top1))
    together(back(1, *finish(1, acc1), q1))

    @pl.when(step == pl.num_programs(0) - 1)
    def _():
        for s in range(sources):
            sl = slice(s * cells, (s + 1) * cells)
            out_ref[s, 2] = (dk_ref[sl].T[:hd] * (1.0 / LOG2E)).astype(BF16)
            out_ref[s, 3] = dv_ref[sl].T[:hd].astype(BF16)


def attention(qkv):
    sources, _, hd, cells = qkv.shape
    length = sources * cells
    block = QUERY_BLOCK
    wide = 128
    full = lambda shape: pl.BlockSpec(shape, lambda i: (0,) * len(shape))
    return pl.pallas_call(
        attention_kernel,
        grid=(length // block // 2,),
        in_specs=[full(qkv.shape)],
        out_specs=full((sources, 4, hd, cells)),
        out_shape=jax.ShapeDtypeStruct((sources, 4, hd, cells), BF16),
        scratch_shapes=[
            pltpu.VMEM((hd, length), BF16),
            pltpu.VMEM((hd + 16, length), BF16),
            pltpu.VMEM((length, wide), BF16),
            pltpu.VMEM((length, wide), BF16),
            pltpu.VMEM((2, length, block), F32),
            pltpu.VMEM((2, length, block), BF16),
            pltpu.VMEM((length, wide), F32),
            pltpu.VMEM((length, wide), F32),
        ],
        compiler_params=params(),
        cost_estimate=cost(12 * length * length * 256, 5e6, length * length),
        name="attention",
    )(qkv)


def gather_heads(got_ref, t):
    return jnp.concatenate(
        [
            jnp.concatenate([got_ref[n * HEADS + h, t] for h in range(HEADS)], axis=0)
            for n in range(2)
        ],
        axis=1,
    )


def tokens_kernel(
    got_ref,
    residual_ref,
    up_ref,
    vec_ref,
    wo_ref,
    wq_ref,
    wk_ref,
    wv_ref,
    block_out_ref,
    rg_ref,
    sums_ref,
):
    residual = residual_ref[...].astype(F32)
    up = up_ref[...].astype(F32)
    mixed = mm(gather_heads(got_ref, 0).T, wo_ref[...])
    block_out_ref[...] = (residual + mixed + vec_ref[5:6]).astype(BF16)
    grad = mm_nt(gather_heads(got_ref, 1).T, wq_ref[...])
    grad += mm_nt(gather_heads(got_ref, 2).T, wk_ref[...])
    grad += mm_nt(gather_heads(got_ref, 3).T, wv_ref[...])
    dev = residual - jnp.mean(residual, axis=1, keepdims=True)
    scale = lax.rsqrt(jnp.mean(dev * dev, axis=1, keepdims=True) + EPSILON)
    standard = dev * scale
    scaled = grad * vec_ref[3:4]
    part = scale * (
        scaled
        - jnp.mean(scaled, axis=1, keepdims=True)
        - standard * jnp.mean(scaled * standard, axis=1, keepdims=True)
    )
    rg = (up + part).astype(BF16)
    rg_ref[...] = rg
    sums_ref[0:1] = jnp.sum(rg.astype(F32), axis=0, keepdims=True)
    sums_ref[1:2] = jnp.sum(grad * standard, axis=0, keepdims=True)
    sums_ref[2:3] = jnp.sum(grad, axis=0, keepdims=True)
    sums_ref[3:4] = jnp.sum(up, axis=0, keepdims=True)


def after_attention(got, residual, up, vec, wo, wq, wk, wv, part):
    channels = residual.shape[1]
    cells = got.shape[3]
    tokens = 2 * cells
    full = lambda shape: pl.BlockSpec(shape, lambda i: (0,) * len(shape))
    rows = pl.BlockSpec((tokens, channels), lambda i: (part, 0))
    square = (channels, channels)
    return pl.pallas_call(
        tokens_kernel,
        grid=(1,),
        in_specs=[full(got.shape), rows, rows, full(vec.shape)] + [full(square)] * 4,
        out_specs=[
            full((tokens, channels)),
            full((tokens, channels)),
            full((4, channels)),
        ],
        out_shape=[
            jax.ShapeDtypeStruct((tokens, channels), BF16),
            jax.ShapeDtypeStruct((tokens, channels), BF16),
            jax.ShapeDtypeStruct((4, channels), F32),
        ],
        compiler_params=params(),
        cost_estimate=cost(8 * tokens * channels**2, 7e6),
        name="after_attention",
    )(got, residual, up, vec, wo, wq, wk, wv)


def wait_all(tasks):
    for task in tasks:
        task.wait()


def emitter(gscale, outs_hbm, part_ref, out_ref, out_sems, outs):
    def emit(entry, p, place, value):
        value = value * gscale
        if part_ref is not None:
            value = value + part_ref[entry].astype(F32)
        out_ref[entry] = value.astype(BF16)
        if len(outs_hbm) == 1:
            targets = [(out_ref.at[entry], outs_hbm[0].at[entry])]
        else:
            rows = value.shape[0] // 2
            targets = [
                (out_ref.at[entry, pl.ds(k * rows, rows)], outs_hbm[2 * p + k].at[place])
                for k in range(2)
            ]
        for k, (source, target) in enumerate(targets):
            outs.append(pltpu.make_async_copy(source, target, out_sems.at[entry, k]))
            outs[-1].start()

    return emit


def proj_kernel(gscale, *refs):
    perm_hbm, *gots_hbm = refs[:5]
    normed_hbm, normed_sib_hbm, up_hbm, up_sib_hbm = refs[5:9]
    outs_hbm, scratch = refs[9:-9], refs[-9:]
    perm_ref, got_ref, up_ref, left_ref, normed_ref, att_ref, out_ref = scratch[:7]
    in_sems, out_sems = scratch[7:]
    copy = pltpu.make_async_copy
    tokens = normed_ref.shape[0] // 2
    half = tokens // 2
    places = [pl.ds(u * tokens, tokens) for u in range(2)]
    got_in = [
        [copy(h.at[:, t], got_ref.at[u, t], in_sems.at[4 * t + u]) for u, h in enumerate(gots_hbm)]
        for t in range(4)
    ]
    perm_in = [copy(perm_hbm, perm_ref, in_sems.at[16])]
    normed_in = [
        copy(h, normed_ref.at[places[u]], in_sems.at[17 + u])
        for u, h in enumerate((normed_hbm, normed_sib_hbm))
    ]
    up_in = [
        copy(h, up_ref.at[places[u]], in_sems.at[19 + u])
        for u, h in enumerate((up_hbm, up_sib_hbm))
    ]
    for tasks in (perm_in, got_in[1], got_in[2], got_in[3], normed_in, got_in[0], up_in):
        for task in tasks:
            task.start()

    def heads(u, t):
        return jnp.concatenate(
            [
                jnp.concatenate([got_ref[u, t, n * HEADS + h] for h in range(HEADS)], axis=0)
                for n in range(2)
            ],
            axis=1,
        )

    outs = []
    emit = emitter(gscale, outs_hbm, None, out_ref, out_sems, outs)
    count = perm_ref.shape[1]
    wait_all(perm_in)
    for p in range(3):
        wait_all(got_in[1 + p])
        for u in range(4):
            left_ref[p * count : (p + 1) * count, u * half : (u + 1) * half] = mm(
                perm_ref[p], heads(u, 1 + p)
            ).astype(BF16)
    wait_all(normed_in)
    value = mm(left_ref[...], normed_ref[...])
    for p in range(3):
        emit(p, p, 3, value[p * count : (p + 1) * count])
    wait_all(got_in[0] + up_in)
    for u in range(4):
        att_ref[u * half : (u + 1) * half] = heads(u, 0).T
    emit(3, 1, 4, mm(mm_nt(perm_ref[1], up_ref[...]).astype(BF16), att_ref[...]))
    wait_all(outs)


def conv_kernel(gscale, part, last, *refs):
    info_ref, perm_hbm, rg_hbm, rg_sib_hbm, own_hbm, sib_hbm, far_hbm, far_sib_hbm = refs[:8]
    inputs = 15 if last else 8
    part_hbm = refs[8] if last else None
    outs_hbm, scratch = refs[inputs:-8], refs[-8:]
    perm_ref, rg_ref, left_ref, right_ref, part_ref, out_ref, in_sems, out_sems = scratch
    copy = pltpu.make_async_copy
    core = info_ref[0]
    half = rg_ref.shape[1]
    rows = pl.ds(part * half, half)
    mine, other = pl.ds(0, half), pl.ds(half, half)
    first_in = [
        copy(perm_hbm, perm_ref, in_sems.at[0]),
        copy(rg_hbm, rg_ref.at[0], in_sems.at[1]),
        copy(rg_sib_hbm, rg_ref.at[1], in_sems.at[2]),
    ]
    hidden_in = [
        copy(own_hbm.at[rows], right_ref.at[1, mine], in_sems.at[3]),
        copy(sib_hbm.at[rows], right_ref.at[2 - 2 * core, mine], in_sems.at[4]),
        copy(far_hbm.at[rows], right_ref.at[2 * core, mine], in_sems.at[5]),
        copy(own_hbm.at[rows], right_ref.at[2 * core, other], in_sems.at[6]),
        copy(sib_hbm.at[rows], right_ref.at[1, other], in_sems.at[7]),
        copy(far_sib_hbm.at[rows], right_ref.at[2 - 2 * core, other], in_sems.at[8]),
    ]
    part_in = [copy(part_hbm, part_ref, in_sems.at[9])] if last else []
    for task in first_in + hidden_in + part_in:
        task.start()
    outs = []
    emit = emitter(gscale, outs_hbm, part_ref if last else None, out_ref, out_sems, outs)
    count = perm_ref.shape[1]
    cells = half // 2
    wait_all(first_in)
    for p in range(3):
        for u in range(2):
            pieces = []
            for n in range(2):
                piece = rg_ref[u, n * cells : (n + 1) * cells]
                if p != 1:
                    piece = shift_rows(piece.astype(F32), p - 1).astype(BF16)
                pieces.append(piece)
            left_ref[p * count : (p + 1) * count, u * half : (u + 1) * half] = mm_nt(
                perm_ref[p], jnp.concatenate(pieces, axis=0)
            ).astype(BF16)
    wait_all(hidden_in + part_in)
    for a in range(3):
        value = mm(left_ref[...], right_ref[a])
        for p in range(3):
            emit(3 * p + a, p, a, value[p * count : (p + 1) * count])
    wait_all(outs)


def part_types(channels, rows):
    types = []
    for _, count in PARTS:
        types += [jax.ShapeDtypeStruct((count, rows // 2, channels), BF16)] * 2
    return types


def proj_grads(gscale, perm, ins):
    channels = perm.shape[2]
    rows = perm.shape[1]
    got = ins[0]
    tokens = 8 * got.shape[3]
    hbm = pl.BlockSpec(memory_space=pl.ANY)
    out_shape = part_types(channels, rows)
    return pl.pallas_call(
        functools.partial(proj_kernel, gscale),
        in_specs=[hbm] * (1 + len(ins)),
        out_specs=[hbm] * len(out_shape),
        out_shape=out_shape,
        scratch_shapes=[
            pltpu.VMEM(perm.shape, BF16),
            pltpu.VMEM((4, 4) + got.shape[:1] + got.shape[2:], BF16),
            pltpu.VMEM((tokens, channels), BF16),
            pltpu.VMEM((3 * rows, tokens), BF16),
            pltpu.VMEM((tokens, channels), BF16),
            pltpu.VMEM((tokens, channels), BF16),
            pltpu.VMEM((4, rows, channels), BF16),
            pltpu.SemaphoreType.DMA((21,)),
            pltpu.SemaphoreType.DMA((4, 2)),
        ],
        compiler_params=params(),
        cost_estimate=cost(16 * rows * tokens * channels, 14e6),
        name="proj_grads",
    )(perm, *ins)


def conv_grads(gscale, part, info, perm, ins, partial=None, parts=()):
    channels = perm.shape[2]
    rows = perm.shape[1]
    tokens = 2 * ins[0].shape[0]
    last = partial is not None
    whole = jax.ShapeDtypeStruct((9, rows, channels), BF16)
    hbm = pl.BlockSpec(memory_space=pl.ANY)
    args = (info, perm, *ins) + ((partial, *parts) if last else ())
    out_shape = part_types(channels, rows) if last else [whole]
    outs = pl.pallas_call(
        functools.partial(conv_kernel, gscale, part, last),
        in_specs=[pl.BlockSpec(memory_space=pltpu.SMEM)] + [hbm] * (len(args) - 1),
        out_specs=[hbm] * len(out_shape),
        out_shape=out_shape,
        input_output_aliases={9 + i: i for i in range(6)} if last else {},
        scratch_shapes=[
            pltpu.VMEM(perm.shape, BF16),
            pltpu.VMEM((2, tokens // 2, channels), BF16),
            pltpu.VMEM((3 * rows, tokens), BF16),
            pltpu.VMEM((3, tokens, channels), BF16),
            pltpu.VMEM(whole.shape, BF16),
            pltpu.VMEM(whole.shape, BF16),
            pltpu.SemaphoreType.DMA((10,)),
            pltpu.SemaphoreType.DMA((9, 2)),
        ],
        compiler_params=params(),
        cost_estimate=cost(24 * rows * tokens * channels, 12e6),
        name="conv_grads",
    )(*args)
    return [list(outs[2 * p : 2 * p + 2]) for p in range(3)] if last else outs[0]


def fold_half_kernel(*refs):
    for p in range(3):
        mine, got, own_ref, send_ref = refs[2 * p], refs[2 * p + 1], refs[6 + 2 * p], refs[7 + 2 * p]
        rows = own_ref.shape[1]
        total = mine[...].astype(F32) + got[...].astype(F32)
        own_ref[...] = total[:, :rows].astype(BF16)
        send_ref[...] = total[:, rows:].astype(BF16)


def fold_half(values):
    shapes = []
    for value in values:
        count, rows, channels = value.shape
        shapes.append(jax.ShapeDtypeStruct((count, rows // 2, channels), BF16))
    return pl.pallas_call(
        fold_half_kernel,
        out_shape=shapes,
        compiler_params=params(),
        cost_estimate=cost(4e6, 8e6),
        name="fold_half",
    )(*values)


def fold_first_kernel(*refs):
    ins, (own_ref, *sends) = refs[:6], refs[6:]
    for p, (first, count) in enumerate(PARTS):
        rows = ins[0].shape[1] // 4
        for e in range(count):
            total = ins[2 * p][e].astype(F32) + ins[2 * p + 1][e].astype(F32)
            own_ref[first + e] = total[:rows]
            place, group = ((e, 0), (e, 1), (PARTS[0][1] + e, 0))[p]
            for k in range(1, 4):
                sends[3 * group + k - 1][place] = total[k * rows : (k + 1) * rows].astype(BF16)


def fold_second_kernel(*refs):
    own_in, got, (own_ref, *sends) = refs[0], refs[1:7], refs[7:]
    rows = own_in.shape[1] // 4
    for p, (first, count) in enumerate(PARTS):
        for e in range(count):
            place, group = ((e, 0), (e, 1), (PARTS[0][1] + e, 0))[p]
            total = own_in[first + e]
            for k in range(3):
                total = total + got[3 * group + k][place].astype(F32)
            own_ref[first + e] = total[:rows]
            place, group = ((e, 0), (PARTS[0][1] + e, 0), (e, 1))[p]
            for k in range(1, 4):
                sends[3 * group + k - 1][place] = total[k * rows : (k + 1) * rows].astype(BF16)


def fold_last_kernel(*refs):
    own_in, got, (conv_ref, q_ref, k_ref, v_ref, o_ref) = refs[0], refs[1:7], refs[7:]
    rows = own_in.shape[1]
    for p, (first, count) in enumerate(PARTS):
        for e in range(count):
            place, group = ((e, 0), (PARTS[0][1] + e, 0), (e, 1))[p]
            total = own_in[first + e]
            for k in range(3):
                total = total + got[3 * group + k][place].astype(F32)
            if e < 3:
                for r in range(rows):
                    conv_ref[e, r, p : p + 1] = total[r : r + 1]
            elif e == 3:
                (q_ref, k_ref, v_ref)[p][...] = total
            else:
                o_ref[...] = total


def fold_first(values):
    _, rows, channels = values[0].shape
    cut = rows // 4
    entries = ENTRIES
    wide = PARTS[0][1] + PARTS[2][1]
    sizes = [wide] * 3 + [PARTS[1][1]] * 3
    return pl.pallas_call(
        fold_first_kernel,
        out_shape=[jax.ShapeDtypeStruct((entries, cut, channels), F32)]
        + [jax.ShapeDtypeStruct((s, cut, channels), BF16) for s in sizes],
        compiler_params=params(),
        cost_estimate=cost(4e6, 7e6),
        name="fold_first",
    )(*values)


def fold_second(values):
    entries, rows, channels = values[0].shape
    cut = rows // 4
    wide = PARTS[0][1] + PARTS[1][1]
    sizes = [wide] * 3 + [PARTS[2][1]] * 3
    return pl.pallas_call(
        fold_second_kernel,
        out_shape=[jax.ShapeDtypeStruct((entries, cut, channels), F32)]
        + [jax.ShapeDtypeStruct((s, cut, channels), BF16) for s in sizes],
        compiler_params=params(),
        cost_estimate=cost(1e6, 2e6),
        name="fold_second",
    )(*values)


def fold_last(values):
    _, rows, channels = values[0].shape
    return pl.pallas_call(
        fold_last_kernel,
        out_shape=[jax.ShapeDtypeStruct((3, rows, 3, channels), F32)]
        + [jax.ShapeDtypeStruct((rows, channels), F32)] * 4,
        compiler_params=params(),
        cost_estimate=cost(3e5, 7e5),
        name="fold_last",
    )(*values)


def coordinates(index):
    dp, strip = index // 16, index % 16
    return {
        "x": dp // 2,
        "z": (strip // 8) * 2 + dp % 2,
        "y": (strip // 2) % 4,
        "core": strip % 2,
    }


def device_index(place):
    dp = place["x"] * 2 + place["z"] % 2
    strip = (place["z"] // 2) * 8 + place["y"] * 2 + place["core"]
    return dp * 16 + strip


def ring_pairs(axis, offset):
    pairs = []
    for source in range(128):
        place = coordinates(source)
        place[axis] = (place[axis] + offset) % 4
        pairs.append((source, device_index(place)))
    return pairs


def row_order(channels, here):
    per = channels // 128
    row = jnp.arange(channels // 2, dtype=jnp.int32)
    r = row % per
    k3 = (row // per) % 4
    k2 = (row // (per * 4)) % 4
    k1 = row // (per * 16)
    flip = (k1 // 2) ^ (3 * (k1 % 2))
    orders = []
    for order in ORDERS:
        place = {"core": here["core"], order[0]: here[order[0]] ^ flip}
        for axis, k in zip(order[1:], (k2, k3)):
            place[axis] = (here[axis] + k) % 4
        orders.append(device_index(place) * per + r)
    return jnp.stack(orders)


def ring_send(value, axis, offset):
    return lax.ppermute(value, ("dp", "strip"), ring_pairs(axis, offset))


def pair_send(value, axis, flip):
    pairs = []
    for source in range(128):
        place = coordinates(source)
        place[axis] = place[axis] ^ flip
        pairs.append((source, device_index(place)))
    return lax.ppermute(value, ("dp", "strip"), pairs)


def ring_sum(joined, vectors):
    own, *sends = joined
    values = [own]
    for i, send in enumerate(sends):
        values.append(ring_send(send, ("x", "y")[i // 3], i % 3 + 1))
    values, vectors = lax.optimization_barrier((values, exchange(vectors, "dp")))
    own, *sends = fold_second(values)
    values = [own]
    for i, send in enumerate(sends):
        values.append(ring_send(send, ("z", "y")[i // 3], i % 3 + 1))
    return fold_last(values), vectors


def backward_kernel(
    gscale,
    info_ref,
    expand_ref,
    pick_ref,
    rg0_ref,
    rg1_ref,
    sib0_ref,
    sib1_ref,
    far0_ref,
    far1_ref,
    sums0_ref,
    sums1_ref,
    x_ref,
    chan_ref,
    vec_ref,
    conv_ref,
    ag_ref,
    payload_ref,
    rows_ref,
    acc_ref,
):
    step = pl.program_id(0)
    images, cells, channels = x_ref.shape
    half = rg0_ref.shape[0]

    @pl.when(step == 0)
    def _():
        core = info_ref[0]
        rows_ref[1, :half] = rg0_ref[...]
        rows_ref[1, half:] = rg1_ref[...]
        rows_ref[2 * core, :half] = sib0_ref[...]
        rows_ref[2 * core, half:] = sib1_ref[...]
        rows_ref[2 - 2 * core, :half] = far0_ref[...]
        rows_ref[2 - 2 * core, half:] = far1_ref[...]

    total = mm_nt(rows_ref[0], conv_ref[0, 0])
    total += mm_nt(rows_ref[1], conv_ref[1, 0])
    total += mm_nt(rows_ref[2], conv_ref[2, 0])

    @pl.when(step == 0)
    def _():
        for n in range(images):
            sl = slice(n * cells, (n + 1) * cells)
            acc_ref[sl] = shift_rows(total[sl], -1)

    @pl.when(step == 1)
    def _():
        acc_ref[...] += total

    @pl.when(step == 2)
    def _():
        gain = vec_ref[0:1]
        plain, weighted = [], []
        for n in range(images):
            sl = slice(n * cells, (n + 1) * cells)
            grad = acc_ref[sl] + shift_rows(total[sl], 1)
            standard = (x_ref[n].astype(F32) - chan_ref[n : n + 1]) * chan_ref[
                images + n : images + n + 1
            ]
            u = standard * gain + vec_ref[1:2]
            sigma = 0.5 + 0.5 * jnp.tanh(0.5 * u)
            ag = grad * (sigma * (1.0 + u * (1.0 - sigma)))
            ag_ref[sl] = ag
            plain.append(jnp.sum(ag, axis=0, keepdims=True))
            weighted.append(jnp.sum(ag * standard, axis=0, keepdims=True))
        all_totals = group_sum(jnp.concatenate(plain + weighted, axis=0) * gain, expand_ref[...])
        sums = sums0_ref[...] + sums1_ref[...]
        vectors = gscale * jnp.concatenate(
            [sum(weighted), sum(plain), sums, jnp.zeros((2, channels), F32)], axis=0
        )
        pieces = []
        for _ in range(3):
            piece = vectors.astype(BF16)
            pieces.append(piece.astype(F32))
            vectors = vectors - pieces[-1]
        picked = mm(jnp.concatenate(pieces, axis=0).astype(BF16), pick_ref[...])
        count = vectors.shape[0]
        picked = picked[:count] + picked[count : 2 * count] + picked[2 * count :]
        for s in range(payload_ref.shape[0]):
            payload_ref[s] = all_totals + picked[:, s * LANES : (s + 1) * LANES]


def backward(gscale, info, expand, pick, rows, sums, x, chan, vec, conv_weight):
    images, cells, channels = x.shape
    tokens = images * cells
    full = lambda shape: pl.BlockSpec(shape, lambda b: (0,) * len(shape))
    payload = (pick.shape[1] // LANES, 2 * images, LANES)
    ins = (expand, pick, *rows, *sums, x, chan, vec)
    return pl.pallas_call(
        functools.partial(backward_kernel, gscale),
        grid=(3,),
        in_specs=[pl.BlockSpec(memory_space=pltpu.SMEM)]
        + [full(v.shape) for v in ins]
        + [pl.BlockSpec((3, 1, channels, channels), lambda b: (0, b, 0, 0))],
        out_specs=[full((tokens, channels)), full(payload)],
        out_shape=[
            jax.ShapeDtypeStruct((tokens, channels), F32),
            jax.ShapeDtypeStruct(payload, F32),
        ],
        scratch_shapes=[
            pltpu.VMEM((3, tokens, channels), BF16),
            pltpu.VMEM((tokens, channels), F32),
        ],
        compiler_params=params(),
        cost_estimate=cost(18 * tokens * channels**2, 12e6, 4e5),
        name="backward_conv",
    )(info, *ins, conv_weight)


def input_kernel(
    totals_ref, expand_ref, rg0_ref, rg1_ref, ag_ref, x_ref, chan_ref, vec_ref,
    out_ref, spread_ref
):
    images, cells, channels = x_ref.shape
    strips = totals_ref.shape[0]
    count = strips * cells * (channels // GROUPS)
    summed = jnp.sum(totals_ref[...], axis=0)
    for d in range(spread_ref.shape[0]):
        spread_ref[d] = summed
    spread_c = spread(summed / count, expand_ref[...])
    for n in range(images):
        u, m = n // 2, n % 2
        sl = slice(m * cells, (m + 1) * cells)
        scale = chan_ref[images + n : images + n + 1]
        standard = (x_ref[n].astype(F32) - chan_ref[n : n + 1]) * scale
        part = scale * (
            ag_ref[n * cells : (n + 1) * cells] * vec_ref[0:1]
            - spread_c[n : n + 1]
            - standard * spread_c[images + n : images + n + 1]
        )
        rg = (rg0_ref, rg1_ref)[u][sl].astype(F32)
        out_ref[n] = (rg + part).astype(BF16)


def input_grad(totals, expand, rg0, rg1, ag, x, chan, vec, copies):
    return pl.pallas_call(
        input_kernel,
        out_shape=[
            jax.ShapeDtypeStruct(x.shape, BF16),
            jax.ShapeDtypeStruct((copies,) + totals.shape[1:], F32),
        ],
        compiler_params=params(),
        cost_estimate=cost(3e6, 4e6),
        name="input_grad",
    )(totals, expand, rg0, rg1, ag, x, chan, vec)


def exchange(value, axis="strip"):
    return lax.all_to_all(value, axis, split_axis=0, concat_axis=0, tiled=True)


def core_mate(value):
    return lax.ppermute(value, "strip", [(i, i ^ 1) for i in range(16)])


def far_row(value):
    pairs = [(i, i + 1) for i in range(1, 15, 2)]
    return lax.ppermute(value, "strip", pairs + [(j, i) for i, j in pairs])


def pick_matrix(channels, groups_dp, strips):
    per = channels // (groups_dp * strips)
    pick = np.zeros((channels, strips * LANES), np.float32)
    for o in range(channels):
        device, r = divmod(o, per)
        dp, strip = divmod(device, strips)
        pick[o, strip * LANES + GROUPS + dp * per + r] = 1.0
    return jnp.asarray(pick, BF16)


def on_device(
    block_in,
    upstream,
    gn_gain,
    gn_bias,
    conv_weight,
    conv_bias,
    ln_gain,
    ln_bias,
    w_query,
    w_key,
    w_value,
    w_out,
    out_bias,
):
    images, strip_rows, cells, channels = block_in.shape
    strips = lax.axis_size("strip")
    groups_dp = lax.axis_size("dp")
    me = lax.axis_index("strip")
    me_dp = lax.axis_index("dp")
    gscale = 1.0 / math.sqrt(cells * strips * images * groups_dp)
    x = block_in.reshape(images, cells, channels)
    up = upstream.reshape(images, cells, channels)
    up_rows = upstream.reshape(images * cells, channels)
    expand = expand_matrix(channels)
    core = me % 2
    inside = jnp.where(core == 0, me > 0, me < strips - 1)
    info = jnp.stack([core, inside.astype(jnp.int32)]).astype(jnp.int32)
    here = coordinates(me_dp * 16 + me)
    order = row_order(channels, here)
    perm = (order[:, :, None] == jnp.arange(channels, dtype=jnp.int32)).astype(BF16)
    perm, info = lax.optimization_barrier((perm, info))

    x_far = far_row(x)
    x_sib = core_mate(x)
    up_sib = core_mate(up_rows)
    stats, vec = local_stats(
        x, expand, (gn_gain, gn_bias, conv_bias, ln_gain, ln_bias, out_bias), strips
    )
    stats = exchange(stats)
    g = upstream_heads(up, w_out)
    hid_own, hid_sib, hid_far, residual, normed, qkv0, qkv1, chan = forward(
        info, stats, expand, vec, x, x_sib, x_far, g, conv_weight, w_query, w_key, w_value
    )
    hid_far_sib = core_mate(hid_far)
    normed_sib = core_mate(normed)
    att0, qkv1 = lax.optimization_barrier((attention(exchange(qkv0)), exchange(qkv1)))
    got0, att1 = lax.optimization_barrier((exchange(att0), attention(qkv1)))
    got1 = exchange(att1)
    got0_sib = core_mate(got0)
    shared = (residual, up_rows, vec, w_out, w_query, w_key, w_value)
    block_out0, rg0, sums0 = after_attention(got0, *shared, 0)
    rg0_sib, rg0_far = core_mate(rg0), far_row(rg0)
    rows_in = (normed, normed_sib, up_rows, up_sib)
    hidden_in = (hid_own, hid_sib, hid_far, hid_far_sib)
    conv_part = conv_grads(gscale, 0, info, perm, (rg0, rg0_sib, *hidden_in))
    got1, conv_part, rg0_far = lax.optimization_barrier((got1, conv_part, rg0_far))
    got1_sib = core_mate(got1)
    block_out1, rg1, sums1 = after_attention(got1, *shared, 1)
    rg1_sib, rg1_far = core_mate(rg1), far_row(rg1)
    block_out = jnp.concatenate([block_out0, block_out1], axis=0)
    blocks = proj_grads(gscale, perm, (got0, got1, got0_sib, got1_sib, *rows_in))
    rg1_sib, rg1_far, blocks = lax.optimization_barrier((rg1_sib, rg1_far, blocks))
    blocks = conv_grads(gscale, 1, info, perm, (rg1, rg1_sib, *hidden_in), conv_part, blocks)
    pick = pick_matrix(channels, groups_dp, strips)
    sends = [pair_send(blocks[p][1], ORDERS[p][0], 1) for p in range(3)]
    ag, payload = backward(
        gscale,
        info,
        expand,
        pick,
        (rg0, rg1, rg0_sib, rg1_sib, rg0_far, rg1_far),
        (sums0, sums1),
        x,
        chan,
        vec,
        conv_weight,
    )
    sends, ag = lax.optimization_barrier((sends, ag))
    halves = fold_half([v for p in range(3) for v in (blocks[p][0], sends[p])])
    halves, totals = lax.optimization_barrier((halves, exchange(payload)))
    sends = [pair_send(halves[2 * p + 1], ORDERS[p][0], 3) for p in range(3)]
    grad_input, vectors = input_grad(totals, expand, rg0, rg1, ag, x, chan, vec, groups_dp)
    sends, grad_input = lax.optimization_barrier((sends, grad_input))
    joined = fold_first([v for p in range(3) for v in (halves[2 * p], sends[p])])
    shards, vectors = ring_sum(joined, vectors)
    conv_shard, q_shard, k_shard, v_shard, o_shard = shards
    per = channels // (strips * groups_dp)
    vectors = jnp.sum(vectors, axis=0)
    shards = lax.dynamic_slice_in_dim(vectors, GROUPS + me_dp * per, per, axis=1)
    shape = block_in.shape
    return (
        block_out.reshape(shape),
        grad_input.reshape(shape),
        conv_shard.transpose(0, 2, 3, 1),
        q_shard.T,
        k_shard.T,
        v_shard.T,
        o_shard.T,
        shards[0],
        shards[1],
        shards[2],
        shards[3],
        shards[4],
        shards[5],
    )


def solution(mesh):
    rows = P("dp", "strip", None, None)
    both = ("dp", "strip")
    in_specs = (rows, rows) + (P(),) * 11
    out_specs = (rows, rows, P(None, None, None, both)) + (P(None, both),) * 4 + (P(both),) * 6
    return jax.shard_map(
        on_device, mesh=mesh, in_specs=in_specs, out_specs=out_specs, check_vma=False
    )
```
